32 devices in a mesh: dp: 16 (over z, y, x), head: 2 (over core).
Axes of the slice: x: 2, y: 2, z: 4, core: 2. Of those that a mesh axis runs over, the one named last changes fastest.
Arguments:
- query_stream: bfloat16 [32768, 512], P('dp'), may hold values from -6 to 6
- kv_stream: bfloat16 [32768, 512], P('dp'), may hold values from -6 to 6
- memory: bfloat16 [32768, 512], P('dp'), may hold values from -6 to 6
- out_grad: bfloat16 [32768, 512], P('dp'), may hold values from -6 to 6
- lengths: int32 [16, 32], P('dp'), may hold values from 1 to 1024, 2048 in all within a row
- obs_rank: int32 [32768], P('dp'), may hold values from 0 to 2047
- obs_count: int32 [32768], P('dp'), may hold values from 0 to 2047
- unit_owner: int32 [256], replicated, may hold values from 0 to 15, as said below
- master: float32 [512, 2, 16, 512], P('dp', 'head'), may hold values from -2 to 2, as said below
- first_moment: float32 [512, 2, 16, 512], P('dp', 'head'), may hold values from -506.85414 to 506.85414
- second_moment: float32 [512, 2, 16, 512], P('dp', 'head'), may hold values from 1310.72 to 64225.28
- norm_master: float32 [4096], P('dp'), may hold values from -0.8 to 1.4
- norm_first: float32 [4096], P('dp'), may hold values from -768 to 768
- norm_second: float32 [4096], P('dp'), may hold values from 65536 to 262144
Outputs:
- output: bfloat16 [32768, 512], P('dp')
- grad_query: bfloat16 [32768, 512], P('dp')
- grad_kv: bfloat16 [32768, 512], P('dp')
- grad_memory: bfloat16 [32768, 512], P('dp')
- weight_grad: float32 [512, 2, 16, 512], P('dp', 'head')
- weight_first: float32 [512, 2, 16, 512], P('dp', 'head')
- weight_second: float32 [512, 2, 16, 512], P('dp', 'head')
- weight_new: float32 [512, 2, 16, 512], P('dp', 'head')
- norm_grad: float32 [4096], P('dp')
- norm_first_new: float32 [4096], P('dp')
- norm_second_new: float32 [4096], P('dp')
- norm_new: float32 [4096], P('dp')
The draws below stay inside these ranges and needn't reach their ends.
Inputs may be any that keep to these rules, and one draw needn't show every extreme that they name: `unit_owner`: every dp index owns at most 32 units and some own exactly 32. `master`: slots that no unit names hold values that are never read.
All inputs are finite; a program needn't handle non-finite values.
Results may differ from the reference program's by a relative error of at most 0.025.
Values may be sent and summed in bfloat16 or wider, within the bound.
A program may use at most 192 MiB of HBM per device.

```python
import math
import jax
import jax.numpy as jnp
import numpy as np
from jax import lax

D = 512
FF = 2048
HEADS = 8
HEAD_DIM = 64
ROW = 2048
DOCS = 32
MOST_LEN = 1024
STEP = 10
UNIT_ROWS = 16
ROWS = 16
TOKENS = 32768
ROWS_W = 4096
UNITS = 256
SLOTS = 32
NORM = 4096
N_DP = 16
N_HEAD = 2


def owner_table(key):
    per_device = UNITS // N_DP
    half_count = N_DP // 2
    tilt = jnp.arange(half_count, dtype=jnp.int32) * per_device // max(half_count - 1, 1)
    by_rank = jnp.stack([per_device + tilt, per_device - tilt], 1).reshape(N_DP).astype(jnp.int32)
    device_order = jax.random.permutation(jax.random.fold_in(key, 101), N_DP)
    counts = jnp.zeros((N_DP,), jnp.int32).at[device_order].set(by_rank)
    unit_places = jnp.arange(UNITS, dtype=jnp.int32)
    holder = jnp.sum((unit_places[:, None] >= jnp.cumsum(counts)[None, :]).astype(jnp.int32), 1)
    shuffle = jax.random.permutation(jax.random.fold_in(key, 102), UNITS)
    return holder[shuffle].astype(jnp.int32)


def slot_units(unit_owner):
    onehot_table = (unit_owner[:, None] == jnp.arange(N_DP, dtype=jnp.int32)[None, :]).astype(jnp.int32)
    before = jnp.cumsum(onehot_table, 0) - onehot_table
    places = unit_owner * SLOTS + jnp.sum(before * onehot_table, 1)
    empty_table = jnp.full((N_DP * SLOTS,), -1, jnp.int32)
    return empty_table.at[places].set(jnp.arange(UNITS, dtype=jnp.int32))


def row_scales(unit_in_slot, table):
    head_cols = D // N_HEAD
    ffn_cols = FF // N_HEAD
    first_row = unit_in_slot * UNIT_ROWS
    slot_scale = jnp.where(first_row < 6 * head_cols, table[0], jnp.where(first_row < 8 * head_cols, table[1], jnp.where(first_row < 8 * head_cols + ffn_cols, table[2], table[3])))
    return jnp.where(unit_in_slot < 0, table[4], slot_scale).astype(jnp.float32)


def gradient_scales(unit_in_slot):
    return row_scales(unit_in_slot, (0.7, 0.2, 0.3, 0.6, 0.2)) * TOKENS ** 0.5


def draw_unit_owner(key, part):
    return owner_table(key)


def draw_master(key, part):
    unit_in_slot = slot_units(owner_table(key))
    key = jax.random.fold_in(key, 7)
    slot_scale = row_scales(unit_in_slot, (D ** (-0.5), 4.0 * D ** (-0.5), D ** (-0.5), FF ** (-0.5), 0.05))
    noise_draw = jax.random.truncated_normal(key, -4.0, 4.0, (N_DP * SLOTS, N_HEAD, UNIT_ROWS, D), jnp.float32)
    return noise_draw * slot_scale[:, None, None, None]


def draw_first_moment(key, part):
    unit_in_slot = slot_units(owner_table(key))
    key = jax.random.fold_in(key, 8)
    noise_draw = jax.random.truncated_normal(key, -4.0, 4.0, (N_DP * SLOTS, N_HEAD, UNIT_ROWS, D), jnp.float32)
    return noise_draw * gradient_scales(unit_in_slot)[:, None, None, None]


def draw_second_moment(key, part):
    unit_in_slot = slot_units(owner_table(key))
    key = jax.random.fold_in(key, 9)
    factor = jnp.exp(jax.random.uniform(key, (N_DP * SLOTS, N_HEAD, UNIT_ROWS, D), jnp.float32, 0.0, jnp.log(4.0)))
    squared = gradient_scales(unit_in_slot) ** 2
    return factor * squared[:, None, None, None]


def draw_norm_master(key, part):
    key = jax.random.fold_in(key, 10)
    gains = jax.random.uniform(jax.random.fold_in(key, 1), (4, D), jnp.float32, 0.6, 1.4)
    shifts = 0.2 * jax.random.truncated_normal(jax.random.fold_in(key, 2), -4.0, 4.0, (4, D), jnp.float32)
    return jnp.stack([gains, shifts], 1).reshape(NORM)


def plant(entries, rng, low, top_value):
    longest = entries.shape.index(max(entries.shape))
    spots = []
    for shift in (0, 1):
        where = [jax.random.randint(jax.random.fold_in(rng, axis), (), 0, length) for axis, length in enumerate(entries.shape)]
        where[longest] = (where[longest] + shift) % entries.shape[longest]
        spots.append(tuple(where))
    return entries.at[spots[0]].set(low).at[spots[1]].set(top_value)


def level_of(rng, dims, cuts, low, high):
    def one(position, parts):
        draws = jax.random.uniform(jax.random.fold_in(jax.random.fold_in(rng, 6), position), (parts,), jnp.float32, low / len(cuts), high / len(cuts))
        return jnp.repeat(jnp.exp(draws), dims[position] // parts).reshape((-1,) + (1,) * (len(dims) - position - 1))

    level = one(*cuts[0])
    for cut in cuts[1:]:
        level = level * one(*cut)
    return level


def split_up(number_of, total, reach, slope):
    portions = [(1 << 20) // math.isqrt(standing ** slope) + 1 for standing in range(2, number_of + 1)]
    spare, holding = total - reach - (number_of - 1), [1] * (number_of - 1)
    while spare > 0:
        candidates = [i for i in range(number_of - 1) if holding[i] < reach]
        whole, budget = sum([portions[i] for i in candidates]), spare
        for i in candidates:
            more = min(reach - holding[i], max(1, budget * portions[i] // whole), spare)
            holding[i] = holding[i] + more
            spare = spare - more
    return np.array([reach] + holding)


def ragged_sizes(key, amount, total, bound, skew):
    if amount == 2:
        one = jax.random.randint(key, (), max(1, total - bound), min(bound, total - 1) + 1)
        return jnp.stack([one, total - one])
    tallies = jnp.asarray(split_up(amount, total, bound, skew), jnp.int32)
    pairs = (amount - 1) // 2
    source_of, sink = tallies[1:1 + 2 * pairs:2], tallies[2:2 + 2 * pairs:2]
    margin = jnp.minimum(source_of - 1, bound - sink)
    moved = jax.random.randint(jax.random.fold_in(key, 1), (pairs,), 0, 1 << 20) % (margin + 1)
    tallies = tallies.at[1:1 + 2 * pairs:2].set(source_of - moved).at[2:2 + 2 * pairs:2].set(sink + moved)
    return tallies[jax.random.permutation(jax.random.fold_in(key, 2), amount)]


def noise(stream_key, extent, width, most, shards=(), kind=jnp.bfloat16):
    gain = level_of(stream_key, extent, shards, -0.22, 0.18) if shards else 1.0
    drawn = jax.random.normal(stream_key, extent, jnp.float32) * width * gain
    return jnp.minimum(jnp.maximum(drawn, -most), most).astype(kind)


def setup_inputs(seed: int = 0) -> dict:
    arg_keys = jax.random.split(jax.random.key(seed), 15)
    return {
        "query_stream": noise(arg_keys[0], (TOKENS, D), 1.0, 6.0, ((0, 16),)),
        "kv_stream": noise(arg_keys[1], (TOKENS, D), 1.0, 6.0, ((0, 16),)),
        "memory": noise(arg_keys[2], (TOKENS, D), 1.0, 6.0, ((0, 16),)),
        "out_grad": noise(arg_keys[3], (TOKENS, D), 1.0, 6.0, ((0, 16),)),
        "lengths": jax.vmap(lambda own: ragged_sizes(own, DOCS, ROW, MOST_LEN, 2))(jax.random.split(arg_keys[4], ROWS)).reshape((ROWS, DOCS)).astype(jnp.int32),
        "obs_rank": plant(jax.random.randint(arg_keys[5], (TOKENS,), 0, ROW), jax.random.fold_in(arg_keys[5], 1), 0, ROW - 1).astype(jnp.int32),
        "obs_count": plant(jax.random.randint(arg_keys[6], (TOKENS,), 0, ROW), jax.random.fold_in(arg_keys[6], 1), 0, ROW - 1).astype(jnp.int32),
        "unit_owner": draw_unit_owner(jax.random.fold_in(arg_keys[14], 71), 0),
        "master": draw_master(jax.random.fold_in(arg_keys[14], 71), 0),
        "first_moment": draw_first_moment(jax.random.fold_in(arg_keys[14], 71), 0),
        "second_moment": draw_second_moment(jax.random.fold_in(arg_keys[14], 71), 0),
        "norm_master": draw_norm_master(jax.random.fold_in(arg_keys[14], 71), 0),
        "norm_first": noise(arg_keys[12], (NORM,), (0.7 * TOKENS ** 0.5), 768.0, ((0, 16),), jnp.float32),
        "norm_second": jnp.clip(jnp.exp(math.log(262144.0) - 1.3862944 * jax.random.uniform(arg_keys[13], (NORM,), jnp.float32) ** level_of(arg_keys[13], (NORM,), ((0, 16),), -0.2, 0.2)), 65536.0, 262144.0),
    }


@jax.custom_vjp
def low(v):
    return lax.optimization_barrier(v.astype(jnp.bfloat16)).astype(jnp.float32)

@jax.custom_vjp
def low_back(v):
    return v

def low_keep(v):
    return (low(v), None)

def low_pass(kept, grad):
    return (grad,)

def back_keep(v):
    return (v, None)

def back_low(kept, grad):
    return (low(grad),)
low.defvjp(low_keep, low_pass)
low_back.defvjp(back_keep, back_low)
EPS_NORM = 1e-05
ADAM_EPS = 1e-08
BETA_ONE = 0.5
BETA_TWO = 0.5
RATE_MATRIX = 0.1
RATE_NORM = 0.3
WEIGHT_DECAY = 0.01
MASKED_SCORE = -1000000000.0
PRECISE = lax.Precision.HIGHEST

def layer_norm(vector, norm_gain, norm_shift):
    row_mean = lax.optimization_barrier(jnp.mean(vector, -1, keepdims=True))
    centred = vector - row_mean
    row_var = lax.optimization_barrier(jnp.mean(centred * centred, -1, keepdims=True))
    return centred * lax.rsqrt(row_var + EPS_NORM) * norm_gain + norm_shift

def slot_places(unit_owner):
    onehot_table = (unit_owner[:, None] == jnp.arange(N_DP, dtype=jnp.int32)[None, :]).astype(jnp.int32)
    before = jnp.cumsum(onehot_table, 0) - onehot_table
    return (unit_owner * SLOTS + lax.optimization_barrier(jnp.sum(before * onehot_table, 1))).astype(jnp.int32)

def split_matrices(flat_rows):
    head_cols = D // N_HEAD
    ffn_cols = FF // N_HEAD
    pieces = [flat_rows[number * head_cols:(number + 1) * head_cols].reshape(D, head_cols) for number in range(6)]
    pieces.append(flat_rows[6 * head_cols:7 * head_cols])
    pieces.append(flat_rows[7 * head_cols:8 * head_cols])
    pieces.append(flat_rows[8 * head_cols:8 * head_cols + ffn_cols].reshape(D, ffn_cols))
    pieces.append(flat_rows[8 * head_cols + ffn_cols:])
    return pieces

def row_layout(row_lengths):
    doc_ends = jnp.cumsum(row_lengths)
    positions = jnp.arange(ROW, dtype=jnp.int32)
    doc_ids = lax.optimization_barrier(jnp.sum((positions[:, None] >= doc_ends[None, :]).astype(jnp.int32), 1))
    doc_match = doc_ids[:, None] == jnp.arange(DOCS, dtype=jnp.int32)[None, :]
    first_pos = lax.optimization_barrier(jnp.sum(jnp.where(doc_match, (doc_ends - row_lengths)[None, :], 0), 1))
    return (positions, doc_ids, first_pos)

def attend(queries, keys, values, allowed):
    query_heads = queries.reshape(ROW, HEADS, HEAD_DIM)
    key_heads = keys.reshape(ROW, HEADS, HEAD_DIM)
    value_heads = values.reshape(ROW, HEADS, HEAD_DIM)
    raw_scores = jnp.einsum('qhe,khe->hqk', query_heads, key_heads, precision=PRECISE)
    scores = jnp.where(allowed[None], low_back(raw_scores) * HEAD_DIM ** (-0.5), MASKED_SCORE)
    largest = lax.optimization_barrier(jnp.max(scores, -1, keepdims=True))
    exponent = jnp.exp(scores - largest)
    attention = low(exponent / lax.optimization_barrier(jnp.sum(exponent, -1, keepdims=True)))
    return jnp.einsum('hqk,khe->qhe', attention, value_heads, precision=PRECISE).reshape(ROW, D)

def project(matrices, shard_inputs, matrix_at):
    return jnp.concatenate([jnp.dot(shard_inputs[shard], matrices[shard][matrix_at], precision=PRECISE) for shard in range(N_HEAD)], 1)

def both_round(vector):
    return low_back(low(vector))

def combine(matrices, mixed_out, matrix_at):
    head_cols = D // N_HEAD
    summed = jnp.zeros((ROW, D), jnp.float32)
    for shard in range(N_HEAD):
        part_cols = mixed_out[:, shard * head_cols:(shard + 1) * head_cols]
        summed = summed + low(jnp.dot(part_cols, matrices[shard][matrix_at], precision=PRECISE))
    return summed

def row_layer(matrices, norm_low, stream_q, stream_kv, source, row_lengths, rank_row, count_row):
    positions, doc_ids, first_pos = row_layout(row_lengths)
    same_doc = doc_ids[:, None] == doc_ids[None, :]
    observed = (positions[None, :] == first_pos[:, None]) | (positions[None, :] != positions[:, None]) & (rank_row[None, :] < count_row[:, None])
    normed_q = low(layer_norm(stream_q, norm_low[0], norm_low[1]))
    normed_kv = low(layer_norm(stream_kv, norm_low[2], norm_low[3]))
    query_inputs = [low_back(normed_q) for shard in range(N_HEAD)]
    kv_inputs = [low_back(normed_kv) for shard in range(N_HEAD)]
    queries = both_round(project(matrices, query_inputs, 0))
    keys = both_round(project(matrices, kv_inputs, 1))
    values = both_round(project(matrices, kv_inputs, 2))
    mixed_self = both_round(attend(queries, keys, values, same_doc & observed))
    residual = stream_q + low_back(combine(matrices, mixed_self, 6))
    normed_c = low(layer_norm(residual, norm_low[4], norm_low[5]))
    cross_inputs = [low_back(normed_c) for shard in range(N_HEAD)]
    source_inputs = [low_back(source) for shard in range(N_HEAD)]
    queries_cross = both_round(project(matrices, cross_inputs, 3))
    keys_cross = both_round(project(matrices, source_inputs, 4))
    values_cross = both_round(project(matrices, source_inputs, 5))
    mixed_cross = both_round(attend(queries_cross, keys_cross, values_cross, same_doc))
    cross_res = residual + low_back(combine(matrices, mixed_cross, 7))
    normed_f = low(layer_norm(cross_res, norm_low[6], norm_low[7]))
    ffn_out = jnp.zeros((ROW, D), jnp.float32)
    for shard in range(N_HEAD):
        pre_act = low_back(jnp.dot(low_back(normed_f), matrices[shard][8], precision=PRECISE))
        activated = low(jax.nn.gelu(pre_act, approximate=False))
        ffn_out = ffn_out + low(jnp.dot(activated, matrices[shard][9], precision=PRECISE))
    return cross_res + low_back(ffn_out)

def adamw_step(gradient, first, second, weight, rate, decay):
    first_new = BETA_ONE * first + (1.0 - BETA_ONE) * gradient
    second_new = BETA_TWO * second + (1.0 - BETA_TWO) * gradient * gradient
    corr_one = 1.0 - BETA_ONE ** STEP
    corr_two = 1.0 - BETA_TWO ** STEP
    direction = first_new / corr_one / (jnp.sqrt(second_new / corr_two) + ADAM_EPS)
    return (first_new, second_new, weight - rate * (direction + decay * weight))

def reference(query_stream, kv_stream, memory, out_grad, lengths, obs_rank, obs_count, unit_owner, master, first_moment, second_moment, norm_master, norm_first, norm_second):
    places = slot_places(unit_owner)
    flat_weights = jnp.transpose(master[places], (1, 0, 2, 3)).reshape(N_HEAD, ROWS_W, D)
    norm_vectors = norm_master.reshape(8, D)

    def forward(flat_w, norm_w, stream_q, stream_kv, source):
        weights = low(flat_w)
        norm_low = low(norm_w)
        matrices = [split_matrices(weights[shard]) for shard in range(N_HEAD)]

        def one_row(row_inputs):
            return row_layer(matrices, norm_low, *row_inputs)
        row_inputs = (stream_q.reshape(ROWS, ROW, D), stream_kv.reshape(ROWS, ROW, D), source.reshape(ROWS, ROW, D), lengths, obs_rank.reshape(ROWS, ROW), obs_count.reshape(ROWS, ROW))
        return lax.map(jax.checkpoint(one_row), row_inputs)
    result, pullback = jax.vjp(forward, flat_weights, norm_vectors, query_stream.astype(jnp.float32), kv_stream.astype(jnp.float32), memory.astype(jnp.float32))
    gradients = pullback(out_grad.astype(jnp.float32).reshape(ROWS, ROW, D))
    output = result.reshape(TOKENS, D).astype(jnp.bfloat16)
    grad_query = gradients[2].astype(jnp.bfloat16)
    grad_kv = gradients[3].astype(jnp.bfloat16)
    grad_memory = gradients[4].astype(jnp.bfloat16)
    unit_grads = jnp.transpose(gradients[0].reshape(N_HEAD, UNITS, UNIT_ROWS, D), (1, 0, 2, 3))
    first_units, second_units, weight_units = adamw_step(unit_grads, first_moment[places], second_moment[places], master[places], RATE_MATRIX, WEIGHT_DECAY)
    empty_slots = jnp.zeros((N_DP * SLOTS, N_HEAD, UNIT_ROWS, D), jnp.float32)
    weight_grad = empty_slots.at[places].set(unit_grads)
    weight_first = empty_slots.at[places].set(first_units)
    weight_second = empty_slots.at[places].set(second_units)
    weight_new = empty_slots.at[places].set(weight_units)
    norm_grad = gradients[1].reshape(NORM)
    norm_first_new, norm_second_new, norm_new = adamw_step(norm_grad, norm_first, norm_second, norm_master, RATE_NORM, 0.0)
    return (output, grad_query, grad_kv, grad_memory, weight_grad, weight_first, weight_second, weight_new, norm_grad, norm_first_new, norm_second_new, norm_new)
```

```python
from functools import partial

import jax
import jax.numpy as jnp
from jax import lax
from jax.experimental import pallas as pl
from jax.experimental.pallas import tpu as pltpu
from jax.sharding import PartitionSpec as P

HEAD_DIM = 64
ROW = 2048
DOCS = 32
STEP = 10


EPS_NORM = 1e-05
ADAM_EPS = 1e-08
BETA_ONE = 0.5
BETA_TWO = 0.5
RATE_MATRIX = 0.1
RATE_NORM = 0.3
WEIGHT_DECAY = 0.01
MASKED_SCORE = -1000000000.0


def layer_norm(vector, norm_gain, norm_shift):
    row_mean = jnp.mean(vector, -1, keepdims=True)
    centred = vector - row_mean
    row_var = jnp.mean(centred * centred, -1, keepdims=True)
    return centred * lax.rsqrt(row_var + EPS_NORM) * norm_gain + norm_shift


def norm_pullback(vector, norm_gain, norm_shift, cotangent):
    unused_value, pullback = jax.vjp(layer_norm, vector, norm_gain, norm_shift)
    return pullback(cotangent)


def product(left_side, right_side):
    return jnp.dot(left_side, right_side, preferred_element_type=jnp.float32)


def inner_rows(left_side, right_side):
    return jnp.einsum("tk,tn->kn", left_side, right_side, preferred_element_type=jnp.float32)


def product_back(left_side, right_side):
    return jnp.einsum("tn,kn->tk", left_side, right_side, preferred_element_type=jnp.float32)


def slot_places(unit_owner, dev_count, slot_count):
    onehot_table = (unit_owner[:, None] == jnp.arange(dev_count, dtype=jnp.int32)[None, :]).astype(
        jnp.int32
    )
    before = jnp.cumsum(onehot_table, 0) - onehot_table
    return unit_owner * slot_count + jnp.sum(before * onehot_table, 1)


def unpack(gathered, places, features, head_shards):
    flat_rows = gathered[places].reshape(-1, features)
    head_cols = features // head_shards
    ffn_cols = (flat_rows.shape[0] - 8 * head_cols) // 2
    pieces = [
        flat_rows[number * head_cols : (number + 1) * head_cols].reshape(features, head_cols)
        for number in range(6)
    ]
    pieces.append(flat_rows[6 * head_cols : 7 * head_cols])
    pieces.append(flat_rows[7 * head_cols : 8 * head_cols])
    pieces.append(flat_rows[8 * head_cols : 8 * head_cols + ffn_cols].reshape(features, ffn_cols))
    pieces.append(flat_rows[8 * head_cols + ffn_cols :])
    return pieces


TQ = 256
TK = 256
FAR = 32768.0
F32 = jnp.float32
BF = jnp.bfloat16

def nt(a, b):
    return lax.dot_general(a, b, (((1,), (1,)), ((), ())), preferred_element_type=F32)

def nn(a, b):
    return lax.dot_general(a, b, (((1,), (0,)), ((), ())), preferred_element_type=F32)

def doc_bounds(len_ref):
    starts = []
    ends = []
    at = jnp.int32(0)
    for d in range(DOCS):
        starts.append(at)
        at = at + len_ref[0, d]
        ends.append(at)
    return starts, ends

def lane_vector(scalars):
    lanes = lax.broadcasted_iota(jnp.int32, (1, 128), 1)
    out = jnp.full((1, 128), -1, jnp.int32)
    for d, value in enumerate(scalars):
        out = jnp.where(lanes == d, value, out)
    return out

def doc_hot_rows(starts, ends, q0):
    pos = lax.broadcasted_iota(jnp.int32, (1, TQ), 1) + q0
    rows = [jnp.where((pos >= starts[d]) & (pos < ends[d]), FAR, 0.0) for d in range(DOCS)]
    return jnp.concatenate(rows, 0)

def key_range(starts, ends, q0):
    low = jnp.int32(0)
    high = jnp.int32(0)
    for d in range(DOCS):
        low = jnp.where(starts[d] <= q0, starts[d], low)
        high = jnp.where(starts[d] <= q0 + TQ - 1, ends[d], high)
    first = lax.div(low, 128) * 128
    steps = lax.div(high - first + TK - 1, TK)
    return first, steps

def head_lanes(pair_rows, h):
    lanes = lax.broadcasted_iota(jnp.int32, pair_rows.shape, 1)
    keep = (lanes < HEAD_DIM) if h % 2 == 0 else (lanes >= HEAD_DIM)
    return jnp.where(keep, pair_rows, jnp.zeros_like(pair_rows))

def doc_hot(start_lane, end_lane, at, rows):
    pos = lax.broadcasted_iota(jnp.int32, (rows, 128), 0) + at
    return (pos >= start_lane) & (pos < end_lane)

def fill_keys(kaug, k_ref, start_lane, end_lane, heads, with_stats):
    lanes = lax.broadcasted_iota(jnp.int32, (TK, 128), 1)
    def one(t, c):
        at = pl.multiple_of(t * TK, TK)
        hot = doc_hot(start_lane, end_lane, at, TK)
        base = jnp.where(hot | (lanes >= DOCS), 0.0, -FAR)
        for h in range(heads):
            pair = k_ref[pl.ds(at, TK), pl.ds(h // 2 * 128, 128)]
            kaug[h, pl.ds(at, TK), 0:128] = (head_lanes(pair, h).astype(F32) * HEAD_DIM ** -0.5).astype(BF)
            aug = base
            if with_stats:
                aug = jnp.where((lanes == 64 + h) | (lanes == 72 + h) | (lanes == 80 + h), -1.0, base)
            kaug[h, pl.ds(at, TK), 128:256] = aug.astype(BF)
        return c
    lax.fori_loop(0, ROW // TK, one, 0)
    for h in range(heads):
        kaug[h, ROW:, 0:128] = jnp.zeros((TK, 128), BF)
        kaug[h, ROW:, 128:256] = jnp.where(lanes < DOCS, -FAR, 0.0).astype(BF)

def fill_ranks(rank_cols, rank_ref, starts):
    pos = lax.broadcasted_iota(jnp.int32, (1, ROW), 1)
    first = jnp.zeros((1, ROW), jnp.bool_)
    for d in range(DOCS):
        first = first | (pos == starts[d])
    rank = jnp.where(first, -1.0, rank_ref[...].astype(F32))
    for t in range(ROW // 128):
        block = jnp.broadcast_to(rank[:, t * 128:(t + 1) * 128], (128, 128))
        rank_cols[t * 128:(t + 1) * 128, :] = block.T
    rank_cols[ROW:, :] = jnp.zeros((TK, 128), F32)

def seen_bias(rank_cols, count_row, k0, q0):
    rank = rank_cols[pl.ds(k0, TK), :]
    rank = jnp.concatenate([rank] * (TQ // 128), 1)
    kpos = lax.broadcasted_iota(jnp.int32, (TK, TQ), 0)
    qpos = lax.broadcasted_iota(jnp.int32, (TK, TQ), 1)
    off_diag = (kpos - qpos) != (q0 - k0)
    allowed = (rank < count_row) & (off_diag | (rank < 0.0))
    return jnp.where(allowed, 0.0, -FAR * FAR)

def attn_fwd_kernel(with_seen, heads, len_ref, q_ref, k_ref, v_ref, rank_ref, count_ref, o_ref, lse_ref,
                    kaug, vt, rank_cols, acc, top, qt):
    starts, ends = doc_bounds(len_ref)
    start_lane, end_lane = lane_vector(starts), lane_vector(ends)
    fill_keys(kaug, k_ref, start_lane, end_lane, heads, False)
    for t in range(ROW // TK):
        vt[:, :HEAD_DIM, t * TK:(t + 1) * TK] = v_ref[t * TK:(t + 1) * TK, :].T.reshape(heads, HEAD_DIM, TK)
    vt[:, :HEAD_DIM, ROW:] = jnp.zeros((heads, HEAD_DIM, TK), BF)
    vt[:, HEAD_DIM:, :] = jnp.ones((heads, 16, ROW + TK), BF)
    if with_seen:
        fill_ranks(rank_cols, rank_ref, starts)

    def one_q(t, c):
        q0 = pl.multiple_of(t * TQ, TQ)
        first, steps = key_range(starts, ends, q0)
        hot = jnp.concatenate([doc_hot_rows(starts, ends, q0), jnp.zeros((128 - DOCS, TQ), F32)], 0).astype(BF)
        for p in range(heads // 2):
            qt[p, 0:128, :] = q_ref[pl.ds(q0, TQ), p * 128:(p + 1) * 128].T
            qt[p, 128:256, :] = hot
        count_row = count_ref[:, pl.ds(q0, TQ)].astype(F32)
        acc[...] = jnp.zeros_like(acc)
        top[...] = jnp.full_like(top, -jnp.inf)

        def one_k(s, c):
            k0 = pl.multiple_of(first + s * TK, 128)
            bias = seen_bias(rank_cols, count_row, k0, q0) if with_seen else None
            old = top[...]
            scores = [nn(kaug[h, pl.ds(k0, TK), :], qt[h // 2]) for h in range(heads)]
            if with_seen:
                scores = [score + bias for score in scores]
            vts = [vt[h, :, pl.ds(k0, TK)] for h in range(heads)]
            accs = [acc[h] for h in range(heads)]
            news, sums = [], []
            for h in range(heads):
                score = scores[h]
                new = jnp.maximum(old[h:h + 1, :], jnp.max(score, 0, keepdims=True))
                p = jnp.exp(score - new).astype(BF)
                news.append(new)
                sums.append(accs[h] * jnp.exp(old[h:h + 1, :] - new) + nn(vts[h], p))
            for h in range(heads):
                acc[h] = sums[h]
            top[...] = jnp.concatenate(news + [old[heads:, :]], 0)
            return c
        lax.fori_loop(0, steps, one_k, 0)
        outs = []
        for h in range(heads):
            a = acc[h]
            total = a[HEAD_DIM:HEAD_DIM + 1, :]
            outs.append(a[:HEAD_DIM, :] / total)
            lse_ref[h:h + 1, pl.ds(q0, TQ)] = top[h:h + 1, :] + jnp.log(total)
        o_ref[pl.ds(q0, TQ), :] = jnp.concatenate(outs, 0).T.astype(BF)
        return c
    lax.fori_loop(0, ROW // TQ, one_q, 0)

def attend_forward(lengths, q, k, v, rank, count, with_seen):
    rows, cols = q.shape
    heads = cols // HEAD_DIM
    V = pl.BlockSpec(memory_space=pltpu.VMEM)
    return pl.pallas_call(
        partial(attn_fwd_kernel, with_seen, heads),
        out_shape=(jax.ShapeDtypeStruct((rows, cols), BF), jax.ShapeDtypeStruct((8, rows), F32)),
        in_specs=[pl.BlockSpec(memory_space=pltpu.SMEM)] + [V] * 5,
        out_specs=(V, V),
        scratch_shapes=[
            pltpu.VMEM((heads, ROW + TK, 256), BF),
            pltpu.VMEM((heads, HEAD_DIM + 16, ROW + TK), BF),
            pltpu.VMEM((ROW + TK, 128), F32),
            pltpu.VMEM((heads, HEAD_DIM + 16, TQ), F32),
            pltpu.VMEM((8, TQ), F32),
            pltpu.VMEM((heads // 2, 256, TQ), BF),
        ],
        compiler_params=pltpu.CompilerParams(vmem_limit_bytes=56 * 2**20),
        name="attend_self_forward" if with_seen else "attend_cross_forward",
    )(lengths, q, k, v, rank, count)

def three_way(value):
    hi = value.astype(BF).astype(F32)
    mid = (value - hi).astype(BF).astype(F32)
    return hi, mid, value - hi - mid

def attn_bwd_kernel(with_seen, heads, len_ref, q_ref, k_ref, v_ref, g_ref, o_ref, lse_ref, rank_ref, count_ref,
                    dq_ref, dk_ref, dv_ref, kaug, vaug, kt, rank_cols, dk_sum, dv_sum, dq_sum, q_diag, g_diag, qt, gt):
    cols = heads * HEAD_DIM
    starts, ends = doc_bounds(len_ref)
    start_lane, end_lane = lane_vector(starts), lane_vector(ends)
    fill_keys(kaug, k_ref, start_lane, end_lane, heads, True)
    lanes = lax.broadcasted_iota(jnp.int32, (TK, 128), 1)
    for h in range(heads):
        picks = (lanes == h) | (lanes == 8 + h) | (lanes == 16 + h)
        side = jnp.where(picks, -1.0, 0.0).astype(BF)
        for t in range(ROW // TK):
            pair = v_ref[t * TK:(t + 1) * TK, h // 2 * 128:h // 2 * 128 + 128]
            vaug[h, t * TK:(t + 1) * TK, 0:128] = head_lanes(pair, h)
            vaug[h, t * TK:(t + 1) * TK, 128:256] = side
        vaug[h, ROW:, :] = jnp.zeros((TK, 256), BF)
    for t in range(ROW // TK):
        kt[:, t * TK:(t + 1) * TK] = k_ref[t * TK:(t + 1) * TK, :].T
    kt[:, ROW:] = jnp.zeros((cols, TK), BF)
    if with_seen:
        fill_ranks(rank_cols, rank_ref, starts)
    dk_sum[...] = jnp.zeros_like(dk_sum)
    dv_sum[...] = jnp.zeros_like(dv_sum)
    sel_row = lax.broadcasted_iota(jnp.int32, (8, cols), 0)
    sel_lane = lax.div(lax.broadcasted_iota(jnp.int32, (8, cols), 1), HEAD_DIM)
    selector = jnp.where(sel_lane == sel_row, 1.0, 0.0).astype(BF)

    def one_q(t, c):
        q0 = pl.multiple_of(t * TQ, TQ)
        first, steps = key_range(starts, ends, q0)
        g = g_ref[pl.ds(q0, TQ), :]
        q = q_ref[pl.ds(q0, TQ), :]
        spread = g.astype(F32) * o_ref[pl.ds(q0, TQ), :].astype(F32)
        spread_hi = spread.astype(BF)
        delta = nt(selector, spread_hi) + nt(selector, (spread - spread_hi.astype(F32)).astype(BF))
        daug = jnp.concatenate(list(three_way(delta)) + [jnp.zeros((104, TQ), F32)], 0).astype(BF)
        lse = lse_ref[:, pl.ds(q0, TQ)]
        hi, mid, lo = three_way(lse)
        side = jnp.concatenate([doc_hot_rows(starts, ends, q0), jnp.zeros((32, TQ), F32), hi, mid, lo, jnp.zeros((40, TQ), F32)], 0).astype(BF)
        for p in range(heads // 2):
            qt[p, 0:128, :] = q[:, p * 128:(p + 1) * 128].T
            qt[p, 128:256, :] = side
            gt[p, 0:128, :] = g[:, p * 128:(p + 1) * 128].T
            gt[p, 128:256, :] = daug
        wide = lax.div(lax.broadcasted_iota(jnp.int32, (TQ, cols), 1), HEAD_DIM)
        for h in range(heads):
            q_diag[h * TQ:(h + 1) * TQ, :] = jnp.where(wide == h, q, jnp.zeros_like(q))
            g_diag[h * TQ:(h + 1) * TQ, :] = jnp.where(wide == h, g, jnp.zeros_like(g))
        count_row = count_ref[:, pl.ds(q0, TQ)].astype(F32)
        dq_sum[...] = jnp.zeros_like(dq_sum)

        def one_k(s, c):
            k0 = pl.multiple_of(first + s * TK, 128)
            bias = seen_bias(rank_cols, count_row, k0, q0) if with_seen else None
            all_ds, all_p, all_dq = [], [], []
            kaugs = [kaug[h, pl.ds(k0, TK), :] for h in range(heads)]
            vaugs = [vaug[h, pl.ds(k0, TK), :] for h in range(heads)]
            keys_t = kt[:, pl.ds(k0, TK)]
            qts = [qt[p] for p in range(heads // 2)]
            gts = [gt[p] for p in range(heads // 2)]
            qd, gd = q_diag[...], g_diag[...]
            scores = [nn(kaugs[h], qts[h // 2]) for h in range(heads)]
            dps = [nn(vaugs[h], gts[h // 2]) for h in range(heads)]
            if with_seen:
                scores = [score + bias for score in scores]
            for h in range(heads):
                p = jnp.exp(scores[h])
                ds = (p * dps[h]).astype(BF)
                all_ds.append(ds)
                all_p.append(p.astype(BF))
                all_dq.append(nn(keys_t[h * HEAD_DIM:(h + 1) * HEAD_DIM, :], ds))
            dk = dk_sum[pl.ds(k0, TK), :] + nn(jnp.concatenate(all_ds, 1), qd)
            dv = dv_sum[pl.ds(k0, TK), :] + nn(jnp.concatenate(all_p, 1), gd)
            dq = dq_sum[...] + jnp.concatenate(all_dq, 0)
            dk_sum[pl.ds(k0, TK), :] = dk
            dv_sum[pl.ds(k0, TK), :] = dv
            dq_sum[...] = dq
            return c
        lax.fori_loop(0, steps, one_k, 0)
        dq_ref[pl.ds(q0, TQ), :] = (dq_sum[...] * HEAD_DIM ** -0.5).T.astype(BF)
        return c
    lax.fori_loop(0, ROW // TQ, one_q, 0)
    dk_ref[...] = (dk_sum[:ROW, :] * HEAD_DIM ** -0.5).astype(BF)
    dv_ref[...] = dv_sum[:ROW, :].astype(BF)

def attend_backward(lengths, q, k, v, g, o, lse, rank, count, with_seen):
    rows, cols = q.shape
    heads = cols // HEAD_DIM
    V = pl.BlockSpec(memory_space=pltpu.VMEM)
    like = jax.ShapeDtypeStruct((rows, cols), BF)
    return pl.pallas_call(
        partial(attn_bwd_kernel, with_seen, heads),
        out_shape=(like, like, like),
        in_specs=[pl.BlockSpec(memory_space=pltpu.SMEM)] + [V] * 8,
        out_specs=(V, V, V),
        scratch_shapes=[
            pltpu.VMEM((heads, ROW + TK, 256), BF),
            pltpu.VMEM((heads, ROW + TK, 256), BF),
            pltpu.VMEM((cols, ROW + TK), BF),
            pltpu.VMEM((ROW + TK, 128), F32),
            pltpu.VMEM((ROW + TK, cols), F32),
            pltpu.VMEM((ROW + TK, cols), F32),
            pltpu.VMEM((cols, TQ), F32),
            pltpu.VMEM((heads * TQ, cols), BF),
            pltpu.VMEM((heads * TQ, cols), BF),
            pltpu.VMEM((heads // 2, 256, TQ), BF),
            pltpu.VMEM((heads // 2, 256, TQ), BF),
        ],
        compiler_params=pltpu.CompilerParams(vmem_limit_bytes=56 * 2**20),
        name="attend_self_backward" if with_seen else "attend_cross_backward",
    )(lengths, q, k, v, g, o, lse, rank, count)


def adamw_step(gradient, first, second, weight, rate, decay):
    first_new = BETA_ONE * first + (1.0 - BETA_ONE) * gradient
    second_new = BETA_TWO * second + (1.0 - BETA_TWO) * gradient * gradient
    corr_one = 1.0 - BETA_ONE**STEP
    corr_two = 1.0 - BETA_TWO**STEP
    direction = first_new / corr_one / (jnp.sqrt(second_new / corr_two) + ADAM_EPS)
    return (first_new, second_new, weight - rate * (direction + decay * weight))


def local(
    query_stream,
    kv_stream,
    memory,
    out_grad,
    lengths,
    obs_rank,
    obs_count,
    unit_owner,
    master,
    first_moment,
    second_moment,
    norm_master,
    norm_first,
    norm_second,
):
    dev_count = lax.axis_size("dp")
    head_shards = lax.axis_size("head")
    my_index = lax.axis_index("dp")
    slot_count = master.shape[0]
    unit_rows = master.shape[2]
    features = query_stream.shape[1]
    unit_total = unit_owner.shape[0]
    places = slot_places(unit_owner, dev_count, slot_count)
    low_master = master.astype(jnp.bfloat16)
    gathered, norm_all = (
        lax.all_gather(low_master, "dp", axis=0, tiled=True),
        lax.all_gather(norm_master.astype(jnp.bfloat16), "dp", axis=0, tiled=True),
    )
    matrices = unpack(gathered, places, features, head_shards)
    norm_params = norm_all.astype(jnp.float32).reshape(8, features)
    rank_row, count_row = obs_rank.reshape(1, ROW), obs_count.reshape(1, ROW)
    stream_q = query_stream.astype(jnp.float32)
    stream_kv = kv_stream.astype(jnp.float32)
    normed_q = layer_norm(stream_q, norm_params[0], norm_params[1]).astype(jnp.bfloat16)
    normed_kv = layer_norm(stream_kv, norm_params[2], norm_params[3]).astype(jnp.bfloat16)
    queries_self = product(normed_q, matrices[0]).astype(jnp.bfloat16)
    keys_self = product(normed_kv, matrices[1]).astype(jnp.bfloat16)
    values_self = product(normed_kv, matrices[2]).astype(jnp.bfloat16)
    mixed_self, totals_self = attend_forward(lengths, queries_self, keys_self, values_self, rank_row, count_row, True)
    self_sum = lax.psum(product(mixed_self, matrices[6]).astype(jnp.bfloat16), "head").astype(
        jnp.float32
    )
    residual = stream_q + self_sum
    normed_c = layer_norm(residual, norm_params[4], norm_params[5]).astype(jnp.bfloat16)
    queries_cross = product(normed_c, matrices[3]).astype(jnp.bfloat16)
    keys_cross = product(memory, matrices[4]).astype(jnp.bfloat16)
    values_cross = product(memory, matrices[5]).astype(jnp.bfloat16)
    mixed_cross, totals_cross = attend_forward(
        lengths, queries_cross, keys_cross, values_cross, rank_row, count_row, False
    )
    cross_sum = lax.psum(product(mixed_cross, matrices[7]).astype(jnp.bfloat16), "head").astype(
        jnp.float32
    )
    cross_res = residual + cross_sum
    normed_f = layer_norm(cross_res, norm_params[6], norm_params[7]).astype(jnp.bfloat16)
    pre_act = product(normed_f, matrices[8])
    hidden = jax.nn.gelu(pre_act, approximate=False).astype(jnp.bfloat16)
    ffn_sum = lax.psum(product(hidden, matrices[9]).astype(jnp.bfloat16), "head").astype(
        jnp.float32
    )
    output = (cross_res + ffn_sum).astype(jnp.bfloat16)
    grad_w2 = inner_rows(hidden, out_grad)
    grad_hidden = product_back(out_grad, matrices[9])
    unused_value, gelu_pull = jax.vjp(partial(jax.nn.gelu, approximate=False), pre_act)
    grad_pre = gelu_pull(grad_hidden)[0].astype(jnp.bfloat16)
    grad_w1 = inner_rows(normed_f, grad_pre)
    normed_f_grad = lax.psum(
        product_back(grad_pre, matrices[8]).astype(jnp.bfloat16), "head"
    ).astype(jnp.float32)
    grad_cross_res, gain_f, shift_f = norm_pullback(
        cross_res, norm_params[6], norm_params[7], normed_f_grad
    )
    grad_cross_res = grad_cross_res + out_grad.astype(jnp.float32)
    cross_low = grad_cross_res.astype(jnp.bfloat16)
    grad_wo_cross = inner_rows(mixed_cross, cross_low)
    grad_mixed_cross = product_back(cross_low, matrices[7]).astype(jnp.bfloat16)
    grad_q_cross, grad_k_cross, grad_v_cross = attend_backward(
        lengths, queries_cross, keys_cross, values_cross, grad_mixed_cross, mixed_cross, totals_cross, rank_row, count_row, False
    )
    grad_wq_cross = inner_rows(normed_c, grad_q_cross)
    grad_wk_cross = inner_rows(memory, grad_k_cross)
    grad_wv_cross = inner_rows(memory, grad_v_cross)
    normed_c_grad, memory_sum = (
        lax.psum(product_back(grad_q_cross, matrices[3]).astype(jnp.bfloat16), "head").astype(
            jnp.float32
        ),
        lax.psum(
            (
                product_back(grad_k_cross, matrices[4]) + product_back(grad_v_cross, matrices[5])
            ).astype(jnp.bfloat16),
            "head",
        ).astype(jnp.float32),
    )
    grad_residual, gain_c, shift_c = norm_pullback(
        residual, norm_params[4], norm_params[5], normed_c_grad
    )
    grad_residual = grad_residual + grad_cross_res
    self_low = grad_residual.astype(jnp.bfloat16)
    grad_wo_self = inner_rows(mixed_self, self_low)
    grad_mixed_self = product_back(self_low, matrices[6]).astype(jnp.bfloat16)
    grad_q_self, grad_k_self, grad_v_self = attend_backward(
        lengths, queries_self, keys_self, values_self, grad_mixed_self, mixed_self, totals_self, rank_row, count_row, True
    )
    grad_wq_self = inner_rows(normed_q, grad_q_self)
    grad_wk_self = inner_rows(normed_kv, grad_k_self)
    grad_wv_self = inner_rows(normed_kv, grad_v_self)
    normed_q_grad, normed_kv_grad = (
        lax.psum(product_back(grad_q_self, matrices[0]).astype(jnp.bfloat16), "head").astype(
            jnp.float32
        ),
        lax.psum(
            (
                product_back(grad_k_self, matrices[1]) + product_back(grad_v_self, matrices[2])
            ).astype(jnp.bfloat16),
            "head",
        ).astype(jnp.float32),
    )
    grad_stream_q, gain_q, shift_q = norm_pullback(
        stream_q, norm_params[0], norm_params[1], normed_q_grad
    )
    grad_stream_kv, gain_kv, shift_kv = norm_pullback(
        stream_kv, norm_params[2], norm_params[3], normed_kv_grad
    )
    grad_query = (grad_stream_q + grad_residual).astype(jnp.bfloat16)
    grad_kv = grad_stream_kv.astype(jnp.bfloat16)
    grad_memory = memory_sum.astype(jnp.bfloat16)
    grad_list = [
        grad_wq_self,
        grad_wk_self,
        grad_wv_self,
        grad_wq_cross,
        grad_wk_cross,
        grad_wv_cross,
        grad_wo_self,
        grad_wo_cross,
        grad_w1,
        grad_w2,
    ]
    flat_grads = jnp.concatenate([piece.reshape(-1, features) for piece in grad_list], 0)
    unit_grads = flat_grads.reshape(unit_total, 1, unit_rows, features)
    norm_grads = jnp.stack(
        [gain_q, shift_q, gain_kv, shift_kv, gain_c, shift_c, gain_f, shift_f]
    ).reshape(-1)
    outgoing = (
        jnp.zeros((dev_count * slot_count, 1, unit_rows, features), jnp.float32)
        .at[places]
        .set(unit_grads)
    )
    slot_grads, norm_share = (
        lax.psum_scatter(outgoing, "dp", scatter_dimension=0, tiled=True),
        lax.psum_scatter(norm_grads, "dp", scatter_dimension=0, tiled=True),
    )
    owned_count = jnp.sum((unit_owner == my_index).astype(jnp.int32))
    slot_live = (jnp.arange(slot_count, dtype=jnp.int32) < owned_count)[:, None, None, None]
    slot_grads = jnp.where(slot_live, slot_grads, 0.0)
    first_new, second_new, weight_updated = adamw_step(
        slot_grads, first_moment, second_moment, master, RATE_MATRIX, WEIGHT_DECAY
    )
    weight_first = jnp.where(slot_live, first_new, 0.0)
    weight_second = jnp.where(slot_live, second_new, 0.0)
    weight_new = jnp.where(slot_live, weight_updated, 0.0)
    norm_first_new, norm_second_new, norm_new = adamw_step(
        norm_share, norm_first, norm_second, norm_master, RATE_NORM, 0.0
    )
    return (
        output,
        grad_query,
        grad_kv,
        grad_memory,
        slot_grads,
        weight_first,
        weight_second,
        weight_new,
        norm_share,
        norm_first_new,
        norm_second_new,
        norm_new,
    )


def solution(mesh):
    in_specs = (
        P("dp", None),
        P("dp", None),
        P("dp", None),
        P("dp", None),
        P("dp", None),
        P("dp"),
        P("dp"),
        P(),
        P("dp", "head", None, None),
        P("dp", "head", None, None),
        P("dp", "head", None, None),
        P("dp"),
        P("dp"),
        P("dp"),
    )
    out_specs = (
        P("dp", None),
        P("dp", None),
        P("dp", None),
        P("dp", None),
        P("dp", "head", None, None),
        P("dp", "head", None, None),
        P("dp", "head", None, None),
        P("dp", "head", None, None),
        P("dp"),
        P("dp"),
        P("dp"),
        P("dp"),
    )
    return jax.shard_map(local, mesh=mesh, in_specs=in_specs, out_specs=out_specs, check_vma=False)
```

```python
from functools import partial

import jax
import jax.numpy as jnp
from jax import lax
from jax.experimental import pallas as pl
from jax.experimental.pallas import tpu as pltpu
from jax.sharding import PartitionSpec as P

HEAD_DIM = 64
ROW = 2048
DOCS = 32
STEP = 10
UNIT = 16

EPS_NORM = 1e-05
ADAM_EPS = 1e-08
BETA_ONE = 0.5
BETA_TWO = 0.5
RATE_MATRIX = 0.1
RATE_NORM = 0.3
WEIGHT_DECAY = 0.01

F32 = jnp.float32
BF = jnp.bfloat16
TQ = 256
TK = 256
FAR = 32768.0

def nt(a, b):
    return lax.dot_general(a, b, (((1,), (1,)), ((), ())), preferred_element_type=F32)

def nn(a, b):
    return lax.dot_general(a, b, (((1,), (0,)), ((), ())), preferred_element_type=F32)

def doc_bounds(len_ref):
    starts = []
    ends = []
    at = jnp.int32(0)
    for d in range(DOCS):
        starts.append(at)
        at = at + len_ref[0, d]
        ends.append(at)
    return starts, ends

def lane_vector(scalars):
    lanes = lax.broadcasted_iota(jnp.int32, (1, 128), 1)
    out = jnp.full((1, 128), -1, jnp.int32)
    for d, value in enumerate(scalars):
        out = jnp.where(lanes == d, value, out)
    return out

def doc_hot_rows(starts, ends, q0):
    pos = lax.broadcasted_iota(jnp.int32, (1, TQ), 1) + q0
    rows = [jnp.where((pos >= starts[d]) & (pos < ends[d]), FAR, 0.0) for d in range(DOCS)]
    return jnp.concatenate(rows, 0)

def key_range(starts, ends, q0):
    low = jnp.int32(0)
    high = jnp.int32(0)
    for d in range(DOCS):
        low = jnp.where(starts[d] <= q0, starts[d], low)
        high = jnp.where(starts[d] <= q0 + TQ - 1, ends[d], high)
    first = lax.div(low, 128) * 128
    steps = lax.div(high - first + TK - 1, TK)
    return first, steps

def head_lanes(pair_rows, h):
    lanes = lax.broadcasted_iota(jnp.int32, pair_rows.shape, 1)
    keep = (lanes < HEAD_DIM) if h % 2 == 0 else (lanes >= HEAD_DIM)
    return jnp.where(keep, pair_rows, jnp.zeros_like(pair_rows))

def doc_hot(start_lane, end_lane, at, rows):
    pos = lax.broadcasted_iota(jnp.int32, (rows, 128), 0) + at
    return (pos >= start_lane) & (pos < end_lane)

def fill_keys(kaug, k_ref, start_lane, end_lane, heads, with_stats):
    lanes = lax.broadcasted_iota(jnp.int32, (TK, 128), 1)
    def one(t, c):
        at = pl.multiple_of(t * TK, TK)
        hot = doc_hot(start_lane, end_lane, at, TK)
        base = jnp.where(hot | (lanes >= DOCS), 0.0, -FAR)
        for h in range(heads):
            pair = k_ref[pl.ds(at, TK), pl.ds(h // 2 * 128, 128)]
            kaug[h, pl.ds(at, TK), 0:128] = (head_lanes(pair, h).astype(F32) * HEAD_DIM ** -0.5).astype(BF)
            aug = base
            if with_stats:
                aug = jnp.where((lanes == 64 + h) | (lanes == 72 + h) | (lanes == 80 + h), -1.0, base)
            kaug[h, pl.ds(at, TK), 128:256] = aug.astype(BF)
        return c
    lax.fori_loop(0, ROW // TK, one, 0)
    for h in range(heads):
        kaug[h, ROW:, 0:128] = jnp.zeros((TK, 128), BF)
        kaug[h, ROW:, 128:256] = jnp.where(lanes < DOCS, -FAR, 0.0).astype(BF)

def fill_ranks(rank_cols, rank_ref, starts):
    pos = lax.broadcasted_iota(jnp.int32, (1, ROW), 1)
    first = jnp.zeros((1, ROW), jnp.bool_)
    for d in range(DOCS):
        first = first | (pos == starts[d])
    rank = jnp.where(first, -1.0, rank_ref[...].astype(F32))
    for t in range(ROW // 128):
        block = jnp.broadcast_to(rank[:, t * 128:(t + 1) * 128], (128, 128))
        rank_cols[t * 128:(t + 1) * 128, :] = block.T
    rank_cols[ROW:, :] = jnp.zeros((TK, 128), F32)

def seen_bias(rank_cols, count_row, k0, q0):
    rank = rank_cols[pl.ds(k0, TK), :]
    rank = jnp.concatenate([rank] * (TQ // 128), 1)
    kpos = lax.broadcasted_iota(jnp.int32, (TK, TQ), 0)
    qpos = lax.broadcasted_iota(jnp.int32, (TK, TQ), 1)
    off_diag = (kpos - qpos) != (q0 - k0)
    allowed = (rank < count_row) & (off_diag | (rank < 0.0))
    return jnp.where(allowed, 0.0, -FAR * FAR)

def attn_fwd_kernel(with_seen, heads, len_ref, q_ref, k_ref, v_ref, rank_ref, count_ref, o_ref, lse_ref,
                    kaug, vt, rank_cols, acc, top, qt):
    starts, ends = doc_bounds(len_ref)
    start_lane, end_lane = lane_vector(starts), lane_vector(ends)
    fill_keys(kaug, k_ref, start_lane, end_lane, heads, False)
    for t in range(ROW // TK):
        vt[:, :HEAD_DIM, t * TK:(t + 1) * TK] = v_ref[t * TK:(t + 1) * TK, :].T.reshape(heads, HEAD_DIM, TK)
    vt[:, :HEAD_DIM, ROW:] = jnp.zeros((heads, HEAD_DIM, TK), BF)
    vt[:, HEAD_DIM:, :] = jnp.ones((heads, 16, ROW + TK), BF)
    if with_seen:
        fill_ranks(rank_cols, rank_ref, starts)

    def one_q(t, c):
        q0 = pl.multiple_of(t * TQ, TQ)
        first, steps = key_range(starts, ends, q0)
        hot = jnp.concatenate([doc_hot_rows(starts, ends, q0), jnp.zeros((128 - DOCS, TQ), F32)], 0).astype(BF)
        for p in range(heads // 2):
            qt[p, 0:128, :] = q_ref[pl.ds(q0, TQ), p * 128:(p + 1) * 128].T
            qt[p, 128:256, :] = hot
        count_row = count_ref[:, pl.ds(q0, TQ)].astype(F32)
        acc[...] = jnp.zeros_like(acc)
        top[...] = jnp.full_like(top, -jnp.inf)

        def one_k(s, c):
            k0 = pl.multiple_of(first + s * TK, 128)
            bias = seen_bias(rank_cols, count_row, k0, q0) if with_seen else None
            old = top[...]
            scores = [nn(kaug[h, pl.ds(k0, TK), :], qt[h // 2]) for h in range(heads)]
            if with_seen:
                scores = [score + bias for score in scores]
            vts = [vt[h, :, pl.ds(k0, TK)] for h in range(heads)]
            accs = [acc[h] for h in range(heads)]
            news, sums = [], []
            for h in range(heads):
                score = scores[h]
                new = jnp.maximum(old[h:h + 1, :], jnp.max(score, 0, keepdims=True))
                p = jnp.exp(score - new).astype(BF)
                news.append(new)
                sums.append(accs[h] * jnp.exp(old[h:h + 1, :] - new) + nn(vts[h], p))
            for h in range(heads):
                acc[h] = sums[h]
            top[...] = jnp.concatenate(news + [old[heads:, :]], 0)
            return c
        lax.fori_loop(0, steps, one_k, 0)
        outs = []
        for h in range(heads):
            a = acc[h]
            total = a[HEAD_DIM:HEAD_DIM + 1, :]
            outs.append(a[:HEAD_DIM, :] / total)
            lse_ref[h:h + 1, pl.ds(q0, TQ)] = top[h:h + 1, :] + jnp.log(total)
        o_ref[pl.ds(q0, TQ), :] = jnp.concatenate(outs, 0).T.astype(BF)
        return c
    lax.fori_loop(0, ROW // TQ, one_q, 0)

def attend_forward(lengths, q, k, v, rank, count, with_seen):
    rows, cols = q.shape
    heads = cols // HEAD_DIM
    V = pl.BlockSpec(memory_space=pltpu.VMEM)
    return pl.pallas_call(
        partial(attn_fwd_kernel, with_seen, heads),
        out_shape=(jax.ShapeDtypeStruct((rows, cols), BF), jax.ShapeDtypeStruct((8, rows), F32)),
        in_specs=[pl.BlockSpec(memory_space=pltpu.SMEM)] + [V] * 5,
        out_specs=(V, V),
        scratch_shapes=[
            pltpu.VMEM((heads, ROW + TK, 256), BF),
            pltpu.VMEM((heads, HEAD_DIM + 16, ROW + TK), BF),
            pltpu.VMEM((ROW + TK, 128), F32),
            pltpu.VMEM((heads, HEAD_DIM + 16, TQ), F32),
            pltpu.VMEM((8, TQ), F32),
            pltpu.VMEM((heads // 2, 256, TQ), BF),
        ],
        compiler_params=pltpu.CompilerParams(vmem_limit_bytes=56 * 2**20),
        name="attend_self_forward" if with_seen else "attend_cross_forward",
    )(lengths, q, k, v, rank, count)

def three_way(value):
    hi = value.astype(BF).astype(F32)
    mid = (value - hi).astype(BF).astype(F32)
    return hi, mid, value - hi - mid

def attn_bwd_kernel(with_seen, heads, len_ref, q_ref, k_ref, v_ref, g_ref, o_ref, lse_ref, rank_ref, count_ref,
                    dq_ref, dk_ref, dv_ref, kaug, vaug, kt, rank_cols, dk_sum, dv_sum, dq_sum, q_diag, g_diag, qt, gt):
    cols = heads * HEAD_DIM
    starts, ends = doc_bounds(len_ref)
    start_lane, end_lane = lane_vector(starts), lane_vector(ends)
    fill_keys(kaug, k_ref, start_lane, end_lane, heads, True)
    lanes = lax.broadcasted_iota(jnp.int32, (TK, 128), 1)
    for h in range(heads):
        picks = (lanes == h) | (lanes == 8 + h) | (lanes == 16 + h)
        side = jnp.where(picks, -1.0, 0.0).astype(BF)
        for t in range(ROW // TK):
            pair = v_ref[t * TK:(t + 1) * TK, h // 2 * 128:h // 2 * 128 + 128]
            vaug[h, t * TK:(t + 1) * TK, 0:128] = head_lanes(pair, h)
            vaug[h, t * TK:(t + 1) * TK, 128:256] = side
        vaug[h, ROW:, :] = jnp.zeros((TK, 256), BF)
    for t in range(ROW // TK):
        kt[:, t * TK:(t + 1) * TK] = k_ref[t * TK:(t + 1) * TK, :].T
    kt[:, ROW:] = jnp.zeros((cols, TK), BF)
    if with_seen:
        fill_ranks(rank_cols, rank_ref, starts)
    dk_sum[...] = jnp.zeros_like(dk_sum)
    dv_sum[...] = jnp.zeros_like(dv_sum)
    sel_row = lax.broadcasted_iota(jnp.int32, (8, cols), 0)
    sel_lane = lax.div(lax.broadcasted_iota(jnp.int32, (8, cols), 1), HEAD_DIM)
    selector = jnp.where(sel_lane == sel_row, 1.0, 0.0).astype(BF)

    def one_q(t, c):
        q0 = pl.multiple_of(t * TQ, TQ)
        first, steps = key_range(starts, ends, q0)
        g = g_ref[pl.ds(q0, TQ), :]
        q = q_ref[pl.ds(q0, TQ), :]
        spread = g.astype(F32) * o_ref[pl.ds(q0, TQ), :].astype(F32)
        spread_hi = spread.astype(BF)
        delta = nt(selector, spread_hi) + nt(selector, (spread - spread_hi.astype(F32)).astype(BF))
        daug = jnp.concatenate(list(three_way(delta)) + [jnp.zeros((104, TQ), F32)], 0).astype(BF)
        lse = lse_ref[:, pl.ds(q0, TQ)]
        hi, mid, lo = three_way(lse)
        side = jnp.concatenate([doc_hot_rows(starts, ends, q0), jnp.zeros((32, TQ), F32), hi, mid, lo, jnp.zeros((40, TQ), F32)], 0).astype(BF)
        for p in range(heads // 2):
            qt[p, 0:128, :] = q[:, p * 128:(p + 1) * 128].T
            qt[p, 128:256, :] = side
            gt[p, 0:128, :] = g[:, p * 128:(p + 1) * 128].T
            gt[p, 128:256, :] = daug
        wide = lax.div(lax.broadcasted_iota(jnp.int32, (TQ, cols), 1), HEAD_DIM)
        for h in range(heads):
            q_diag[h * TQ:(h + 1) * TQ, :] = jnp.where(wide == h, q, jnp.zeros_like(q))
            g_diag[h * TQ:(h + 1) * TQ, :] = jnp.where(wide == h, g, jnp.zeros_like(g))
        count_row = count_ref[:, pl.ds(q0, TQ)].astype(F32)
        dq_sum[...] = jnp.zeros_like(dq_sum)

        def one_k(s, c):
            k0 = pl.multiple_of(first + s * TK, 128)
            bias = seen_bias(rank_cols, count_row, k0, q0) if with_seen else None
            all_ds, all_p, all_dq = [], [], []
            kaugs = [kaug[h, pl.ds(k0, TK), :] for h in range(heads)]
            vaugs = [vaug[h, pl.ds(k0, TK), :] for h in range(heads)]
            keys_t = kt[:, pl.ds(k0, TK)]
            qts = [qt[p] for p in range(heads // 2)]
            gts = [gt[p] for p in range(heads // 2)]
            qd, gd = q_diag[...], g_diag[...]
            scores = [nn(kaugs[h], qts[h // 2]) for h in range(heads)]
            dps = [nn(vaugs[h], gts[h // 2]) for h in range(heads)]
            if with_seen:
                scores = [score + bias for score in scores]
            for h in range(heads):
                p = jnp.exp(scores[h])
                ds = (p * dps[h]).astype(BF)
                all_ds.append(ds)
                all_p.append(p.astype(BF))
                all_dq.append(nn(keys_t[h * HEAD_DIM:(h + 1) * HEAD_DIM, :], ds))
            dk = dk_sum[pl.ds(k0, TK), :] + nn(jnp.concatenate(all_ds, 1), qd)
            dv = dv_sum[pl.ds(k0, TK), :] + nn(jnp.concatenate(all_p, 1), gd)
            dq = dq_sum[...] + jnp.concatenate(all_dq, 0)
            dk_sum[pl.ds(k0, TK), :] = dk
            dv_sum[pl.ds(k0, TK), :] = dv
            dq_sum[...] = dq
            return c
        lax.fori_loop(0, steps, one_k, 0)
        dq_ref[pl.ds(q0, TQ), :] = (dq_sum[...] * HEAD_DIM ** -0.5).T.astype(BF)
        return c
    lax.fori_loop(0, ROW // TQ, one_q, 0)
    dk_ref[...] = (dk_sum[:ROW, :] * HEAD_DIM ** -0.5).astype(BF)
    dv_ref[...] = dv_sum[:ROW, :].astype(BF)

def attend_backward(lengths, q, k, v, g, o, lse, rank, count, with_seen):
    rows, cols = q.shape
    heads = cols // HEAD_DIM
    V = pl.BlockSpec(memory_space=pltpu.VMEM)
    like = jax.ShapeDtypeStruct((rows, cols), BF)
    return pl.pallas_call(
        partial(attn_bwd_kernel, with_seen, heads),
        out_shape=(like, like, like),
        in_specs=[pl.BlockSpec(memory_space=pltpu.SMEM)] + [V] * 8,
        out_specs=(V, V, V),
        scratch_shapes=[
            pltpu.VMEM((heads, ROW + TK, 256), BF),
            pltpu.VMEM((heads, ROW + TK, 256), BF),
            pltpu.VMEM((cols, ROW + TK), BF),
            pltpu.VMEM((ROW + TK, 128), F32),
            pltpu.VMEM((ROW + TK, cols), F32),
            pltpu.VMEM((ROW + TK, cols), F32),
            pltpu.VMEM((cols, TQ), F32),
            pltpu.VMEM((heads * TQ, cols), BF),
            pltpu.VMEM((heads * TQ, cols), BF),
            pltpu.VMEM((heads // 2, 256, TQ), BF),
            pltpu.VMEM((heads // 2, 256, TQ), BF),
        ],
        compiler_params=pltpu.CompilerParams(vmem_limit_bytes=56 * 2**20),
        name="attend_self_backward" if with_seen else "attend_cross_backward",
    )(lengths, q, k, v, g, o, lse, rank, count)


def send(src, dst, send_sem, recv_sem, **where):
    copy = pltpu.make_async_remote_copy(src_ref=src, dst_ref=dst, send_sem=send_sem, recv_sem=recv_sem,
                                        device_id=where, device_id_type=pl.DeviceIdType.MESH)
    copy.start()
    return copy

def greet(peers):
    barrier = pltpu.get_barrier_semaphore()
    for where in peers:
        pl.semaphore_signal(barrier, inc=1, device_id=where, device_id_type=pl.DeviceIdType.MESH)
    pl.semaphore_wait(barrier, len(peers))

def places_of(count):
    me = lax.axis_index("dp")
    across = count // 4
    x, y, z = lax.rem(me, 2), lax.rem(lax.div(me, 2), 2), lax.div(me, 4)
    xpeer, ypeer = me + 1 - 2 * x, me + 2 - 4 * y
    order = sorted(range(1, across), key=lambda d: min(d, across - d))
    ahead = lambda d: lax.rem(z + d, across) * 4 + y * 2 + x
    behind = lambda d: lax.rem(z + across - d, across) * 4 + y * 2 + x
    return me, x, y, z, xpeer, ypeer, order, ahead, behind

def spread_blocks(count, out, rows, places, zs, xs, ys, gx, gy):
    me, x, y, z, xpeer, ypeer, order, ahead, behind = places
    half = rows // 32 * 16
    whole = pl.ds(0, rows)
    sent, recv = [], {}
    def go(src_block, at, sem, d, to):
        copy = send(out.at[src_block, at], out.at[src_block, at], sem.at[0, d], sem.at[1, d], dp=to)
        sent.append(copy)
        return copy
    near = go(me, whole, xs, 0, xpeer), go(me, whole, ys, 0, ypeer)
    recv[0] = near
    zcopies = {}
    for d in order:
        zcopies[d] = go(me, whole, zs, d, ahead(d))
    steps = [0] + order
    diag = []
    for k, d in enumerate(steps):
        if d:
            zcopies[d].wait_recv()
            recv[d] = go(behind(d), whole, xs, d, xpeer), go(behind(d), whole, ys, d, ypeer)
        if k:
            forward(go, diag, recv, steps[k - 1], behind, places, half, rows, gx, gy)
    forward(go, diag, recv, steps[-1], behind, places, half, rows, gx, gy)
    for copy in diag:
        copy.wait_recv()
    for copy in sent:
        copy.wait_send()

def forward(go, diag, recv, d, behind, places, half, rows, gx, gy):
    me, x, y, z, xpeer, ypeer, order, ahead, _ = places
    base = behind(d) if d else me
    recv[d][0].wait_recv()
    diag.append(go(base + 1 - 2 * x, pl.ds(0, half), gy, d, ypeer))
    recv[d][1].wait_recv()
    diag.append(go(base + 2 - 4 * y, pl.ds(half, rows - half), gx, d, xpeer))

def gather_kernel(count, in_ref, out_ref, local_sem, zs, xs, ys, gx, gy):
    places = places_of(count)
    me, x, y, z, xpeer, ypeer, order, ahead, behind = places
    rows = in_ref.shape[0]
    own = pltpu.make_async_copy(in_ref, out_ref.at[me], local_sem)
    own.start()
    greet([{"dp": xpeer}, {"dp": ypeer}] + [{"dp": ahead(d)} for d in order])
    own.wait()
    spread_blocks(count, out_ref, rows, places, zs, xs, ys, gx, gy)

def gather_blocks(block, count, number=0):
    rows, cols = block.shape
    across = count // 4
    sems = pltpu.SemaphoreType.DMA((2, across))
    return pl.pallas_call(
        partial(gather_kernel, count),
        out_shape=jax.ShapeDtypeStruct((count, rows, cols), block.dtype),
        in_specs=[pl.BlockSpec(memory_space=pltpu.VMEM)],
        out_specs=pl.BlockSpec(memory_space=pltpu.VMEM),
        scratch_shapes=[pltpu.SemaphoreType.DMA] + [sems] * 5,
        compiler_params=pltpu.CompilerParams(collective_id=number, has_side_effects=True, vmem_limit_bytes=56 * 2**20),
        name="gather_units",
    )(block)

def reduce_kernel(count, in_ref, out_ref, keep, r1, r2, r3, s1, s2, s3, zs, xs, ys, gx, gy):
    places = places_of(count)
    me, x, y, z, xpeer, ypeer, order, ahead, behind = places
    across = count // 4
    rows = in_ref.shape[1]
    half = rows // 2
    greet([{"dp": xpeer}, {"dp": ypeer}] + [{"dp": ahead(d)} for d in order])
    steps = order + [0]
    base = lambda d: lax.rem(z + d, across) * 4
    part_rows = [pl.ds(0, half), pl.ds(half, half)]
    def at(d, first, second, part):
        return base(d) + (first + 2 * second if part == 0 else 2 * first + second)
    mine = [(x, y), (y, x)]
    peers = [(xpeer, ypeer), (ypeer, xpeer)]
    first_copies = {}
    for d in steps:
        for part in (0, 1):
            f, s = mine[part]
            for t in (0, 1):
                second = s if t else 1 - s
                first_copies[d, part, t] = send(in_ref.at[at(d, 1 - f, second, part), part_rows[part]], r1.at[part, d, t],
                                                s1.at[0, part, d, t], s1.at[1, part, d, t], dp=peers[part][0])
    second_copies, third_copies = {}, {}
    def second_stage(d):
        for part in (0, 1):
            f, s = mine[part]
            for t in (0, 1):
                second = s if t else 1 - s
                first_copies[d, part, t].wait_recv()
                total = (in_ref[at(d, f, second, part), part_rows[part], :].astype(F32) + r1[part, d, t].astype(F32)).astype(BF)
                keep[part, d, t] = total
                if t == 0:
                    second_copies[d, part] = send(keep.at[part, d, 0], r2.at[part, d], s2.at[0, part, d], s2.at[1, part, d],
                                                  dp=peers[part][1])
    def third_stage(d):
        for part in (0, 1):
            second_copies[d, part].wait_recv()
            total = (keep[part, d, 1].astype(F32) + r2[part, d].astype(F32)).astype(BF)
            keep[part, d, 1] = total
            if d:
                third_copies[d, part] = send(keep.at[part, d, 1], r3.at[part, d], s3.at[0, part, d], s3.at[1, part, d], dp=ahead(d))
    for k, d in enumerate(steps):
        second_stage(d)
        if k:
            third_stage(steps[k - 1])
    third_stage(0)
    for part in (0, 1):
        total = keep[part, 0, 1].astype(F32)
        for d in order:
            third_copies[d, part].wait_recv()
            total = total + r3[part, d].astype(F32)
        out_ref[me, part_rows[part], :] = total.astype(BF)
    spread_blocks(count, out_ref, rows, places, zs, xs, ys, gx, gy)
    for copies in (first_copies, second_copies, third_copies):
        for copy in copies.values():
            copy.wait_send()

def reduce_blocks(flat, count, number=1):
    total_rows, cols = flat.shape
    rows = total_rows // count
    half = rows // 2
    across = count // 4
    sems = pltpu.SemaphoreType.DMA((2, across))
    D = pltpu.SemaphoreType.DMA
    return pl.pallas_call(
        partial(reduce_kernel, count),
        out_shape=jax.ShapeDtypeStruct((count, rows, cols), BF),
        in_specs=[pl.BlockSpec(memory_space=pltpu.VMEM)],
        out_specs=pl.BlockSpec(memory_space=pltpu.VMEM),
        scratch_shapes=[
            pltpu.VMEM((2, across, 2, half, cols), BF),
            pltpu.VMEM((2, across, 2, half, cols), BF),
            pltpu.VMEM((2, across, half, cols), BF),
            pltpu.VMEM((2, across, half, cols), BF),
            D((2, 2, across, 2)), D((2, 2, across)), D((2, 2, across)),
        ] + [sems] * 5,
        compiler_params=pltpu.CompilerParams(collective_id=number, has_side_effects=True, vmem_limit_bytes=56 * 2**20),
        name="reduce_gradients",
    )(flat.reshape(count, rows, cols)).reshape(total_rows, cols)


CHUNK = 256


def tn(a, b):
    return lax.dot_general(a, b, (((0,), (0,)), ((), ())), preferred_element_type=F32)


def normalise(value):
    centred = value - jnp.mean(value, -1, keepdims=True)
    scale = lax.rsqrt(jnp.mean(centred * centred, -1, keepdims=True) + EPS_NORM)
    return centred * scale, scale


def norm_back(unit, scale, gain, grad):
    inner = grad * gain
    return scale * (inner - jnp.mean(inner, -1, keepdims=True) - unit * jnp.mean(inner * unit, -1, keepdims=True))


def fold_rows(value):
    return jnp.sum(value.reshape(value.shape[0] // 8, 8, value.shape[1]), 0)


def interleave(size):
    row = lax.broadcasted_iota(jnp.int32, (size, size), 0)
    col = lax.broadcasted_iota(jnp.int32, (size, size), 1)
    source = jnp.where((row & 1) == 0, row >> 1, (row >> 1) + size // 2)
    return jnp.where(col == source, 1.0, 0.0).astype(BF)


def part_rows(matrix, order):
    return lax.dot_general(order, matrix, (((0,), (0,)), ((), ())), preferred_element_type=F32).astype(BF)


def as_units(gradient, order):
    parted = part_rows(gradient.astype(BF), order)
    half = parted.shape[0] // 2
    return jnp.concatenate([parted[:half], parted[half:]], 1)


def other_core(mine, theirs, sems, step):
    rows = pl.ds(step * CHUNK, CHUNK)
    return pltpu.make_async_remote_copy(
        src_ref=mine.at[rows], dst_ref=theirs.at[rows], send_sem=sems.at[0, step], recv_sem=sems.at[1, step],
        device_id={"head": 1 - lax.axis_index("head")}, device_id_type=pl.DeviceIdType.MESH)


def greet_core():
    greet([{"head": 1 - lax.axis_index("head")}])


def chunks(total, body):
    def one(step, carry):
        body(step, pl.ds(pl.multiple_of(step * CHUNK, CHUNK), CHUNK))
        return carry
    lax.fori_loop(0, total // CHUNK, one, 0)


def drain(total, mine, theirs, sems):
    def body(step, rows):
        other_core(mine, theirs, sems, step).wait_send()
    chunks(total, body)


def project_kernel(owner_ref, gathered, norms, query_ref, kv_ref, memory_ref,
                   nq_ref, nkv_ref, q_ref, k_ref, v_ref, kc_ref, vc_ref, ws_ref, wc_ref, wos_ref, woc_ref, w1_ref, w2_ref,
                   flat, used):
    tokens, features = query_ref.shape
    devices = gathered.shape[0]
    units = owner_ref.shape[0]
    for d in range(devices):
        used[d] = 0

    def one_unit(u, carry):
        owner = owner_ref[u]
        slot = used[owner]
        used[owner] = slot + 1
        flat[pl.ds(pl.multiple_of(u * UNIT, UNIT), UNIT), :] = gathered[owner, pl.ds(pl.multiple_of(slot * UNIT, UNIT), UNIT), :]
        return carry
    lax.fori_loop(0, units, one_unit, 0, unroll=4)
    order = interleave(features)
    cols = q_ref.shape[1]
    for number in range(6):
        rows = flat[number * cols:(number + 1) * cols, :]
        stacked = jnp.concatenate([rows[:, :cols], rows[:, cols:]], 0)
        matrix = nn(order, stacked).astype(BF)
        if number < 3:
            ws_ref[number] = matrix
        else:
            wc_ref[number - 3] = matrix
    wos_ref[...] = flat[6 * cols:7 * cols, :]
    woc_ref[...] = flat[7 * cols:8 * cols, :]
    hidden = w2_ref.shape[0]
    for block in range(hidden // features):
        at = 8 * cols + block * features
        parted = part_rows(flat[at:at + features, :], order)
        half = features // 2
        w1_ref[block * half:(block + 1) * half, :] = jnp.concatenate([parted[:half], parted[half:]], 1)
    w2_ref[...] = flat[8 * cols + hidden:, :]

    def body(step, rows):
        nq = (normalise(query_ref[rows, :].astype(F32))[0] * norms[0:1, :] + norms[1:2, :]).astype(BF)
        nkv = (normalise(kv_ref[rows, :].astype(F32))[0] * norms[2:3, :] + norms[3:4, :]).astype(BF)
        source = memory_ref[rows, :]
        nq_ref[rows, :] = nq
        nkv_ref[rows, :] = nkv
        q_ref[rows, :] = nn(nq, ws_ref[0]).astype(BF)
        k_ref[rows, :] = nn(nkv, ws_ref[1]).astype(BF)
        v_ref[rows, :] = nn(nkv, ws_ref[2]).astype(BF)
        kc_ref[rows, :] = nn(source, wc_ref[1]).astype(BF)
        vc_ref[rows, :] = nn(source, wc_ref[2]).astype(BF)
    chunks(tokens, body)


def call(kernel, name, args, smem, outs, scratch, number=None):
    V = pl.BlockSpec(memory_space=pltpu.VMEM)
    S = pl.BlockSpec(memory_space=pltpu.SMEM)
    extra = {} if number is None else dict(collective_id=number, has_side_effects=True)
    return pl.pallas_call(
        kernel,
        out_shape=tuple(jax.ShapeDtypeStruct(shape, dtype) for shape, dtype in outs),
        in_specs=[S] * smem + [V] * (len(args) - smem),
        out_specs=tuple(V for _ in outs),
        scratch_shapes=scratch,
        compiler_params=pltpu.CompilerParams(vmem_limit_bytes=60 * 2**20, **extra),
        name=name,
    )(*args)


def pair_sems(tokens):
    return pltpu.SemaphoreType.DMA((2, tokens // CHUNK))


def project(unit_owner, gathered, norms, query_stream, kv_stream, memory, cols, hidden):
    tokens, features = query_stream.shape
    wide, narrow = ((tokens, features), BF), ((tokens, cols), BF)
    outs = [wide, wide] + [narrow] * 5 + [
        ((3, features, cols), BF), ((3, features, cols), BF), ((cols, features), BF), ((cols, features), BF),
        ((features, hidden), BF), ((hidden, features), BF)]
    return call(project_kernel, "project", [unit_owner, gathered, norms, query_stream, kv_stream, memory], 1, outs,
                [pltpu.VMEM((8 * cols + 2 * hidden, features), BF), pltpu.SMEM((gathered.shape[0],), jnp.int32)])


def self_out_kernel(mixed, wo, query, wc, norms, res_ref, nc_ref, q_ref, mine, theirs, sems):
    tokens = query.shape[0]
    greet_core()

    def give(step, rows):
        mine[rows, :] = nn(mixed[rows, :], wo[...]).astype(BF)
        other_core(mine, theirs, sems, step).start()
    chunks(tokens, give)

    def take(step, rows):
        other_core(mine, theirs, sems, step).wait_recv()
        res = query[rows, :].astype(F32) + (mine[rows, :].astype(F32) + theirs[rows, :].astype(F32))
        res_ref[rows, :] = res
        nc = (normalise(res)[0] * norms[4:5, :] + norms[5:6, :]).astype(BF)
        nc_ref[rows, :] = nc
        q_ref[rows, :] = nn(nc, wc[0]).astype(BF)
    chunks(tokens, take)
    drain(tokens, mine, theirs, sems)


def self_out(mixed, wo, query, wc, norms):
    tokens, features = query.shape
    outs = [((tokens, features), F32), ((tokens, features), BF), (mixed.shape, BF)]
    wide = pltpu.VMEM((tokens, features), BF)
    return call(self_out_kernel, "self_out", [mixed, wo, query, wc, norms], 0, outs, [wide, wide, pair_sems(tokens)], 2)


def gelu_parts(value):
    size = jnp.abs(value)
    bell = jnp.exp(-0.5 * value * value)
    t = 1.0 / (1.0 + (0.3275911 * 0.7071067811865476) * size)
    poly = ((((1.061405429 * t - 1.453152027) * t + 1.421413741) * t - 0.284496736) * t + 0.254829592) * t
    tail = 0.5 * poly * bell
    below = jnp.where(value < 0.0, tail, 1.0 - tail)
    return value * below, below + value * (bell * 0.3989422804014327)


def feed_forward_kernel(mixed, wo, res, w1, w2, out_grad, norms,
                        out_ref, gres_ref, gmix_ref, gw1_ref, gw2_ref, gwo_ref, sums_ref,
                        mine, theirs, nf_all, hid_all, pre_all, low_all, mine_o, theirs_o, mine_g, theirs_g,
                        sems, sems_o, sems_g):
    tokens, features = out_grad.shape
    hidden = w2.shape[0]
    greet_core()

    def give(step, rows):
        mine[rows, :] = nn(mixed[rows, :], wo[...]).astype(BF)
        other_core(mine, theirs, sems, step).start()
    chunks(tokens, give)

    def middle(step, rows):
        other_core(mine, theirs, sems, step).wait_recv()
        value = res[rows, :] + (mine[rows, :].astype(F32) + theirs[rows, :].astype(F32))
        gres_ref[rows, :] = value
        nf = (normalise(value)[0] * norms[6:7, :] + norms[7:8, :]).astype(BF)
        nf_all[rows, :] = nf
        grad = out_grad[rows, :]
        out_part = jnp.zeros((CHUNK, features), F32)
        grad_part = jnp.zeros((CHUNK, features), F32)
        for block in range(hidden // 256):
            at = slice(block * 256, (block + 1) * 256)
            act, slope = gelu_parts(nn(nf, w1[:, at]))
            act = act.astype(BF)
            hid_all[rows, at] = act
            pre = (slope * nt(grad, w2[at, :])).astype(BF)
            pre_all[rows, at] = pre
            out_part = out_part + nn(act, w2[at, :])
            grad_part = grad_part + nt(pre, w1[:, at])
        mine_o[rows, :] = out_part.astype(BF)
        other_core(mine_o, theirs_o, sems_o, step).start()
        mine_g[rows, :] = grad_part.astype(BF)
        other_core(mine_g, theirs_g, sems_g, step).start()
    chunks(tokens, middle)

    order = interleave(features)
    half = features // 2
    for block in range(hidden // 256):
        at = slice(block * 256, (block + 1) * 256)
        gw2_ref[at, :] = tn(hid_all[:, at], out_grad[...]).astype(BF)
    for block in range(hidden // features):
        gradient = tn(nf_all[:, block * half:(block + 1) * half], pre_all[...]).astype(BF)
        stacked = jnp.concatenate([gradient[:, :features], gradient[:, features:]], 0)
        gw1_ref[block * features:(block + 1) * features, :] = nn(order, stacked).astype(BF)
    sums_ref[...] = jnp.zeros_like(sums_ref)

    def close(step, rows):
        other_core(mine_o, theirs_o, sems_o, step).wait_recv()
        other_core(mine_g, theirs_g, sems_g, step).wait_recv()
        value = gres_ref[rows, :]
        out_ref[rows, :] = (value + (mine_o[rows, :].astype(F32) + theirs_o[rows, :].astype(F32))).astype(BF)
        grad = mine_g[rows, :].astype(F32) + theirs_g[rows, :].astype(F32)
        unit, scale = normalise(value)
        gres = norm_back(unit, scale, norms[6:7, :], grad) + out_grad[rows, :].astype(F32)
        gres_ref[rows, :] = gres
        sums_ref[0:8, :] += fold_rows(grad * unit)
        sums_ref[8:16, :] += fold_rows(grad)
        low = gres.astype(BF)
        low_all[rows, :] = low
        gmix_ref[rows, :] = nt(low, wo[...]).astype(BF)
    chunks(tokens, close)
    gwo_ref[...] = tn(mixed[...], low_all[...]).astype(BF)
    drain(tokens, mine, theirs, sems)
    drain(tokens, mine_o, theirs_o, sems_o)
    drain(tokens, mine_g, theirs_g, sems_g)


def feed_forward(mixed, wo, res, w1, w2, out_grad, norms):
    tokens, features = out_grad.shape
    hidden = w2.shape[0]
    outs = [((tokens, features), BF), ((tokens, features), F32), (mixed.shape, BF), ((hidden, features), BF),
            ((hidden, features), BF), (wo.shape, BF), ((16, features), F32)]
    wide = pltpu.VMEM((tokens, features), BF)
    deep = pltpu.VMEM((tokens, hidden), BF)
    return call(feed_forward_kernel, "feed_forward", [mixed, wo, res, w1, w2, out_grad, norms], 0, outs,
                [wide, wide, wide, deep, deep, wide, wide, wide, wide, wide] + [pair_sems(tokens)] * 3, 3)


def branch_back(first_in, second_in, dq, dk, dv, weights, gw_ref, mine_a, theirs_a, mine_b, theirs_b, sems_a, sems_b):
    tokens, features = first_in.shape
    cols = dq.shape[1]
    greet_core()

    def give(step, rows):
        mine_a[rows, :] = nt(dq[rows, :], weights[0]).astype(BF)
        other_core(mine_a, theirs_a, sems_a, step).start()
        mine_b[rows, :] = (nt(dk[rows, :], weights[1]) + nt(dv[rows, :], weights[2])).astype(BF)
        other_core(mine_b, theirs_b, sems_b, step).start()
    chunks(tokens, give)
    order = interleave(features)
    for number, (entering, grad) in enumerate(((first_in, dq), (second_in, dk), (second_in, dv))):
        gw_ref[number * cols:(number + 1) * cols, :] = as_units(tn(entering[...], grad[...]), order)


def cross_back_kernel(dq, dk, dv, wc, nc, memory, res, gres, mixed, wo, norms,
                      gmem_ref, gnew_ref, gmix_ref, gw_ref, gwo_ref, sums_ref,
                      mine_a, theirs_a, mine_b, theirs_b, low_all, sems_a, sems_b):
    tokens, features = nc.shape
    branch_back(nc, memory, dq, dk, dv, wc, gw_ref, mine_a, theirs_a, mine_b, theirs_b, sems_a, sems_b)
    sums_ref[...] = jnp.zeros_like(sums_ref)

    def close(step, rows):
        other_core(mine_a, theirs_a, sems_a, step).wait_recv()
        grad = mine_a[rows, :].astype(F32) + theirs_a[rows, :].astype(F32)
        unit, scale = normalise(res[rows, :])
        gnew = norm_back(unit, scale, norms[4:5, :], grad) + gres[rows, :]
        gnew_ref[rows, :] = gnew
        sums_ref[0:8, :] += fold_rows(grad * unit)
        sums_ref[8:16, :] += fold_rows(grad)
        low = gnew.astype(BF)
        low_all[rows, :] = low
        gmix_ref[rows, :] = nt(low, wo[...]).astype(BF)
        other_core(mine_b, theirs_b, sems_b, step).wait_recv()
        gmem_ref[rows, :] = (mine_b[rows, :].astype(F32) + theirs_b[rows, :].astype(F32)).astype(BF)
    chunks(tokens, close)
    gwo_ref[...] = tn(mixed[...], low_all[...]).astype(BF)
    drain(tokens, mine_a, theirs_a, sems_a)
    drain(tokens, mine_b, theirs_b, sems_b)


def cross_back(dq, dk, dv, wc, nc, memory, res, gres, mixed, wo, norms):
    tokens, features = nc.shape
    cols = dq.shape[1]
    outs = [((tokens, features), BF), ((tokens, features), F32), (dq.shape, BF), ((3 * cols, features), BF),
            (wo.shape, BF), ((16, features), F32)]
    wide = pltpu.VMEM((tokens, features), BF)
    return call(cross_back_kernel, "cross_back", [dq, dk, dv, wc, nc, memory, res, gres, mixed, wo, norms], 0, outs,
                [wide] * 5 + [pair_sems(tokens)] * 2, 4)


def self_back_kernel(dq, dk, dv, ws, nq, nkv, query, kv, gres, norms, sums_c, sums_f,
                     gquery_ref, gkv_ref, gw_ref, gnorm_ref,
                     mine_a, theirs_a, mine_b, theirs_b, sums, sems_a, sems_b):
    tokens, features = nq.shape
    branch_back(nq, nkv, dq, dk, dv, ws, gw_ref, mine_a, theirs_a, mine_b, theirs_b, sems_a, sems_b)
    sums[...] = jnp.zeros_like(sums)

    def close(step, rows):
        other_core(mine_a, theirs_a, sems_a, step).wait_recv()
        grad = mine_a[rows, :].astype(F32) + theirs_a[rows, :].astype(F32)
        unit, scale = normalise(query[rows, :].astype(F32))
        gquery_ref[rows, :] = (norm_back(unit, scale, norms[0:1, :], grad) + gres[rows, :]).astype(BF)
        sums[0:8, :] += fold_rows(grad * unit)
        sums[8:16, :] += fold_rows(grad)
        other_core(mine_b, theirs_b, sems_b, step).wait_recv()
        grad = mine_b[rows, :].astype(F32) + theirs_b[rows, :].astype(F32)
        unit, scale = normalise(kv[rows, :].astype(F32))
        gkv_ref[rows, :] = norm_back(unit, scale, norms[2:3, :], grad).astype(BF)
        sums[16:24, :] += fold_rows(grad * unit)
        sums[24:32, :] += fold_rows(grad)
    chunks(tokens, close)
    parts = [sums[8 * i:8 * i + 8, :] for i in range(4)]
    parts += [sums_c[0:8, :], sums_c[8:16, :], sums_f[0:8, :], sums_f[8:16, :]]
    vectors = [jnp.sum(part, 0, keepdims=True) for part in parts]
    gnorm_ref[...] = jnp.concatenate(vectors + [jnp.zeros((8, features), F32)], 0).astype(BF)
    drain(tokens, mine_a, theirs_a, sems_a)
    drain(tokens, mine_b, theirs_b, sems_b)


def self_back(dq, dk, dv, ws, nq, nkv, query, kv, gres, norms, sums_c, sums_f):
    tokens, features = nq.shape
    cols = dq.shape[1]
    outs = [((tokens, features), BF), ((tokens, features), BF), ((3 * cols, features), BF), ((16, features), BF)]
    wide = pltpu.VMEM((tokens, features), BF)
    return call(self_back_kernel, "self_back", [dq, dk, dv, ws, nq, nkv, query, kv, gres, norms, sums_c, sums_f], 0, outs,
                [wide] * 4 + [pltpu.VMEM((32, features), F32)] + [pair_sems(tokens)] * 2, 5)


def update_kernel(owner_ref, me_ref, summed, master, first, second, grad_ref, first_ref, second_ref, new_ref, held):
    units = owner_ref.shape[0]
    slots = master.shape[0]
    me = me_ref[0]

    def find(u, count):
        held[count] = u
        return count + (owner_ref[u] == me).astype(jnp.int32)
    count = lax.fori_loop(0, units, find, jnp.int32(0), unroll=4)

    def one(slot, carry):
        @pl.when(slot < count)
        def _():
            unit = held[slot]
            gradient = summed[pl.ds(pl.multiple_of(unit * UNIT, UNIT), UNIT), :].astype(F32)
            first_new, second_new, weight = adamw_step(gradient, first[slot], second[slot], master[slot], RATE_MATRIX, WEIGHT_DECAY)
            grad_ref[slot] = gradient
            first_ref[slot] = first_new
            second_ref[slot] = second_new
            new_ref[slot] = weight

        @pl.when(slot >= count)
        def _():
            for ref in (grad_ref, first_ref, second_ref, new_ref):
                ref[slot] = jnp.zeros(ref.shape[1:], F32)
        return carry
    lax.fori_loop(0, slots, one, 0)


def update(unit_owner, me, summed, master, first, second):
    outs = [(master.shape, F32)] * 4
    return call(update_kernel, "update", [unit_owner, me, summed, master, first, second], 2, outs,
                [pltpu.SMEM((unit_owner.shape[0] + 8,), jnp.int32)])


def adamw_step(gradient, first, second, weight, rate, decay):
    first_new = BETA_ONE * first + (1.0 - BETA_ONE) * gradient
    second_new = BETA_TWO * second + (1.0 - BETA_TWO) * gradient * gradient
    corr_one = 1.0 - BETA_ONE**STEP
    corr_two = 1.0 - BETA_TWO**STEP
    direction = first_new / corr_one / (jnp.sqrt(second_new / corr_two) + ADAM_EPS)
    return (first_new, second_new, weight - rate * (direction + decay * weight))


def local(
    query_stream, kv_stream, memory, out_grad, lengths, obs_rank, obs_count, unit_owner,
    master, first_moment, second_moment, norm_master, norm_first, norm_second,
):
    devices = lax.axis_size("dp")
    shards = lax.axis_size("head")
    me = lax.axis_index("dp")
    slots, unit_rows, features = master.shape[0], master.shape[2], master.shape[3]
    units = unit_owner.shape[0]
    norm_share = norm_master.shape[0]
    cols = features // shards
    hidden = (units * unit_rows - 8 * cols) // 2

    own = master.astype(BF).reshape(slots * unit_rows, features)
    norm_row = jnp.pad(norm_master.astype(BF).reshape(1, norm_share), ((0, UNIT - 1), (0, features - norm_share)))
    gathered = gather_blocks(jnp.concatenate([own, norm_row], 0), devices)
    norms = gathered[:, slots * unit_rows, :norm_share].reshape(8, features).astype(F32)

    rank_row, count_row = obs_rank.reshape(1, ROW), obs_count.reshape(1, ROW)
    nq, nkv, q, k, v, kc, vc, ws, wc, wo_self, wo_cross, w1, w2 = project(
        unit_owner, gathered, norms, query_stream, kv_stream, memory, cols, hidden)
    mixed_self, total_self = attend_forward(lengths, q, k, v, rank_row, count_row, True)
    residual, nc, qc = self_out(mixed_self, wo_self, query_stream, wc, norms)
    mixed_cross, total_cross = attend_forward(lengths, qc, kc, vc, rank_row, count_row, False)
    output, grad_cross_res, grad_mixed, gw1, gw2, gwo_cross, sums_f = feed_forward(
        mixed_cross, wo_cross, residual, w1, w2, out_grad, norms)
    dq, dk, dv = attend_backward(lengths, qc, kc, vc, grad_mixed, mixed_cross, total_cross, rank_row, count_row, False)
    grad_memory, grad_residual, grad_mixed, gw_cross, gwo_self, sums_c = cross_back(
        dq, dk, dv, wc, nc, memory, residual, grad_cross_res, mixed_self, wo_self, norms)
    dq, dk, dv = attend_backward(lengths, q, k, v, grad_mixed, mixed_self, total_self, rank_row, count_row, True)
    grad_query, grad_kv, gw_self, gnorm = self_back(
        dq, dk, dv, ws, nq, nkv, query_stream, kv_stream, grad_residual, norms, sums_c, sums_f)

    pieces = [gw_self, gw_cross, gwo_self, gwo_cross, gw1, gw2, gnorm]
    used = units * unit_rows + UNIT
    whole = -(-used // (devices * 2 * UNIT)) * (devices * 2 * UNIT)
    flat = jnp.concatenate(pieces + [jnp.zeros((whole - used, features), BF)], 0)
    summed = reduce_blocks(flat, devices)
    shape = (slots, unit_rows, features)
    weight_grad, weight_first, weight_second, weight_new = [
        part.reshape(master.shape)
        for part in update(unit_owner, me.reshape(1), summed, master.reshape(shape), first_moment.reshape(shape),
                           second_moment.reshape(shape))]
    norm_grads = summed[units * unit_rows:units * unit_rows + 8].reshape(-1).astype(F32)
    norm_grad = lax.dynamic_slice_in_dim(norm_grads, me * norm_share, norm_share)
    norm_first_new, norm_second_new, norm_new = adamw_step(
        norm_grad, norm_first, norm_second, norm_master, RATE_NORM, 0.0)
    return (
        output, grad_query, grad_kv, grad_memory, weight_grad, weight_first, weight_second, weight_new,
        norm_grad, norm_first_new, norm_second_new, norm_new,
    )


def solution(mesh):
    in_specs = (
        P("dp", None),
        P("dp", None),
        P("dp", None),
        P("dp", None),
        P("dp", None),
        P("dp"),
        P("dp"),
        P(),
        P("dp", "head", None, None),
        P("dp", "head", None, None),
        P("dp", "head", None, None),
        P("dp"),
        P("dp"),
        P("dp"),
    )
    out_specs = (
        P("dp", None),
        P("dp", None),
        P("dp", None),
        P("dp", None),
        P("dp", "head", None, None),
        P("dp", "head", None, None),
        P("dp", "head", None, None),
        P("dp", "head", None, None),
        P("dp"),
        P("dp"),
        P("dp"),
        P("dp"),
    )
    return jax.shard_map(local, mesh=mesh, in_specs=in_specs, out_specs=out_specs, check_vma=False)
```

```python
from functools import partial

import jax
import jax.numpy as jnp
from jax import lax
from jax.experimental import pallas as pl
from jax.experimental.pallas import tpu as pltpu
from jax.sharding import PartitionSpec as P

HEAD_DIM = 64
ROW = 2048
DOCS = 32
STEP = 10
UNIT = 16

EPS_NORM = 1e-05
ADAM_EPS = 1e-08
BETA_ONE = 0.5
BETA_TWO = 0.5
RATE_MATRIX = 0.1
RATE_NORM = 0.3
WEIGHT_DECAY = 0.01

F32 = jnp.float32
BF = jnp.bfloat16
TQ = 256
TK = 256
FAR = 32768.0

def nt(a, b):
    return lax.dot_general(a, b, (((1,), (1,)), ((), ())), preferred_element_type=F32)

def nn(a, b):
    return lax.dot_general(a, b, (((1,), (0,)), ((), ())), preferred_element_type=F32)

def doc_bounds(len_ref):
    starts = []
    ends = []
    at = jnp.int32(0)
    for d in range(DOCS):
        starts.append(at)
        at = at + len_ref[0, d]
        ends.append(at)
    return starts, ends

def lane_vector(scalars):
    lanes = lax.broadcasted_iota(jnp.int32, (1, 128), 1)
    out = jnp.full((1, 128), -1, jnp.int32)
    for d, value in enumerate(scalars):
        out = jnp.where(lanes == d, value, out)
    return out

def doc_hot_rows(starts, ends, q0):
    pos = lax.broadcasted_iota(jnp.int32, (1, TQ), 1) + q0
    rows = [jnp.where((pos >= starts[d]) & (pos < ends[d]), FAR, 0.0) for d in range(DOCS)]
    return jnp.concatenate(rows, 0)

def key_range(starts, ends, q0):
    low = jnp.int32(0)
    high = jnp.int32(0)
    for d in range(DOCS):
        low = jnp.where(starts[d] <= q0, starts[d], low)
        high = jnp.where(starts[d] <= q0 + TQ - 1, ends[d], high)
    first = lax.div(low, 128) * 128
    steps = lax.div(high - first + TK - 1, TK)
    return first, steps

def head_lanes(pair_rows, h):
    lanes = lax.broadcasted_iota(jnp.int32, pair_rows.shape, 1)
    keep = (lanes < HEAD_DIM) if h % 2 == 0 else (lanes >= HEAD_DIM)
    return jnp.where(keep, pair_rows, jnp.zeros_like(pair_rows))

def doc_hot(start_lane, end_lane, at, rows):
    pos = lax.broadcasted_iota(jnp.int32, (rows, 128), 0) + at
    return (pos >= start_lane) & (pos < end_lane)

def fill_keys(kaug, k_ref, start_lane, end_lane, heads, with_stats):
    lanes = lax.broadcasted_iota(jnp.int32, (TK, 128), 1)
    def one(t, c):
        at = pl.multiple_of(t * TK, TK)
        hot = doc_hot(start_lane, end_lane, at, TK)
        base = jnp.where(hot | (lanes >= DOCS), 0.0, -FAR)
        for h in range(heads):
            pair = k_ref[pl.ds(at, TK), pl.ds(h // 2 * 128, 128)]
            kaug[h, pl.ds(at, TK), 0:128] = (head_lanes(pair, h).astype(F32) * HEAD_DIM ** -0.5).astype(BF)
            aug = base
            if with_stats:
                aug = jnp.where((lanes == 64 + h) | (lanes == 72 + h) | (lanes == 80 + h), -1.0, base)
            kaug[h, pl.ds(at, TK), 128:256] = aug.astype(BF)
        return c
    lax.fori_loop(0, ROW // TK, one, 0)
    for h in range(heads):
        kaug[h, ROW:, 0:128] = jnp.zeros((TK, 128), BF)
        kaug[h, ROW:, 128:256] = jnp.where(lanes < DOCS, -FAR, 0.0).astype(BF)

def fill_ranks(rank_cols, rank_ref, starts):
    pos = lax.broadcasted_iota(jnp.int32, (1, ROW), 1)
    first = jnp.zeros((1, ROW), jnp.bool_)
    for d in range(DOCS):
        first = first | (pos == starts[d])
    rank = jnp.where(first, -1.0, rank_ref[...].astype(F32))
    for t in range(ROW // 128):
        block = jnp.broadcast_to(rank[:, t * 128:(t + 1) * 128], (128, 128))
        rank_cols[t * 128:(t + 1) * 128, :] = block.T
    rank_cols[ROW:, :] = jnp.zeros((TK, 128), F32)

def seen_bias(rank_cols, count_row, k0, q0):
    rank = rank_cols[pl.ds(k0, TK), :]
    rank = jnp.concatenate([rank] * (TQ // 128), 1)
    kpos = lax.broadcasted_iota(jnp.int32, (TK, TQ), 0)
    qpos = lax.broadcasted_iota(jnp.int32, (TK, TQ), 1)
    off_diag = (kpos - qpos) != (q0 - k0)
    allowed = (rank < count_row) & (off_diag | (rank < 0.0))
    return jnp.where(allowed, 0.0, -FAR * FAR)

def attn_fwd_kernel(with_seen, heads, len_ref, q_ref, k_ref, v_ref, rank_ref, count_ref, o_ref, lse_ref,
                    kaug, vt, rank_cols, acc, top, qt):
    starts, ends = doc_bounds(len_ref)
    start_lane, end_lane = lane_vector(starts), lane_vector(ends)
    fill_keys(kaug, k_ref, start_lane, end_lane, heads, False)
    for t in range(ROW // TK):
        vt[:, :HEAD_DIM, t * TK:(t + 1) * TK] = v_ref[t * TK:(t + 1) * TK, :].T.reshape(heads, HEAD_DIM, TK)
    vt[:, :HEAD_DIM, ROW:] = jnp.zeros((heads, HEAD_DIM, TK), BF)
    vt[:, HEAD_DIM:, :] = jnp.ones((heads, 16, ROW + TK), BF)
    if with_seen:
        fill_ranks(rank_cols, rank_ref, starts)

    def one_q(t, c):
        q0 = pl.multiple_of(t * TQ, TQ)
        first, steps = key_range(starts, ends, q0)
        hot = jnp.concatenate([doc_hot_rows(starts, ends, q0), jnp.zeros((128 - DOCS, TQ), F32)], 0).astype(BF)
        for p in range(heads // 2):
            qt[p, 0:128, :] = q_ref[pl.ds(q0, TQ), p * 128:(p + 1) * 128].T
            qt[p, 128:256, :] = hot
        count_row = count_ref[:, pl.ds(q0, TQ)].astype(F32)
        acc[...] = jnp.zeros_like(acc)
        top[...] = jnp.full_like(top, -jnp.inf)

        def one_k(s, c):
            k0 = pl.multiple_of(first + s * TK, 128)
            bias = seen_bias(rank_cols, count_row, k0, q0) if with_seen else None
            old = top[...]
            scores = [nn(kaug[h, pl.ds(k0, TK), :], qt[h // 2]) for h in range(heads)]
            if with_seen:
                scores = [score + bias for score in scores]
            vts = [vt[h, :, pl.ds(k0, TK)] for h in range(heads)]
            accs = [acc[h] for h in range(heads)]
            news, sums = [], []
            for h in range(heads):
                score = scores[h]
                new = jnp.maximum(old[h:h + 1, :], jnp.max(score, 0, keepdims=True))
                p = jnp.exp(score - new).astype(BF)
                news.append(new)
                sums.append(accs[h] * jnp.exp(old[h:h + 1, :] - new) + nn(vts[h], p))
            for h in range(heads):
                acc[h] = sums[h]
            top[...] = jnp.concatenate(news + [old[heads:, :]], 0)
            return c
        lax.fori_loop(0, steps, one_k, 0)
        outs = []
        for h in range(heads):
            a = acc[h]
            total = a[HEAD_DIM:HEAD_DIM + 1, :]
            outs.append(a[:HEAD_DIM, :] / total)
            lse_ref[h:h + 1, pl.ds(q0, TQ)] = top[h:h + 1, :] + jnp.log(total)
        o_ref[pl.ds(q0, TQ), :] = jnp.concatenate(outs, 0).T.astype(BF)
        return c
    lax.fori_loop(0, ROW // TQ, one_q, 0)

def attend_forward(lengths, q, k, v, rank, count, with_seen):
    rows, cols = q.shape
    heads = cols // HEAD_DIM
    V = pl.BlockSpec(memory_space=pltpu.VMEM)
    return pl.pallas_call(
        partial(attn_fwd_kernel, with_seen, heads),
        out_shape=(jax.ShapeDtypeStruct((rows, cols), BF), jax.ShapeDtypeStruct((8, rows), F32)),
        in_specs=[pl.BlockSpec(memory_space=pltpu.SMEM)] + [V] * 5,
        out_specs=(V, V),
        scratch_shapes=[
            pltpu.VMEM((heads, ROW + TK, 256), BF),
            pltpu.VMEM((heads, HEAD_DIM + 16, ROW + TK), BF),
            pltpu.VMEM((ROW + TK, 128), F32),
            pltpu.VMEM((heads, HEAD_DIM + 16, TQ), F32),
            pltpu.VMEM((8, TQ), F32),
            pltpu.VMEM((heads // 2, 256, TQ), BF),
        ],
        compiler_params=pltpu.CompilerParams(vmem_limit_bytes=56 * 2**20),
        cost_estimate=pl.CostEstimate(flops=4 * 10**10, bytes_accessed=16 * 2**20, transcendentals=0),
        name="attend_self_forward" if with_seen else "attend_cross_forward",
    )(lengths, q, k, v, rank, count)

def three_way(value):
    hi = value.astype(BF).astype(F32)
    mid = (value - hi).astype(BF).astype(F32)
    return hi, mid, value - hi - mid

def attn_bwd_kernel(with_seen, heads, len_ref, q_ref, k_ref, v_ref, g_ref, o_ref, lse_ref, rank_ref, count_ref, pass_in,
                    dq_ref, dk_ref, dv_ref, pass_out,
                    kaug, vaug, kt, rank_cols, dk_sum, dv_sum, dq_sum, q_diag, g_diag, qt, gt, held, pass_sem):
    entering = pltpu.make_async_copy(pass_in, held, pass_sem.at[0])
    entering.start()
    cols = heads * HEAD_DIM
    starts, ends = doc_bounds(len_ref)
    start_lane, end_lane = lane_vector(starts), lane_vector(ends)
    fill_keys(kaug, k_ref, start_lane, end_lane, heads, True)
    lanes = lax.broadcasted_iota(jnp.int32, (TK, 128), 1)
    for h in range(heads):
        picks = (lanes == h) | (lanes == 8 + h) | (lanes == 16 + h)
        side = jnp.where(picks, -1.0, 0.0).astype(BF)
        for t in range(ROW // TK):
            pair = v_ref[t * TK:(t + 1) * TK, h // 2 * 128:h // 2 * 128 + 128]
            vaug[h, t * TK:(t + 1) * TK, 0:128] = head_lanes(pair, h)
            vaug[h, t * TK:(t + 1) * TK, 128:256] = side
        vaug[h, ROW:, :] = jnp.zeros((TK, 256), BF)
    for t in range(ROW // TK):
        kt[:, t * TK:(t + 1) * TK] = k_ref[t * TK:(t + 1) * TK, :].T
    kt[:, ROW:] = jnp.zeros((cols, TK), BF)
    if with_seen:
        fill_ranks(rank_cols, rank_ref, starts)
    entering.wait()
    leaving = pltpu.make_async_copy(held, pass_out, pass_sem.at[1])
    leaving.start()
    dk_sum[...] = jnp.zeros_like(dk_sum)
    dv_sum[...] = jnp.zeros_like(dv_sum)
    sel_row = lax.broadcasted_iota(jnp.int32, (8, cols), 0)
    sel_lane = lax.div(lax.broadcasted_iota(jnp.int32, (8, cols), 1), HEAD_DIM)
    selector = jnp.where(sel_lane == sel_row, 1.0, 0.0).astype(BF)

    def one_q(t, c):
        q0 = pl.multiple_of(t * TQ, TQ)
        first, steps = key_range(starts, ends, q0)
        g = g_ref[pl.ds(q0, TQ), :]
        q = q_ref[pl.ds(q0, TQ), :]
        spread = g.astype(F32) * o_ref[pl.ds(q0, TQ), :].astype(F32)
        spread_hi = spread.astype(BF)
        delta = nt(selector, spread_hi) + nt(selector, (spread - spread_hi.astype(F32)).astype(BF))
        daug = jnp.concatenate(list(three_way(delta)) + [jnp.zeros((104, TQ), F32)], 0).astype(BF)
        lse = lse_ref[:, pl.ds(q0, TQ)]
        hi, mid, lo = three_way(lse)
        side = jnp.concatenate([doc_hot_rows(starts, ends, q0), jnp.zeros((32, TQ), F32), hi, mid, lo, jnp.zeros((40, TQ), F32)], 0).astype(BF)
        for p in range(heads // 2):
            qt[p, 0:128, :] = q[:, p * 128:(p + 1) * 128].T
            qt[p, 128:256, :] = side
            gt[p, 0:128, :] = g[:, p * 128:(p + 1) * 128].T
            gt[p, 128:256, :] = daug
        wide = lax.div(lax.broadcasted_iota(jnp.int32, (TQ, cols), 1), HEAD_DIM)
        for h in range(heads):
            q_diag[h * TQ:(h + 1) * TQ, :] = jnp.where(wide == h, q, jnp.zeros_like(q))
            g_diag[h * TQ:(h + 1) * TQ, :] = jnp.where(wide == h, g, jnp.zeros_like(g))
        count_row = count_ref[:, pl.ds(q0, TQ)].astype(F32)
        dq_sum[...] = jnp.zeros_like(dq_sum)

        def one_k(s, c):
            k0 = pl.multiple_of(first + s * TK, 128)
            bias = seen_bias(rank_cols, count_row, k0, q0) if with_seen else None
            all_ds, all_p, all_dq = [], [], []
            kaugs = [kaug[h, pl.ds(k0, TK), :] for h in range(heads)]
            vaugs = [vaug[h, pl.ds(k0, TK), :] for h in range(heads)]
            keys_t = kt[:, pl.ds(k0, TK)]
            qts = [qt[p] for p in range(heads // 2)]
            gts = [gt[p] for p in range(heads // 2)]
            qd, gd = q_diag[...], g_diag[...]
            scores = [nn(kaugs[h], qts[h // 2]) for h in range(heads)]
            dps = [nn(vaugs[h], gts[h // 2]) for h in range(heads)]
            if with_seen:
                scores = [score + bias for score in scores]
            for h in range(heads):
                p = jnp.exp(scores[h])
                ds = (p * dps[h]).astype(BF)
                all_ds.append(ds)
                all_p.append(p.astype(BF))
                all_dq.append(nn(keys_t[h * HEAD_DIM:(h + 1) * HEAD_DIM, :], ds))
            dk = dk_sum[pl.ds(k0, TK), :] + nn(jnp.concatenate(all_ds, 1), qd)
            dv = dv_sum[pl.ds(k0, TK), :] + nn(jnp.concatenate(all_p, 1), gd)
            dq = dq_sum[...] + jnp.concatenate(all_dq, 0)
            dk_sum[pl.ds(k0, TK), :] = dk
            dv_sum[pl.ds(k0, TK), :] = dv
            dq_sum[...] = dq
            return c
        lax.fori_loop(0, steps, one_k, 0)
        dq_ref[pl.ds(q0, TQ), :] = (dq_sum[...] * HEAD_DIM ** -0.5).T.astype(BF)
        return c
    lax.fori_loop(0, ROW // TQ, one_q, 0)
    dk_ref[...] = (dk_sum[:ROW, :] * HEAD_DIM ** -0.5).astype(BF)
    dv_ref[...] = dv_sum[:ROW, :].astype(BF)
    leaving.wait()

def attend_backward(lengths, q, k, v, g, o, lse, rank, count, passed, with_seen):
    rows, cols = q.shape
    heads = cols // HEAD_DIM
    V = pl.BlockSpec(memory_space=pltpu.VMEM)
    like = jax.ShapeDtypeStruct((rows, cols), BF)
    return pl.pallas_call(
        partial(attn_bwd_kernel, with_seen, heads),
        out_shape=(like, like, like, jax.ShapeDtypeStruct(passed.shape, passed.dtype)),
        in_specs=[pl.BlockSpec(memory_space=pltpu.SMEM)] + [V] * 8 + [pl.BlockSpec(memory_space=pl.ANY)],
        out_specs=(V, V, V, pl.BlockSpec(memory_space=pl.ANY)),
        scratch_shapes=[
            pltpu.VMEM((heads, ROW + TK, 256), BF),
            pltpu.VMEM((heads, ROW + TK, 256), BF),
            pltpu.VMEM((cols, ROW + TK), BF),
            pltpu.VMEM((ROW + TK, 128), F32),
            pltpu.VMEM((ROW + TK, cols), F32),
            pltpu.VMEM((ROW + TK, cols), F32),
            pltpu.VMEM((cols, TQ), F32),
            pltpu.VMEM((heads * TQ, cols), BF),
            pltpu.VMEM((heads * TQ, cols), BF),
            pltpu.VMEM((heads // 2, 256, TQ), BF),
            pltpu.VMEM((heads // 2, 256, TQ), BF),
            pltpu.VMEM(passed.shape, passed.dtype),
            pltpu.SemaphoreType.DMA((2,)),
        ],
        compiler_params=pltpu.CompilerParams(vmem_limit_bytes=56 * 2**20),
        cost_estimate=pl.CostEstimate(flops=4 * 10**10, bytes_accessed=16 * 2**20, transcendentals=0),
        name="attend_self_backward" if with_seen else "attend_cross_backward",
    )(lengths, q, k, v, g, o, lse, rank, count, passed)


def send(src, dst, send_sem, recv_sem, **where):
    copy = pltpu.make_async_remote_copy(src_ref=src, dst_ref=dst, send_sem=send_sem, recv_sem=recv_sem,
                                        device_id=where, device_id_type=pl.DeviceIdType.MESH)
    copy.start()
    return copy

def greet(peers):
    barrier = pltpu.get_barrier_semaphore()
    for where in peers:
        pl.semaphore_signal(barrier, inc=1, device_id=where, device_id_type=pl.DeviceIdType.MESH)
    pl.semaphore_wait(barrier, len(peers))

def places_of(count):
    me = lax.axis_index("dp")
    across = count // 4
    x, y, z = lax.rem(me, 2), lax.rem(lax.div(me, 2), 2), lax.div(me, 4)
    xpeer, ypeer = me + 1 - 2 * x, me + 2 - 4 * y
    order = sorted(range(1, across), key=lambda d: min(d, across - d))
    ahead = lambda d: lax.rem(z + d, across) * 4 + y * 2 + x
    behind = lambda d: lax.rem(z + across - d, across) * 4 + y * 2 + x
    return me, x, y, z, xpeer, ypeer, order, ahead, behind

def spread_blocks(count, out, rows, places, zs, xs, ys, gx, gy):
    me, x, y, z, xpeer, ypeer, order, ahead, behind = places
    half = rows // 32 * 16
    whole = pl.ds(0, rows)
    sent, recv = [], {}
    def go(src_block, at, sem, d, to):
        copy = send(out.at[src_block, at], out.at[src_block, at], sem.at[0, d], sem.at[1, d], dp=to)
        sent.append(copy)
        return copy
    near = go(me, whole, xs, 0, xpeer), go(me, whole, ys, 0, ypeer)
    recv[0] = near
    zcopies = {}
    for d in order:
        zcopies[d] = go(me, whole, zs, d, ahead(d))
    steps = [0] + order
    diag = []
    for k, d in enumerate(steps):
        if d:
            zcopies[d].wait_recv()
            recv[d] = go(behind(d), whole, xs, d, xpeer), go(behind(d), whole, ys, d, ypeer)
        if k:
            forward(go, diag, recv, steps[k - 1], behind, places, half, rows, gx, gy)
    forward(go, diag, recv, steps[-1], behind, places, half, rows, gx, gy)
    for copy in diag:
        copy.wait_recv()
    for copy in sent:
        copy.wait_send()

def forward(go, diag, recv, d, behind, places, half, rows, gx, gy):
    me, x, y, z, xpeer, ypeer, order, ahead, _ = places
    base = behind(d) if d else me
    recv[d][0].wait_recv()
    diag.append(go(base + 1 - 2 * x, pl.ds(0, half), gy, d, ypeer))
    recv[d][1].wait_recv()
    diag.append(go(base + 2 - 4 * y, pl.ds(half, rows - half), gx, d, xpeer))

def gather_kernel(count, master, norm, out_ref, zs, xs, ys, gx, gy):
    places = places_of(count)
    me, x, y, z, xpeer, ypeer, order, ahead, behind = places
    rows = master.shape[0]
    out_ref[me, 0:rows, :] = master[...].astype(BF)
    out_ref[me, rows:rows + UNIT, :] = jnp.broadcast_to(norm[...], (UNIT, norm.shape[1])).astype(BF)
    greet([{"dp": xpeer}, {"dp": ypeer}] + [{"dp": ahead(d)} for d in order])
    spread_blocks(count, out_ref, rows + UNIT, places, zs, xs, ys, gx, gy)


def gather_blocks(master, norm, count):
    rows, cols = master.shape
    sems = pltpu.SemaphoreType.DMA((2, count // 4))
    return call(partial(gather_kernel, count), "gather_units", [master, norm], "VV",
                [((count, rows + UNIT, cols), BF, "V")], [sems] * 5, 0)[0]


def part_sizes(rows):
    first = rows // 2 // UNIT * UNIT
    return [(part, pl.ds(start, size), size) for part, start, size in ((0, 0, first), (1, first, rows - first)) if size]


class BlockSum:
    def __init__(self, count, places, source, out, keep, r1, r2, r3, s1, s2, s3):
        self.count, self.places, self.source, self.out = count, places, source, out
        self.keep, self.r1, self.r2, self.r3, self.s1, self.s2, self.s3 = keep, r1, r2, r3, s1, s2, s3
        self.parts = part_sizes(source.shape[1])
        self.first, self.second, self.third = {}, {}, {}

    def at(self, d, first, second, part):
        z, across = self.places[3], self.count // 4
        return lax.rem(z + d, across) * 4 + (first + 2 * second if part == 0 else 2 * first + second)

    def start(self):
        me, x, y, z, xpeer, ypeer, order, ahead, behind = self.places
        self.steps = order + [0]
        self.mine = [(x, y), (y, x)]
        self.peers = [(xpeer, ypeer), (ypeer, xpeer)]
        for d in self.steps:
            for part, rows, size in self.parts:
                f, s = self.mine[part]
                for t in (0, 1):
                    second = s if t else 1 - s
                    self.first[d, part, t] = send(
                        self.source.at[self.at(d, 1 - f, second, part), rows], self.r1.at[part, d, t, pl.ds(0, size)],
                        self.s1.at[0, part, d, t], self.s1.at[1, part, d, t], dp=self.peers[part][0])

    def second_stage(self, d):
        for part, rows, size in self.parts:
            f, s = self.mine[part]
            into = pl.ds(0, size)
            for t in (0, 1):
                second = s if t else 1 - s
                self.first[d, part, t].wait_recv()
                self.keep[part, d, t, into, :] = (self.source[self.at(d, f, second, part), rows, :].astype(F32)
                                                  + self.r1[part, d, t, into, :].astype(F32)).astype(BF)
                if t == 0:
                    self.second[d, part] = send(self.keep.at[part, d, 0, into], self.r2.at[part, d, into],
                                                self.s2.at[0, part, d], self.s2.at[1, part, d], dp=self.peers[part][1])

    def third_stage(self, d):
        ahead = self.places[7]
        for part, rows, size in self.parts:
            into = pl.ds(0, size)
            self.second[d, part].wait_recv()
            self.keep[part, d, 1, into, :] = (self.keep[part, d, 1, into, :].astype(F32)
                                              + self.r2[part, d, into, :].astype(F32)).astype(BF)
            if d:
                self.third[d, part] = send(self.keep.at[part, d, 1, into], self.r3.at[part, d, into],
                                           self.s3.at[0, part, d], self.s3.at[1, part, d], dp=ahead(d))

    def finish(self):
        me, order = self.places[0], self.places[6]
        for k, d in enumerate(self.steps):
            self.second_stage(d)
            if k:
                self.third_stage(self.steps[k - 1])
        self.third_stage(0)
        for part, rows, size in self.parts:
            into = pl.ds(0, size)
            total = self.keep[part, 0, 1, into, :].astype(F32)
            for d in order:
                self.third[d, part].wait_recv()
                total = total + self.r3[part, d, into, :].astype(F32)
            self.out[me, rows, :] = total.astype(BF)

    def drain(self):
        for copies in (self.first, self.second, self.third):
            for copy in copies.values():
                copy.wait_send()


def block_sum_scratch(count, rows, cols):
    across = count // 4
    size = max(size for _, _, size in part_sizes(rows))
    D = pltpu.SemaphoreType.DMA
    return [
        pltpu.VMEM((2, across, 2, size, cols), BF), pltpu.VMEM((2, across, 2, size, cols), BF),
        pltpu.VMEM((2, across, size, cols), BF), pltpu.VMEM((2, across, size, cols), BF),
        D((2, 2, across, 2)), D((2, 2, across)), D((2, 2, across))]


def plane_swap(value, count, f):
    return lax.ppermute(value, "dp", [(i, i // 4 * 4 + (i % 4 ^ f)) for i in range(count)])


def plane_offset(places, f):
    x, y = places[1], places[2]
    return lax.rem(x + f % 2, 2) + 2 * lax.rem(y + f // 2, 2)


def call(kernel, name, args, kinds, outs, scratch, number=None):
    space = {"V": pltpu.VMEM, "S": pltpu.SMEM, "A": pl.ANY}
    extra = {} if number is None else dict(collective_id=number, has_side_effects=True)
    return pl.pallas_call(
        kernel,
        out_shape=tuple(jax.ShapeDtypeStruct(shape, dtype) for shape, dtype, _ in outs),
        in_specs=[pl.BlockSpec(memory_space=space[kind]) for kind in kinds],
        out_specs=tuple(pl.BlockSpec(memory_space=space[kind]) for _, _, kind in outs),
        scratch_shapes=scratch,
        compiler_params=pltpu.CompilerParams(vmem_limit_bytes=60 * 2**20, **extra),
        cost_estimate=pl.CostEstimate(flops=4 * 10**10, bytes_accessed=16 * 2**20, transcendentals=0),
        name=name,
    )(*args)


CHUNK = 256


def tn(a, b):
    return lax.dot_general(a, b, (((0,), (0,)), ((), ())), preferred_element_type=F32)


def normalise(value):
    centred = value - jnp.mean(value, -1, keepdims=True)
    scale = lax.rsqrt(jnp.mean(centred * centred, -1, keepdims=True) + EPS_NORM)
    return centred * scale, scale


def norm_back(unit, scale, gain, grad):
    inner = grad * gain
    return scale * (inner - jnp.mean(inner, -1, keepdims=True) - unit * jnp.mean(inner * unit, -1, keepdims=True))


def fold_rows(value):
    return jnp.sum(value.reshape(value.shape[0] // 8, 8, value.shape[1]), 0)


def interleave(size):
    row = lax.broadcasted_iota(jnp.int32, (size, size), 0)
    col = lax.broadcasted_iota(jnp.int32, (size, size), 1)
    source = jnp.where((row & 1) == 0, row >> 1, (row >> 1) + size // 2)
    return jnp.where(col == source, 1.0, 0.0).astype(BF)


def part_rows(matrix, order):
    return lax.dot_general(order, matrix, (((0,), (0,)), ((), ())), preferred_element_type=F32).astype(BF)


def as_units(gradient, order):
    parted = part_rows(gradient.astype(BF), order)
    half = parted.shape[0] // 2
    return jnp.concatenate([parted[:half], parted[half:]], 1)


def other_core(mine, theirs, sems, step):
    rows = pl.ds(step * CHUNK, CHUNK)
    return pltpu.make_async_remote_copy(
        src_ref=mine.at[rows], dst_ref=theirs.at[rows], send_sem=sems.at[0, step], recv_sem=sems.at[1, step],
        device_id={"head": 1 - lax.axis_index("head")}, device_id_type=pl.DeviceIdType.MESH)


def greet_core():
    greet([{"head": 1 - lax.axis_index("head")}])


def chunks(total, body):
    def one(step, carry):
        body(step, pl.ds(pl.multiple_of(step * CHUNK, CHUNK), CHUNK))
        return carry
    lax.fori_loop(0, total // CHUNK, one, 0)


def drain(total, mine, theirs, sems):
    def body(step, rows):
        other_core(mine, theirs, sems, step).wait_send()
    chunks(total, body)


class Late:
    def __init__(self, pairs, sems):
        self.copies = [pltpu.make_async_copy(source, held, sems.at[i]) for i, (source, held) in enumerate(pairs)]
        for copy in self.copies:
            copy.start()

    def wait(self, *which):
        for i in which:
            self.copies[i].wait()


class Out:
    def __init__(self, pairs, sems):
        self.pairs, self.sems = pairs, sems

    def copy(self, i, step):
        held, out = self.pairs[i]
        rows = pl.ds(pl.multiple_of(step * CHUNK, CHUNK), CHUNK)
        return pltpu.make_async_copy(held.at[rows], out.at[rows], self.sems.at[i, step])

    def start(self, i, step):
        self.copy(i, step).start()

    def drain(self, tokens):
        def body(step, rows):
            for i in range(len(self.pairs)):
                self.copy(i, step).wait()
        chunks(tokens, body)


def project_kernel(owner_ref, gathered, norms, query_hbm, kv_hbm, memory_hbm,
                   nq_out, nkv_out, q_out, k_out, v_out, kc_out, vc_out, ws_ref, wc_ref, wos_ref, woc_ref, w1_ref, w2_ref,
                   flat, used, query_ref, kv_ref, memory_ref, nq_ref, nkv_ref, q_ref, k_ref, v_ref, kc_ref, vc_ref,
                   late_sems, out_sems):
    tokens, features = query_ref.shape
    devices = gathered.shape[0]
    units = owner_ref.shape[0]
    late = Late([(query_hbm, query_ref), (kv_hbm, kv_ref), (memory_hbm, memory_ref)], late_sems)
    out = Out([(nq_ref, nq_out), (nkv_ref, nkv_out), (q_ref, q_out), (k_ref, k_out), (v_ref, v_out), (kc_ref, kc_out),
               (vc_ref, vc_out)], out_sems)
    for d in range(devices):
        used[d] = 0

    def one_unit(u, carry):
        owner = owner_ref[u]
        slot = used[owner]
        used[owner] = slot + 1
        flat[pl.ds(pl.multiple_of(u * UNIT, UNIT), UNIT), :] = gathered[owner, pl.ds(pl.multiple_of(slot * UNIT, UNIT), UNIT), :]
        return carry
    lax.fori_loop(0, units, one_unit, 0, unroll=4)
    order = interleave(features)
    cols = q_ref.shape[1]
    for number in range(6):
        rows = flat[number * cols:(number + 1) * cols, :]
        stacked = jnp.concatenate([rows[:, :cols], rows[:, cols:]], 0)
        matrix = nn(order, stacked).astype(BF)
        if number < 3:
            ws_ref[number] = matrix
        else:
            wc_ref[number - 3] = matrix
    wos_ref[...] = flat[6 * cols:7 * cols, :]
    woc_ref[...] = flat[7 * cols:8 * cols, :]
    hidden = w2_ref.shape[0]
    for block in range(hidden // features):
        at = 8 * cols + block * features
        parted = part_rows(flat[at:at + features, :], order)
        half = features // 2
        w1_ref[block * half:(block + 1) * half, :] = jnp.concatenate([parted[:half], parted[half:]], 1)
    w2_ref[...] = flat[8 * cols + hidden:, :]
    late.wait(0, 1, 2)

    def body(step, rows):
        nq = (normalise(query_ref[rows, :].astype(F32))[0] * norms[0:1, :] + norms[1:2, :]).astype(BF)
        nkv = (normalise(kv_ref[rows, :].astype(F32))[0] * norms[2:3, :] + norms[3:4, :]).astype(BF)
        source = memory_ref[rows, :]
        results = [nq, nkv, nn(nq, ws_ref[0]), nn(nkv, ws_ref[1]), nn(nkv, ws_ref[2]), nn(source, wc_ref[1]), nn(source, wc_ref[2])]
        for i, (ref, result) in enumerate(zip((nq_ref, nkv_ref, q_ref, k_ref, v_ref, kc_ref, vc_ref), results)):
            ref[rows, :] = result.astype(BF)
            out.start(i, step)
    chunks(tokens, body)
    out.drain(tokens)


def pair_sems(tokens):
    return pltpu.SemaphoreType.DMA((2, tokens // CHUNK))


def out_semaphores(count, tokens):
    return pltpu.SemaphoreType.DMA((count, tokens // CHUNK))


def project(unit_owner, gathered, norms, query_stream, kv_stream, memory, cols, hidden):
    tokens, features = query_stream.shape
    wide, narrow = (tokens, features), (tokens, cols)
    outs = [(wide, BF, "A")] * 2 + [(narrow, BF, "A")] * 5 + [
        ((3, features, cols), BF, "V"), ((3, features, cols), BF, "V"), ((cols, features), BF, "V"), ((cols, features), BF, "V"),
        ((features, hidden), BF, "V"), ((hidden, features), BF, "V")]
    scratch = [pltpu.VMEM((8 * cols + 2 * hidden, features), BF), pltpu.SMEM((gathered.shape[0],), jnp.int32)]
    scratch += [pltpu.VMEM(wide, BF)] * 5 + [pltpu.VMEM(narrow, BF)] * 5
    scratch += [pltpu.SemaphoreType.DMA((3,)), out_semaphores(7, tokens)]
    return call(project_kernel, "project", [unit_owner, gathered, norms, query_stream, kv_stream, memory], "SVVAAA", outs, scratch)


def self_out_kernel(mixed, wo, query_hbm, wc, norms, res_out, nc_out, q_out,
                    query, res_ref, nc_ref, q_ref, mine, theirs, sems, late_sems, out_sems):
    tokens = query.shape[0]
    late = Late([(query_hbm, query)], late_sems)
    out = Out([(res_ref, res_out), (nc_ref, nc_out), (q_ref, q_out)], out_sems)
    greet_core()

    def give(step, rows):
        mine[rows, :] = nn(mixed[rows, :], wo[...]).astype(BF)
        other_core(mine, theirs, sems, step).start()
    chunks(tokens, give)
    late.wait(0)

    def take(step, rows):
        other_core(mine, theirs, sems, step).wait_recv()
        res = query[rows, :].astype(F32) + (mine[rows, :].astype(F32) + theirs[rows, :].astype(F32))
        res_ref[rows, :] = res
        out.start(0, step)
        nc = (normalise(res)[0] * norms[4:5, :] + norms[5:6, :]).astype(BF)
        nc_ref[rows, :] = nc
        out.start(1, step)
        q_ref[rows, :] = nn(nc, wc[0]).astype(BF)
        out.start(2, step)
    chunks(tokens, take)
    drain(tokens, mine, theirs, sems)
    out.drain(tokens)


def self_out(mixed, wo, query, wc, norms):
    tokens, features = query.shape
    wide = (tokens, features)
    outs = [(wide, F32, "A"), (wide, BF, "A"), (mixed.shape, BF, "A")]
    scratch = [pltpu.VMEM(wide, BF), pltpu.VMEM(wide, F32), pltpu.VMEM(wide, BF), pltpu.VMEM(mixed.shape, BF),
               pltpu.VMEM(wide, BF), pltpu.VMEM(wide, BF), pair_sems(tokens), pltpu.SemaphoreType.DMA((1,)),
               out_semaphores(3, tokens)]
    return call(self_out_kernel, "self_out", [mixed, wo, query, wc, norms], "VVAVV", outs, scratch, 2)


def gelu_parts(value):
    size = jnp.abs(value)
    bell = jnp.exp(-0.5 * value * value)
    t = 1.0 / (1.0 + (0.3275911 * 0.7071067811865476) * size)
    poly = ((((1.061405429 * t - 1.453152027) * t + 1.421413741) * t - 0.284496736) * t + 0.254829592) * t
    tail = 0.5 * poly * bell
    below = jnp.where(value < 0.0, tail, 1.0 - tail)
    return value * below, below + value * (bell * 0.3989422804014327)


def spread_flat(devices, places, flat, refs):
    rows = flat.shape[0] // devices
    for f, ref in enumerate(refs):
        place = plane_offset(places, f)
        for level in range(devices // 4):
            ref[level, ref.shape[1] - rows:, :] = flat[pl.ds(pl.multiple_of((level * 4 + place) * rows, UNIT), rows), :]


def feed_forward_kernel(devices, mixed, wo, res_hbm, w1, w2, out_grad_hbm, norms,
                        out_out, gres_out, gmix_out, part0, part1, part2, part3, gwo_ref, sums_ref,
                        res, out_grad, out_ref, gres_ref, gmix_ref, flat,
                        mine, theirs, nf_all, hid_all, pre_all, low_all, mine_o, theirs_o, mine_g, theirs_g,
                        sems, sems_o, sems_g, late_sems, out_sems):
    tokens, features = out_grad.shape
    hidden = w2.shape[0]
    places = places_of(devices)
    late = Late([(res_hbm, res), (out_grad_hbm, out_grad)], late_sems)
    out = Out([(out_ref, out_out), (gres_ref, gres_out), (gmix_ref, gmix_out)], out_sems)
    greet_core()

    def give(step, rows):
        mine[rows, :] = nn(mixed[rows, :], wo[...]).astype(BF)
        other_core(mine, theirs, sems, step).start()
    chunks(tokens, give)
    late.wait(0, 1)

    def middle(step, rows):
        other_core(mine, theirs, sems, step).wait_recv()
        value = res[rows, :] + (mine[rows, :].astype(F32) + theirs[rows, :].astype(F32))
        gres_ref[rows, :] = value
        nf = (normalise(value)[0] * norms[6:7, :] + norms[7:8, :]).astype(BF)
        nf_all[rows, :] = nf
        grad = out_grad[rows, :]
        out_part = jnp.zeros((CHUNK, features), F32)
        grad_part = jnp.zeros((CHUNK, features), F32)
        for block in range(hidden // 256):
            at = slice(block * 256, (block + 1) * 256)
            act, slope = gelu_parts(nn(nf, w1[:, at]))
            act = act.astype(BF)
            hid_all[rows, at] = act
            pre = (slope * nt(grad, w2[at, :])).astype(BF)
            pre_all[rows, at] = pre
            out_part = out_part + nn(act, w2[at, :])
            grad_part = grad_part + nt(pre, w1[:, at])
        mine_o[rows, :] = out_part.astype(BF)
        other_core(mine_o, theirs_o, sems_o, step).start()
        mine_g[rows, :] = grad_part.astype(BF)
        other_core(mine_g, theirs_g, sems_g, step).start()
    chunks(tokens, middle)

    order = interleave(features)
    half = features // 2
    for block in range(hidden // 256):
        at = slice(block * 256, (block + 1) * 256)
        flat[hidden + block * 256:hidden + (block + 1) * 256, :] = tn(hid_all[:, at], out_grad[...]).astype(BF)
    for block in range(hidden // features):
        gradient = tn(nf_all[:, block * half:(block + 1) * half], pre_all[...]).astype(BF)
        stacked = jnp.concatenate([gradient[:, :features], gradient[:, features:]], 0)
        flat[block * features:(block + 1) * features, :] = nn(order, stacked).astype(BF)
    spread_flat(devices, places, flat, (part0, part1, part2, part3))
    sums_ref[...] = jnp.zeros_like(sums_ref)

    def close(step, rows):
        other_core(mine_o, theirs_o, sems_o, step).wait_recv()
        other_core(mine_g, theirs_g, sems_g, step).wait_recv()
        value = gres_ref[rows, :]
        out_ref[rows, :] = (value + (mine_o[rows, :].astype(F32) + theirs_o[rows, :].astype(F32))).astype(BF)
        out.start(0, step)
        grad = mine_g[rows, :].astype(F32) + theirs_g[rows, :].astype(F32)
        unit, scale = normalise(value)
        gres = norm_back(unit, scale, norms[6:7, :], grad) + out_grad[rows, :].astype(F32)
        gres_ref[rows, :] = gres
        out.start(1, step)
        sums_ref[0:8, :] += fold_rows(grad * unit)
        sums_ref[8:16, :] += fold_rows(grad)
        low = gres.astype(BF)
        low_all[rows, :] = low
        gmix_ref[rows, :] = nt(low, wo[...]).astype(BF)
        out.start(2, step)
    chunks(tokens, close)
    gwo_ref[...] = tn(mixed[...], low_all[...]).astype(BF)
    out.drain(tokens)
    drain(tokens, mine, theirs, sems)
    drain(tokens, mine_o, theirs_o, sems_o)
    drain(tokens, mine_g, theirs_g, sems_g)


def feed_forward(devices, mixed, wo, res, w1, w2, out_grad, norms):
    tokens, features = out_grad.shape
    hidden = w2.shape[0]
    part = ((devices // 4, 2 * hidden // devices, features), BF, "V")
    wide = (tokens, features)
    outs = [(wide, BF, "A"), (wide, F32, "A"), (mixed.shape, BF, "A")] + [part] * 4 + [
        (wo.shape, BF, "V"), ((16, features), F32, "V")]
    deep, narrow = pltpu.VMEM((tokens, hidden), BF), pltpu.VMEM(wide, BF)
    scratch = [pltpu.VMEM(wide, F32), narrow, narrow, pltpu.VMEM(wide, F32), pltpu.VMEM(mixed.shape, BF),
               pltpu.VMEM((2 * hidden, features), BF), narrow, narrow, narrow, deep, deep, narrow] + [narrow] * 4
    scratch += [pair_sems(tokens)] * 3 + [pltpu.SemaphoreType.DMA((2,)), out_semaphores(3, tokens)]
    return call(partial(feed_forward_kernel, devices), "feed_forward", [mixed, wo, res, w1, w2, out_grad, norms], "VVAVVAV",
                outs, scratch, 3)


def branch_give(dq, dk, dv, weights, mine_a, theirs_a, mine_b, theirs_b, sems_a, sems_b):
    def give(step, rows):
        mine_a[rows, :] = nt(dq[rows, :], weights[0]).astype(BF)
        other_core(mine_a, theirs_a, sems_a, step).start()
        mine_b[rows, :] = (nt(dk[rows, :], weights[1]) + nt(dv[rows, :], weights[2])).astype(BF)
        other_core(mine_b, theirs_b, sems_b, step).start()
    chunks(dq.shape[0], give)


def branch_weights(first_in, second_in, dq, dk, dv, flat):
    cols = dq.shape[1]
    order = interleave(first_in.shape[1])
    for number, (entering, grad) in enumerate(((first_in, dq), (second_in, dk), (second_in, dv))):
        flat[number * cols:(number + 1) * cols, :] = as_units(tn(entering[...], grad[...]), order)


def z_sum_start(devices, places, pieces, landed, sems):
    me, x, y, z, xpeer, ypeer, order, ahead, behind = places
    return [send(pieces.at[lax.rem(z + d, devices // 4)], landed.at[d], sems.at[0, d], sems.at[1, d], dp=ahead(d)) for d in order]


def z_sum_end(places, pieces, landed, copies):
    z, order = places[3], places[6]
    total = pieces[z].astype(F32)
    for copy, d in zip(copies, order):
        copy.wait_recv()
        total = total + landed[d].astype(F32)
    return total.astype(BF)


def four_sum(parts, at):
    return (parts[0][at].astype(F32) + parts[1][at].astype(F32) + parts[2][at].astype(F32) + parts[3][at].astype(F32)).astype(BF)


def cross_back_kernel(devices, dq, dk, dv, wc, nc_hbm, memory_hbm, res_hbm, gres_hbm, mixed, wo, norms, gwo_cross,
                      part0, part1, part2, part3,
                      gmem_out, gnew_out, gmix_out, give0, give1, give2, give3, sums_ref,
                      nc, memory, res, gres, gmem_ref, gnew_ref, gmix_ref, flat, pieces, landed, blocks,
                      mine_a, theirs_a, mine_b, theirs_b, low_all, sems_a, sems_b, late_sems, out_sems, z_sems, zz_sems):
    tokens, features = nc.shape
    cols = dq.shape[1]
    across = devices // 4
    places = places_of(devices)
    me, x, y, z, xpeer, ypeer, order, ahead, behind = places
    late = Late([(nc_hbm, nc), (memory_hbm, memory), (res_hbm, res), (gres_hbm, gres)], late_sems)
    out = Out([(gmem_ref, gmem_out), (gnew_ref, gnew_out), (gmix_ref, gmix_out)], out_sems)
    for level in range(across):
        pieces[level] = four_sum((part0, part1, part2, part3), level)
    greet([{"head": 1 - lax.axis_index("head")}] + [{"dp": ahead(d)} for d in order])
    z_copies = z_sum_start(devices, places, pieces, landed, z_sems)
    branch_give(dq, dk, dv, wc, mine_a, theirs_a, mine_b, theirs_b, sems_a, sems_b)
    late.wait(0, 1)
    branch_weights(nc, memory, dq, dk, dv, flat)
    blocks[0] = z_sum_end(places, pieces, landed, z_copies)
    zz_copies = [send(blocks.at[0], blocks.at[d], zz_sems.at[0, d], zz_sems.at[1, d], dp=ahead(d)) for d in order]
    sums_ref[...] = jnp.zeros_like(sums_ref)
    late.wait(2, 3)

    def close(step, rows):
        other_core(mine_a, theirs_a, sems_a, step).wait_recv()
        grad = mine_a[rows, :].astype(F32) + theirs_a[rows, :].astype(F32)
        unit, scale = normalise(res[rows, :])
        gnew = norm_back(unit, scale, norms[4:5, :], grad) + gres[rows, :]
        gnew_ref[rows, :] = gnew
        out.start(1, step)
        sums_ref[0:8, :] += fold_rows(grad * unit)
        sums_ref[8:16, :] += fold_rows(grad)
        low = gnew.astype(BF)
        low_all[rows, :] = low
        gmix_ref[rows, :] = nt(low, wo[...]).astype(BF)
        out.start(2, step)
        other_core(mine_b, theirs_b, sems_b, step).wait_recv()
        gmem_ref[rows, :] = (mine_b[rows, :].astype(F32) + theirs_b[rows, :].astype(F32)).astype(BF)
        out.start(0, step)
    chunks(tokens, close)
    flat[3 * cols:4 * cols, :] = tn(mixed[...], low_all[...]).astype(BF)
    flat[4 * cols:5 * cols, :] = gwo_cross[...]
    if flat.shape[0] > 5 * cols:
        flat[5 * cols:, :] = jnp.zeros((flat.shape[0] - 5 * cols, features), BF)
    gives = (give0, give1, give2, give3)
    spread_flat(devices, places, flat, gives)
    for copy in zz_copies:
        copy.wait_recv()
    ready_rows = blocks.shape[1]
    for ref in gives:
        for d in range(across):
            ref[d, 0:ready_rows, :] = blocks[d]
    for copy in z_copies + zz_copies:
        copy.wait_send()
    out.drain(tokens)
    drain(tokens, mine_a, theirs_a, sems_a)
    drain(tokens, mine_b, theirs_b, sems_b)


def cross_back(devices, dq, dk, dv, wc, nc, memory, res, gres, mixed, wo, norms, gwo_cross, parts):
    tokens, features = nc.shape
    cols = dq.shape[1]
    across, ready_rows = devices // 4, parts[0].shape[1]
    flat_rows = -(-5 * cols // (devices * UNIT)) * devices * UNIT
    give = ((across, ready_rows + flat_rows // devices, features), BF, "V")
    wide = (tokens, features)
    outs = [(wide, BF, "A"), (wide, F32, "A"), (dq.shape, BF, "A")] + [give] * 4 + [((16, features), F32, "V")]
    low, high = pltpu.VMEM(wide, BF), pltpu.VMEM(wide, F32)
    small = pltpu.VMEM((across, ready_rows, features), BF)
    z_sems = pltpu.SemaphoreType.DMA((2, across))
    scratch = [low, low, high, high, low, high, pltpu.VMEM(dq.shape, BF), pltpu.VMEM((flat_rows, features), BF), small, small, small]
    scratch += [low] * 5 + [pair_sems(tokens)] * 2 + [pltpu.SemaphoreType.DMA((4,)), out_semaphores(3, tokens), z_sems, z_sems]
    return call(partial(cross_back_kernel, devices), "cross_back",
                [dq, dk, dv, wc, nc, memory, res, gres, mixed, wo, norms, gwo_cross] + parts, "VVVVAAAAVVVVVVVV", outs, scratch, 4)


def self_back_kernel(devices, ready_rows, dq, dk, dv, ws, nq_hbm, nkv_hbm, query_hbm, kv_hbm, gres_hbm, norms, sums_c, sums_f,
                     part0, part1, part2, part3,
                     gquery_out, gkv_out, summed, gnorm_ref,
                     nq, nkv, query, kv, gres, gquery_ref, gkv_ref, flat, source, pieces, landed, norm_mine, norm_all,
                     mine_a, theirs_a, mine_b, theirs_b, sums, sems_a, sems_b, late_sems, out_sems, z_sems, n_sems, *block_refs):
    tokens, features = nq.shape
    across = devices // 4
    places = places_of(devices)
    me, x, y, z, xpeer, ypeer, order, ahead, behind = places
    late = Late([(nq_hbm, nq), (nkv_hbm, nkv), (query_hbm, query), (kv_hbm, kv), (gres_hbm, gres)], late_sems)
    out = Out([(gquery_ref, gquery_out), (gkv_ref, gkv_out)], out_sems)
    more_rows = part0.shape[1] - ready_rows
    for level in range(across):
        pieces[level] = four_sum((part0, part1, part2, part3), (level, pl.ds(ready_rows, more_rows)))
    others = [lax.rem(me + d, devices) for d in range(1, devices)]
    greet([{"head": 1 - lax.axis_index("head")}] + [{"dp": other} for other in others])
    z_copies = z_sum_start(devices, places, pieces, landed, z_sems)
    branch_give(dq, dk, dv, ws, mine_a, theirs_a, mine_b, theirs_b, sems_a, sems_b)
    late.wait(0, 1)
    branch_weights(nq, nkv, dq, dk, dv, flat)
    rows = source.shape[1]
    if flat.shape[0] > 3 * dq.shape[1]:
        flat[3 * dq.shape[1]:, :] = jnp.zeros((flat.shape[0] - 3 * dq.shape[1], features), BF)
    for block in range(devices):
        source[block] = flat[block * rows:(block + 1) * rows, :]
    block_sum = BlockSum(devices, places, source, summed, *block_refs[:7])
    block_sum.start()
    summed[me, pl.ds(rows, more_rows), :] = z_sum_end(places, pieces, landed, z_copies)
    sums[...] = jnp.zeros_like(sums)
    late.wait(2, 3, 4)

    def close(step, rows):
        other_core(mine_a, theirs_a, sems_a, step).wait_recv()
        grad = mine_a[rows, :].astype(F32) + theirs_a[rows, :].astype(F32)
        unit, scale = normalise(query[rows, :].astype(F32))
        gquery_ref[rows, :] = (norm_back(unit, scale, norms[0:1, :], grad) + gres[rows, :]).astype(BF)
        out.start(0, step)
        sums[0:8, :] += fold_rows(grad * unit)
        sums[8:16, :] += fold_rows(grad)
        other_core(mine_b, theirs_b, sems_b, step).wait_recv()
        grad = mine_b[rows, :].astype(F32) + theirs_b[rows, :].astype(F32)
        unit, scale = normalise(kv[rows, :].astype(F32))
        gkv_ref[rows, :] = norm_back(unit, scale, norms[2:3, :], grad).astype(BF)
        out.start(1, step)
        sums[16:24, :] += fold_rows(grad * unit)
        sums[24:32, :] += fold_rows(grad)
    chunks(tokens, close)
    parts = [sums[8 * i:8 * i + 8, :] for i in range(4)]
    parts += [sums_c[0:8, :], sums_c[8:16, :], sums_f[0:8, :], sums_f[8:16, :]]
    norm_mine[...] = jnp.concatenate([jnp.sum(part, 0, keepdims=True) for part in parts], 0)
    n_copies = [send(norm_mine, norm_all.at[d], n_sems.at[0, d], n_sems.at[1, d], dp=other)
                for d, other in zip(range(1, devices), others)]
    block_sum.finish()
    spread_blocks(devices, summed, summed.shape[1], places, *block_refs[7:])
    total = norm_mine[...]
    for d, copy in zip(range(1, devices), n_copies):
        copy.wait_recv()
        total = total + norm_all[d]
    gnorm_ref[...] = total
    block_sum.drain()
    for copy in z_copies + n_copies:
        copy.wait_send()
    out.drain(tokens)
    drain(tokens, mine_a, theirs_a, sems_a)
    drain(tokens, mine_b, theirs_b, sems_b)


def self_back(devices, ready_rows, dq, dk, dv, ws, nq, nkv, query, kv, gres, norms, sums_c, sums_f, parts):
    tokens, features = nq.shape
    cols = dq.shape[1]
    across, more_rows = devices // 4, parts[0].shape[1] - ready_rows
    flat_rows = -(-3 * cols // (devices * UNIT)) * devices * UNIT
    rows = flat_rows // devices
    wide = (tokens, features)
    outs = [(wide, BF, "A"), (wide, BF, "A"), ((devices, rows + more_rows, features), BF, "V"), ((8, features), F32, "V")]
    low, high = pltpu.VMEM(wide, BF), pltpu.VMEM(wide, F32)
    small = pltpu.VMEM((across, more_rows, features), BF)
    D = pltpu.SemaphoreType.DMA
    scratch = [low, low, low, low, high, low, low, pltpu.VMEM((flat_rows, features), BF), pltpu.VMEM((devices, rows, features), BF),
               small, small, pltpu.VMEM((8, features), F32), pltpu.VMEM((devices, 8, features), F32)]
    scratch += [low] * 4 + [pltpu.VMEM((32, features), F32)] + [pair_sems(tokens)] * 2
    scratch += [D((5,)), out_semaphores(2, tokens), D((2, across)), D((2, devices))]
    scratch += block_sum_scratch(devices, rows, features) + [D((2, across))] * 5
    return call(partial(self_back_kernel, devices, ready_rows), "self_back",
                [dq, dk, dv, ws, nq, nkv, query, kv, gres, norms, sums_c, sums_f] + parts, "VVVVAAAAAVVVVVVV", outs, scratch, 5)


def update_kernel(devices, early_unit, late_unit, own_rows, last_rows, owner_ref, me_ref, summed, part0, part1, part2, part3,
                  master, first, second, gquery_in, gkv_in, grad_ref, first_ref, second_ref, new_ref, gquery_out, gkv_out,
                  held, taken, held_q, held_kv, sems):
    units = owner_ref.shape[0]
    slots = master.shape[0]
    across = devices // 4
    more_rows = summed.shape[1] - own_rows
    me = me_ref[0]
    entering = Late([(gquery_in, held_q), (gkv_in, held_kv)], sems.at[0])
    here, level = lax.rem(me, 4), lax.div(me, 4)

    def find(u, count):
        held[count] = u
        return count + (owner_ref[u] == me).astype(jnp.int32)
    count = lax.fori_loop(0, units, find, jnp.int32(0), unroll=4)
    entering.wait(0, 1)
    leaving = Late([(held_q, gquery_out), (held_kv, gkv_out)], sems.at[1])

    def rows_of(row, size, start):
        return pl.ds(pl.multiple_of(lax.rem(row, size) + start, UNIT), UNIT)

    def one(slot, carry):
        @pl.when(slot < count)
        def _():
            unit = held[slot]

            @pl.when(unit < early_unit)
            def _():
                row = unit * UNIT
                taken[...] = summed[lax.div(row, own_rows), rows_of(row, own_rows, 0), :]

            @pl.when((unit >= early_unit) & (unit < late_unit))
            def _():
                row = (unit - early_unit) * UNIT
                taken[...] = summed[lax.div(row, more_rows), rows_of(row, more_rows, own_rows), :]

            @pl.when(unit >= late_unit)
            def _():
                row = (unit - late_unit) * UNIT
                block = lax.div(row, last_rows)
                behind = lax.rem(level - lax.div(block, 4) + across, across)
                for f, part in enumerate((part0, part1, part2, part3)):
                    @pl.when(lax.rem(block, 4) == here ^ f)
                    def _():
                        taken[...] = part[behind, rows_of(row, last_rows, 0), :]
            gradient = taken[...].astype(F32)
            first_new, second_new, weight = adamw_step(gradient, first[slot], second[slot], master[slot], RATE_MATRIX, WEIGHT_DECAY)
            grad_ref[slot] = gradient
            first_ref[slot] = first_new
            second_ref[slot] = second_new
            new_ref[slot] = weight

        @pl.when(slot >= count)
        def _():
            for ref in (grad_ref, first_ref, second_ref, new_ref):
                ref[slot] = jnp.zeros(ref.shape[1:], F32)
        return carry
    lax.fori_loop(0, slots, one, 0)
    leaving.wait(0, 1)


def update(devices, early_unit, late_unit, own_rows, last_rows, unit_owner, me, summed, parts, master, first, second, gquery, gkv):
    outs = [(master.shape, F32, "V")] * 4 + [(gquery.shape, BF, "A")] * 2
    kernel = partial(update_kernel, devices, early_unit, late_unit, own_rows, last_rows)
    return call(kernel, "update", [unit_owner, me, summed] + parts + [master, first, second, gquery, gkv], "SSVVVVVVVVAA", outs,
                [pltpu.SMEM((unit_owner.shape[0] + 8,), jnp.int32), pltpu.VMEM((UNIT, master.shape[2]), BF),
                 pltpu.VMEM(gquery.shape, BF), pltpu.VMEM(gkv.shape, BF), pltpu.SemaphoreType.DMA((2, 2))])


def adamw_step(gradient, first, second, weight, rate, decay):
    first_new = BETA_ONE * first + (1.0 - BETA_ONE) * gradient
    second_new = BETA_TWO * second + (1.0 - BETA_TWO) * gradient * gradient
    corr_one = 1.0 - BETA_ONE**STEP
    corr_two = 1.0 - BETA_TWO**STEP
    direction = first_new / corr_one / (jnp.sqrt(second_new / corr_two) + ADAM_EPS)
    return (first_new, second_new, weight - rate * (direction + decay * weight))


def local(
    query_stream, kv_stream, memory, out_grad, lengths, obs_rank, obs_count, unit_owner,
    master, first_moment, second_moment, norm_master, norm_first, norm_second,
):
    devices = lax.axis_size("dp")
    shards = lax.axis_size("head")
    me = lax.axis_index("dp")
    slots, unit_rows, features = master.shape[0], master.shape[2], master.shape[3]
    units = unit_owner.shape[0]
    norm_share = norm_master.shape[0]
    cols = features // shards
    hidden = (units * unit_rows - 8 * cols) // 2

    shape = (slots, unit_rows, features)
    norm_row = jnp.pad(norm_master.reshape(1, norm_share), ((0, 0), (0, features - norm_share)))
    gathered = gather_blocks(master.reshape(slots * unit_rows, features), norm_row, devices)
    norms = gathered[:, slots * unit_rows, :norm_share].reshape(8, features).astype(F32)

    rank_row, count_row = obs_rank.reshape(1, ROW), obs_count.reshape(1, ROW)
    nq, nkv, q, k, v, kc, vc, ws, wc, wo_self, wo_cross, w1, w2 = project(
        unit_owner, gathered, norms, query_stream, kv_stream, memory, cols, hidden)
    mixed_self, total_self = attend_forward(lengths, q, k, v, rank_row, count_row, True)
    residual, nc, qc = self_out(mixed_self, wo_self, query_stream, wc, norms)
    mixed_cross, total_cross = attend_forward(lengths, qc, kc, vc, rank_row, count_row, False)
    output, grad_cross_res, grad_mixed, *parts, gwo_cross, sums_f = feed_forward(
        devices, mixed_cross, wo_cross, residual, w1, w2, out_grad, norms)
    tie = lax.optimization_barrier
    ready_rows = parts[0].shape[1]
    parts = [parts[0]] + [plane_swap(parts[f], devices, f) for f in (1, 2, 3)]
    dq, dk, dv, output = attend_backward(
        lengths, qc, kc, vc, grad_mixed, mixed_cross, total_cross, rank_row, count_row, output, False)
    parts, dq = tie((parts, dq))
    grad_memory, grad_residual, grad_mixed, *parts, sums_c = cross_back(
        devices, dq, dk, dv, wc, nc, memory, residual, grad_cross_res, mixed_self, wo_self, norms, gwo_cross, parts)
    parts = [parts[0]] + [plane_swap(parts[f], devices, f) for f in (1, 2, 3)]
    dq, dk, dv, grad_memory = attend_backward(
        lengths, q, k, v, grad_mixed, mixed_self, total_self, rank_row, count_row, grad_memory, True)
    parts, dq = tie((parts, dq))
    grad_query, grad_kv, summed, norm_grads = self_back(
        devices, ready_rows, dq, dk, dv, ws, nq, nkv, query_stream, kv_stream, grad_residual, norms, sums_c, sums_f, parts)

    early, late = 3 * cols // unit_rows, 8 * cols // unit_rows
    own_rows = -(-3 * cols // (devices * UNIT)) * UNIT
    weight_grad, weight_first, weight_second, weight_new, grad_query, grad_kv = update(
        devices, early, late, own_rows, ready_rows, unit_owner, me.reshape(1), summed, parts, master.reshape(shape),
        first_moment.reshape(shape), second_moment.reshape(shape), grad_query, grad_kv)
    weight_grad, weight_first, weight_second, weight_new = [
        part.reshape(master.shape) for part in (weight_grad, weight_first, weight_second, weight_new)]
    norm_grad = lax.dynamic_slice_in_dim(norm_grads.reshape(-1), me * norm_share, norm_share)
    norm_first_new, norm_second_new, norm_new = adamw_step(
        norm_grad, norm_first, norm_second, norm_master, RATE_NORM, 0.0)
    return (
        output, grad_query, grad_kv, grad_memory, weight_grad, weight_first, weight_second, weight_new,
        norm_grad, norm_first_new, norm_second_new, norm_new,
    )


def solution(mesh):
    in_specs = (
        P("dp", None),
        P("dp", None),
        P("dp", None),
        P("dp", None),
        P("dp", None),
        P("dp"),
        P("dp"),
        P(),
        P("dp", "head", None, None),
        P("dp", "head", None, None),
        P("dp", "head", None, None),
        P("dp"),
        P("dp"),
        P("dp"),
    )
    out_specs = (
        P("dp", None),
        P("dp", None),
        P("dp", None),
        P("dp", None),
        P("dp", "head", None, None),
        P("dp", "head", None, None),
        P("dp", "head", None, None),
        P("dp", "head", None, None),
        P("dp"),
        P("dp"),
        P("dp"),
        P("dp"),
    )
    return jax.shard_map(local, mesh=mesh, in_specs=in_specs, out_specs=out_specs, check_vma=False)
```

```python
from functools import partial

import jax
import jax.numpy as jnp
from jax import lax
from jax.experimental import pallas as pl
from jax.experimental.pallas import tpu as pltpu
from jax.sharding import PartitionSpec as P

HEAD_DIM = 64
ROW = 2048
DOCS = 32
STEP = 10
UNIT = 16

EPS_NORM = 1e-05
ADAM_EPS = 1e-08
BETA_ONE = 0.5
BETA_TWO = 0.5
RATE_MATRIX = 0.1
RATE_NORM = 0.3
WEIGHT_DECAY = 0.01

F32 = jnp.float32
BF = jnp.bfloat16
TQ = 256
TK = 256
FAR = 32768.0
LANES = (64, 72, 80)


def nt(a, b):
    return lax.dot_general(a, b, (((1,), (1,)), ((), ())), preferred_element_type=F32)


def nn(a, b):
    return lax.dot_general(a, b, (((1,), (0,)), ((), ())), preferred_element_type=F32)


def doc_bounds(len_ref):
    starts, ends = [], []
    at = jnp.int32(0)
    for d in range(DOCS):
        starts.append(at)
        at = at + len_ref[0, d]
        ends.append(at)
    return starts, ends


def key_range(starts, ends, q0):
    low = jnp.int32(0)
    high = jnp.int32(0)
    for d in range(DOCS):
        low = jnp.where(starts[d] <= q0, starts[d], low)
        high = jnp.where(starts[d] <= q0 + TQ - 1, ends[d], high)
    first = lax.div(low, 128) * 128
    steps = lax.div(high - first + TK - 1, TK)
    return jnp.minimum(first, ROW - steps * TK), steps


def mask_tables(len_ref, rank_ref, side_ref, hot_ref, rank_cols):
    starts, ends = doc_bounds(len_ref)
    lanes = lax.broadcasted_iota(jnp.int32, (1, 128), 1)
    start_lane = jnp.full((1, 128), -1, jnp.int32)
    end_lane = jnp.full((1, 128), -1, jnp.int32)
    for d in range(DOCS):
        start_lane = jnp.where(lanes == d, starts[d], start_lane)
        end_lane = jnp.where(lanes == d, ends[d], end_lane)
    one = (lanes == LANES[0]) | (lanes == LANES[1]) | (lanes == LANES[2])
    for t in range(ROW // 256):
        pos = lax.broadcasted_iota(jnp.int32, (256, 128), 0) + t * 256
        hot = (pos >= start_lane) & (pos < end_lane)
        side = jnp.where(hot | (lanes >= DOCS), jnp.where(one, -1.0, 0.0), -FAR)
        side_ref[t * 256:(t + 1) * 256, :] = side.astype(BF)
    pos = lax.broadcasted_iota(jnp.int32, (1, ROW), 1)
    first = jnp.zeros((1, ROW), jnp.bool_)
    rows = []
    for d in range(DOCS):
        first = first | (pos == starts[d])
        rows.append(jnp.where((pos >= starts[d]) & (pos < ends[d]), FAR, 0.0))
    hot_ref[...] = jnp.concatenate(rows + [jnp.zeros((128 - DOCS, ROW), F32)], 0).astype(BF)
    rank = jnp.where(first, -1.0, rank_ref[...].astype(F32))
    for t in range(ROW // 128):
        rank_cols[t * 128:(t + 1) * 128, :] = jnp.broadcast_to(rank[:, t * 128:(t + 1) * 128], (128, 128)).T


STEPS = (ROW // TQ) * (ROW // TK) + 8


def step_table(len_ref, table):
    starts, ends = doc_bounds(len_ref)
    idle = ROW // TQ

    def put(at, tile, first):
        table[0, at] = tile
        table[1, at] = first
    put(0, idle, ROW)
    put(1, idle, ROW)
    at = jnp.int32(2)
    for tile in range(idle):
        first, steps = key_range(starts, ends, tile * TQ)

        def fill(s, at):
            put(at, tile, first + s * TK)
            return at + 1
        at = lax.fori_loop(0, steps, fill, at)
    put(at, idle, ROW)
    put(at + 1, idle, ROW)
    table[0, STEPS - 1] = at


def step_of(table, i):
    return table[0, i], pl.multiple_of(table[1, i], 128)


def real_step(table, i):
    return jnp.minimum(table[0, i], ROW // TQ - 1), pl.multiple_of(jnp.minimum(table[1, i], ROW - TK), 128)


def seen_bias(rank_cols, counts, tile, k0):
    rank = rank_cols[pl.ds(k0, TK), :]
    rank = jnp.concatenate([rank] * (TQ // 128), 1)
    kpos = lax.broadcasted_iota(jnp.int32, (TK, TQ), 0)
    qpos = lax.broadcasted_iota(jnp.int32, (TK, TQ), 1)
    off_diag = (kpos - qpos) != (tile * TQ - k0)
    allowed = (rank < counts[tile, 0:1, :]) & (off_diag | (rank < 0.0))
    return jnp.where(allowed, 0.0, -FAR * FAR)


def count_tiles(counts, count_ref):
    for tile in range(ROW // TQ):
        counts[tile] = jnp.broadcast_to(count_ref[:, tile * TQ:(tile + 1) * TQ].astype(F32), (8, TQ))


def query_columns(qt, qt_ref, side, tile, h, q0):
    rows = qt_ref[h * HEAD_DIM:(h + 1) * HEAD_DIM, pl.ds(q0, TQ)].astype(F32) * HEAD_DIM ** -0.5
    own, other = h % 2 * HEAD_DIM, (1 - h % 2) * HEAD_DIM
    qt[tile, h, own:own + HEAD_DIM, :] = rows.astype(BF)
    qt[tile, h, other:other + HEAD_DIM, :] = jnp.zeros((HEAD_DIM, TQ), BF)
    qt[tile, h, 128:256, :] = side


def pair_rows(ref, side_ref, h, k0):
    return jnp.concatenate([ref[pl.ds(k0, TK), h // 2 * 128:(h // 2 + 1) * 128], side_ref[pl.ds(k0, TK), :]], 1)


def attn_fwd_kernel(with_seen, heads, table, qt_ref, k_ref, vt_ref, side_ref, hot_ref, *refs):
    if with_seen:
        rank_cols, count_ref, *refs = refs
    o_ref, ot_ref, lse_ref, qt, acc, top, sc, probs, fade, counts = refs
    tiles = ROW // TQ
    lse_ref[...] = jnp.zeros_like(lse_ref)
    acc[...] = jnp.zeros_like(acc)
    top[...] = jnp.full_like(top, -jnp.inf)
    if with_seen:
        count_tiles(counts, count_ref)

    def prepare(tile, c):
        q0 = pl.multiple_of(tile * TQ, TQ)
        for h in range(heads):
            query_columns(qt, qt_ref, hot_ref[:, pl.ds(q0, TQ)], tile, h, q0)
        return c
    lax.fori_loop(0, tiles, prepare, 0)
    ones = jnp.ones((16, TK), BF)

    def one_step(s, c):
        out_tile, _ = step_of(table, s)
        _, out_k = real_step(table, s)
        mid_tile, _ = step_of(table, s + 1)
        in_tile, in_k = real_step(table, s + 2)
        sums = []
        for h in range(heads):
            values = jnp.concatenate([vt_ref[h * HEAD_DIM:(h + 1) * HEAD_DIM, pl.ds(out_k, TK)], ones], 0)
            sums.append(acc[out_tile, h] * fade[h:h + 1, :] + nn(values, probs[h]))
        old = top[mid_tile]
        news = []
        for h in range(heads):
            score = sc[h]
            new = jnp.maximum(old[h:h + 1, :], jnp.max(score, 0, keepdims=True))
            probs[h] = jnp.exp(score - new).astype(BF)
            news.append(new)
        new = jnp.concatenate(news + [old[heads:, :]], 0)
        fade[...] = jnp.exp(old - new)
        bias = seen_bias(rank_cols, counts, in_tile, in_k) if with_seen else None
        for h in range(heads):
            score = nn(pair_rows(k_ref, side_ref, h, in_k), qt[in_tile, h])
            sc[h] = score + bias if with_seen else score
        top[mid_tile] = new
        for h in range(heads):
            acc[out_tile, h] = sums[h]
        return c
    lax.fori_loop(0, table[0, STEPS - 1], one_step, 0)

    def finish(tile, c):
        q0 = pl.multiple_of(tile * TQ, TQ)
        outs = []
        peak = top[tile]
        for h in range(heads):
            a = acc[tile, h]
            total = a[HEAD_DIM:HEAD_DIM + 1, :]
            outs.append(a[:HEAD_DIM, :] * (1.0 / total))
            lse_ref[h:h + 1, pl.ds(q0, TQ)] = peak[h:h + 1, :] + jnp.log(total)
        out = jnp.concatenate(outs, 0)
        ot_ref[:, pl.ds(q0, TQ)] = out.astype(BF)
        o_ref[pl.ds(q0, TQ), :] = out.T.astype(BF)
        return c
    lax.fori_loop(0, tiles, finish, 0)


def attend_forward(steps, qt, k, vt, tables, count, with_seen):
    cols, rows = qt.shape
    heads = cols // HEAD_DIM
    side, hot, rank_cols = tables
    args = [steps, qt, k, vt, side, hot] + ([rank_cols, count] if with_seen else [])
    return call(partial(attn_fwd_kernel, with_seen, heads), "attend_self_forward" if with_seen else "attend_cross_forward",
                args, "S" + "V" * (len(args) - 1), [((rows, cols), BF, "V"), ((cols, rows), BF, "V"), ((8, rows), F32, "V")],
                [pltpu.VMEM((ROW // TQ, heads, 256, TQ), BF), pltpu.VMEM((ROW // TQ + 1, heads, HEAD_DIM + 16, TQ), F32),
                 pltpu.VMEM((ROW // TQ + 1, 8, TQ), F32), pltpu.VMEM((heads, TK, TQ), F32), pltpu.VMEM((heads, TK, TQ), BF),
                 pltpu.VMEM((8, TQ), F32)] + [pltpu.VMEM((ROW // TQ, 8, TQ), F32)])


def three_rows(value):
    high = value.astype(BF).astype(F32)
    middle = (value - high).astype(BF).astype(F32)
    row = lax.broadcasted_iota(jnp.int32, (128, value.shape[1]), 0)
    return jnp.where(row == LANES[0], high, jnp.where(row == LANES[1], middle, jnp.where(row == LANES[2], value - high - middle, 0.0)))


def attn_bwd_kernel(with_seen, heads, table, qt_ref, k_ref, kt_ref, v_ref, gt_ref, ot_ref, lse_ref,
                    side_ref, hot_ref, *refs):
    if with_seen:
        rank_cols, count_ref, *refs = refs
    (pass_in, dq_ref, dk_ref, dv_ref, pass_out, dk_sum, dv_sum, dq_sum, qt, gt, sc, dps, all_ds, all_p,
     held, pass_sem, counts) = refs
    entering = pltpu.make_async_copy(pass_in, held, pass_sem.at[0])
    entering.start()
    tiles = ROW // TQ
    dk_sum[...] = jnp.zeros_like(dk_sum)
    dv_sum[...] = jnp.zeros_like(dv_sum)
    dq_sum[...] = jnp.zeros_like(dq_sum)
    if with_seen:
        count_tiles(counts, count_ref)
    entering.wait()
    leaving = pltpu.make_async_copy(held, pass_out, pass_sem.at[1])
    leaving.start()

    def prepare(tile, c):
        q0 = pl.multiple_of(tile * TQ, TQ)
        hot = hot_ref[:, pl.ds(q0, TQ)].astype(F32)
        for h in range(heads):
            rows = slice(h * HEAD_DIM, (h + 1) * HEAD_DIM)
            side = hot + three_rows(lse_ref[h:h + 1, pl.ds(q0, TQ)])
            query_columns(qt, qt_ref, side.astype(BF), tile, h, q0)
            grads = gt_ref[rows, pl.ds(q0, TQ)]
            delta = jnp.sum(grads.astype(F32) * ot_ref[rows, pl.ds(q0, TQ)].astype(F32), 0, keepdims=True)
            other = (1 - h % 2) * HEAD_DIM
            gt[tile, h, h % 2 * HEAD_DIM:(h % 2 + 1) * HEAD_DIM, :] = grads
            gt[tile, h, other:other + HEAD_DIM, :] = jnp.zeros((HEAD_DIM, TQ), BF)
            gt[tile, h, 128:256, :] = three_rows(delta).astype(BF)
        return c
    lax.fori_loop(0, tiles, prepare, 0)

    def one_step(s, c):
        out_tile, out_k = step_of(table, s)
        read_tile, read_k = real_step(table, s)
        in_tile, in_k = real_step(table, s + 2)
        keys = pl.ds(out_k, TK)
        queries = pl.ds(pl.multiple_of(read_tile * TQ, TQ), TQ)
        own = [slice(h * HEAD_DIM, (h + 1) * HEAD_DIM) for h in range(heads)]
        dk = [dk_sum[h, :, keys] + nt(qt_ref[own[h], queries], all_ds[h]) for h in range(heads)]
        dv = [dv_sum[h, :, keys] + nt(gt_ref[own[h], queries], all_p[h]) for h in range(heads)]
        dq = [dq_sum[out_tile, h] + nn(kt_ref[own[h], pl.ds(read_k, TK)], all_ds[h]) for h in range(heads)]
        for h in range(heads):
            p = jnp.exp(sc[h])
            all_ds[h] = (p * dps[h]).astype(BF)
            all_p[h] = p.astype(BF)
        bias = seen_bias(rank_cols, counts, in_tile, in_k) if with_seen else None
        for h in range(heads):
            score = nn(pair_rows(k_ref, side_ref, h, in_k), qt[in_tile, h])
            sc[h] = score + bias if with_seen else score
            dps[h] = nn(pair_rows(v_ref, side_ref, h, in_k), gt[in_tile, h])
        for h in range(heads):
            dk_sum[h, :, keys] = dk[h]
            dv_sum[h, :, keys] = dv[h]
            dq_sum[out_tile, h] = dq[h]
        return c
    lax.fori_loop(0, table[0, STEPS - 1], one_step, 0)

    def finish(tile, c):
        q0 = pl.multiple_of(tile * TQ, TQ)
        rows = pl.ds(q0, TQ)
        dq = jnp.concatenate([dq_sum[tile, h] for h in range(heads)], 0) * HEAD_DIM ** -0.5
        dk = jnp.concatenate([dk_sum[h, :, rows] for h in range(heads)], 0) * HEAD_DIM ** -0.5
        dv = jnp.concatenate([dv_sum[h, :, rows] for h in range(heads)], 0)
        for ref, value in ((dq_ref, dq), (dk_ref, dk), (dv_ref, dv)):
            ref[rows, :] = value.astype(BF).T
        return c
    lax.fori_loop(0, tiles, finish, 0)
    leaving.wait()


def attend_backward(steps, qt, k, kt, v, gt, ot, lse, tables, count, passed, with_seen):
    rows, cols = v.shape
    heads = cols // HEAD_DIM
    side, hot, rank_cols = tables
    args = [steps, qt, k, kt, v, gt, ot, lse, side, hot] + ([rank_cols, count] if with_seen else []) + [passed]
    like = ((rows, cols), BF, "V")
    tiles = ROW // TQ
    summed = pltpu.VMEM((heads, HEAD_DIM, rows + TK), F32)
    columns, square = pltpu.VMEM((tiles, heads, 256, TQ), BF), pltpu.VMEM((heads, TK, TQ), F32)
    small = pltpu.VMEM((heads, TK, TQ), BF)
    return call(partial(attn_bwd_kernel, with_seen, heads), "attend_self_backward" if with_seen else "attend_cross_backward",
                args, "S" + "V" * (len(args) - 2) + "A", [like, like, like, (passed.shape, passed.dtype, "A")],
                [summed, summed, pltpu.VMEM((tiles + 1, heads, HEAD_DIM, TQ), F32), columns, columns, square, square,
                 small, small, pltpu.VMEM(passed.shape, passed.dtype), pltpu.SemaphoreType.DMA((2,))] + [pltpu.VMEM((ROW // TQ, 8, TQ), F32)])


def send(src, dst, send_sem, recv_sem, **where):
    copy = pltpu.make_async_remote_copy(src_ref=src, dst_ref=dst, send_sem=send_sem, recv_sem=recv_sem,
                                        device_id=where, device_id_type=pl.DeviceIdType.MESH)
    copy.start()
    return copy

def greet(peers):
    barrier = pltpu.get_barrier_semaphore()
    for where in peers:
        pl.semaphore_signal(barrier, inc=1, device_id=where, device_id_type=pl.DeviceIdType.MESH)
    pl.semaphore_wait(barrier, len(peers))

def places_of(count):
    me = lax.axis_index("dp")
    across = count // 4
    x, y, z = lax.rem(me, 2), lax.rem(lax.div(me, 2), 2), lax.div(me, 4)
    xpeer, ypeer = me + 1 - 2 * x, me + 2 - 4 * y
    order = sorted(range(1, across), key=lambda d: min(d, across - d))
    ahead = lambda d: lax.rem(z + d, across) * 4 + y * 2 + x
    behind = lambda d: lax.rem(z + across - d, across) * 4 + y * 2 + x
    return me, x, y, z, xpeer, ypeer, order, ahead, behind

def spread_blocks(count, piece, rows, half, places, zs, xs, ys, gx, gy, meanwhile=None):
    me, x, y, z, xpeer, ypeer, order, ahead, behind = places
    whole = (0, rows)
    sent, recv = [], {}
    def go(src_block, at, sem, d, to):
        copy = send(piece(src_block, *at), piece(src_block, *at), sem.at[0, d], sem.at[1, d], dp=to)
        sent.append(copy)
        return copy
    near = go(me, whole, xs, 0, xpeer), go(me, whole, ys, 0, ypeer)
    recv[0] = near
    zcopies = {}
    for d in order:
        zcopies[d] = go(me, whole, zs, d, ahead(d))
    if meanwhile is not None:
        meanwhile()
    steps = [0] + order
    diag = []
    for k, d in enumerate(steps):
        if d:
            zcopies[d].wait_recv()
            recv[d] = go(behind(d), whole, xs, d, xpeer), go(behind(d), whole, ys, d, ypeer)
        if k:
            forward(go, diag, recv, steps[k - 1], behind, places, half, rows, gx, gy)
    forward(go, diag, recv, steps[-1], behind, places, half, rows, gx, gy)
    for copy in diag:
        copy.wait_recv()
    for copy in sent:
        copy.wait_send()

def forward(go, diag, recv, d, behind, places, half, rows, gx, gy):
    me, x, y, z, xpeer, ypeer, order, ahead, _ = places
    base = behind(d) if d else me
    recv[d][0].wait_recv()
    diag.append(go(base + 1 - 2 * x, (0, half), gy, d, ypeer))
    recv[d][1].wait_recv()
    diag.append(go(base + 2 - 4 * y, (half, rows - half), gx, d, xpeer))

def part_sizes(rows):
    first = rows // 2 // UNIT * UNIT
    return [(part, pl.ds(start, size), size) for part, start, size in ((0, 0, first), (1, first, rows - first)) if size]


class BlockSum:
    def __init__(self, count, places, source, out, keep, r1, r2, r3, s1, s2, s3):
        self.count, self.places, self.source, self.out = count, places, source, out
        self.keep, self.r1, self.r2, self.r3, self.s1, self.s2, self.s3 = keep, r1, r2, r3, s1, s2, s3
        self.parts = part_sizes(source.shape[1])
        self.first, self.second, self.third = {}, {}, {}

    def at(self, d, first, second, part):
        z, across = self.places[3], self.count // 4
        return lax.rem(z + d, across) * 4 + (first + 2 * second if part == 0 else 2 * first + second)

    def start(self):
        me, x, y, z, xpeer, ypeer, order, ahead, behind = self.places
        self.steps = order + [0]
        self.mine = [(x, y), (y, x)]
        self.peers = [(xpeer, ypeer), (ypeer, xpeer)]
        for d in self.steps:
            for part, rows, size in self.parts:
                f, s = self.mine[part]
                for t in (0, 1):
                    second = s if t else 1 - s
                    self.first[d, part, t] = send(
                        self.source.at[self.at(d, 1 - f, second, part), rows], self.r1.at[part, d, t, pl.ds(0, size)],
                        self.s1.at[0, part, d, t], self.s1.at[1, part, d, t], dp=self.peers[part][0])

    def second_stage(self, d):
        for part, rows, size in self.parts:
            f, s = self.mine[part]
            into = pl.ds(0, size)
            for t in (0, 1):
                second = s if t else 1 - s
                self.first[d, part, t].wait_recv()
                self.keep[part, d, t, into, :] = (self.source[self.at(d, f, second, part), rows, :].astype(F32)
                                                  + self.r1[part, d, t, into, :].astype(F32)).astype(BF)
                if t == 0:
                    self.second[d, part] = send(self.keep.at[part, d, 0, into], self.r2.at[part, d, into],
                                                self.s2.at[0, part, d], self.s2.at[1, part, d], dp=self.peers[part][1])

    def third_stage(self, d):
        ahead = self.places[7]
        for part, rows, size in self.parts:
            into = pl.ds(0, size)
            self.second[d, part].wait_recv()
            self.keep[part, d, 1, into, :] = (self.keep[part, d, 1, into, :].astype(F32)
                                              + self.r2[part, d, into, :].astype(F32)).astype(BF)
            if d:
                self.third[d, part] = send(self.keep.at[part, d, 1, into], self.r3.at[part, d, into],
                                           self.s3.at[0, part, d], self.s3.at[1, part, d], dp=ahead(d))

    def finish(self):
        me, order = self.places[0], self.places[6]
        for k, d in enumerate(self.steps):
            self.second_stage(d)
            if k:
                self.third_stage(self.steps[k - 1])
        self.third_stage(0)
        for part, rows, size in self.parts:
            into = pl.ds(0, size)
            total = self.keep[part, 0, 1, into, :].astype(F32)
            for d in order:
                self.third[d, part].wait_recv()
                total = total + self.r3[part, d, into, :].astype(F32)
            self.out[me, rows, :] = total.astype(BF)

    def drain(self):
        for copies in (self.first, self.second, self.third):
            for copy in copies.values():
                copy.wait_send()


def block_sum_scratch(count, rows, cols):
    across = count // 4
    size = max(size for _, _, size in part_sizes(rows))
    D = pltpu.SemaphoreType.DMA
    return [
        pltpu.VMEM((2, across, 2, size, cols), BF), pltpu.VMEM((2, across, 2, size, cols), BF),
        pltpu.VMEM((2, across, size, cols), BF), pltpu.VMEM((2, across, size, cols), BF),
        D((2, 2, across, 2)), D((2, 2, across)), D((2, 2, across))]


def plane_swap(value, count, f):
    return lax.ppermute(value, "dp", [(i, i // 4 * 4 + (i % 4 ^ f)) for i in range(count)])


def plane_offset(places, f):
    x, y = places[1], places[2]
    return lax.rem(x + f % 2, 2) + 2 * lax.rem(y + f // 2, 2)


def call(kernel, name, args, kinds, outs, scratch, number=None):
    space = {"V": pltpu.VMEM, "S": pltpu.SMEM, "A": pl.ANY}
    extra = {} if number is None else dict(collective_id=number, has_side_effects=True)
    return pl.pallas_call(
        kernel,
        out_shape=tuple(jax.ShapeDtypeStruct(shape, dtype) for shape, dtype, _ in outs),
        in_specs=[pl.BlockSpec(memory_space=space[kind]) for kind in kinds],
        out_specs=tuple(pl.BlockSpec(memory_space=space[kind]) for _, _, kind in outs),
        scratch_shapes=scratch,
        compiler_params=pltpu.CompilerParams(vmem_limit_bytes=60 * 2**20, **extra),
        cost_estimate=pl.CostEstimate(flops=4 * 10**10, bytes_accessed=16 * 2**20, transcendentals=0),
        name=name,
    )(*args)


CHUNK = 256


def tn(a, b):
    return lax.dot_general(a, b, (((0,), (0,)), ((), ())), preferred_element_type=F32)


def normalise(value):
    centred = value - jnp.mean(value, -1, keepdims=True)
    scale = lax.rsqrt(jnp.mean(centred * centred, -1, keepdims=True) + EPS_NORM)
    return centred * scale, scale


def norm_back(unit, scale, gain, grad):
    inner = grad * gain
    return scale * (inner - jnp.mean(inner, -1, keepdims=True) - unit * jnp.mean(inner * unit, -1, keepdims=True))


def fold_rows(value):
    return jnp.sum(value.reshape(value.shape[0] // 8, 8, value.shape[1]), 0)


def interleave(size):
    row = lax.broadcasted_iota(jnp.int32, (size, size), 0)
    col = lax.broadcasted_iota(jnp.int32, (size, size), 1)
    source = jnp.where((row & 1) == 0, row >> 1, (row >> 1) + size // 2)
    return jnp.where(col == source, 1.0, 0.0).astype(BF)


def part_rows(matrix, order):
    return lax.dot_general(order, matrix, (((0,), (0,)), ((), ())), preferred_element_type=F32).astype(BF)


def as_units(gradient, order):
    parted = part_rows(gradient.astype(BF), order)
    half = parted.shape[0] // 2
    return jnp.concatenate([parted[:half], parted[half:]], 1)


def other_core(mine, theirs, sems, step):
    rows = pl.ds(step * CHUNK, CHUNK)
    return pltpu.make_async_remote_copy(
        src_ref=mine.at[rows], dst_ref=theirs.at[rows], send_sem=sems.at[0, step], recv_sem=sems.at[1, step],
        device_id={"head": 1 - lax.axis_index("head")}, device_id_type=pl.DeviceIdType.MESH)


def greet_core():
    greet([{"head": 1 - lax.axis_index("head")}])


def chunks(total, body):
    def one(step, carry):
        body(step, pl.ds(pl.multiple_of(step * CHUNK, CHUNK), CHUNK))
        return carry
    lax.fori_loop(0, total // CHUNK, one, 0)


def drain(total, mine, theirs, sems):
    def body(step, rows):
        other_core(mine, theirs, sems, step).wait_send()
    chunks(total, body)


class Late:
    def __init__(self, pairs, sems):
        self.copies = [pltpu.make_async_copy(source, held, sems.at[i]) for i, (source, held) in enumerate(pairs)]
        for copy in self.copies:
            copy.start()

    def wait(self, *which):
        for i in which:
            self.copies[i].wait()


class Out:
    def __init__(self, pairs, sems):
        self.pairs, self.sems = pairs, sems

    def copy(self, i, step):
        held, out = self.pairs[i]
        part = pl.ds(pl.multiple_of(step * CHUNK, CHUNK), CHUNK)
        if held.shape[0] < held.shape[1]:
            held, out = held.at[:, part], out.at[:, part]
        else:
            held, out = held.at[part], out.at[part]
        return pltpu.make_async_copy(held, out, self.sems.at[i, step])

    def start(self, i, step):
        self.copy(i, step).start()

    def drain(self, tokens):
        def body(step, rows):
            for i in range(len(self.pairs)):
                self.copy(i, step).wait()
        chunks(tokens, body)


def plan_kernel(block, owner_ref, len_ref, place_ref, table, used):
    for d in range(used.shape[0]):
        used[d] = 0

    def one_unit(u, carry):
        owner = owner_ref[u]
        slot = used[owner]
        place_ref[u] = owner * block + slot
        used[owner] = slot + 1
        return carry
    lax.fori_loop(0, owner_ref.shape[0], one_unit, 0, unroll=4)
    step_table(len_ref, table)


def plan(unit_owner, lengths, devices, block):
    return call(partial(plan_kernel, block), "plan", [unit_owner, lengths], "SS",
                [(unit_owner.shape, jnp.int32, "S"), ((2, STEPS), jnp.int32, "S")], [pltpu.SMEM((devices,), jnp.int32)])


def project_kernel(devices, place_ref, len_ref, master, norm_row, rank_ref, query_hbm, kv_hbm, memory_hbm,
                   nq_out, nkv_out, qt_out, k_out, kt_out, v_out, vt_out, kc_out, kct_out, vc_out, vct_out,
                   ws_ref, wc_ref, wos_ref, woc_ref, w1_ref, w2_ref, norms, side_ref, hot_ref, rank_cols,
                   gathered, flat, query_ref, kv_ref, memory_ref, unit_q, unit_kv,
                   nq_ref, nkv_ref, qt_ref, k_ref, kt_ref, v_ref, vt_ref, kc_ref, kct_ref, vc_ref, vct_ref,
                   late_sems, out_sems, zs, xs, ys, gx, gy):
    tokens, features = query_ref.shape
    units = place_ref.shape[0]
    late = Late([(query_hbm, query_ref), (kv_hbm, kv_ref), (memory_hbm, memory_ref)], late_sems)
    held = (nq_ref, nkv_ref, qt_ref, k_ref, kt_ref, v_ref, vt_ref, kc_ref, kct_ref, vc_ref, vct_ref)
    out = Out(list(zip(held, (nq_out, nkv_out, qt_out, k_out, kt_out, v_out, vt_out, kc_out, kct_out, vc_out, vct_out))), out_sems)
    places = places_of(devices)
    me, x, y, z, xpeer, ypeer, order, ahead, behind = places
    slots = master.shape[0]
    block = slots + 1
    gathered[pl.ds(me * block, slots)] = master[...].astype(BF)
    gathered[me * block + slots] = jnp.broadcast_to(norm_row[...], (UNIT, features)).astype(BF)
    greet([{"dp": xpeer}, {"dp": ypeer}] + [{"dp": ahead(d)} for d in order])

    def meanwhile():
        mask_tables(len_ref, rank_ref, side_ref, hot_ref, rank_cols)
        late.wait(0, 1, 2)

        def units_of(step, rows):
            unit_q[rows, :] = normalise(query_ref[rows, :].astype(F32))[0]
            unit_kv[rows, :] = normalise(kv_ref[rows, :].astype(F32))[0]
        chunks(tokens, units_of)
    spread_blocks(devices, lambda number, start, size: gathered.at[pl.ds(number * block + start, size)], block, block // 2,
                  places, zs, xs, ys, gx, gy, meanwhile)

    share = devices // 8
    vectors = []
    for number in range(8):
        pieces = [gathered[(number * share + i) * block + slots].astype(F32) for i in range(share)]
        total = pieces[0]
        for piece in pieces[1:]:
            total = total + piece
        vectors.append(total[0:1, :])
    norms[...] = jnp.concatenate(vectors, 0)

    def one_unit(u, carry):
        flat[pl.ds(pl.multiple_of(u * UNIT, UNIT), UNIT), :] = gathered[place_ref[u]]
        return carry
    lax.fori_loop(0, units, one_unit, 0, unroll=4)
    order = interleave(features)
    cols = v_ref.shape[1]
    for number in range(6):
        rows = flat[number * cols:(number + 1) * cols, :]
        stacked = jnp.concatenate([rows[:, :cols], rows[:, cols:]], 0)
        matrix = nn(order, stacked).astype(BF)
        if number < 3:
            ws_ref[number] = matrix
        else:
            wc_ref[number - 3] = matrix
    wos_ref[...] = flat[6 * cols:7 * cols, :]
    woc_ref[...] = flat[7 * cols:8 * cols, :]
    hidden = w2_ref.shape[0]
    for block in range(hidden // features):
        at = 8 * cols + block * features
        parted = part_rows(flat[at:at + features, :], order)
        half = features // 2
        w1_ref[block * half:(block + 1) * half, :] = jnp.concatenate([parted[:half], parted[half:]], 1)
    w2_ref[...] = flat[8 * cols + hidden:, :]

    def body(step, rows):
        nq = (unit_q[rows, :] * norms[0:1, :] + norms[1:2, :]).astype(BF)
        nkv = (unit_kv[rows, :] * norms[2:3, :] + norms[3:4, :]).astype(BF)
        source = memory_ref[rows, :]
        low = lambda left, right: nn(left, right).astype(BF)
        k, v, kc, vc = low(nkv, ws_ref[1]), low(nkv, ws_ref[2]), low(source, wc_ref[1]), low(source, wc_ref[2])
        results = [nq, nkv, low(nq, ws_ref[0]).T, k, k.T, v, v.T, kc, kc.T, vc, vc.T]
        for i, (ref, result) in enumerate(zip(held, results)):
            if ref.shape[0] < ref.shape[1]:
                ref[:, rows] = result
            else:
                ref[rows, :] = result
            out.start(i, step)
    chunks(tokens, body)
    out.drain(tokens)


def pair_sems(tokens):
    return pltpu.SemaphoreType.DMA((2, tokens // CHUNK))


def out_semaphores(count, tokens):
    return pltpu.SemaphoreType.DMA((count, tokens // CHUNK))


def project(devices, place_of, lengths, master, norm_row, rank_row, query_stream, kv_stream, memory, cols, hidden):
    tokens, features = query_stream.shape
    wide, narrow, across = (tokens, features), (tokens, cols), (cols, tokens)
    shapes = [wide, wide, across] + [narrow, across] * 4
    outs = [(shape, BF, "A") for shape in shapes] + [
        ((3, features, cols), BF, "V"), ((3, features, cols), BF, "V"), ((cols, features), BF, "V"), ((cols, features), BF, "V"),
        ((features, hidden), BF, "V"), ((hidden, features), BF, "V"), ((8, features), F32, "V"),
        ((ROW, 128), BF, "V"), ((128, ROW), BF, "V"), ((ROW, 128), F32, "V")]
    D = pltpu.SemaphoreType.DMA
    scratch = [pltpu.VMEM((devices * (master.shape[0] + 1), UNIT, features), BF), pltpu.VMEM((8 * cols + 2 * hidden, features), BF)]
    scratch += [pltpu.VMEM(wide, BF)] * 3 + [pltpu.VMEM(wide, F32)] * 2 + [pltpu.VMEM(shape, BF) for shape in shapes]
    scratch += [D((3,)), out_semaphores(len(shapes), tokens)] + [D((2, devices // 4))] * 5
    return call(partial(project_kernel, devices), "project",
                [place_of, lengths, master, norm_row, rank_row, query_stream, kv_stream, memory], "SSVVVAAA",
                outs, scratch, 0)


def self_out_kernel(mixed, wo, query_hbm, wc, norms, res_out, nc_out, q_out,
                    query, res_ref, nc_ref, q_ref, mine, theirs, sems, late_sems, out_sems):
    tokens = query.shape[0]
    late = Late([(query_hbm, query)], late_sems)
    out = Out([(res_ref, res_out), (nc_ref, nc_out), (q_ref, q_out)], out_sems)
    greet_core()

    def give(step, rows):
        mine[rows, :] = nn(mixed[rows, :], wo[...]).astype(BF)
        other_core(mine, theirs, sems, step).start()
    chunks(tokens, give)
    late.wait(0)

    def take(step, rows):
        other_core(mine, theirs, sems, step).wait_recv()
        res = query[rows, :].astype(F32) + (mine[rows, :].astype(F32) + theirs[rows, :].astype(F32))
        res_ref[rows, :] = res
        out.start(0, step)
        nc = (normalise(res)[0] * norms[4:5, :] + norms[5:6, :]).astype(BF)
        nc_ref[rows, :] = nc
        out.start(1, step)
        q_ref[:, rows] = nn(nc, wc[0]).astype(BF).T
        out.start(2, step)
    chunks(tokens, take)
    drain(tokens, mine, theirs, sems)
    out.drain(tokens)


def self_out(mixed, wo, query, wc, norms):
    tokens, features = query.shape
    wide = (tokens, features)
    across = (mixed.shape[1], tokens)
    outs = [(wide, F32, "A"), (wide, BF, "A"), (across, BF, "A")]
    scratch = [pltpu.VMEM(wide, BF), pltpu.VMEM(wide, F32), pltpu.VMEM(wide, BF), pltpu.VMEM(across, BF),
               pltpu.VMEM(wide, BF), pltpu.VMEM(wide, BF), pair_sems(tokens), pltpu.SemaphoreType.DMA((1,)),
               out_semaphores(3, tokens)]
    return call(self_out_kernel, "self_out", [mixed, wo, query, wc, norms], "VVAVV", outs, scratch, 2)


def gelu_parts(value):
    size = jnp.abs(value)
    bell = jnp.exp(-0.5 * value * value)
    t = 1.0 / (1.0 + (0.3275911 * 0.7071067811865476) * size)
    poly = ((((1.061405429 * t - 1.453152027) * t + 1.421413741) * t - 0.284496736) * t + 0.254829592) * t
    tail = 0.5 * poly * bell
    below = jnp.where(value < 0.0, tail, 1.0 - tail)
    return value * below, below + value * (bell * 0.3989422804014327)


def spread_flat(devices, places, flat, refs):
    rows = flat.shape[0] // devices
    for f, ref in enumerate(refs):
        place = plane_offset(places, f)
        for level in range(devices // 4):
            ref[level, ref.shape[1] - rows:, :] = flat[pl.ds(pl.multiple_of((level * 4 + place) * rows, UNIT), rows), :]


def feed_forward_kernel(devices, mixed, wo, res_hbm, w1, w2, out_grad_hbm, norms,
                        out_out, gres_out, gmix_out, part0, part1, part2, part3, gwo_ref, sums_ref,
                        res, out_grad, out_ref, gres_ref, gmix_ref, flat,
                        mine, theirs, nf_all, hid_all, pre_all, low_all, mine_o, theirs_o, mine_g, theirs_g,
                        sems, sems_o, sems_g, late_sems, out_sems):
    tokens, features = out_grad.shape
    hidden = w2.shape[0]
    places = places_of(devices)
    late = Late([(res_hbm, res), (out_grad_hbm, out_grad)], late_sems)
    out = Out([(out_ref, out_out), (gres_ref, gres_out), (gmix_ref, gmix_out)], out_sems)
    greet_core()

    def give(step, rows):
        mine[rows, :] = nn(mixed[rows, :], wo[...]).astype(BF)
        other_core(mine, theirs, sems, step).start()
    chunks(tokens, give)
    late.wait(0, 1)

    def middle(step, rows):
        other_core(mine, theirs, sems, step).wait_recv()
        value = res[rows, :] + (mine[rows, :].astype(F32) + theirs[rows, :].astype(F32))
        gres_ref[rows, :] = value
        nf = (normalise(value)[0] * norms[6:7, :] + norms[7:8, :]).astype(BF)
        nf_all[rows, :] = nf
        grad = out_grad[rows, :]
        out_part = jnp.zeros((CHUNK, features), F32)
        grad_part = jnp.zeros((CHUNK, features), F32)
        for block in range(hidden // 256):
            at = slice(block * 256, (block + 1) * 256)
            act, slope = gelu_parts(nn(nf, w1[:, at]))
            act = act.astype(BF)
            hid_all[rows, at] = act
            pre = (slope * nt(grad, w2[at, :])).astype(BF)
            pre_all[rows, at] = pre
            out_part = out_part + nn(act, w2[at, :])
            grad_part = grad_part + nt(pre, w1[:, at])
        mine_o[rows, :] = out_part.astype(BF)
        other_core(mine_o, theirs_o, sems_o, step).start()
        mine_g[rows, :] = grad_part.astype(BF)
        other_core(mine_g, theirs_g, sems_g, step).start()
    chunks(tokens, middle)

    order = interleave(features)
    half = features // 2
    for block in range(hidden // 256):
        at = slice(block * 256, (block + 1) * 256)
        flat[hidden + block * 256:hidden + (block + 1) * 256, :] = tn(hid_all[:, at], out_grad[...]).astype(BF)
    for block in range(hidden // features):
        gradient = tn(nf_all[:, block * half:(block + 1) * half], pre_all[...]).astype(BF)
        stacked = jnp.concatenate([gradient[:, :features], gradient[:, features:]], 0)
        flat[block * features:(block + 1) * features, :] = nn(order, stacked).astype(BF)
    spread_flat(devices, places, flat, (part0, part1, part2, part3))
    sums_ref[...] = jnp.zeros_like(sums_ref)

    def close(step, rows):
        other_core(mine_o, theirs_o, sems_o, step).wait_recv()
        other_core(mine_g, theirs_g, sems_g, step).wait_recv()
        value = gres_ref[rows, :]
        out_ref[rows, :] = (value + (mine_o[rows, :].astype(F32) + theirs_o[rows, :].astype(F32))).astype(BF)
        out.start(0, step)
        grad = mine_g[rows, :].astype(F32) + theirs_g[rows, :].astype(F32)
        unit, scale = normalise(value)
        gres = norm_back(unit, scale, norms[6:7, :], grad) + out_grad[rows, :].astype(F32)
        gres_ref[rows, :] = gres
        out.start(1, step)
        sums_ref[0:8, :] += fold_rows(grad * unit)
        sums_ref[8:16, :] += fold_rows(grad)
        low = gres.astype(BF)
        low_all[rows, :] = low
        gmix_ref[:, rows] = nt(low, wo[...]).astype(BF).T
        out.start(2, step)
    chunks(tokens, close)
    gwo_ref[...] = tn(mixed[...], low_all[...]).astype(BF)
    out.drain(tokens)
    drain(tokens, mine, theirs, sems)
    drain(tokens, mine_o, theirs_o, sems_o)
    drain(tokens, mine_g, theirs_g, sems_g)


def feed_forward(devices, mixed, wo, res, w1, w2, out_grad, norms):
    tokens, features = out_grad.shape
    hidden = w2.shape[0]
    part = ((devices // 4, 2 * hidden // devices, features), BF, "V")
    wide = (tokens, features)
    across = (mixed.shape[1], tokens)
    outs = [(wide, BF, "A"), (wide, F32, "A"), (across, BF, "A")] + [part] * 4 + [
        (wo.shape, BF, "V"), ((16, features), F32, "V")]
    deep, narrow = pltpu.VMEM((tokens, hidden), BF), pltpu.VMEM(wide, BF)
    scratch = [pltpu.VMEM(wide, F32), narrow, narrow, pltpu.VMEM(wide, F32), pltpu.VMEM(across, BF),
               pltpu.VMEM((2 * hidden, features), BF), narrow, narrow, narrow, deep, deep, narrow] + [narrow] * 4
    scratch += [pair_sems(tokens)] * 3 + [pltpu.SemaphoreType.DMA((2,)), out_semaphores(3, tokens)]
    return call(partial(feed_forward_kernel, devices), "feed_forward", [mixed, wo, res, w1, w2, out_grad, norms], "VVAVVAV",
                outs, scratch, 3)


def branch_give(dq, dk, dv, weights, mine_a, theirs_a, mine_b, theirs_b, sems_a, sems_b):
    def give(step, rows):
        mine_a[rows, :] = nt(dq[rows, :], weights[0]).astype(BF)
        other_core(mine_a, theirs_a, sems_a, step).start()
        mine_b[rows, :] = (nt(dk[rows, :], weights[1]) + nt(dv[rows, :], weights[2])).astype(BF)
        other_core(mine_b, theirs_b, sems_b, step).start()
    chunks(dq.shape[0], give)


def branch_weights(first_in, second_in, dq, dk, dv, flat):
    cols = dq.shape[1]
    order = interleave(first_in.shape[1])
    for number, (entering, grad) in enumerate(((first_in, dq), (second_in, dk), (second_in, dv))):
        flat[number * cols:(number + 1) * cols, :] = as_units(tn(entering[...], grad[...]), order)


def z_sum_start(devices, places, pieces, landed, sems):
    me, x, y, z, xpeer, ypeer, order, ahead, behind = places
    return [send(pieces.at[lax.rem(z + d, devices // 4)], landed.at[d], sems.at[0, d], sems.at[1, d], dp=ahead(d)) for d in order]


def z_sum_end(places, pieces, landed, copies):
    z, order = places[3], places[6]
    total = pieces[z].astype(F32)
    for copy, d in zip(copies, order):
        copy.wait_recv()
        total = total + landed[d].astype(F32)
    return total.astype(BF)


def four_sum(parts, at):
    return (parts[0][at].astype(F32) + parts[1][at].astype(F32) + parts[2][at].astype(F32) + parts[3][at].astype(F32)).astype(BF)


def cross_back_kernel(devices, dq, dk, dv, wc, nc_hbm, memory_hbm, res_hbm, gres_hbm, mixed, wo, norms, gwo_cross,
                      part0, part1, part2, part3,
                      gmem_out, gnew_out, gmix_out, give0, give1, give2, give3, sums_ref,
                      nc, memory, res, gres, gmem_ref, gnew_ref, gmix_ref, flat, pieces, landed, blocks,
                      mine_a, theirs_a, mine_b, theirs_b, low_all, sems_a, sems_b, late_sems, out_sems, z_sems, zz_sems):
    tokens, features = nc.shape
    cols = dq.shape[1]
    across = devices // 4
    places = places_of(devices)
    me, x, y, z, xpeer, ypeer, order, ahead, behind = places
    late = Late([(nc_hbm, nc), (memory_hbm, memory), (res_hbm, res), (gres_hbm, gres)], late_sems)
    out = Out([(gmem_ref, gmem_out), (gnew_ref, gnew_out), (gmix_ref, gmix_out)], out_sems)
    for level in range(across):
        pieces[level] = four_sum((part0, part1, part2, part3), level)
    greet([{"head": 1 - lax.axis_index("head")}] + [{"dp": ahead(d)} for d in order])
    z_copies = z_sum_start(devices, places, pieces, landed, z_sems)
    branch_give(dq, dk, dv, wc, mine_a, theirs_a, mine_b, theirs_b, sems_a, sems_b)
    late.wait(0, 1)
    branch_weights(nc, memory, dq, dk, dv, flat)
    blocks[0] = z_sum_end(places, pieces, landed, z_copies)
    zz_copies = [send(blocks.at[0], blocks.at[d], zz_sems.at[0, d], zz_sems.at[1, d], dp=ahead(d)) for d in order]
    sums_ref[...] = jnp.zeros_like(sums_ref)
    late.wait(2, 3)

    def close(step, rows):
        other_core(mine_a, theirs_a, sems_a, step).wait_recv()
        grad = mine_a[rows, :].astype(F32) + theirs_a[rows, :].astype(F32)
        unit, scale = normalise(res[rows, :])
        gnew = norm_back(unit, scale, norms[4:5, :], grad) + gres[rows, :]
        gnew_ref[rows, :] = gnew
        out.start(1, step)
        sums_ref[0:8, :] += fold_rows(grad * unit)
        sums_ref[8:16, :] += fold_rows(grad)
        low = gnew.astype(BF)
        low_all[rows, :] = low
        gmix_ref[:, rows] = nt(low, wo[...]).astype(BF).T
        out.start(2, step)
        other_core(mine_b, theirs_b, sems_b, step).wait_recv()
        gmem_ref[rows, :] = (mine_b[rows, :].astype(F32) + theirs_b[rows, :].astype(F32)).astype(BF)
        out.start(0, step)
    chunks(tokens, close)
    flat[3 * cols:4 * cols, :] = tn(mixed[...], low_all[...]).astype(BF)
    flat[4 * cols:5 * cols, :] = gwo_cross[...]
    if flat.shape[0] > 5 * cols:
        flat[5 * cols:, :] = jnp.zeros((flat.shape[0] - 5 * cols, features), BF)
    gives = (give0, give1, give2, give3)
    spread_flat(devices, places, flat, gives)
    for copy in zz_copies:
        copy.wait_recv()
    ready_rows = blocks.shape[1]
    for ref in gives:
        for d in range(across):
            ref[d, 0:ready_rows, :] = blocks[d]
    for copy in z_copies + zz_copies:
        copy.wait_send()
    out.drain(tokens)
    drain(tokens, mine_a, theirs_a, sems_a)
    drain(tokens, mine_b, theirs_b, sems_b)


def cross_back(devices, dq, dk, dv, wc, nc, memory, res, gres, mixed, wo, norms, gwo_cross, parts):
    tokens, features = nc.shape
    cols = dq.shape[1]
    across, ready_rows = devices // 4, parts[0].shape[1]
    flat_rows = -(-5 * cols // (devices * UNIT)) * devices * UNIT
    give = ((across, ready_rows + flat_rows // devices, features), BF, "V")
    wide = (tokens, features)
    outs = [(wide, BF, "A"), (wide, F32, "A"), ((cols, tokens), BF, "A")] + [give] * 4 + [((16, features), F32, "V")]
    low, high = pltpu.VMEM(wide, BF), pltpu.VMEM(wide, F32)
    small = pltpu.VMEM((across, ready_rows, features), BF)
    z_sems = pltpu.SemaphoreType.DMA((2, across))
    scratch = [low, low, high, high, low, high, pltpu.VMEM((cols, tokens), BF), pltpu.VMEM((flat_rows, features), BF), small, small, small]
    scratch += [low] * 5 + [pair_sems(tokens)] * 2 + [pltpu.SemaphoreType.DMA((4,)), out_semaphores(3, tokens), z_sems, z_sems]
    return call(partial(cross_back_kernel, devices), "cross_back",
                [dq, dk, dv, wc, nc, memory, res, gres, mixed, wo, norms, gwo_cross] + parts, "VVVVAAAAVVVVVVVV", outs, scratch, 4)


def self_back_kernel(devices, ready_rows, dq, dk, dv, ws, nq_hbm, nkv_hbm, query_hbm, kv_hbm, gres_hbm, norms, sums_c, sums_f,
                     part0, part1, part2, part3,
                     gquery_out, gkv_out, summed, gnorm_ref,
                     nq, nkv, query, kv, gres, gquery_ref, gkv_ref, flat, source, pieces, landed, norm_mine, norm_all,
                     mine_a, theirs_a, mine_b, theirs_b, sums, sems_a, sems_b, late_sems, out_sems, z_sems, n_sems, *block_refs):
    tokens, features = nq.shape
    across = devices // 4
    places = places_of(devices)
    me, x, y, z, xpeer, ypeer, order, ahead, behind = places
    late = Late([(nq_hbm, nq), (nkv_hbm, nkv), (query_hbm, query), (kv_hbm, kv), (gres_hbm, gres)], late_sems)
    out = Out([(gquery_ref, gquery_out), (gkv_ref, gkv_out)], out_sems)
    more_rows = part0.shape[1] - ready_rows
    for level in range(across):
        pieces[level] = four_sum((part0, part1, part2, part3), (level, pl.ds(ready_rows, more_rows)))
    others = [lax.rem(me + d, devices) for d in range(1, devices)]
    greet([{"head": 1 - lax.axis_index("head")}] + [{"dp": other} for other in others])
    z_copies = z_sum_start(devices, places, pieces, landed, z_sems)
    branch_give(dq, dk, dv, ws, mine_a, theirs_a, mine_b, theirs_b, sems_a, sems_b)
    late.wait(0, 1)
    branch_weights(nq, nkv, dq, dk, dv, flat)
    rows = source.shape[1]
    if flat.shape[0] > 3 * dq.shape[1]:
        flat[3 * dq.shape[1]:, :] = jnp.zeros((flat.shape[0] - 3 * dq.shape[1], features), BF)
    for block in range(devices):
        source[block] = flat[block * rows:(block + 1) * rows, :]
    block_sum = BlockSum(devices, places, source, summed, *block_refs[:7])
    block_sum.start()
    summed[me, pl.ds(rows, more_rows), :] = z_sum_end(places, pieces, landed, z_copies)
    sums[...] = jnp.zeros_like(sums)
    late.wait(2, 3, 4)

    def close(step, rows):
        other_core(mine_a, theirs_a, sems_a, step).wait_recv()
        grad = mine_a[rows, :].astype(F32) + theirs_a[rows, :].astype(F32)
        unit, scale = normalise(query[rows, :].astype(F32))
        gquery_ref[rows, :] = (norm_back(unit, scale, norms[0:1, :], grad) + gres[rows, :]).astype(BF)
        out.start(0, step)
        sums[0:8, :] += fold_rows(grad * unit)
        sums[8:16, :] += fold_rows(grad)
        other_core(mine_b, theirs_b, sems_b, step).wait_recv()
        grad = mine_b[rows, :].astype(F32) + theirs_b[rows, :].astype(F32)
        unit, scale = normalise(kv[rows, :].astype(F32))
        gkv_ref[rows, :] = norm_back(unit, scale, norms[2:3, :], grad).astype(BF)
        out.start(1, step)
        sums[16:24, :] += fold_rows(grad * unit)
        sums[24:32, :] += fold_rows(grad)
    chunks(tokens, close)
    parts = [sums[8 * i:8 * i + 8, :] for i in range(4)]
    parts += [sums_c[0:8, :], sums_c[8:16, :], sums_f[0:8, :], sums_f[8:16, :]]
    norm_mine[...] = jnp.concatenate([jnp.sum(part, 0, keepdims=True) for part in parts], 0)
    n_copies = [send(norm_mine, norm_all.at[d], n_sems.at[0, d], n_sems.at[1, d], dp=other)
                for d, other in zip(range(1, devices), others)]
    block_sum.finish()
    out_rows = summed.shape[1]
    spread_blocks(devices, lambda block, start, size: summed.at[block, pl.ds(start, size)], out_rows, out_rows // 2 // UNIT * UNIT,
                  places, *block_refs[7:])
    total = norm_mine[...]
    for d, copy in zip(range(1, devices), n_copies):
        copy.wait_recv()
        total = total + norm_all[d]
    gnorm_ref[...] = total
    block_sum.drain()
    for copy in z_copies + n_copies:
        copy.wait_send()
    out.drain(tokens)
    drain(tokens, mine_a, theirs_a, sems_a)
    drain(tokens, mine_b, theirs_b, sems_b)


def self_back(devices, ready_rows, dq, dk, dv, ws, nq, nkv, query, kv, gres, norms, sums_c, sums_f, parts):
    tokens, features = nq.shape
    cols = dq.shape[1]
    across, more_rows = devices // 4, parts[0].shape[1] - ready_rows
    flat_rows = -(-3 * cols // (devices * UNIT)) * devices * UNIT
    rows = flat_rows // devices
    wide = (tokens, features)
    outs = [(wide, BF, "A"), (wide, BF, "A"), ((devices, rows + more_rows, features), BF, "V"), ((8, features), F32, "V")]
    low, high = pltpu.VMEM(wide, BF), pltpu.VMEM(wide, F32)
    small = pltpu.VMEM((across, more_rows, features), BF)
    D = pltpu.SemaphoreType.DMA
    scratch = [low, low, low, low, high, low, low, pltpu.VMEM((flat_rows, features), BF), pltpu.VMEM((devices, rows, features), BF),
               small, small, pltpu.VMEM((8, features), F32), pltpu.VMEM((devices, 8, features), F32)]
    scratch += [low] * 4 + [pltpu.VMEM((32, features), F32)] + [pair_sems(tokens)] * 2
    scratch += [D((5,)), out_semaphores(2, tokens), D((2, across)), D((2, devices))]
    scratch += block_sum_scratch(devices, rows, features) + [D((2, across))] * 5
    return call(partial(self_back_kernel, devices, ready_rows), "self_back",
                [dq, dk, dv, ws, nq, nkv, query, kv, gres, norms, sums_c, sums_f] + parts, "VVVVAAAAAVVVVVVV", outs, scratch, 5)


def update_kernel(devices, early_unit, late_unit, own_rows, last_rows, owner_ref, me_ref, summed, part0, part1, part2, part3,
                  master, first, second, gquery_in, gkv_in, grad_ref, first_ref, second_ref, new_ref, gquery_out, gkv_out,
                  held, taken, held_q, held_kv, sems):
    units = owner_ref.shape[0]
    slots = master.shape[0]
    across = devices // 4
    more_rows = summed.shape[1] - own_rows
    me = me_ref[0]
    entering = Late([(gquery_in, held_q), (gkv_in, held_kv)], sems.at[0])
    here, level = lax.rem(me, 4), lax.div(me, 4)

    def find(u, count):
        held[count] = u
        return count + (owner_ref[u] == me).astype(jnp.int32)
    count = lax.fori_loop(0, units, find, jnp.int32(0), unroll=4)
    entering.wait(0, 1)
    leaving = Late([(held_q, gquery_out), (held_kv, gkv_out)], sems.at[1])

    def rows_of(row, size, start):
        return pl.ds(pl.multiple_of(lax.rem(row, size) + start, UNIT), UNIT)

    def one(slot, carry):
        @pl.when(slot < count)
        def _():
            unit = held[slot]

            @pl.when(unit < early_unit)
            def _():
                row = unit * UNIT
                taken[...] = summed[lax.div(row, own_rows), rows_of(row, own_rows, 0), :]

            @pl.when((unit >= early_unit) & (unit < late_unit))
            def _():
                row = (unit - early_unit) * UNIT
                taken[...] = summed[lax.div(row, more_rows), rows_of(row, more_rows, own_rows), :]

            @pl.when(unit >= late_unit)
            def _():
                row = (unit - late_unit) * UNIT
                block = lax.div(row, last_rows)
                behind = lax.rem(level - lax.div(block, 4) + across, across)
                for f, part in enumerate((part0, part1, part2, part3)):
                    @pl.when(lax.rem(block, 4) == here ^ f)
                    def _():
                        taken[...] = part[behind, rows_of(row, last_rows, 0), :]
            gradient = taken[...].astype(F32)
            first_new, second_new, weight = adamw_step(gradient, first[slot], second[slot], master[slot], RATE_MATRIX, WEIGHT_DECAY)
            grad_ref[slot] = gradient
            first_ref[slot] = first_new
            second_ref[slot] = second_new
            new_ref[slot] = weight

        @pl.when(slot >= count)
        def _():
            for ref in (grad_ref, first_ref, second_ref, new_ref):
                ref[slot] = jnp.zeros(ref.shape[1:], F32)
        return carry
    lax.fori_loop(0, slots, one, 0)
    leaving.wait(0, 1)


def update(devices, early_unit, late_unit, own_rows, last_rows, unit_owner, me, summed, parts, master, first, second, gquery, gkv):
    outs = [(master.shape, F32, "V")] * 4 + [(gquery.shape, BF, "A")] * 2
    kernel = partial(update_kernel, devices, early_unit, late_unit, own_rows, last_rows)
    return call(kernel, "update", [unit_owner, me, summed] + parts + [master, first, second, gquery, gkv], "SSVVVVVVVVAA", outs,
                [pltpu.SMEM((unit_owner.shape[0] + 8,), jnp.int32), pltpu.VMEM((UNIT, master.shape[2]), BF),
                 pltpu.VMEM(gquery.shape, BF), pltpu.VMEM(gkv.shape, BF), pltpu.SemaphoreType.DMA((2, 2))])


def adamw_step(gradient, first, second, weight, rate, decay):
    first_new = BETA_ONE * first + (1.0 - BETA_ONE) * gradient
    second_new = BETA_TWO * second + (1.0 - BETA_TWO) * gradient * gradient
    corr_one = 1.0 - BETA_ONE**STEP
    corr_two = 1.0 - BETA_TWO**STEP
    direction = first_new / corr_one / (jnp.sqrt(second_new / corr_two) + ADAM_EPS)
    return (first_new, second_new, weight - rate * (direction + decay * weight))


def local(
    query_stream, kv_stream, memory, out_grad, lengths, obs_rank, obs_count, unit_owner,
    master, first_moment, second_moment, norm_master, norm_first, norm_second,
):
    devices = lax.axis_size("dp")
    shards = lax.axis_size("head")
    me = lax.axis_index("dp")
    slots, unit_rows, features = master.shape[0], master.shape[2], master.shape[3]
    units = unit_owner.shape[0]
    norm_share = norm_master.shape[0]
    cols = features // shards
    hidden = (units * unit_rows - 8 * cols) // 2

    shape = (slots, unit_rows, features)
    norm_row = lax.dynamic_update_slice(
        jnp.zeros((1, features), F32), norm_master.reshape(1, norm_share), (0, lax.rem(me * norm_share, features)))
    rank_row, count_row = obs_rank.reshape(1, ROW), obs_count.reshape(1, ROW)
    place_of, steps = plan(unit_owner, lengths, devices, slots + 1)
    nq, nkv, qt, k, kt, v, vt, kc, kct, vc, vct, ws, wc, wo_self, wo_cross, w1, w2, norms, *tables = project(
        devices, place_of, lengths, master.reshape(shape), norm_row, rank_row,
        query_stream, kv_stream, memory, cols, hidden)
    mixed_self, mixed_self_t, total_self = attend_forward(steps, qt, k, vt, tables, count_row, True)
    residual, nc, qct = self_out(mixed_self, wo_self, query_stream, wc, norms)
    mixed_cross, mixed_cross_t, total_cross = attend_forward(steps, qct, kc, vct, tables, count_row, False)
    output, grad_cross_res, grad_mixed, *parts, gwo_cross, sums_f = feed_forward(
        devices, mixed_cross, wo_cross, residual, w1, w2, out_grad, norms)
    tie = lax.optimization_barrier
    ready_rows = parts[0].shape[1]
    parts = [parts[0]] + [plane_swap(parts[f], devices, f) for f in (1, 2, 3)]
    dq, dk, dv, output = attend_backward(
        steps, qct, kc, kct, vc, grad_mixed, mixed_cross_t, total_cross, tables, count_row, output, False)
    parts, dq = tie((parts, dq))
    grad_memory, grad_residual, grad_mixed, *parts, sums_c = cross_back(
        devices, dq, dk, dv, wc, nc, memory, residual, grad_cross_res, mixed_self, wo_self, norms, gwo_cross, parts)
    parts = [parts[0]] + [plane_swap(parts[f], devices, f) for f in (1, 2, 3)]
    dq, dk, dv, grad_memory = attend_backward(
        steps, qt, k, kt, v, grad_mixed, mixed_self_t, total_self, tables, count_row, grad_memory, True)
    parts, dq = tie((parts, dq))
    grad_query, grad_kv, summed, norm_grads = self_back(
        devices, ready_rows, dq, dk, dv, ws, nq, nkv, query_stream, kv_stream, grad_residual, norms, sums_c, sums_f, parts)

    early, late = 3 * cols // unit_rows, 8 * cols // unit_rows
    own_rows = -(-3 * cols // (devices * UNIT)) * UNIT
    weight_grad, weight_first, weight_second, weight_new, grad_query, grad_kv = update(
        devices, early, late, own_rows, ready_rows, unit_owner, me.reshape(1), summed, parts, master.reshape(shape),
        first_moment.reshape(shape), second_moment.reshape(shape), grad_query, grad_kv)
    weight_grad, weight_first, weight_second, weight_new = [
        part.reshape(master.shape) for part in (weight_grad, weight_first, weight_second, weight_new)]
    norm_grad = lax.dynamic_slice_in_dim(norm_grads.reshape(-1), me * norm_share, norm_share)
    norm_first_new, norm_second_new, norm_new = adamw_step(
        norm_grad, norm_first, norm_second, norm_master, RATE_NORM, 0.0)
    return (
        output, grad_query, grad_kv, grad_memory, weight_grad, weight_first, weight_second, weight_new,
        norm_grad, norm_first_new, norm_second_new, norm_new,
    )


def solution(mesh):
    in_specs = (
        P("dp", None),
        P("dp", None),
        P("dp", None),
        P("dp", None),
        P("dp", None),
        P("dp"),
        P("dp"),
        P(),
        P("dp", "head", None, None),
        P("dp", "head", None, None),
        P("dp", "head", None, None),
        P("dp"),
        P("dp"),
        P("dp"),
    )
    out_specs = (
        P("dp", None),
        P("dp", None),
        P("dp", None),
        P("dp", None),
        P("dp", "head", None, None),
        P("dp", "head", None, None),
        P("dp", "head", None, None),
        P("dp", "head", None, None),
        P("dp"),
        P("dp"),
        P("dp"),
        P("dp"),
    )
    return jax.shard_map(local, mesh=mesh, in_specs=in_specs, out_specs=out_specs, check_vma=False)
```

```python
from functools import partial

import jax
import jax.numpy as jnp
from jax import lax
from jax.experimental import pallas as pl
from jax.experimental.pallas import tpu as pltpu
from jax.sharding import PartitionSpec as P

HEAD_DIM = 64
ROW = 2048
DOCS = 32
STEP = 10
UNIT = 16

EPS_NORM = 1e-05
ADAM_EPS = 1e-08
BETA_ONE = 0.5
BETA_TWO = 0.5
RATE_MATRIX = 0.1
RATE_NORM = 0.3
WEIGHT_DECAY = 0.01

F32 = jnp.float32
BF = jnp.bfloat16
TQ = 256
TK = 384
FAR = 32768.0
LANES = (64, 72, 80)


def nt(a, b):
    return lax.dot_general(a, b, (((1,), (1,)), ((), ())), preferred_element_type=F32)


def nn(a, b):
    return lax.dot_general(a, b, (((1,), (0,)), ((), ())), preferred_element_type=F32)


def doc_bounds(len_ref):
    starts, ends = [], []
    at = jnp.int32(0)
    for d in range(DOCS):
        starts.append(at)
        at = at + len_ref[0, d]
        ends.append(at)
    return starts, ends


def key_range(starts, ends, q0):
    low = jnp.int32(0)
    high = jnp.int32(0)
    for d in range(DOCS):
        low = jnp.where(starts[d] <= q0, starts[d], low)
        high = jnp.where(starts[d] <= q0 + TQ - 1, ends[d], high)
    first = lax.div(low, 128) * 128
    steps = lax.div(high - first + TK - 1, TK)
    return first, steps


def mask_tables(len_ref, rank_ref, side_ref, hot_ref, rank_cols):
    starts, ends = doc_bounds(len_ref)
    lanes = lax.broadcasted_iota(jnp.int32, (1, 128), 1)
    start_lane = jnp.full((1, 128), -1, jnp.int32)
    end_lane = jnp.full((1, 128), -1, jnp.int32)
    for d in range(DOCS):
        start_lane = jnp.where(lanes == d, starts[d], start_lane)
        end_lane = jnp.where(lanes == d, ends[d], end_lane)
    one = (lanes == LANES[0]) | (lanes == LANES[1]) | (lanes == LANES[2])
    for t in range(ROW // 256):
        pos = lax.broadcasted_iota(jnp.int32, (256, 128), 0) + t * 256
        hot = (pos >= start_lane) & (pos < end_lane)
        side = jnp.where(hot | (lanes >= DOCS), jnp.where(one, -1.0, 0.0), -FAR)
        side_ref[t * 256:(t + 1) * 256, :] = side.astype(BF)
    pos = lax.broadcasted_iota(jnp.int32, (1, ROW), 1)
    first = jnp.zeros((1, ROW), jnp.bool_)
    rows = []
    for d in range(DOCS):
        first = first | (pos == starts[d])
        rows.append(jnp.where((pos >= starts[d]) & (pos < ends[d]), FAR, 0.0))
    hot_ref[...] = jnp.concatenate(rows + [jnp.zeros((128 - DOCS, ROW), F32)], 0).astype(BF)
    rank = jnp.where(first, -1.0, rank_ref[...].astype(F32))
    for t in range(ROW // 128):
        rank_cols[t * 128:(t + 1) * 128, :] = jnp.broadcast_to(rank[:, t * 128:(t + 1) * 128], (128, 128)).T


STEPS = (ROW // TQ) * -(-ROW // TK) + 8


def step_table(len_ref, table):
    starts, ends = doc_bounds(len_ref)
    idle = ROW // TQ

    def put(at, tile, first):
        table[0, at] = tile
        table[1, at] = first
    put(0, idle, ROW)
    put(1, idle, ROW)
    at = jnp.int32(2)
    for tile in range(idle):
        first, steps = key_range(starts, ends, tile * TQ)

        def fill(s, at):
            put(at, tile, first + s * TK)
            return at + 1
        at = lax.fori_loop(0, steps, fill, at)
    put(at, idle, ROW)
    put(at + 1, idle, ROW)
    table[0, STEPS - 1] = at


def step_of(table, i):
    return table[0, i], pl.multiple_of(table[1, i], 128)


def real_step(table, i):
    return jnp.minimum(table[0, i], ROW // TQ - 1), pl.multiple_of(table[1, i], 128)


def padded(ref):
    return ref.at[pl.ds(0, ROW)] if ref.shape[0] > ref.shape[1] else ref.at[:, pl.ds(0, ROW)]


def fill_padding(refs, side_ref):
    for ref in refs:
        if ref.shape[0] > ref.shape[1]:
            ref[ROW:, :] = jnp.zeros((TK, ref.shape[1]), ref.dtype)
        else:
            ref[:, ROW:] = jnp.zeros((ref.shape[0], TK), ref.dtype)
    lanes = lax.broadcasted_iota(jnp.int32, (TK, 128), 1)
    side_ref[ROW:, :] = jnp.where(lanes < DOCS, -FAR, 0.0).astype(BF)


def seen_bias(rank_cols, counts, tile, k0):
    rank = rank_cols[pl.ds(k0, TK), :]
    rank = jnp.concatenate([rank] * (TQ // 128), 1)
    kpos = lax.broadcasted_iota(jnp.int32, (TK, TQ), 0)
    qpos = lax.broadcasted_iota(jnp.int32, (TK, TQ), 1)
    off_diag = (kpos - qpos) != (tile * TQ - k0)
    allowed = (rank < counts[tile, 0:1, :]) & (off_diag | (rank < 0.0))
    return jnp.where(allowed, 0.0, -FAR * FAR)


def count_tiles(counts, count_ref):
    for tile in range(ROW // TQ):
        counts[tile] = jnp.broadcast_to(count_ref[:, tile * TQ:(tile + 1) * TQ].astype(F32), (8, TQ))


def query_columns(qt, qt_ref, side, tile, h, q0):
    rows = qt_ref[h * HEAD_DIM:(h + 1) * HEAD_DIM, pl.ds(q0, TQ)].astype(F32) * HEAD_DIM ** -0.5
    own, other = h % 2 * HEAD_DIM, (1 - h % 2) * HEAD_DIM
    qt[tile, h, own:own + HEAD_DIM, :] = rows.astype(BF)
    qt[tile, h, other:other + HEAD_DIM, :] = jnp.zeros((HEAD_DIM, TQ), BF)
    qt[tile, h, 128:256, :] = side


def pair_rows(ref, side_ref, h, k0):
    return jnp.concatenate([ref[pl.ds(k0, TK), h // 2 * 128:(h // 2 + 1) * 128], side_ref[pl.ds(k0, TK), :]], 1)


def attn_fwd_kernel(with_seen, heads, table, count_ref, qt_hbm, hot_hbm, k_hbm, vt_hbm, side_hbm, rank_hbm,
                    o_out, ot_out, lse_ref, qt, acc, top, sc, probs, fade, counts,
                    qt_ref, hot_ref, k_ref, vt_ref, side_ref, rank_cols, o_ref, ot_ref, late_sems, out_sems):
    pairs = [(qt_hbm, qt_ref), (hot_hbm, hot_ref), (k_hbm, padded(k_ref)), (vt_hbm, padded(vt_ref)),
             (side_hbm, padded(side_ref))]
    late = Late(pairs + ([(rank_hbm, padded(rank_cols))] if with_seen else []), late_sems)
    fill_padding((k_ref, vt_ref, rank_cols), side_ref)
    out = Out([(o_ref, o_out), (ot_ref, ot_out)], out_sems)
    tiles = ROW // TQ
    lse_ref[...] = jnp.zeros_like(lse_ref)
    acc[...] = jnp.zeros_like(acc)
    top[...] = jnp.full_like(top, -jnp.inf)
    if with_seen:
        count_tiles(counts, count_ref)
    late.wait(0, 1)

    def prepare(tile, c):
        q0 = pl.multiple_of(tile * TQ, TQ)
        for h in range(heads):
            query_columns(qt, qt_ref, hot_ref[:, pl.ds(q0, TQ)], tile, h, q0)
        return c
    lax.fori_loop(0, tiles, prepare, 0)
    late.wait(*range(2, 6 if with_seen else 5))
    ones = jnp.ones((16, TK), BF)

    def one_step(s, c):
        out_tile, _ = step_of(table, s)
        _, out_k = real_step(table, s)
        mid_tile, _ = step_of(table, s + 1)
        in_tile, in_k = real_step(table, s + 2)
        sums = []
        for h in range(heads):
            values = jnp.concatenate([vt_ref[h * HEAD_DIM:(h + 1) * HEAD_DIM, pl.ds(out_k, TK)], ones], 0)
            sums.append(acc[out_tile, h] * fade[h:h + 1, :] + nn(values, probs[h]))
        old = top[mid_tile]
        news = []
        for h in range(heads):
            score = sc[h]
            new = jnp.maximum(old[h:h + 1, :], jnp.max(score, 0, keepdims=True))
            probs[h] = jnp.exp(score - new).astype(BF)
            news.append(new)
        new = jnp.concatenate(news + [old[heads:, :]], 0)
        fade[...] = jnp.exp(old - new)
        bias = seen_bias(rank_cols, counts, in_tile, in_k) if with_seen else None
        for h in range(heads):
            score = nn(pair_rows(k_ref, side_ref, h, in_k), qt[in_tile, h])
            sc[h] = score + bias if with_seen else score
        top[mid_tile] = new
        for h in range(heads):
            acc[out_tile, h] = sums[h]
        return c
    lax.fori_loop(0, table[0, STEPS - 1], one_step, 0)

    def finish(tile, c):
        q0 = pl.multiple_of(tile * TQ, TQ)
        outs = []
        peak = top[tile]
        for h in range(heads):
            a = acc[tile, h]
            total = a[HEAD_DIM:HEAD_DIM + 1, :]
            outs.append(a[:HEAD_DIM, :] * (1.0 / total))
            lse_ref[h:h + 1, pl.ds(q0, TQ)] = peak[h:h + 1, :] + jnp.log(total)
        mixed = jnp.concatenate(outs, 0).astype(BF)
        ot_ref[:, pl.ds(q0, TQ)] = mixed
        out.start(1, tile)
        o_ref[pl.ds(q0, TQ), :] = mixed.T
        out.start(0, tile)
        return c
    lax.fori_loop(0, tiles, finish, 0)
    out.drain(ROW)


def attend_forward(steps, qt, k, vt, tables, count, with_seen):
    cols, rows = qt.shape
    heads = cols // HEAD_DIM
    side, hot, rank_cols = tables
    args = [steps, count, qt, hot, k, vt, side, rank_cols]
    across, down = (cols, rows), (rows, cols)
    held = [pltpu.VMEM(arg.shape, BF) for arg in (qt, hot)] + [
        pltpu.VMEM((rows + TK, cols), BF), pltpu.VMEM((cols, rows + TK), BF), pltpu.VMEM((rows + TK, 128), BF),
        pltpu.VMEM((rows + TK, 128), F32)]
    return call(partial(attn_fwd_kernel, with_seen, heads), "attend_self_forward" if with_seen else "attend_cross_forward",
                args, "SV" + "A" * 6, [(down, BF, "A"), (across, BF, "A"), ((8, rows), F32, "V")],
                [pltpu.VMEM((ROW // TQ, heads, 256, TQ), BF), pltpu.VMEM((ROW // TQ + 1, heads, HEAD_DIM + 16, TQ), F32),
                 pltpu.VMEM((ROW // TQ + 1, 8, TQ), F32), pltpu.VMEM((heads, TK, TQ), F32), pltpu.VMEM((heads, TK, TQ), BF),
                 pltpu.VMEM((8, TQ), F32), pltpu.VMEM((ROW // TQ, 8, TQ), F32)] + held
                + [pltpu.VMEM(down, BF), pltpu.VMEM(across, BF), pltpu.SemaphoreType.DMA((6,)), out_semaphores(2, rows)])


def three_rows(value):
    high = value.astype(BF).astype(F32)
    middle = (value - high).astype(BF).astype(F32)
    row = lax.broadcasted_iota(jnp.int32, (128, value.shape[1]), 0)
    return jnp.where(row == LANES[0], high, jnp.where(row == LANES[1], middle, jnp.where(row == LANES[2], value - high - middle, 0.0)))


def attn_bwd_kernel(with_seen, heads, table, count_ref, lse_ref, qt_hbm, hot_hbm, gt_hbm, ot_hbm, k_hbm, kt_hbm, v_hbm, side_hbm,
                    rank_hbm, pass_in,
                    dq_out, dk_out, dv_out, pass_out, dk_sum, dv_sum, dq_sum, qt, gt, q_own, g_own, sc, dps, all_ds, all_p, counts,
                    qt_ref, hot_ref, gt_ref, ot_ref, k_ref, kt_ref, v_ref, side_ref, rank_cols, held, dq_ref, dk_ref, dv_ref,
                    late_sems, out_sems, pass_sem):
    pairs = [(qt_hbm, qt_ref), (hot_hbm, hot_ref), (gt_hbm, gt_ref), (ot_hbm, ot_ref), (k_hbm, padded(k_ref)),
             (kt_hbm, padded(kt_ref)), (v_hbm, padded(v_ref)), (side_hbm, padded(side_ref))]
    late = Late(pairs + ([(rank_hbm, padded(rank_cols))] if with_seen else []), late_sems)
    fill_padding((k_ref, kt_ref, v_ref, rank_cols), side_ref)
    entering = pltpu.make_async_copy(pass_in, held, pass_sem.at[0])
    entering.start()
    out = Out([(dq_ref, dq_out), (dk_ref, dk_out), (dv_ref, dv_out)], out_sems)
    tiles = ROW // TQ
    dk_sum[...] = jnp.zeros_like(dk_sum)
    dv_sum[...] = jnp.zeros_like(dv_sum)
    dq_sum[...] = jnp.zeros_like(dq_sum)
    if with_seen:
        count_tiles(counts, count_ref)
    late.wait(0, 1, 2, 3)

    def prepare(tile, c):
        q0 = pl.multiple_of(tile * TQ, TQ)
        hot = hot_ref[:, pl.ds(q0, TQ)].astype(F32)
        for h in range(heads):
            rows = slice(h * HEAD_DIM, (h + 1) * HEAD_DIM)
            side = hot + three_rows(lse_ref[h:h + 1, pl.ds(q0, TQ)])
            query_columns(qt, qt_ref, side.astype(BF), tile, h, q0)
            grads = gt_ref[rows, pl.ds(q0, TQ)]
            delta = jnp.sum(grads.astype(F32) * ot_ref[rows, pl.ds(q0, TQ)].astype(F32), 0, keepdims=True)
            other = (1 - h % 2) * HEAD_DIM
            gt[tile, h, h % 2 * HEAD_DIM:(h % 2 + 1) * HEAD_DIM, :] = grads
            gt[tile, h, other:other + HEAD_DIM, :] = jnp.zeros((HEAD_DIM, TQ), BF)
            gt[tile, h, 128:256, :] = three_rows(delta).astype(BF)
        lane = lax.broadcasted_iota(jnp.int32, (TQ, heads * HEAD_DIM), 1)
        for held_rows, source in ((q_own, qt_ref), (g_own, gt_ref)):
            rows = source[:, pl.ds(q0, TQ)].T
            for h in range(heads):
                own = (lane >= h * HEAD_DIM) & (lane < (h + 1) * HEAD_DIM)
                held_rows[tile, h * TQ:(h + 1) * TQ, :] = jnp.where(own, rows, jnp.zeros_like(rows))
        return c
    lax.fori_loop(0, tiles, prepare, 0)
    late.wait(*range(4, 9 if with_seen else 8))
    entering.wait()
    leaving = pltpu.make_async_copy(held, pass_out, pass_sem.at[1])
    leaving.start()

    def one_step(s, c):
        out_tile, out_k = step_of(table, s)
        read_tile, read_k = real_step(table, s)
        in_tile, in_k = real_step(table, s + 2)
        keys = pl.ds(out_k, TK)
        own = [slice(h * HEAD_DIM, (h + 1) * HEAD_DIM) for h in range(heads)]
        dk = dk_sum[keys, :] + nn(all_ds[...], q_own[read_tile])
        dv = dv_sum[keys, :] + nn(all_p[...], g_own[read_tile])
        dq = [dq_sum[out_tile, h] + nn(kt_ref[own[h], pl.ds(read_k, TK)], all_ds[:, h * TQ:(h + 1) * TQ]) for h in range(heads)]
        for h in range(heads):
            p = jnp.exp(sc[h])
            all_ds[:, h * TQ:(h + 1) * TQ] = (p * dps[h]).astype(BF)
            all_p[:, h * TQ:(h + 1) * TQ] = p.astype(BF)
        bias = seen_bias(rank_cols, counts, in_tile, in_k) if with_seen else None
        for h in range(heads):
            score = nn(pair_rows(k_ref, side_ref, h, in_k), qt[in_tile, h])
            sc[h] = score + bias if with_seen else score
            dps[h] = nn(pair_rows(v_ref, side_ref, h, in_k), gt[in_tile, h])
        dk_sum[keys, :] = dk
        dv_sum[keys, :] = dv
        for h in range(heads):
            dq_sum[out_tile, h] = dq[h]
        return c
    lax.fori_loop(0, table[0, STEPS - 1], one_step, 0)

    def finish(tile, c):
        q0 = pl.multiple_of(tile * TQ, TQ)
        rows = pl.ds(q0, TQ)
        dq = jnp.concatenate([dq_sum[tile, h] for h in range(heads)], 0) * HEAD_DIM ** -0.5
        dk = dk_sum[rows, :] * HEAD_DIM ** -0.5
        for i, (ref, value) in enumerate(((dq_ref, dq.astype(BF).T), (dk_ref, dk.astype(BF)), (dv_ref, dv_sum[rows, :].astype(BF)))):
            ref[rows, :] = value
            out.start(i, tile)
        return c
    lax.fori_loop(0, tiles, finish, 0)
    out.drain(ROW)
    leaving.wait()


def attend_backward(steps, qt, k, kt, v, gt, ot, lse, tables, count, passed, with_seen):
    rows, cols = v.shape
    heads = cols // HEAD_DIM
    side, hot, rank_cols = tables
    args = [steps, count, lse, qt, hot, gt, ot, k, kt, v, side, rank_cols, passed]
    tiles = ROW // TQ
    like = ((rows, cols), BF, "A")
    summed, own = pltpu.VMEM((rows + TK, cols), F32), pltpu.VMEM((tiles, heads * TQ, cols), BF)
    columns, square = pltpu.VMEM((tiles, heads, 256, TQ), BF), pltpu.VMEM((heads, TK, TQ), F32)
    small = pltpu.VMEM((TK, heads * TQ), BF)
    keys, keys_t = pltpu.VMEM((rows + TK, cols), BF), pltpu.VMEM((cols, rows + TK), BF)
    held = [pltpu.VMEM(arg.shape, BF) for arg in (qt, hot, gt, ot)] + [
        keys, keys_t, keys, pltpu.VMEM((rows + TK, 128), BF), pltpu.VMEM((rows + TK, 128), F32),
        pltpu.VMEM(passed.shape, passed.dtype)]
    return call(partial(attn_bwd_kernel, with_seen, heads), "attend_self_backward" if with_seen else "attend_cross_backward",
                args, "SVV" + "A" * 10, [like, like, like, (passed.shape, passed.dtype, "A")],
                [summed, summed, pltpu.VMEM((tiles + 1, heads, HEAD_DIM, TQ), F32), columns, columns, own, own, square, square,
                 small, small, pltpu.VMEM((ROW // TQ, 8, TQ), F32)] + held + [pltpu.VMEM((rows, cols), BF)] * 3
                + [pltpu.SemaphoreType.DMA((9,)), out_semaphores(3, rows), pltpu.SemaphoreType.DMA((2,))])


def send(src, dst, send_sem, recv_sem, **where):
    copy = pltpu.make_async_remote_copy(src_ref=src, dst_ref=dst, send_sem=send_sem, recv_sem=recv_sem,
                                        device_id=where, device_id_type=pl.DeviceIdType.MESH)
    copy.start()
    return copy

def greet(peers):
    barrier = pltpu.get_barrier_semaphore()
    for where in peers:
        pl.semaphore_signal(barrier, inc=1, device_id=where, device_id_type=pl.DeviceIdType.MESH)
    pl.semaphore_wait(barrier, len(peers))

def places_of(count):
    me = lax.axis_index("dp")
    across = count // 4
    x, y, z = lax.rem(me, 2), lax.rem(lax.div(me, 2), 2), lax.div(me, 4)
    xpeer, ypeer = me + 1 - 2 * x, me + 2 - 4 * y
    order = sorted(range(1, across), key=lambda d: min(d, across - d))
    ahead = lambda d: lax.rem(z + d, across) * 4 + y * 2 + x
    behind = lambda d: lax.rem(z + across - d, across) * 4 + y * 2 + x
    return me, x, y, z, xpeer, ypeer, order, ahead, behind

def spread_blocks(count, piece, rows, half, places, zs, xs, ys, gx, gy, meanwhile=None):
    me, x, y, z, xpeer, ypeer, order, ahead, behind = places
    whole = (0, rows)
    sent, recv = [], {}
    def go(src_block, at, sem, d, to):
        copy = send(piece(src_block, *at), piece(src_block, *at), sem.at[0, d], sem.at[1, d], dp=to)
        sent.append(copy)
        return copy
    near = go(me, whole, xs, 0, xpeer), go(me, whole, ys, 0, ypeer)
    recv[0] = near
    zcopies = {}
    for d in order:
        zcopies[d] = go(me, whole, zs, d, ahead(d))
    if meanwhile is not None:
        meanwhile()
    steps = [0] + order
    diag = []
    for k, d in enumerate(steps):
        if d:
            zcopies[d].wait_recv()
            recv[d] = go(behind(d), whole, xs, d, xpeer), go(behind(d), whole, ys, d, ypeer)
        if k:
            forward(go, diag, recv, steps[k - 1], behind, places, half, rows, gx, gy)
    forward(go, diag, recv, steps[-1], behind, places, half, rows, gx, gy)
    for copy in diag:
        copy.wait_recv()
    for copy in sent:
        copy.wait_send()

def forward(go, diag, recv, d, behind, places, half, rows, gx, gy):
    me, x, y, z, xpeer, ypeer, order, ahead, _ = places
    base = behind(d) if d else me
    recv[d][0].wait_recv()
    diag.append(go(base + 1 - 2 * x, (0, half), gy, d, ypeer))
    recv[d][1].wait_recv()
    diag.append(go(base + 2 - 4 * y, (half, rows - half), gx, d, xpeer))

class Spread:
    def __init__(self, places, out, zs, xs, ys, gx, gy):
        self.places, self.out, self.sems = places, out, dict(z=zs, x=xs, y=ys, gx=gx, gy=gy)
        self.rows = out.shape[2]
        self.half = self.rows // 2 // UNIT * UNIT
        self.copies = {}

    def go(self, name, d, f_from, d_from, f_to, d_to, to, start, size):
        part, sems = pl.ds(start, size), self.sems[name]
        self.copies[name, d] = send(self.out.at[f_from, d_from, part], self.out.at[f_to, d_to, part],
                                    sems.at[0, d], sems.at[1, d], dp=to)

    def over_plane(self, d):
        xpeer, ypeer = self.places[4], self.places[5]
        self.go("x", d, 0, d, 1, d, xpeer, 0, self.rows)
        self.go("y", d, 0, d, 2, d, ypeer, 0, self.rows)

    def start(self):
        order, ahead = self.places[6], self.places[7]
        for d in order:
            self.go("z", d, 0, 0, 0, d, ahead(d), 0, self.rows)
        self.over_plane(0)

    def relay(self):
        for d in self.places[6]:
            self.copies["z", d].wait_recv()
            self.over_plane(d)

    def diagonal(self):
        xpeer, ypeer, order = self.places[4:7]
        for d in [0] + order:
            self.copies["x", d].wait_recv()
            if self.half:
                self.go("gy", d, 1, d, 3, d, ypeer, 0, self.half)
            self.copies["y", d].wait_recv()
            self.go("gx", d, 2, d, 3, d, xpeer, self.half, self.rows - self.half)

    def finish(self):
        for (name, d), copy in self.copies.items():
            if name in ("gx", "gy"):
                copy.wait_recv()

    def drain(self):
        for copy in self.copies.values():
            copy.wait_send()


def plane_swap(value, count, f):
    return lax.ppermute(value, "dp", [(i, i // 4 * 4 + (i % 4 ^ f)) for i in range(count)])


def plane_offset(places, f):
    x, y = places[1], places[2]
    return lax.rem(x + f % 2, 2) + 2 * lax.rem(y + f // 2, 2)


def call(kernel, name, args, kinds, outs, scratch, number=None):
    space = {"V": pltpu.VMEM, "S": pltpu.SMEM, "A": pl.ANY}
    extra = {} if number is None else dict(collective_id=number, has_side_effects=True)
    return pl.pallas_call(
        kernel,
        out_shape=tuple(jax.ShapeDtypeStruct(shape, dtype) for shape, dtype, _ in outs),
        in_specs=[pl.BlockSpec(memory_space=space[kind]) for kind in kinds],
        out_specs=tuple(pl.BlockSpec(memory_space=space[kind]) for _, _, kind in outs),
        scratch_shapes=scratch,
        compiler_params=pltpu.CompilerParams(vmem_limit_bytes=60 * 2**20, **extra),
        cost_estimate=pl.CostEstimate(flops=4 * 10**10, bytes_accessed=16 * 2**20, transcendentals=0),
        name=name,
    )(*args)


CHUNK = 256


def tn(a, b):
    return lax.dot_general(a, b, (((0,), (0,)), ((), ())), preferred_element_type=F32)


def normalise(value):
    centred = value - jnp.mean(value, -1, keepdims=True)
    scale = lax.rsqrt(jnp.mean(centred * centred, -1, keepdims=True) + EPS_NORM)
    return centred * scale, scale


def norm_back(unit, scale, gain, grad):
    inner = grad * gain
    return scale * (inner - jnp.mean(inner, -1, keepdims=True) - unit * jnp.mean(inner * unit, -1, keepdims=True))


def fold_rows(value):
    return jnp.sum(value.reshape(value.shape[0] // 8, 8, value.shape[1]), 0)


def interleave(size):
    row = lax.broadcasted_iota(jnp.int32, (size, size), 0)
    col = lax.broadcasted_iota(jnp.int32, (size, size), 1)
    source = jnp.where((row & 1) == 0, row >> 1, (row >> 1) + size // 2)
    return jnp.where(col == source, 1.0, 0.0).astype(BF)


def part_rows(matrix, order):
    return lax.dot_general(order, matrix, (((0,), (0,)), ((), ())), preferred_element_type=F32).astype(BF)


def as_units(gradient, order):
    parted = part_rows(gradient.astype(BF), order)
    half = parted.shape[0] // 2
    return jnp.concatenate([parted[:half], parted[half:]], 1)


def other_core(mine, theirs, sems, step):
    rows = pl.ds(step * CHUNK, CHUNK)
    return pltpu.make_async_remote_copy(
        src_ref=mine.at[rows], dst_ref=theirs.at[rows], send_sem=sems.at[0, step], recv_sem=sems.at[1, step],
        device_id={"head": 1 - lax.axis_index("head")}, device_id_type=pl.DeviceIdType.MESH)


def greet_core():
    greet([{"head": 1 - lax.axis_index("head")}])


def chunks(total, body, begin=0):
    def one(step, carry):
        body(step, pl.ds(pl.multiple_of(step * CHUNK, CHUNK), CHUNK))
        return carry
    lax.fori_loop(begin // CHUNK, total // CHUNK, one, 0)


def drain(total, mine, theirs, sems):
    def body(step, rows):
        other_core(mine, theirs, sems, step).wait_send()
    chunks(total, body)


class Late:
    def __init__(self, pairs, sems):
        self.copies = [pltpu.make_async_copy(source, held, sems.at[i]) for i, (source, held) in enumerate(pairs)]
        for copy in self.copies:
            copy.start()

    def wait(self, *which):
        for i in which:
            self.copies[i].wait()


class Out:
    def __init__(self, pairs, sems):
        self.pairs, self.sems = pairs, sems

    def copy(self, i, step):
        held, out = self.pairs[i]
        part = pl.ds(pl.multiple_of(step * CHUNK, CHUNK), CHUNK)
        if held.shape[0] < held.shape[1]:
            held, out = held.at[:, part], out.at[:, part]
        else:
            held, out = held.at[part], out.at[part]
        return pltpu.make_async_copy(held, out, self.sems.at[i, step])

    def start(self, i, step):
        self.copy(i, step).start()

    def drain(self, tokens):
        def body(step, rows):
            for i in range(len(self.pairs)):
                self.copy(i, step).wait()
        chunks(tokens, body)


def plan_kernel(block, owner_ref, len_ref, place_ref, table, used):
    for d in range(used.shape[0]):
        used[d] = 0

    def one_unit(u, carry):
        owner = owner_ref[u]
        slot = used[owner]
        place_ref[u] = owner * block + slot
        used[owner] = slot + 1
        return carry
    lax.fori_loop(0, owner_ref.shape[0], one_unit, 0, unroll=4)
    step_table(len_ref, table)


def plan(unit_owner, lengths, devices, block):
    return call(partial(plan_kernel, block), "plan", [unit_owner, lengths], "SS",
                [(unit_owner.shape, jnp.int32, "S"), ((2, STEPS), jnp.int32, "S")], [pltpu.SMEM((devices,), jnp.int32)])


def project_kernel(devices, place_ref, len_ref, master, norm_row, rank_ref, query_hbm, kv_hbm, memory_hbm,
                   nq_out, nkv_out, qt_out, k_out, kt_out, v_out, vt_out, kc_out, kct_out, vc_out, vct_out,
                   ws_ref, wc_ref, wos_ref, woc_ref, w1_ref, w2_ref, norms, side_ref, hot_ref, rank_cols,
                   gathered, flat, query_ref, kv_ref, memory_ref, unit_q, unit_kv,
                   nq_ref, nkv_ref, qt_ref, k_ref, kt_ref, v_ref, vt_ref, kc_ref, kct_ref, vc_ref, vct_ref,
                   late_sems, out_sems, zs, xs, ys, gx, gy):
    tokens, features = query_ref.shape
    units = place_ref.shape[0]
    late = Late([(query_hbm, query_ref), (kv_hbm, kv_ref), (memory_hbm, memory_ref)], late_sems)
    held = (nq_ref, nkv_ref, qt_ref, k_ref, kt_ref, v_ref, vt_ref, kc_ref, kct_ref, vc_ref, vct_ref)
    out = Out(list(zip(held, (nq_out, nkv_out, qt_out, k_out, kt_out, v_out, vt_out, kc_out, kct_out, vc_out, vct_out))), out_sems)
    places = places_of(devices)
    me, x, y, z, xpeer, ypeer, order, ahead, behind = places
    slots = master.shape[0]
    block = slots + 1
    gathered[pl.ds(me * block, slots)] = master[...].astype(BF)
    gathered[me * block + slots] = jnp.broadcast_to(norm_row[...], (UNIT, features)).astype(BF)
    greet([{"dp": xpeer}, {"dp": ypeer}] + [{"dp": ahead(d)} for d in order])

    def meanwhile():
        mask_tables(len_ref, rank_ref, side_ref, hot_ref, rank_cols)
        late.wait(0, 1, 2)

        def units_of(step, rows):
            unit_q[rows, :] = normalise(query_ref[rows, :].astype(F32))[0]
            unit_kv[rows, :] = normalise(kv_ref[rows, :].astype(F32))[0]
        chunks(tokens, units_of)
    spread_blocks(devices, lambda number, start, size: gathered.at[pl.ds(number * block + start, size)], block, block // 2,
                  places, zs, xs, ys, gx, gy, meanwhile)

    share = devices // 8
    vectors = []
    for number in range(8):
        pieces = [gathered[(number * share + i) * block + slots].astype(F32) for i in range(share)]
        total = pieces[0]
        for piece in pieces[1:]:
            total = total + piece
        vectors.append(total[0:1, :])
    norms[...] = jnp.concatenate(vectors, 0)

    def one_unit(u, carry):
        flat[pl.ds(pl.multiple_of(u * UNIT, UNIT), UNIT), :] = gathered[place_ref[u]]
        return carry
    lax.fori_loop(0, units, one_unit, 0, unroll=4)
    order = interleave(features)
    cols = v_ref.shape[1]
    for number in range(6):
        rows = flat[number * cols:(number + 1) * cols, :]
        stacked = jnp.concatenate([rows[:, :cols], rows[:, cols:]], 0)
        matrix = nn(order, stacked).astype(BF)
        if number < 3:
            ws_ref[number] = matrix
        else:
            wc_ref[number - 3] = matrix
    wos_ref[...] = flat[6 * cols:7 * cols, :]
    woc_ref[...] = flat[7 * cols:8 * cols, :]
    hidden = w2_ref.shape[0]
    for block in range(hidden // features):
        at = 8 * cols + block * features
        parted = part_rows(flat[at:at + features, :], order)
        half = features // 2
        w1_ref[block * half:(block + 1) * half, :] = jnp.concatenate([parted[:half], parted[half:]], 1)
    w2_ref[...] = flat[8 * cols + hidden:, :]

    def body(step, rows):
        nq = (unit_q[rows, :] * norms[0:1, :] + norms[1:2, :]).astype(BF)
        nkv = (unit_kv[rows, :] * norms[2:3, :] + norms[3:4, :]).astype(BF)
        source = memory_ref[rows, :]
        low = lambda left, right: nn(left, right).astype(BF)
        k, v, kc, vc = low(nkv, ws_ref[1]), low(nkv, ws_ref[2]), low(source, wc_ref[1]), low(source, wc_ref[2])
        results = [nq, nkv, low(nq, ws_ref[0]).T, k, k.T, v, v.T, kc, kc.T, vc, vc.T]
        for i, (ref, result) in enumerate(zip(held, results)):
            if ref.shape[0] < ref.shape[1]:
                ref[:, rows] = result
            else:
                ref[rows, :] = result
            out.start(i, step)
    chunks(tokens, body)
    out.drain(tokens)


def pair_sems(tokens):
    return pltpu.SemaphoreType.DMA((2, tokens // CHUNK))


def out_semaphores(count, tokens):
    return pltpu.SemaphoreType.DMA((count, tokens // CHUNK))


def project(devices, place_of, lengths, master, norm_row, rank_row, query_stream, kv_stream, memory, cols, hidden):
    tokens, features = query_stream.shape
    wide, narrow, across = (tokens, features), (tokens, cols), (cols, tokens)
    shapes = [wide, wide, across] + [narrow, across] * 4
    outs = [(shape, BF, "A") for shape in shapes] + [
        ((3, features, cols), BF, "V"), ((3, features, cols), BF, "V"), ((cols, features), BF, "V"), ((cols, features), BF, "V"),
        ((features, hidden), BF, "V"), ((hidden, features), BF, "V"), ((8, features), F32, "V"),
        ((ROW, 128), BF, "V"), ((128, ROW), BF, "V"), ((ROW, 128), F32, "V")]
    D = pltpu.SemaphoreType.DMA
    scratch = [pltpu.VMEM((devices * (master.shape[0] + 1), UNIT, features), BF), pltpu.VMEM((8 * cols + 2 * hidden, features), BF)]
    scratch += [pltpu.VMEM(wide, BF)] * 3 + [pltpu.VMEM(wide, F32)] * 2 + [pltpu.VMEM(shape, BF) for shape in shapes]
    scratch += [D((3,)), out_semaphores(len(shapes), tokens)] + [D((2, devices // 4))] * 5
    return call(partial(project_kernel, devices), "project",
                [place_of, lengths, master, norm_row, rank_row, query_stream, kv_stream, memory], "SSVVVAAA",
                outs, scratch, 0)


def self_out_kernel(mixed, wo, query_hbm, wc, norms, res_out, nc_out, q_out,
                    query, res_ref, nc_ref, q_ref, mine, theirs, sems, late_sems, out_sems):
    tokens = query.shape[0]
    late = Late([(query_hbm, query)], late_sems)
    out = Out([(res_ref, res_out), (nc_ref, nc_out), (q_ref, q_out)], out_sems)
    greet_core()

    def give(step, rows):
        mine[rows, :] = nn(mixed[rows, :], wo[...]).astype(BF)
        other_core(mine, theirs, sems, step).start()
    chunks(tokens, give)
    late.wait(0)

    def take(step, rows):
        other_core(mine, theirs, sems, step).wait_recv()
        res = query[rows, :].astype(F32) + (mine[rows, :].astype(F32) + theirs[rows, :].astype(F32))
        res_ref[rows, :] = res
        out.start(0, step)
        nc = (normalise(res)[0] * norms[4:5, :] + norms[5:6, :]).astype(BF)
        nc_ref[rows, :] = nc
        out.start(1, step)
        q_ref[:, rows] = nn(nc, wc[0]).astype(BF).T
        out.start(2, step)
    chunks(tokens, take)
    drain(tokens, mine, theirs, sems)
    out.drain(tokens)


def self_out(mixed, wo, query, wc, norms):
    tokens, features = query.shape
    wide = (tokens, features)
    across = (mixed.shape[1], tokens)
    outs = [(wide, F32, "A"), (wide, BF, "A"), (across, BF, "A")]
    scratch = [pltpu.VMEM(wide, BF), pltpu.VMEM(wide, F32), pltpu.VMEM(wide, BF), pltpu.VMEM(across, BF),
               pltpu.VMEM(wide, BF), pltpu.VMEM(wide, BF), pair_sems(tokens), pltpu.SemaphoreType.DMA((1,)),
               out_semaphores(3, tokens)]
    return call(self_out_kernel, "self_out", [mixed, wo, query, wc, norms], "VVAVV", outs, scratch, 2)


def gelu_parts(value):
    size = jnp.abs(value)
    bell = jnp.exp(-0.5 * value * value)
    t = 1.0 / (1.0 + (0.3275911 * 0.7071067811865476) * size)
    poly = ((((1.061405429 * t - 1.453152027) * t + 1.421413741) * t - 0.284496736) * t + 0.254829592) * t
    tail = 0.5 * poly * bell
    below = jnp.where(value < 0.0, tail, 1.0 - tail)
    return value * below, below + value * (bell * 0.3989422804014327)


def spread_flat(devices, places, flat, refs):
    rows = flat.shape[0] // devices
    for f, ref in enumerate(refs):
        place = plane_offset(places, f)
        for level in range(devices // 4):
            ref[level, ref.shape[1] - rows:, :] = flat[pl.ds(pl.multiple_of((level * 4 + place) * rows, UNIT), rows), :]


def feed_forward_kernel(devices, mixed, wo, res_hbm, w1, w2, out_grad_hbm, norms,
                        out_out, gres_out, gmix_out, part0, part1, part2, part3, sums_ref,
                        res, out_grad, out_ref, gres_ref, gmix_ref, flat,
                        mine, theirs, nf_all, hid_all, pre_all, low_all, mine_o, theirs_o, mine_g, theirs_g,
                        sems, sems_o, sems_g, late_sems, out_sems):
    tokens, features = out_grad.shape
    hidden = w2.shape[0]
    places = places_of(devices)
    late = Late([(res_hbm, res), (out_grad_hbm, out_grad)], late_sems)
    out = Out([(out_ref, out_out), (gres_ref, gres_out), (gmix_ref, gmix_out)], out_sems)
    greet_core()

    def give(step, rows):
        mine[rows, :] = nn(mixed[rows, :], wo[...]).astype(BF)
        other_core(mine, theirs, sems, step).start()
    chunks(tokens, give)
    late.wait(0, 1)

    def middle(step, rows):
        other_core(mine, theirs, sems, step).wait_recv()
        value = res[rows, :] + (mine[rows, :].astype(F32) + theirs[rows, :].astype(F32))
        gres_ref[rows, :] = value
        nf = (normalise(value)[0] * norms[6:7, :] + norms[7:8, :]).astype(BF)
        nf_all[rows, :] = nf
        grad = out_grad[rows, :]
        out_part = jnp.zeros((CHUNK, features), F32)
        grad_part = jnp.zeros((CHUNK, features), F32)
        for block in range(hidden // 256):
            at = slice(block * 256, (block + 1) * 256)
            act, slope = gelu_parts(nn(nf, w1[:, at]))
            act = act.astype(BF)
            hid_all[rows, at] = act
            pre = (slope * nt(grad, w2[at, :])).astype(BF)
            pre_all[rows, at] = pre
            out_part = out_part + nn(act, w2[at, :])
            grad_part = grad_part + nt(pre, w1[:, at])
        mine_o[rows, :] = out_part.astype(BF)
        other_core(mine_o, theirs_o, sems_o, step).start()
        mine_g[rows, :] = grad_part.astype(BF)
        other_core(mine_g, theirs_g, sems_g, step).start()
    chunks(tokens, middle)

    order = interleave(features)
    half, cols = features // 2, mixed.shape[1]
    for block in range(hidden // 256):
        at = slice(block * 256, (block + 1) * 256)
        flat[cols + hidden + block * 256:cols + hidden + (block + 1) * 256, :] = tn(hid_all[:, at], out_grad[...]).astype(BF)
    for block in range(hidden // features):
        gradient = tn(nf_all[:, block * half:(block + 1) * half], pre_all[...]).astype(BF)
        stacked = jnp.concatenate([gradient[:, :features], gradient[:, features:]], 0)
        flat[cols + block * features:cols + (block + 1) * features, :] = nn(order, stacked).astype(BF)
    sums_ref[...] = jnp.zeros_like(sums_ref)

    def close(step, rows):
        other_core(mine_o, theirs_o, sems_o, step).wait_recv()
        other_core(mine_g, theirs_g, sems_g, step).wait_recv()
        value = gres_ref[rows, :]
        out_ref[rows, :] = (value + (mine_o[rows, :].astype(F32) + theirs_o[rows, :].astype(F32))).astype(BF)
        out.start(0, step)
        grad = mine_g[rows, :].astype(F32) + theirs_g[rows, :].astype(F32)
        unit, scale = normalise(value)
        gres = norm_back(unit, scale, norms[6:7, :], grad) + out_grad[rows, :].astype(F32)
        gres_ref[rows, :] = gres
        out.start(1, step)
        sums_ref[0:8, :] += fold_rows(grad * unit)
        sums_ref[8:16, :] += fold_rows(grad)
        low = gres.astype(BF)
        low_all[rows, :] = low
        gmix_ref[:, rows] = nt(low, wo[...]).astype(BF).T
        out.start(2, step)
    chunks(tokens, close)
    flat[0:cols, :] = tn(mixed[...], low_all[...]).astype(BF)
    if flat.shape[0] > cols + 2 * hidden:
        flat[cols + 2 * hidden:, :] = jnp.zeros((flat.shape[0] - cols - 2 * hidden, features), BF)
    spread_flat(devices, places, flat, (part0, part1, part2, part3))
    out.drain(tokens)
    drain(tokens, mine, theirs, sems)
    drain(tokens, mine_o, theirs_o, sems_o)
    drain(tokens, mine_g, theirs_g, sems_g)


def whole_blocks(rows, devices):
    return -(-rows // (devices * UNIT)) * devices * UNIT


def feed_forward(devices, mixed, wo, res, w1, w2, out_grad, norms):
    tokens, features = out_grad.shape
    hidden = w2.shape[0]
    flat_rows = whole_blocks(wo.shape[0] + 2 * hidden, devices)
    part = ((devices // 4, flat_rows // devices, features), BF, "V")
    wide = (tokens, features)
    across = (mixed.shape[1], tokens)
    outs = [(wide, BF, "A"), (wide, F32, "A"), (across, BF, "A")] + [part] * 4 + [((16, features), F32, "V")]
    deep, narrow = pltpu.VMEM((tokens, hidden), BF), pltpu.VMEM(wide, BF)
    scratch = [pltpu.VMEM(wide, F32), narrow, narrow, pltpu.VMEM(wide, F32), pltpu.VMEM(across, BF),
               pltpu.VMEM((flat_rows, features), BF), narrow, narrow, narrow, deep, deep, narrow] + [narrow] * 4
    scratch += [pair_sems(tokens)] * 3 + [pltpu.SemaphoreType.DMA((2,)), out_semaphores(3, tokens)]
    return call(partial(feed_forward_kernel, devices), "feed_forward", [mixed, wo, res, w1, w2, out_grad, norms], "VVAVVAV",
                outs, scratch, 3)


def branch_give(dq, dk, dv, weights, mine_a, theirs_a, mine_b, theirs_b, sems_a, sems_b):
    def give(step, rows):
        mine_a[rows, :] = nt(dq[rows, :], weights[0]).astype(BF)
        other_core(mine_a, theirs_a, sems_a, step).start()
        mine_b[rows, :] = (nt(dk[rows, :], weights[1]) + nt(dv[rows, :], weights[2])).astype(BF)
        other_core(mine_b, theirs_b, sems_b, step).start()
    chunks(dq.shape[0], give)


def branch_weights(first_in, second_in, dq, dk, dv, flat):
    cols = dq.shape[1]
    order = interleave(first_in.shape[1])
    for number, (entering, grad) in enumerate(((first_in, dq), (second_in, dk), (second_in, dv))):
        flat[number * cols:(number + 1) * cols, :] = as_units(tn(entering[...], grad[...]), order)


def z_sum_start(devices, places, pieces, landed, sems):
    me, x, y, z, xpeer, ypeer, order, ahead, behind = places
    return [send(pieces.at[lax.rem(z + d, devices // 4)], landed.at[d], sems.at[0, d], sems.at[1, d], dp=ahead(d)) for d in order]


def z_sum_end(places, pieces, landed, copies):
    z, order = places[3], places[6]
    total = pieces[z].astype(F32)
    for copy, d in zip(copies, order):
        copy.wait_recv()
        total = total + landed[d].astype(F32)
    return total.astype(BF)


def four_sum(parts, at):
    return (parts[0][at].astype(F32) + parts[1][at].astype(F32) + parts[2][at].astype(F32) + parts[3][at].astype(F32)).astype(BF)


def cross_back_kernel(devices, dq, dk, dv, wc, nc_hbm, memory_hbm, res_hbm, gres_hbm, mixed, wo, norms,
                      part0, part1, part2, part3,
                      gmem_out, gnew_out, gmix_out, give0, give1, give2, give3, sums_ref,
                      nc, memory, res, gres, gmem_ref, gnew_ref, gmix_ref, flat, pieces, landed, blocks,
                      mine_a, theirs_a, mine_b, theirs_b, low_all, sems_a, sems_b, late_sems, out_sems, z_sems, zz_sems):
    tokens, features = nc.shape
    cols = dq.shape[1]
    across = devices // 4
    places = places_of(devices)
    me, x, y, z, xpeer, ypeer, order, ahead, behind = places
    late = Late([(nc_hbm, nc), (memory_hbm, memory), (res_hbm, res), (gres_hbm, gres)], late_sems)
    out = Out([(gmem_ref, gmem_out), (gnew_ref, gnew_out), (gmix_ref, gmix_out)], out_sems)
    for level in range(across):
        pieces[level] = four_sum((part0, part1, part2, part3), level)
    greet([{"head": 1 - lax.axis_index("head")}] + [{"dp": ahead(d)} for d in order])
    z_copies = z_sum_start(devices, places, pieces, landed, z_sems)
    branch_give(dq, dk, dv, wc, mine_a, theirs_a, mine_b, theirs_b, sems_a, sems_b)
    late.wait(0, 1)
    branch_weights(nc, memory, dq, dk, dv, flat)
    blocks[0] = z_sum_end(places, pieces, landed, z_copies)
    zz_copies = [send(blocks.at[0], blocks.at[d], zz_sems.at[0, d], zz_sems.at[1, d], dp=ahead(d)) for d in order]
    sums_ref[...] = jnp.zeros_like(sums_ref)
    late.wait(2, 3)

    def close(step, rows):
        other_core(mine_a, theirs_a, sems_a, step).wait_recv()
        grad = mine_a[rows, :].astype(F32) + theirs_a[rows, :].astype(F32)
        unit, scale = normalise(res[rows, :])
        gnew = norm_back(unit, scale, norms[4:5, :], grad) + gres[rows, :]
        gnew_ref[rows, :] = gnew
        out.start(1, step)
        sums_ref[0:8, :] += fold_rows(grad * unit)
        sums_ref[8:16, :] += fold_rows(grad)
        low = gnew.astype(BF)
        low_all[rows, :] = low
        gmix_ref[:, rows] = nt(low, wo[...]).astype(BF).T
        out.start(2, step)
        other_core(mine_b, theirs_b, sems_b, step).wait_recv()
        gmem_ref[rows, :] = (mine_b[rows, :].astype(F32) + theirs_b[rows, :].astype(F32)).astype(BF)
        out.start(0, step)
    chunks(tokens, close)
    flat[3 * cols:4 * cols, :] = tn(mixed[...], low_all[...]).astype(BF)
    if flat.shape[0] > 4 * cols:
        flat[4 * cols:, :] = jnp.zeros((flat.shape[0] - 4 * cols, features), BF)
    gives = (give0, give1, give2, give3)
    spread_flat(devices, places, flat, gives)
    for copy in zz_copies:
        copy.wait_recv()
    ready_rows = blocks.shape[1]
    for ref in gives:
        for d in range(across):
            ref[d, 0:ready_rows, :] = blocks[d]
    for copy in z_copies + zz_copies:
        copy.wait_send()
    out.drain(tokens)
    drain(tokens, mine_a, theirs_a, sems_a)
    drain(tokens, mine_b, theirs_b, sems_b)


def cross_back(devices, dq, dk, dv, wc, nc, memory, res, gres, mixed, wo, norms, parts):
    tokens, features = nc.shape
    cols = dq.shape[1]
    across, ready_rows = devices // 4, parts[0].shape[1]
    flat_rows = whole_blocks(4 * cols, devices)
    give = ((across, ready_rows + flat_rows // devices, features), BF, "V")
    wide = (tokens, features)
    outs = [(wide, BF, "A"), (wide, F32, "A"), ((cols, tokens), BF, "A")] + [give] * 4 + [((16, features), F32, "V")]
    low, high = pltpu.VMEM(wide, BF), pltpu.VMEM(wide, F32)
    small = pltpu.VMEM((across, ready_rows, features), BF)
    z_sems = pltpu.SemaphoreType.DMA((2, across))
    scratch = [low, low, high, high, low, high, pltpu.VMEM((cols, tokens), BF), pltpu.VMEM((flat_rows, features), BF), small, small, small]
    scratch += [low] * 5 + [pair_sems(tokens)] * 2 + [pltpu.SemaphoreType.DMA((4,)), out_semaphores(3, tokens), z_sems, z_sems]
    return call(partial(cross_back_kernel, devices), "cross_back",
                [dq, dk, dv, wc, nc, memory, res, gres, mixed, wo, norms] + parts, "VVVVAAAAVVVVVVV", outs, scratch, 4)


def self_back_kernel(devices, ready_rows, dq, dk, dv, ws, nq_hbm, nkv_hbm, query_hbm, kv_hbm, gres_hbm, norms, sums_c, sums_f,
                     part0, part1, part2, part3,
                     gquery_out, gkv_out, last_ref, more_ref, gnorm_ref,
                     nq, nkv, query, kv, gres, gquery_ref, gkv_ref, flat, source, landing, pieces, landed, more_pieces, more_landed,
                     norm_mine, norm_all, mine_a, theirs_a, mine_b, theirs_b, sums, sems_a, sems_b, late_sems, out_sems,
                     z_sems, more_z_sems, plane_sems, n_sems, *spread_sems):
    tokens, features = nq.shape
    across = devices // 4
    places = places_of(devices)
    me, x, y, z, xpeer, ypeer, order, ahead, behind = places
    late = Late([(nq_hbm, nq), (nkv_hbm, nkv), (query_hbm, query), (kv_hbm, kv), (gres_hbm, gres)], late_sems)
    out = Out([(gquery_ref, gquery_out), (gkv_ref, gkv_out)], out_sems)
    more_rows = more_ref.shape[2]
    for level in range(across):
        more_pieces[level] = four_sum((part0, part1, part2, part3), (level, pl.ds(ready_rows, more_rows)))
    others = [lax.rem(me + d, devices) for d in range(1, devices)]
    greet([{"head": 1 - lax.axis_index("head")}] + [{"dp": other} for other in others])
    more_copies = z_sum_start(devices, places, more_pieces, more_landed, more_z_sems)
    branch_give(dq, dk, dv, ws, mine_a, theirs_a, mine_b, theirs_b, sems_a, sems_b)
    late.wait(0, 1)
    branch_weights(nq, nkv, dq, dk, dv, flat)
    if flat.shape[0] > 3 * dq.shape[1]:
        flat[3 * dq.shape[1]:, :] = jnp.zeros((flat.shape[0] - 3 * dq.shape[1], features), BF)
    spread_flat(devices, places, flat, [source.at[f] for f in range(4)])
    plane_copies = [send(source.at[f], landing.at[f], plane_sems.at[0, f], plane_sems.at[1, f], dp=peer)
                    for f, peer in ((3, me + 3 - 2 * x - 4 * y), (1, xpeer), (2, ypeer))]
    more_ref[0, 0] = z_sum_end(places, more_pieces, more_landed, more_copies)
    more = Spread(places, more_ref, *spread_sems[:5])
    more.start()
    sums[...] = jnp.zeros_like(sums)
    late.wait(2, 3, 4)

    def close(step, rows):
        other_core(mine_a, theirs_a, sems_a, step).wait_recv()
        grad = mine_a[rows, :].astype(F32) + theirs_a[rows, :].astype(F32)
        unit, scale = normalise(query[rows, :].astype(F32))
        gquery_ref[rows, :] = (norm_back(unit, scale, norms[0:1, :], grad) + gres[rows, :]).astype(BF)
        out.start(0, step)
        sums[0:8, :] += fold_rows(grad * unit)
        sums[8:16, :] += fold_rows(grad)
        other_core(mine_b, theirs_b, sems_b, step).wait_recv()
        grad = mine_b[rows, :].astype(F32) + theirs_b[rows, :].astype(F32)
        unit, scale = normalise(kv[rows, :].astype(F32))
        gkv_ref[rows, :] = norm_back(unit, scale, norms[2:3, :], grad).astype(BF)
        out.start(1, step)
        sums[16:24, :] += fold_rows(grad * unit)
        sums[24:32, :] += fold_rows(grad)
    middle = tokens // 2
    chunks(middle, close)
    more.relay()
    chunks(tokens, close, middle)
    parts = [sums[8 * i:8 * i + 8, :] for i in range(4)]
    parts += [sums_c[0:8, :], sums_c[8:16, :], sums_f[0:8, :], sums_f[8:16, :]]
    norm_mine[...] = jnp.concatenate([jnp.sum(part, 0, keepdims=True) for part in parts], 0)
    for copy in plane_copies:
        copy.wait_recv()
    for level in range(across):
        pieces[level] = four_sum((source.at[0], landing.at[1], landing.at[2], landing.at[3]), level)
    z_copies = z_sum_start(devices, places, pieces, landed, z_sems)
    n_copies = [send(norm_mine, norm_all.at[d], n_sems.at[0, d], n_sems.at[1, d], dp=other)
                for d, other in zip(range(1, devices), others)]
    more.diagonal()
    last_ref[0, 0] = z_sum_end(places, pieces, landed, z_copies)
    last = Spread(places, last_ref, *spread_sems[5:])
    last.start()
    last.relay()
    last.diagonal()
    total = norm_mine[...]
    for d, copy in zip(range(1, devices), n_copies):
        copy.wait_recv()
        total = total + norm_all[d]
    gnorm_ref[...] = total
    more.finish()
    last.finish()
    more.drain()
    last.drain()
    for copy in more_copies + plane_copies + z_copies + n_copies:
        copy.wait_send()
    out.drain(tokens)
    drain(tokens, mine_a, theirs_a, sems_a)
    drain(tokens, mine_b, theirs_b, sems_b)


def self_back(devices, ready_rows, dq, dk, dv, ws, nq, nkv, query, kv, gres, norms, sums_c, sums_f, parts):
    tokens, features = nq.shape
    cols = dq.shape[1]
    across, more_rows = devices // 4, parts[0].shape[1] - ready_rows
    flat_rows = whole_blocks(3 * cols, devices)
    rows = flat_rows // devices
    wide = (tokens, features)
    outs = [(wide, BF, "A"), (wide, BF, "A"), ((4, across, rows, features), BF, "V"), ((4, across, more_rows, features), BF, "V"),
            ((8, features), F32, "V")]
    low, high = pltpu.VMEM(wide, BF), pltpu.VMEM(wide, F32)
    small, tiny = pltpu.VMEM((across, more_rows, features), BF), pltpu.VMEM((across, rows, features), BF)
    four = pltpu.VMEM((4, across, rows, features), BF)
    D = pltpu.SemaphoreType.DMA
    scratch = [low, low, low, low, high, low, low, pltpu.VMEM((flat_rows, features), BF), four, four, tiny, tiny, small, small,
               pltpu.VMEM((8, features), F32), pltpu.VMEM((devices, 8, features), F32)]
    scratch += [low] * 4 + [pltpu.VMEM((32, features), F32)] + [pair_sems(tokens)] * 2
    scratch += [D((5,)), out_semaphores(2, tokens), D((2, across)), D((2, across)), D((2, 4)), D((2, devices))]
    scratch += [D((2, across))] * 10
    return call(partial(self_back_kernel, devices, ready_rows), "self_back",
                [dq, dk, dv, ws, nq, nkv, query, kv, gres, norms, sums_c, sums_f] + parts, "VVVVAAAAAVVVVVVV", outs, scratch, 5)


def update_kernel(devices, early_unit, late_unit, late_rows, owner_ref, me_ref, last, more, part0, part1, part2, part3,
                  master, first, second, gquery_in, gkv_in, grad_ref, first_ref, second_ref, new_ref, gquery_out, gkv_out,
                  held, taken, held_q, held_kv, sems):
    units = owner_ref.shape[0]
    slots = master.shape[0]
    across = devices // 4
    me = me_ref[0]
    here, level = lax.rem(me, 4), lax.div(me, 4)
    entering = Late([(gquery_in, held_q), (gkv_in, held_kv)], sems.at[0])

    def find(u, count):
        held[count] = u
        return count + (owner_ref[u] == me).astype(jnp.int32)
    count = lax.fori_loop(0, units, find, jnp.int32(0), unroll=4)
    entering.wait(0, 1)
    leaving = Late([(held_q, gquery_out), (held_kv, gkv_out)], sems.at[1])

    def lookup(row, size):
        block = lax.div(row, size)
        behind = lax.rem(level - lax.div(block, 4) + across, across)
        return lax.rem(block, 4) ^ here, behind, pl.ds(pl.multiple_of(lax.rem(row, size), UNIT), UNIT)

    def one(slot, carry):
        @pl.when(slot < count)
        def _():
            unit = held[slot]

            @pl.when(unit < early_unit)
            def _():
                taken[...] = last[lookup(unit * UNIT, last.shape[2])]

            @pl.when((unit >= early_unit) & (unit < late_unit))
            def _():
                taken[...] = more[lookup((unit - early_unit) * UNIT, more.shape[2])]

            @pl.when(unit >= late_unit)
            def _():
                offset, behind, rows = lookup((unit - late_unit) * UNIT, late_rows)
                for f, part in enumerate((part0, part1, part2, part3)):
                    @pl.when(offset == f)
                    def _():
                        taken[...] = part[behind, rows]
            gradient = taken[...].astype(F32)
            first_new, second_new, weight = adamw_step(gradient, first[slot], second[slot], master[slot], RATE_MATRIX, WEIGHT_DECAY)
            grad_ref[slot] = gradient
            first_ref[slot] = first_new
            second_ref[slot] = second_new
            new_ref[slot] = weight

        @pl.when(slot >= count)
        def _():
            for ref in (grad_ref, first_ref, second_ref, new_ref):
                ref[slot] = jnp.zeros(ref.shape[1:], F32)
        return carry
    lax.fori_loop(0, slots, one, 0)
    leaving.wait(0, 1)


def update(devices, early_unit, late_unit, late_rows, unit_owner, me, last, more, parts, master, first, second, gquery, gkv):
    outs = [(master.shape, F32, "V")] * 4 + [(gquery.shape, BF, "A")] * 2
    kernel = partial(update_kernel, devices, early_unit, late_unit, late_rows)
    return call(kernel, "update", [unit_owner, me, last, more] + parts + [master, first, second, gquery, gkv], "SSVVVVVVVVVAA", outs,
                [pltpu.SMEM((unit_owner.shape[0] + 8,), jnp.int32), pltpu.VMEM((UNIT, master.shape[2]), BF),
                 pltpu.VMEM(gquery.shape, BF), pltpu.VMEM(gkv.shape, BF), pltpu.SemaphoreType.DMA((2, 2))])


def adamw_step(gradient, first, second, weight, rate, decay):
    first_new = BETA_ONE * first + (1.0 - BETA_ONE) * gradient
    second_new = BETA_TWO * second + (1.0 - BETA_TWO) * gradient * gradient
    corr_one = 1.0 - BETA_ONE**STEP
    corr_two = 1.0 - BETA_TWO**STEP
    direction = first_new / corr_one / (jnp.sqrt(second_new / corr_two) + ADAM_EPS)
    return (first_new, second_new, weight - rate * (direction + decay * weight))


def local(
    query_stream, kv_stream, memory, out_grad, lengths, obs_rank, obs_count, unit_owner,
    master, first_moment, second_moment, norm_master, norm_first, norm_second,
):
    devices = lax.axis_size("dp")
    shards = lax.axis_size("head")
    me = lax.axis_index("dp")
    slots, unit_rows, features = master.shape[0], master.shape[2], master.shape[3]
    units = unit_owner.shape[0]
    norm_share = norm_master.shape[0]
    cols = features // shards
    hidden = (units * unit_rows - 8 * cols) // 2

    shape = (slots, unit_rows, features)
    norm_row = lax.dynamic_update_slice(
        jnp.zeros((1, features), F32), norm_master.reshape(1, norm_share), (0, lax.rem(me * norm_share, features)))
    rank_row, count_row = obs_rank.reshape(1, ROW), obs_count.reshape(1, ROW)
    place_of, steps = plan(unit_owner, lengths, devices, slots + 1)
    nq, nkv, qt, k, kt, v, vt, kc, kct, vc, vct, ws, wc, wo_self, wo_cross, w1, w2, norms, *tables = project(
        devices, place_of, lengths, master.reshape(shape), norm_row, rank_row,
        query_stream, kv_stream, memory, cols, hidden)
    mixed_self, mixed_self_t, total_self = attend_forward(steps, qt, k, vt, tables, count_row, True)
    residual, nc, qct = self_out(mixed_self, wo_self, query_stream, wc, norms)
    mixed_cross, mixed_cross_t, total_cross = attend_forward(steps, qct, kc, vct, tables, count_row, False)
    output, grad_cross_res, grad_mixed, *parts, sums_f = feed_forward(
        devices, mixed_cross, wo_cross, residual, w1, w2, out_grad, norms)
    tie = lax.optimization_barrier
    ready_rows = parts[0].shape[1]
    parts = [parts[0]] + [plane_swap(parts[f], devices, f) for f in (1, 2, 3)]
    dq, dk, dv, output = attend_backward(
        steps, qct, kc, kct, vc, grad_mixed, mixed_cross_t, total_cross, tables, count_row, output, False)
    parts, dq = tie((parts, dq))
    grad_memory, grad_residual, grad_mixed, *parts, sums_c = cross_back(
        devices, dq, dk, dv, wc, nc, memory, residual, grad_cross_res, mixed_self, wo_self, norms, parts)
    parts = [parts[0]] + [plane_swap(parts[f], devices, f) for f in (1, 2, 3)]
    dq, dk, dv, grad_memory = attend_backward(
        steps, qt, k, kt, v, grad_mixed, mixed_self_t, total_self, tables, count_row, grad_memory, True)
    parts, dq = tie((parts, dq))
    grad_query, grad_kv, last, more, norm_grads = self_back(
        devices, ready_rows, dq, dk, dv, ws, nq, nkv, query_stream, kv_stream, grad_residual, norms, sums_c, sums_f, parts)

    early, late = 3 * cols // unit_rows, 7 * cols // unit_rows
    weight_grad, weight_first, weight_second, weight_new, grad_query, grad_kv = update(
        devices, early, late, ready_rows, unit_owner, me.reshape(1), last, more, parts, master.reshape(shape),
        first_moment.reshape(shape), second_moment.reshape(shape), grad_query, grad_kv)
    weight_grad, weight_first, weight_second, weight_new = [
        part.reshape(master.shape) for part in (weight_grad, weight_first, weight_second, weight_new)]
    norm_grad = lax.dynamic_slice_in_dim(norm_grads.reshape(-1), me * norm_share, norm_share)
    norm_first_new, norm_second_new, norm_new = adamw_step(
        norm_grad, norm_first, norm_second, norm_master, RATE_NORM, 0.0)
    return (
        output, grad_query, grad_kv, grad_memory, weight_grad, weight_first, weight_second, weight_new,
        norm_grad, norm_first_new, norm_second_new, norm_new,
    )


def solution(mesh):
    in_specs = (
        P("dp", None),
        P("dp", None),
        P("dp", None),
        P("dp", None),
        P("dp", None),
        P("dp"),
        P("dp"),
        P(),
        P("dp", "head", None, None),
        P("dp", "head", None, None),
        P("dp", "head", None, None),
        P("dp"),
        P("dp"),
        P("dp"),
    )
    out_specs = (
        P("dp", None),
        P("dp", None),
        P("dp", None),
        P("dp", None),
        P("dp", "head", None, None),
        P("dp", "head", None, None),
        P("dp", "head", None, None),
        P("dp", "head", None, None),
        P("dp"),
        P("dp"),
        P("dp"),
        P("dp"),
    )
    return jax.shard_map(local, mesh=mesh, in_specs=in_specs, out_specs=out_specs, check_vma=False)
```

```python
from functools import partial

import jax
import jax.numpy as jnp
from jax import lax
from jax.experimental import pallas as pl
from jax.experimental.pallas import tpu as pltpu
from jax.sharding import PartitionSpec as P

HEAD_DIM = 64
ROW = 2048
DOCS = 32
STEP = 10
UNIT = 16

EPS_NORM = 1e-05
ADAM_EPS = 1e-08
BETA_ONE = 0.5
BETA_TWO = 0.5
RATE_MATRIX = 0.1
RATE_NORM = 0.3
WEIGHT_DECAY = 0.01

F32 = jnp.float32
BF = jnp.bfloat16
TQ = 256
TK = 384
FAR = 32768.0
LANES = (64, 72, 80)


def nt(a, b):
    return lax.dot_general(a, b, (((1,), (1,)), ((), ())), preferred_element_type=F32)


def nn(a, b):
    return lax.dot_general(a, b, (((1,), (0,)), ((), ())), preferred_element_type=F32)


def doc_bounds(len_ref):
    starts, ends = [], []
    at = jnp.int32(0)
    for d in range(DOCS):
        starts.append(at)
        at = at + len_ref[0, d]
        ends.append(at)
    return starts, ends


def key_range(starts, ends, q0):
    low = jnp.int32(0)
    high = jnp.int32(0)
    for d in range(DOCS):
        low = jnp.where(starts[d] <= q0, starts[d], low)
        high = jnp.where(starts[d] <= q0 + TQ - 1, ends[d], high)
    first = lax.div(low, 128) * 128
    steps = lax.div(high - first + TK - 1, TK)
    return first, steps


def mask_tables(len_ref, rank_ref, side_ref, hot_ref, rank_cols):
    starts, ends = doc_bounds(len_ref)
    lanes = lax.broadcasted_iota(jnp.int32, (1, 128), 1)
    start_lane = jnp.full((1, 128), -1, jnp.int32)
    end_lane = jnp.full((1, 128), -1, jnp.int32)
    for d in range(DOCS):
        start_lane = jnp.where(lanes == d, starts[d], start_lane)
        end_lane = jnp.where(lanes == d, ends[d], end_lane)
    one = (lanes == LANES[0]) | (lanes == LANES[1]) | (lanes == LANES[2])
    for t in range(ROW // 256):
        pos = lax.broadcasted_iota(jnp.int32, (256, 128), 0) + t * 256
        hot = (pos >= start_lane) & (pos < end_lane)
        side = jnp.where(hot | (lanes >= DOCS), jnp.where(one, -1.0, 0.0), -FAR)
        side_ref[t * 256:(t + 1) * 256, :] = side.astype(BF)
    pos = lax.broadcasted_iota(jnp.int32, (1, ROW), 1)
    first = jnp.zeros((1, ROW), jnp.bool_)
    rows = []
    for d in range(DOCS):
        first = first | (pos == starts[d])
        rows.append(jnp.where((pos >= starts[d]) & (pos < ends[d]), FAR, 0.0))
    hot_ref[...] = jnp.concatenate(rows + [jnp.zeros((128 - DOCS, ROW), F32)], 0).astype(BF)
    rank = jnp.where(first, -1.0, rank_ref[...].astype(F32))
    for t in range(ROW // 128):
        rank_cols[t * 128:(t + 1) * 128, :] = jnp.broadcast_to(rank[:, t * 128:(t + 1) * 128], (128, 128)).T


STEPS = (ROW // TQ) * -(-ROW // TK) + 8


def step_table(len_ref, table):
    starts, ends = doc_bounds(len_ref)
    idle = ROW // TQ

    def put(at, tile, first):
        table[0, at] = tile
        table[1, at] = first
    put(0, idle, ROW)
    put(1, idle, ROW)
    at = jnp.int32(2)
    for tile in range(idle):
        first, steps = key_range(starts, ends, tile * TQ)

        def fill(s, at):
            put(at, tile, first + s * TK)
            return at + 1
        at = lax.fori_loop(0, steps, fill, at)
    put(at, idle, ROW)
    put(at + 1, idle, ROW)
    table[0, STEPS - 1] = at


def step_of(table, i):
    return table[0, i], pl.multiple_of(table[1, i], 128)


def real_step(table, i):
    return jnp.minimum(table[0, i], ROW // TQ - 1), pl.multiple_of(table[1, i], 128)


def padded(ref):
    return ref.at[pl.ds(0, ROW)] if ref.shape[0] > ref.shape[1] else ref.at[:, pl.ds(0, ROW)]


def fill_padding(refs, side_ref):
    for ref in refs:
        if ref.shape[0] > ref.shape[1]:
            ref[ROW:, :] = jnp.zeros((TK, ref.shape[1]), ref.dtype)
        else:
            ref[:, ROW:] = jnp.zeros((ref.shape[0], TK), ref.dtype)
    lanes = lax.broadcasted_iota(jnp.int32, (TK, 128), 1)
    side_ref[ROW:, :] = jnp.where(lanes < DOCS, -FAR, 0.0).astype(BF)


def seen_bias(rank_cols, counts, tile, k0):
    rank = rank_cols[pl.ds(k0, TK), :]
    rank = jnp.concatenate([rank] * (TQ // 128), 1)
    kpos = lax.broadcasted_iota(jnp.int32, (TK, TQ), 0)
    qpos = lax.broadcasted_iota(jnp.int32, (TK, TQ), 1)
    off_diag = (kpos - qpos) != (tile * TQ - k0)
    allowed = (rank < counts[tile, 0:1, :]) & (off_diag | (rank < 0.0))
    return jnp.where(allowed, 0.0, -FAR * FAR)


def count_tiles(counts, count_ref):
    for tile in range(ROW // TQ):
        counts[tile] = jnp.broadcast_to(count_ref[:, tile * TQ:(tile + 1) * TQ].astype(F32), (8, TQ))


def query_columns(qt, qt_ref, side, tile, h, q0):
    rows = qt_ref[h * HEAD_DIM:(h + 1) * HEAD_DIM, pl.ds(q0, TQ)].astype(F32) * HEAD_DIM ** -0.5
    own, other = h % 2 * HEAD_DIM, (1 - h % 2) * HEAD_DIM
    qt[tile, h, own:own + HEAD_DIM, :] = rows.astype(BF)
    qt[tile, h, other:other + HEAD_DIM, :] = jnp.zeros((HEAD_DIM, TQ), BF)
    qt[tile, h, 128:256, :] = side


def pair_rows(ref, side_ref, h, k0):
    return jnp.concatenate([ref[pl.ds(k0, TK), h // 2 * 128:(h // 2 + 1) * 128], side_ref[pl.ds(k0, TK), :]], 1)


def attn_fwd_kernel(with_seen, heads, table, count_ref, qt_hbm, hot_hbm, k_hbm, vt_hbm, side_hbm, rank_hbm,
                    o_out, ot_out, lse_ref, qt, acc, top, sc, probs, fade, counts,
                    qt_ref, hot_ref, k_ref, vt_ref, side_ref, rank_cols, o_ref, ot_ref, late_sems, out_sems):
    pairs = [(qt_hbm, qt_ref), (hot_hbm, hot_ref), (k_hbm, padded(k_ref)), (vt_hbm, padded(vt_ref)),
             (side_hbm, padded(side_ref))]
    late = Late(pairs + ([(rank_hbm, padded(rank_cols))] if with_seen else []), late_sems)
    fill_padding((k_ref, vt_ref, rank_cols), side_ref)
    out = Out([(o_ref, o_out), (ot_ref, ot_out)], out_sems)
    tiles = ROW // TQ
    lse_ref[...] = jnp.zeros_like(lse_ref)
    acc[...] = jnp.zeros_like(acc)
    top[...] = jnp.full_like(top, -jnp.inf)
    if with_seen:
        count_tiles(counts, count_ref)
    late.wait(0, 1)

    def prepare(tile, c):
        q0 = pl.multiple_of(tile * TQ, TQ)
        for h in range(heads):
            query_columns(qt, qt_ref, hot_ref[:, pl.ds(q0, TQ)], tile, h, q0)
        return c
    lax.fori_loop(0, tiles, prepare, 0)
    late.wait(*range(2, 6 if with_seen else 5))
    ones = jnp.ones((16, TK), BF)

    def one_step(s, c):
        out_tile, _ = step_of(table, s)
        _, out_k = real_step(table, s)
        mid_tile, _ = step_of(table, s + 1)
        in_tile, in_k = real_step(table, s + 2)
        sums = []
        for h in range(heads):
            values = jnp.concatenate([vt_ref[h * HEAD_DIM:(h + 1) * HEAD_DIM, pl.ds(out_k, TK)], ones], 0)
            sums.append(acc[out_tile, h] * fade[h:h + 1, :] + nn(values, probs[h]))
        old = top[mid_tile]
        news = []
        for h in range(heads):
            score = sc[h]
            new = jnp.maximum(old[h:h + 1, :], jnp.max(score, 0, keepdims=True))
            probs[h] = jnp.exp(score - new).astype(BF)
            news.append(new)
        new = jnp.concatenate(news + [old[heads:, :]], 0)
        fade[...] = jnp.exp(old - new)
        bias = seen_bias(rank_cols, counts, in_tile, in_k) if with_seen else None
        for h in range(heads):
            score = nn(pair_rows(k_ref, side_ref, h, in_k), qt[in_tile, h])
            sc[h] = score + bias if with_seen else score
        top[mid_tile] = new
        for h in range(heads):
            acc[out_tile, h] = sums[h]
        return c
    lax.fori_loop(0, table[0, STEPS - 1], one_step, 0)

    def finish(tile, c):
        q0 = pl.multiple_of(tile * TQ, TQ)
        outs = []
        peak = top[tile]
        for h in range(heads):
            a = acc[tile, h]
            total = a[HEAD_DIM:HEAD_DIM + 1, :]
            outs.append(a[:HEAD_DIM, :] * (1.0 / total))
            lse_ref[h:h + 1, pl.ds(q0, TQ)] = peak[h:h + 1, :] + jnp.log(total)
        mixed = jnp.concatenate(outs, 0).astype(BF)
        ot_ref[:, pl.ds(q0, TQ)] = mixed
        out.start(1, tile)
        o_ref[pl.ds(q0, TQ), :] = mixed.T
        out.start(0, tile)
        return c
    lax.fori_loop(0, tiles, finish, 0)
    out.drain(ROW)


def attend_forward(steps, qt, k, vt, tables, count, with_seen):
    cols, rows = qt.shape
    heads = cols // HEAD_DIM
    side, hot, rank_cols = tables
    args = [steps, count, qt, hot, k, vt, side, rank_cols]
    across, down = (cols, rows), (rows, cols)
    held = [pltpu.VMEM(arg.shape, BF) for arg in (qt, hot)] + [
        pltpu.VMEM((rows + TK, cols), BF), pltpu.VMEM((cols, rows + TK), BF), pltpu.VMEM((rows + TK, 128), BF),
        pltpu.VMEM((rows + TK, 128), F32)]
    return call(partial(attn_fwd_kernel, with_seen, heads), "attend_self_forward" if with_seen else "attend_cross_forward",
                args, "SV" + "A" * 6, [(down, BF, "A"), (across, BF, "A"), ((8, rows), F32, "V")],
                [pltpu.VMEM((ROW // TQ, heads, 256, TQ), BF), pltpu.VMEM((ROW // TQ + 1, heads, HEAD_DIM + 16, TQ), F32),
                 pltpu.VMEM((ROW // TQ + 1, 8, TQ), F32), pltpu.VMEM((heads, TK, TQ), F32), pltpu.VMEM((heads, TK, TQ), BF),
                 pltpu.VMEM((8, TQ), F32), pltpu.VMEM((ROW // TQ, 8, TQ), F32)] + held
                + [pltpu.VMEM(down, BF), pltpu.VMEM(across, BF), pltpu.SemaphoreType.DMA((6,)), out_semaphores(2, rows)])


def three_rows(value):
    high = value.astype(BF).astype(F32)
    middle = (value - high).astype(BF).astype(F32)
    row = lax.broadcasted_iota(jnp.int32, (128, value.shape[1]), 0)
    return jnp.where(row == LANES[0], high, jnp.where(row == LANES[1], middle, jnp.where(row == LANES[2], value - high - middle, 0.0)))


def attn_bwd_kernel(with_seen, heads, table, count_ref, lse_ref, qt_hbm, hot_hbm, gt_hbm, ot_hbm, k_hbm, kt_hbm, v_hbm, side_hbm,
                    rank_hbm, pass_in,
                    dq_out, dk_out, dv_out, pass_out, dk_sum, dv_sum, dq_sum, qt, gt, q_own, g_own, sc, dps, all_ds, all_p, counts,
                    qt_ref, hot_ref, gt_ref, ot_ref, k_ref, kt_ref, v_ref, side_ref, rank_cols, held, dq_ref, dk_ref, dv_ref,
                    late_sems, out_sems, pass_sem):
    pairs = [(qt_hbm, qt_ref), (hot_hbm, hot_ref), (gt_hbm, gt_ref), (ot_hbm, ot_ref), (k_hbm, padded(k_ref)),
             (kt_hbm, padded(kt_ref)), (v_hbm, padded(v_ref)), (side_hbm, padded(side_ref))]
    late = Late(pairs + ([(rank_hbm, padded(rank_cols))] if with_seen else []), late_sems)
    fill_padding((k_ref, kt_ref, v_ref, rank_cols), side_ref)
    entering = pltpu.make_async_copy(pass_in, held, pass_sem.at[0])
    entering.start()
    out = Out([(dq_ref, dq_out), (dk_ref, dk_out), (dv_ref, dv_out)], out_sems)
    tiles = ROW // TQ
    dk_sum[...] = jnp.zeros_like(dk_sum)
    dv_sum[...] = jnp.zeros_like(dv_sum)
    dq_sum[...] = jnp.zeros_like(dq_sum)
    if with_seen:
        count_tiles(counts, count_ref)
    late.wait(0, 1, 2, 3)

    def prepare(tile, c):
        q0 = pl.multiple_of(tile * TQ, TQ)
        hot = hot_ref[:, pl.ds(q0, TQ)].astype(F32)
        for h in range(heads):
            rows = slice(h * HEAD_DIM, (h + 1) * HEAD_DIM)
            side = hot + three_rows(lse_ref[h:h + 1, pl.ds(q0, TQ)])
            query_columns(qt, qt_ref, side.astype(BF), tile, h, q0)
            grads = gt_ref[rows, pl.ds(q0, TQ)]
            delta = jnp.sum(grads.astype(F32) * ot_ref[rows, pl.ds(q0, TQ)].astype(F32), 0, keepdims=True)
            other = (1 - h % 2) * HEAD_DIM
            gt[tile, h, h % 2 * HEAD_DIM:(h % 2 + 1) * HEAD_DIM, :] = grads
            gt[tile, h, other:other + HEAD_DIM, :] = jnp.zeros((HEAD_DIM, TQ), BF)
            gt[tile, h, 128:256, :] = three_rows(delta).astype(BF)
        lane = lax.broadcasted_iota(jnp.int32, (TQ, heads * HEAD_DIM), 1)
        for held_rows, source in ((q_own, qt_ref), (g_own, gt_ref)):
            rows = source[:, pl.ds(q0, TQ)].T
            for h in range(heads):
                own = (lane >= h * HEAD_DIM) & (lane < (h + 1) * HEAD_DIM)
                held_rows[tile, h * TQ:(h + 1) * TQ, :] = jnp.where(own, rows, jnp.zeros_like(rows))
        return c
    lax.fori_loop(0, tiles, prepare, 0)
    late.wait(*range(4, 9 if with_seen else 8))
    entering.wait()
    leaving = pltpu.make_async_copy(held, pass_out, pass_sem.at[1])
    leaving.start()

    def one_step(s, c):
        out_tile, out_k = step_of(table, s)
        read_tile, read_k = real_step(table, s)
        in_tile, in_k = real_step(table, s + 2)
        keys = pl.ds(out_k, TK)
        own = [slice(h * HEAD_DIM, (h + 1) * HEAD_DIM) for h in range(heads)]
        dk = dk_sum[keys, :] + nn(all_ds[...], q_own[read_tile])
        dv = dv_sum[keys, :] + nn(all_p[...], g_own[read_tile])
        dq = [dq_sum[out_tile, h] + nn(kt_ref[own[h], pl.ds(read_k, TK)], all_ds[:, h * TQ:(h + 1) * TQ]) for h in range(heads)]
        for h in range(heads):
            p = jnp.exp(sc[h])
            all_ds[:, h * TQ:(h + 1) * TQ] = (p * dps[h]).astype(BF)
            all_p[:, h * TQ:(h + 1) * TQ] = p.astype(BF)
        bias = seen_bias(rank_cols, counts, in_tile, in_k) if with_seen else None
        for h in range(heads):
            score = nn(pair_rows(k_ref, side_ref, h, in_k), qt[in_tile, h])
            sc[h] = score + bias if with_seen else score
            dps[h] = nn(pair_rows(v_ref, side_ref, h, in_k), gt[in_tile, h])
        dk_sum[keys, :] = dk
        dv_sum[keys, :] = dv
        for h in range(heads):
            dq_sum[out_tile, h] = dq[h]
        return c
    lax.fori_loop(0, table[0, STEPS - 1], one_step, 0)

    def finish(tile, c):
        q0 = pl.multiple_of(tile * TQ, TQ)
        rows = pl.ds(q0, TQ)
        dq = jnp.concatenate([dq_sum[tile, h] for h in range(heads)], 0) * HEAD_DIM ** -0.5
        dk = dk_sum[rows, :] * HEAD_DIM ** -0.5
        for i, (ref, value) in enumerate(((dq_ref, dq.astype(BF).T), (dk_ref, dk.astype(BF)), (dv_ref, dv_sum[rows, :].astype(BF)))):
            ref[rows, :] = value
            out.start(i, tile)
        return c
    lax.fori_loop(0, tiles, finish, 0)
    out.drain(ROW)
    leaving.wait()


def attend_backward(steps, qt, k, kt, v, gt, ot, lse, tables, count, passed, with_seen):
    rows, cols = v.shape
    heads = cols // HEAD_DIM
    side, hot, rank_cols = tables
    args = [steps, count, lse, qt, hot, gt, ot, k, kt, v, side, rank_cols, passed]
    tiles = ROW // TQ
    like = ((rows, cols), BF, "A")
    summed, own = pltpu.VMEM((rows + TK, cols), F32), pltpu.VMEM((tiles, heads * TQ, cols), BF)
    columns, square = pltpu.VMEM((tiles, heads, 256, TQ), BF), pltpu.VMEM((heads, TK, TQ), F32)
    small = pltpu.VMEM((TK, heads * TQ), BF)
    keys, keys_t = pltpu.VMEM((rows + TK, cols), BF), pltpu.VMEM((cols, rows + TK), BF)
    held = [pltpu.VMEM(arg.shape, BF) for arg in (qt, hot, gt, ot)] + [
        keys, keys_t, keys, pltpu.VMEM((rows + TK, 128), BF), pltpu.VMEM((rows + TK, 128), F32),
        pltpu.VMEM(passed.shape, passed.dtype)]
    return call(partial(attn_bwd_kernel, with_seen, heads), "attend_self_backward" if with_seen else "attend_cross_backward",
                args, "SVV" + "A" * 10, [like, like, like, (passed.shape, passed.dtype, "A")],
                [summed, summed, pltpu.VMEM((tiles + 1, heads, HEAD_DIM, TQ), F32), columns, columns, own, own, square, square,
                 small, small, pltpu.VMEM((ROW // TQ, 8, TQ), F32)] + held + [pltpu.VMEM((rows, cols), BF)] * 3
                + [pltpu.SemaphoreType.DMA((9,)), out_semaphores(3, rows), pltpu.SemaphoreType.DMA((2,))])


def send(src, dst, send_sem, recv_sem, **where):
    copy = pltpu.make_async_remote_copy(src_ref=src, dst_ref=dst, send_sem=send_sem, recv_sem=recv_sem,
                                        device_id=where, device_id_type=pl.DeviceIdType.MESH)
    copy.start()
    return copy

def greet(peers):
    barrier = pltpu.get_barrier_semaphore()
    for where in peers:
        pl.semaphore_signal(barrier, inc=1, device_id=where, device_id_type=pl.DeviceIdType.MESH)
    pl.semaphore_wait(barrier, len(peers))

def places_of(count):
    me = lax.axis_index("dp")
    across = count // 4
    x, y, z = lax.rem(me, 2), lax.rem(lax.div(me, 2), 2), lax.div(me, 4)
    xpeer, ypeer = me + 1 - 2 * x, me + 2 - 4 * y
    order = sorted(range(1, across), key=lambda d: min(d, across - d))
    ahead = lambda d: lax.rem(z + d, across) * 4 + y * 2 + x
    behind = lambda d: lax.rem(z + across - d, across) * 4 + y * 2 + x
    return me, x, y, z, xpeer, ypeer, order, ahead, behind

class LineGather:
    def __init__(self, count, piece, units, cut, places, zs, ds, xs, ys, gx, gy):
        self.across, self.piece, self.units, self.cut = count // 4, piece, units, cut
        self.places = places
        self.sems = dict(z=zs, d=ds, x=xs, y=ys, gx=gx, gy=gy)

    def copy(self, name, side, k, arriving=False):
        me, x, y, z, xpeer, ypeer = self.places[:6]
        place = x + 2 * y
        place = dict(z=place, x=place, y=place, d=3 - place, gy=place + 1 - 2 * x, gx=place + 2 - 4 * y)[name]
        if arriving:
            place = {"x": x + 2 * y + 1 - 2 * x, "y": x + 2 * y + 2 - 4 * y, "gx": 3 - x - 2 * y, "gy": 3 - x - 2 * y}.get(name, place)
        level = z + k * (2 * side - 1)
        whole = isinstance(k, int) and k == 0
        half = self.units // 2 if whole else (self.units - self.cut) // 2
        first = 0 if whole else self.cut
        start, size = dict(d=(0, self.cut), gy=(first, half), gx=(first + half, self.units - first - half)).get(name, (0, self.units))
        to = dict(x=xpeer, gx=xpeer, y=ypeer, gy=ypeer).get(name, me + 4 * (1 - 2 * side))
        hop = 1 if name in ("z", "d") and not arriving else 0
        if arriving:
            to = xpeer
        part, sems = self.piece(level * 4 + place, start, size), self.sems[name]
        return pltpu.make_async_remote_copy(
            src_ref=part, dst_ref=part, send_sem=sems.at[0, side, k], recv_sem=sems.at[1, side, k + hop],
            device_id={"dp": to}, device_id_type=pl.DeviceIdType.MESH)

    def here(self, side, k):
        z = self.places[3]
        return z >= k if side == 0 else z + k < self.across

    def onward(self, side):
        z = self.places[3]
        return z + 1 < self.across if side == 0 else z > 0

    def along(self, name, side, k, act):
        pl.when(self.here(side, k) & self.onward(side))(lambda: act(self.copy(name, side, k)))

    def run(self, meanwhile):
        start, wait_send = (lambda copy: copy.start()), (lambda copy: copy.wait_send())

        def diagonal(side, k):
            self.copy("x", side, k, True).wait_recv()
            self.copy("gy", side, k).start()
            self.copy("y", side, k, True).wait_recv()
            self.copy("gx", side, k).start()

        def later(side, k):
            diagonal(side, k)
            self.copy("d", side, k, True).wait_recv()
            pl.when(self.onward(side))(lambda: self.copy("d", side, k).start())
        for side in (0, 1):
            self.along("z", side, 0, start)
        self.copy("x", 0, 0).start()
        self.copy("y", 0, 0).start()
        meanwhile()
        diagonal(0, 0)

        def level(k, carry):
            for side in (0, 1):
                @pl.when(self.here(side, k))
                def _():
                    self.copy("z", side, k, True).wait_recv()
                    pl.when(self.onward(side))(lambda: self.copy("z", side, k).start())
                    self.copy("x", side, k).start()
                    self.copy("y", side, k).start()

            @pl.when(k == 1)
            def _():
                self.copy("gy", 0, 0, True).wait_recv()
                self.copy("gx", 0, 0, True).wait_recv()
                for side in (0, 1):
                    self.along("d", side, 0, start)

            @pl.when(k > 1)
            def _():
                for side in (0, 1):
                    pl.when(self.here(side, k - 1))(lambda: later(side, k - 1))
            return carry
        lax.fori_loop(1, self.across, level, 0)
        for side in (0, 1):
            pl.when(self.here(side, self.across - 1))(lambda: later(side, self.across - 1))

        def settle(k, carry):
            for side in (0, 1):
                @pl.when(self.here(side, k))
                def _():
                    for name in ("gy", "gx"):
                        self.copy(name, side, k, True).wait_recv()
                    for name in ("x", "y", "gy", "gx"):
                        self.copy(name, side, k).wait_send()
                for name in ("z", "d"):
                    self.along(name, side, k, wait_send)
            return carry
        lax.fori_loop(1, self.across, settle, 0)
        for name in ("x", "y", "gy", "gx"):
            self.copy(name, 0, 0).wait_send()
        for side in (0, 1):
            for name in ("z", "d"):
                self.along(name, side, 0, wait_send)


class Spread:
    def __init__(self, places, out, zs, xs, ys, gx, gy):
        self.places, self.out, self.sems = places, out, dict(z=zs, x=xs, y=ys, gx=gx, gy=gy)
        self.rows = out.shape[2]
        self.half = self.rows // 2 // UNIT * UNIT
        self.copies = {}

    def go(self, name, d, f_from, d_from, f_to, d_to, to, start, size):
        part, sems = pl.ds(start, size), self.sems[name]
        self.copies[name, d] = send(self.out.at[f_from, d_from, part], self.out.at[f_to, d_to, part],
                                    sems.at[0, d], sems.at[1, d], dp=to)

    def over_plane(self, d):
        xpeer, ypeer = self.places[4], self.places[5]
        self.go("x", d, 0, d, 1, d, xpeer, 0, self.rows)
        self.go("y", d, 0, d, 2, d, ypeer, 0, self.rows)

    def start(self):
        order, ahead = self.places[6], self.places[7]
        for d in order:
            self.go("z", d, 0, 0, 0, d, ahead(d), 0, self.rows)
        self.over_plane(0)

    def relay(self):
        for d in self.places[6]:
            self.copies["z", d].wait_recv()
            self.over_plane(d)

    def diagonal(self):
        xpeer, ypeer, order = self.places[4:7]
        for d in [0] + order:
            self.copies["x", d].wait_recv()
            if self.half:
                self.go("gy", d, 1, d, 3, d, ypeer, 0, self.half)
            self.copies["y", d].wait_recv()
            self.go("gx", d, 2, d, 3, d, xpeer, self.half, self.rows - self.half)

    def finish(self):
        for (name, d), copy in self.copies.items():
            if name in ("gx", "gy"):
                copy.wait_recv()

    def drain(self):
        for copy in self.copies.values():
            copy.wait_send()


def plane_swap(value, count, f):
    return lax.ppermute(value, "dp", [(i, i // 4 * 4 + (i % 4 ^ f)) for i in range(count)])


def plane_offset(places, f):
    x, y = places[1], places[2]
    return lax.rem(x + f % 2, 2) + 2 * lax.rem(y + f // 2, 2)


def call(kernel, name, args, kinds, outs, scratch, number=None):
    space = {"V": pltpu.VMEM, "S": pltpu.SMEM, "A": pl.ANY}
    extra = {} if number is None else dict(collective_id=number, has_side_effects=True)
    return pl.pallas_call(
        kernel,
        out_shape=tuple(jax.ShapeDtypeStruct(shape, dtype) for shape, dtype, _ in outs),
        in_specs=[pl.BlockSpec(memory_space=space[kind]) for kind in kinds],
        out_specs=tuple(pl.BlockSpec(memory_space=space[kind]) for _, _, kind in outs),
        scratch_shapes=scratch,
        compiler_params=pltpu.CompilerParams(vmem_limit_bytes=60 * 2**20, **extra),
        cost_estimate=pl.CostEstimate(flops=4 * 10**10, bytes_accessed=16 * 2**20, transcendentals=0),
        name=name,
    )(*args)


CHUNK = 256


def tn(a, b):
    return lax.dot_general(a, b, (((0,), (0,)), ((), ())), preferred_element_type=F32)


def normalise(value):
    centred = value - jnp.mean(value, -1, keepdims=True)
    scale = lax.rsqrt(jnp.mean(centred * centred, -1, keepdims=True) + EPS_NORM)
    return centred * scale, scale


def norm_back(unit, scale, gain, grad):
    inner = grad * gain
    return scale * (inner - jnp.mean(inner, -1, keepdims=True) - unit * jnp.mean(inner * unit, -1, keepdims=True))


def fold_rows(value):
    return jnp.sum(value.reshape(value.shape[0] // 8, 8, value.shape[1]), 0)


def interleave(size):
    row = lax.broadcasted_iota(jnp.int32, (size, size), 0)
    col = lax.broadcasted_iota(jnp.int32, (size, size), 1)
    source = jnp.where((row & 1) == 0, row >> 1, (row >> 1) + size // 2)
    return jnp.where(col == source, 1.0, 0.0).astype(BF)


def part_rows(matrix, order):
    return lax.dot_general(order, matrix, (((0,), (0,)), ((), ())), preferred_element_type=F32).astype(BF)


def as_units(gradient, order):
    parted = part_rows(gradient.astype(BF), order)
    half = parted.shape[0] // 2
    return jnp.concatenate([parted[:half], parted[half:]], 1)


def other_core(mine, theirs, sems, step):
    rows = pl.ds(step * CHUNK, CHUNK)
    return pltpu.make_async_remote_copy(
        src_ref=mine.at[rows], dst_ref=theirs.at[rows], send_sem=sems.at[0, step], recv_sem=sems.at[1, step],
        device_id={"head": 1 - lax.axis_index("head")}, device_id_type=pl.DeviceIdType.MESH)


def greet_core():
    greet([{"head": 1 - lax.axis_index("head")}])


def chunks(total, body, begin=0):
    def one(step, carry):
        body(step, pl.ds(pl.multiple_of(step * CHUNK, CHUNK), CHUNK))
        return carry
    lax.fori_loop(begin // CHUNK, total // CHUNK, one, 0)


def drain(total, mine, theirs, sems):
    def body(step, rows):
        other_core(mine, theirs, sems, step).wait_send()
    chunks(total, body)


class Late:
    def __init__(self, pairs, sems):
        self.copies = [pltpu.make_async_copy(source, held, sems.at[i]) for i, (source, held) in enumerate(pairs)]
        for copy in self.copies:
            copy.start()

    def wait(self, *which):
        for i in which:
            self.copies[i].wait()


class Out:
    def __init__(self, pairs, sems):
        self.pairs, self.sems = pairs, sems

    def copy(self, i, step):
        held, out = self.pairs[i]
        part = pl.ds(pl.multiple_of(step * CHUNK, CHUNK), CHUNK)
        if held.shape[0] < held.shape[1]:
            held, out = held.at[:, part], out.at[:, part]
        else:
            held, out = held.at[part], out.at[part]
        return pltpu.make_async_copy(held, out, self.sems.at[i, step])

    def start(self, i, step):
        self.copy(i, step).start()

    def drain(self, tokens):
        def body(step, rows):
            for i in range(len(self.pairs)):
                self.copy(i, step).wait()
        chunks(tokens, body)


def plan_kernel(block, owner_ref, len_ref, place_ref, table, used):
    for d in range(used.shape[0]):
        used[d] = 0

    def one_unit(u, carry):
        owner = owner_ref[u]
        slot = used[owner]
        place_ref[u] = owner * block + slot
        used[owner] = slot + 1
        return carry
    lax.fori_loop(0, owner_ref.shape[0], one_unit, 0, unroll=4)
    step_table(len_ref, table)


def plan(unit_owner, lengths, devices, block):
    return call(partial(plan_kernel, block), "plan", [unit_owner, lengths], "SS",
                [(unit_owner.shape, jnp.int32, "S"), ((2, STEPS), jnp.int32, "S")], [pltpu.SMEM((devices,), jnp.int32)])


def project_kernel(devices, place_ref, len_ref, master, norm_row, rank_ref, query_hbm, kv_hbm, memory_hbm,
                   nq_out, nkv_out, qt_out, k_out, kt_out, v_out, vt_out, kc_out, kct_out, vc_out, vct_out,
                   ws_ref, wc_ref, wos_ref, woc_ref, w1_ref, w2_ref, norms, side_ref, hot_ref, rank_cols,
                   gathered, flat, query_ref, kv_ref, memory_ref, unit_q, unit_kv,
                   nq_ref, nkv_ref, qt_ref, k_ref, kt_ref, v_ref, vt_ref, kc_ref, kct_ref, vc_ref, vct_ref,
                   late_sems, out_sems, *line_sems):
    tokens, features = query_ref.shape
    units = place_ref.shape[0]
    late = Late([(query_hbm, query_ref), (kv_hbm, kv_ref), (memory_hbm, memory_ref)], late_sems)
    held = (nq_ref, nkv_ref, qt_ref, k_ref, kt_ref, v_ref, vt_ref, kc_ref, kct_ref, vc_ref, vct_ref)
    out = Out(list(zip(held, (nq_out, nkv_out, qt_out, k_out, kt_out, v_out, vt_out, kc_out, kct_out, vc_out, vct_out))), out_sems)
    places = places_of(devices)
    me, x, y, z, xpeer, ypeer, order, ahead, behind = places
    slots = master.shape[0]
    block = slots + 1
    gathered[pl.ds(me * block, slots)] = master[...].astype(BF)
    gathered[me * block + slots] = jnp.broadcast_to(norm_row[...], (UNIT, features)).astype(BF)
    greet([{"dp": xpeer}, {"dp": ypeer}] + [{"dp": ahead(d)} for d in order])

    def meanwhile():
        mask_tables(len_ref, rank_ref, side_ref, hot_ref, rank_cols)
        late.wait(0, 1, 2)

        def units_of(step, rows):
            unit_q[rows, :] = normalise(query_ref[rows, :].astype(F32))[0]
            unit_kv[rows, :] = normalise(kv_ref[rows, :].astype(F32))[0]
        chunks(tokens, units_of)
    LineGather(devices, lambda number, start, size: gathered.at[pl.ds(number * block + start, size)], block, block * 3 // 5,
               places, *line_sems).run(meanwhile)

    share = devices // 8
    vectors = []
    for number in range(8):
        pieces = [gathered[(number * share + i) * block + slots].astype(F32) for i in range(share)]
        total = pieces[0]
        for piece in pieces[1:]:
            total = total + piece
        vectors.append(total[0:1, :])
    norms[...] = jnp.concatenate(vectors, 0)

    def one_unit(u, carry):
        flat[pl.ds(pl.multiple_of(u * UNIT, UNIT), UNIT), :] = gathered[place_ref[u]]
        return carry
    lax.fori_loop(0, units, one_unit, 0, unroll=4)
    order = interleave(features)
    cols = v_ref.shape[1]
    for number in range(6):
        rows = flat[number * cols:(number + 1) * cols, :]
        stacked = jnp.concatenate([rows[:, :cols], rows[:, cols:]], 0)
        matrix = nn(order, stacked).astype(BF)
        if number < 3:
            ws_ref[number] = matrix
        else:
            wc_ref[number - 3] = matrix
    wos_ref[...] = flat[6 * cols:7 * cols, :]
    woc_ref[...] = flat[7 * cols:8 * cols, :]
    hidden = w2_ref.shape[0]
    for block in range(hidden // features):
        at = 8 * cols + block * features
        parted = part_rows(flat[at:at + features, :], order)
        half = features // 2
        w1_ref[block * half:(block + 1) * half, :] = jnp.concatenate([parted[:half], parted[half:]], 1)
    w2_ref[...] = flat[8 * cols + hidden:, :]

    def body(step, rows):
        nq = (unit_q[rows, :] * norms[0:1, :] + norms[1:2, :]).astype(BF)
        nkv = (unit_kv[rows, :] * norms[2:3, :] + norms[3:4, :]).astype(BF)
        source = memory_ref[rows, :]
        low = lambda left, right: nn(left, right).astype(BF)
        k, v, kc, vc = low(nkv, ws_ref[1]), low(nkv, ws_ref[2]), low(source, wc_ref[1]), low(source, wc_ref[2])
        results = [nq, nkv, low(nq, ws_ref[0]).T, k, k.T, v, v.T, kc, kc.T, vc, vc.T]
        for i, (ref, result) in enumerate(zip(held, results)):
            if ref.shape[0] < ref.shape[1]:
                ref[:, rows] = result
            else:
                ref[rows, :] = result
            out.start(i, step)
    chunks(tokens, body)
    out.drain(tokens)


def pair_sems(tokens):
    return pltpu.SemaphoreType.DMA((2, tokens // CHUNK))


def out_semaphores(count, tokens):
    return pltpu.SemaphoreType.DMA((count, tokens // CHUNK))


def project(devices, place_of, lengths, master, norm_row, rank_row, query_stream, kv_stream, memory, cols, hidden):
    tokens, features = query_stream.shape
    wide, narrow, across = (tokens, features), (tokens, cols), (cols, tokens)
    shapes = [wide, wide, across] + [narrow, across] * 4
    outs = [(shape, BF, "A") for shape in shapes] + [
        ((3, features, cols), BF, "V"), ((3, features, cols), BF, "V"), ((cols, features), BF, "V"), ((cols, features), BF, "V"),
        ((features, hidden), BF, "V"), ((hidden, features), BF, "V"), ((8, features), F32, "V"),
        ((ROW, 128), BF, "V"), ((128, ROW), BF, "V"), ((ROW, 128), F32, "V")]
    D = pltpu.SemaphoreType.DMA
    scratch = [pltpu.VMEM((devices * (master.shape[0] + 1), UNIT, features), BF), pltpu.VMEM((8 * cols + 2 * hidden, features), BF)]
    scratch += [pltpu.VMEM(wide, BF)] * 3 + [pltpu.VMEM(wide, F32)] * 2 + [pltpu.VMEM(shape, BF) for shape in shapes]
    scratch += [D((3,)), out_semaphores(len(shapes), tokens)] + [D((2, 2, devices // 4 + 1))] * 6
    return call(partial(project_kernel, devices), "project",
                [place_of, lengths, master, norm_row, rank_row, query_stream, kv_stream, memory], "SSVVVAAA",
                outs, scratch, 0)


def self_out_kernel(mixed, wo, query_hbm, wc, norms, res_out, nc_out, q_out,
                    query, res_ref, nc_ref, q_ref, mine, theirs, sems, late_sems, out_sems):
    tokens = query.shape[0]
    late = Late([(query_hbm, query)], late_sems)
    out = Out([(res_ref, res_out), (nc_ref, nc_out), (q_ref, q_out)], out_sems)
    greet_core()

    def give(step, rows):
        mine[rows, :] = nn(mixed[rows, :], wo[...]).astype(BF)
        other_core(mine, theirs, sems, step).start()
    chunks(tokens, give)
    late.wait(0)

    def take(step, rows):
        other_core(mine, theirs, sems, step).wait_recv()
        res = query[rows, :].astype(F32) + (mine[rows, :].astype(F32) + theirs[rows, :].astype(F32))
        res_ref[rows, :] = res
        out.start(0, step)
        nc = (normalise(res)[0] * norms[4:5, :] + norms[5:6, :]).astype(BF)
        nc_ref[rows, :] = nc
        out.start(1, step)
        q_ref[:, rows] = nn(nc, wc[0]).astype(BF).T
        out.start(2, step)
    chunks(tokens, take)
    drain(tokens, mine, theirs, sems)
    out.drain(tokens)


def self_out(mixed, wo, query, wc, norms):
    tokens, features = query.shape
    wide = (tokens, features)
    across = (mixed.shape[1], tokens)
    outs = [(wide, F32, "A"), (wide, BF, "A"), (across, BF, "A")]
    scratch = [pltpu.VMEM(wide, BF), pltpu.VMEM(wide, F32), pltpu.VMEM(wide, BF), pltpu.VMEM(across, BF),
               pltpu.VMEM(wide, BF), pltpu.VMEM(wide, BF), pair_sems(tokens), pltpu.SemaphoreType.DMA((1,)),
               out_semaphores(3, tokens)]
    return call(self_out_kernel, "self_out", [mixed, wo, query, wc, norms], "VVAVV", outs, scratch, 2)


def gelu_parts(value):
    size = jnp.abs(value)
    bell = jnp.exp(-0.5 * value * value)
    t = 1.0 / (1.0 + (0.3275911 * 0.7071067811865476) * size)
    poly = ((((1.061405429 * t - 1.453152027) * t + 1.421413741) * t - 0.284496736) * t + 0.254829592) * t
    tail = 0.5 * poly * bell
    below = jnp.where(value < 0.0, tail, 1.0 - tail)
    return value * below, below + value * (bell * 0.3989422804014327)


def spread_flat(devices, places, flat, refs):
    rows = flat.shape[0] // devices
    for f, ref in enumerate(refs):
        place = plane_offset(places, f)
        for level in range(devices // 4):
            ref[level, ref.shape[1] - rows:, :] = flat[pl.ds(pl.multiple_of((level * 4 + place) * rows, UNIT), rows), :]


def feed_forward_kernel(devices, mixed, wo, res_hbm, w1, w2, out_grad_hbm, norms,
                        out_out, gres_out, gmix_out, part0, part1, part2, part3, sums_ref,
                        res, out_grad, out_ref, gres_ref, gmix_ref, flat,
                        mine, theirs, nf_all, hid_all, pre_all, low_all, mine_o, theirs_o, mine_g, theirs_g,
                        sems, sems_o, sems_g, late_sems, out_sems):
    tokens, features = out_grad.shape
    hidden = w2.shape[0]
    places = places_of(devices)
    late = Late([(res_hbm, res), (out_grad_hbm, out_grad)], late_sems)
    out = Out([(out_ref, out_out), (gres_ref, gres_out), (gmix_ref, gmix_out)], out_sems)
    greet_core()

    def give(step, rows):
        mine[rows, :] = nn(mixed[rows, :], wo[...]).astype(BF)
        other_core(mine, theirs, sems, step).start()
    chunks(tokens, give)
    late.wait(0, 1)

    def middle(step, rows):
        other_core(mine, theirs, sems, step).wait_recv()
        value = res[rows, :] + (mine[rows, :].astype(F32) + theirs[rows, :].astype(F32))
        gres_ref[rows, :] = value
        nf = (normalise(value)[0] * norms[6:7, :] + norms[7:8, :]).astype(BF)
        nf_all[rows, :] = nf
        grad = out_grad[rows, :]
        out_part = jnp.zeros((CHUNK, features), F32)
        grad_part = jnp.zeros((CHUNK, features), F32)
        for block in range(hidden // 256):
            at = slice(block * 256, (block + 1) * 256)
            act, slope = gelu_parts(nn(nf, w1[:, at]))
            act = act.astype(BF)
            hid_all[rows, at] = act
            pre = (slope * nt(grad, w2[at, :])).astype(BF)
            pre_all[rows, at] = pre
            out_part = out_part + nn(act, w2[at, :])
            grad_part = grad_part + nt(pre, w1[:, at])
        mine_o[rows, :] = out_part.astype(BF)
        other_core(mine_o, theirs_o, sems_o, step).start()
        mine_g[rows, :] = grad_part.astype(BF)
        other_core(mine_g, theirs_g, sems_g, step).start()
    chunks(tokens, middle)

    order = interleave(features)
    half, cols = features // 2, mixed.shape[1]
    for block in range(hidden // 256):
        at = slice(block * 256, (block + 1) * 256)
        flat[cols + hidden + block * 256:cols + hidden + (block + 1) * 256, :] = tn(hid_all[:, at], out_grad[...]).astype(BF)
    for block in range(hidden // features):
        gradient = tn(nf_all[:, block * half:(block + 1) * half], pre_all[...]).astype(BF)
        stacked = jnp.concatenate([gradient[:, :features], gradient[:, features:]], 0)
        flat[cols + block * features:cols + (block + 1) * features, :] = nn(order, stacked).astype(BF)
    sums_ref[...] = jnp.zeros_like(sums_ref)

    def close(step, rows):
        other_core(mine_o, theirs_o, sems_o, step).wait_recv()
        other_core(mine_g, theirs_g, sems_g, step).wait_recv()
        value = gres_ref[rows, :]
        out_ref[rows, :] = (value + (mine_o[rows, :].astype(F32) + theirs_o[rows, :].astype(F32))).astype(BF)
        out.start(0, step)
        grad = mine_g[rows, :].astype(F32) + theirs_g[rows, :].astype(F32)
        unit, scale = normalise(value)
        gres = norm_back(unit, scale, norms[6:7, :], grad) + out_grad[rows, :].astype(F32)
        gres_ref[rows, :] = gres
        out.start(1, step)
        sums_ref[0:8, :] += fold_rows(grad * unit)
        sums_ref[8:16, :] += fold_rows(grad)
        low = gres.astype(BF)
        low_all[rows, :] = low
        gmix_ref[:, rows] = nt(low, wo[...]).astype(BF).T
        out.start(2, step)
    chunks(tokens, close)
    flat[0:cols, :] = tn(mixed[...], low_all[...]).astype(BF)
    if flat.shape[0] > cols + 2 * hidden:
        flat[cols + 2 * hidden:, :] = jnp.zeros((flat.shape[0] - cols - 2 * hidden, features), BF)
    spread_flat(devices, places, flat, (part0, part1, part2, part3))
    out.drain(tokens)
    drain(tokens, mine, theirs, sems)
    drain(tokens, mine_o, theirs_o, sems_o)
    drain(tokens, mine_g, theirs_g, sems_g)


def whole_blocks(rows, devices):
    return -(-rows // (devices * UNIT)) * devices * UNIT


def feed_forward(devices, mixed, wo, res, w1, w2, out_grad, norms):
    tokens, features = out_grad.shape
    hidden = w2.shape[0]
    flat_rows = whole_blocks(wo.shape[0] + 2 * hidden, devices)
    part = ((devices // 4, flat_rows // devices, features), BF, "V")
    wide = (tokens, features)
    across = (mixed.shape[1], tokens)
    outs = [(wide, BF, "A"), (wide, F32, "A"), (across, BF, "A")] + [part] * 4 + [((16, features), F32, "V")]
    deep, narrow = pltpu.VMEM((tokens, hidden), BF), pltpu.VMEM(wide, BF)
    scratch = [pltpu.VMEM(wide, F32), narrow, narrow, pltpu.VMEM(wide, F32), pltpu.VMEM(across, BF),
               pltpu.VMEM((flat_rows, features), BF), narrow, narrow, narrow, deep, deep, narrow] + [narrow] * 4
    scratch += [pair_sems(tokens)] * 3 + [pltpu.SemaphoreType.DMA((2,)), out_semaphores(3, tokens)]
    return call(partial(feed_forward_kernel, devices), "feed_forward", [mixed, wo, res, w1, w2, out_grad, norms], "VVAVVAV",
                outs, scratch, 3)


def branch_give(dq, dk, dv, weights, mine_a, theirs_a, mine_b, theirs_b, sems_a, sems_b):
    def give(step, rows):
        mine_a[rows, :] = nt(dq[rows, :], weights[0]).astype(BF)
        other_core(mine_a, theirs_a, sems_a, step).start()
        mine_b[rows, :] = (nt(dk[rows, :], weights[1]) + nt(dv[rows, :], weights[2])).astype(BF)
        other_core(mine_b, theirs_b, sems_b, step).start()
    chunks(dq.shape[0], give)


def branch_weights(first_in, second_in, dq, dk, dv, flat):
    cols = dq.shape[1]
    order = interleave(first_in.shape[1])
    for number, (entering, grad) in enumerate(((first_in, dq), (second_in, dk), (second_in, dv))):
        flat[number * cols:(number + 1) * cols, :] = as_units(tn(entering[...], grad[...]), order)


def z_sum_start(devices, places, pieces, landed, sems):
    me, x, y, z, xpeer, ypeer, order, ahead, behind = places
    return [send(pieces.at[lax.rem(z + d, devices // 4)], landed.at[d], sems.at[0, d], sems.at[1, d], dp=ahead(d)) for d in order]


def z_sum_end(places, pieces, landed, copies):
    z, order = places[3], places[6]
    total = pieces[z].astype(F32)
    for copy, d in zip(copies, order):
        copy.wait_recv()
        total = total + landed[d].astype(F32)
    return total.astype(BF)


def four_sum(parts, at):
    return (parts[0][at].astype(F32) + parts[1][at].astype(F32) + parts[2][at].astype(F32) + parts[3][at].astype(F32)).astype(BF)


def cross_back_kernel(devices, dq, dk, dv, wc, nc_hbm, memory_hbm, res_hbm, gres_hbm, mixed, wo, norms,
                      part0, part1, part2, part3,
                      gmem_out, gnew_out, gmix_out, give0, give1, give2, give3, sums_ref,
                      nc, memory, res, gres, gmem_ref, gnew_ref, gmix_ref, flat, pieces, landed, blocks,
                      mine_a, theirs_a, mine_b, theirs_b, low_all, sems_a, sems_b, late_sems, out_sems, z_sems, zz_sems):
    tokens, features = nc.shape
    cols = dq.shape[1]
    across = devices // 4
    places = places_of(devices)
    me, x, y, z, xpeer, ypeer, order, ahead, behind = places
    late = Late([(nc_hbm, nc), (memory_hbm, memory), (res_hbm, res), (gres_hbm, gres)], late_sems)
    out = Out([(gmem_ref, gmem_out), (gnew_ref, gnew_out), (gmix_ref, gmix_out)], out_sems)
    for level in range(across):
        pieces[level] = four_sum((part0, part1, part2, part3), level)
    greet([{"head": 1 - lax.axis_index("head")}] + [{"dp": ahead(d)} for d in order])
    z_copies = z_sum_start(devices, places, pieces, landed, z_sems)
    branch_give(dq, dk, dv, wc, mine_a, theirs_a, mine_b, theirs_b, sems_a, sems_b)
    late.wait(0, 1)
    branch_weights(nc, memory, dq, dk, dv, flat)
    blocks[0] = z_sum_end(places, pieces, landed, z_copies)
    zz_copies = [send(blocks.at[0], blocks.at[d], zz_sems.at[0, d], zz_sems.at[1, d], dp=ahead(d)) for d in order]
    sums_ref[...] = jnp.zeros_like(sums_ref)
    late.wait(2, 3)

    def close(step, rows):
        other_core(mine_a, theirs_a, sems_a, step).wait_recv()
        grad = mine_a[rows, :].astype(F32) + theirs_a[rows, :].astype(F32)
        unit, scale = normalise(res[rows, :])
        gnew = norm_back(unit, scale, norms[4:5, :], grad) + gres[rows, :]
        gnew_ref[rows, :] = gnew
        out.start(1, step)
        sums_ref[0:8, :] += fold_rows(grad * unit)
        sums_ref[8:16, :] += fold_rows(grad)
        low = gnew.astype(BF)
        low_all[rows, :] = low
        gmix_ref[:, rows] = nt(low, wo[...]).astype(BF).T
        out.start(2, step)
        other_core(mine_b, theirs_b, sems_b, step).wait_recv()
        gmem_ref[rows, :] = (mine_b[rows, :].astype(F32) + theirs_b[rows, :].astype(F32)).astype(BF)
        out.start(0, step)
    chunks(tokens, close)
    flat[3 * cols:4 * cols, :] = tn(mixed[...], low_all[...]).astype(BF)
    if flat.shape[0] > 4 * cols:
        flat[4 * cols:, :] = jnp.zeros((flat.shape[0] - 4 * cols, features), BF)
    gives = (give0, give1, give2, give3)
    spread_flat(devices, places, flat, gives)
    for copy in zz_copies:
        copy.wait_recv()
    ready_rows = blocks.shape[1]
    for ref in gives:
        for d in range(across):
            ref[d, 0:ready_rows, :] = blocks[d]
    for copy in z_copies + zz_copies:
        copy.wait_send()
    out.drain(tokens)
    drain(tokens, mine_a, theirs_a, sems_a)
    drain(tokens, mine_b, theirs_b, sems_b)


def cross_back(devices, dq, dk, dv, wc, nc, memory, res, gres, mixed, wo, norms, parts):
    tokens, features = nc.shape
    cols = dq.shape[1]
    across, ready_rows = devices // 4, parts[0].shape[1]
    flat_rows = whole_blocks(4 * cols, devices)
    give = ((across, ready_rows + flat_rows // devices, features), BF, "V")
    wide = (tokens, features)
    outs = [(wide, BF, "A"), (wide, F32, "A"), ((cols, tokens), BF, "A")] + [give] * 4 + [((16, features), F32, "V")]
    low, high = pltpu.VMEM(wide, BF), pltpu.VMEM(wide, F32)
    small = pltpu.VMEM((across, ready_rows, features), BF)
    z_sems = pltpu.SemaphoreType.DMA((2, across))
    scratch = [low, low, high, high, low, high, pltpu.VMEM((cols, tokens), BF), pltpu.VMEM((flat_rows, features), BF), small, small, small]
    scratch += [low] * 5 + [pair_sems(tokens)] * 2 + [pltpu.SemaphoreType.DMA((4,)), out_semaphores(3, tokens), z_sems, z_sems]
    return call(partial(cross_back_kernel, devices), "cross_back",
                [dq, dk, dv, wc, nc, memory, res, gres, mixed, wo, norms] + parts, "VVVVAAAAVVVVVVV", outs, scratch, 4)


def self_back_kernel(devices, ready_rows, dq, dk, dv, ws, nq_hbm, nkv_hbm, query_hbm, kv_hbm, gres_hbm, norms, sums_c, sums_f,
                     part0, part1, part2, part3,
                     gquery_out, gkv_out, last_ref, more_ref, gnorm_ref,
                     nq, nkv, query, kv, gres, gquery_ref, gkv_ref, flat, source, landing, pieces, landed, more_pieces, more_landed,
                     norm_mine, norm_all, mine_a, theirs_a, mine_b, theirs_b, sums, sems_a, sems_b, late_sems, out_sems,
                     z_sems, more_z_sems, plane_sems, n_sems, *spread_sems):
    tokens, features = nq.shape
    across = devices // 4
    places = places_of(devices)
    me, x, y, z, xpeer, ypeer, order, ahead, behind = places
    late = Late([(nq_hbm, nq), (nkv_hbm, nkv), (query_hbm, query), (kv_hbm, kv), (gres_hbm, gres)], late_sems)
    out = Out([(gquery_ref, gquery_out), (gkv_ref, gkv_out)], out_sems)
    more_rows = more_ref.shape[2]
    for level in range(across):
        more_pieces[level] = four_sum((part0, part1, part2, part3), (level, pl.ds(ready_rows, more_rows)))
    others = [lax.rem(me + d, devices) for d in range(1, devices)]
    greet([{"head": 1 - lax.axis_index("head")}] + [{"dp": other} for other in others])
    more_copies = z_sum_start(devices, places, more_pieces, more_landed, more_z_sems)
    branch_give(dq, dk, dv, ws, mine_a, theirs_a, mine_b, theirs_b, sems_a, sems_b)
    late.wait(0, 1)
    branch_weights(nq, nkv, dq, dk, dv, flat)
    if flat.shape[0] > 3 * dq.shape[1]:
        flat[3 * dq.shape[1]:, :] = jnp.zeros((flat.shape[0] - 3 * dq.shape[1], features), BF)
    spread_flat(devices, places, flat, [source.at[f] for f in range(4)])
    plane_copies = [send(source.at[f], landing.at[f], plane_sems.at[0, f], plane_sems.at[1, f], dp=peer)
                    for f, peer in ((3, me + 3 - 2 * x - 4 * y), (1, xpeer), (2, ypeer))]
    more_ref[0, 0] = z_sum_end(places, more_pieces, more_landed, more_copies)
    more = Spread(places, more_ref, *spread_sems[:5])
    more.start()
    sums[...] = jnp.zeros_like(sums)
    late.wait(2, 3, 4)

    def close(step, rows):
        other_core(mine_a, theirs_a, sems_a, step).wait_recv()
        grad = mine_a[rows, :].astype(F32) + theirs_a[rows, :].astype(F32)
        unit, scale = normalise(query[rows, :].astype(F32))
        gquery_ref[rows, :] = (norm_back(unit, scale, norms[0:1, :], grad) + gres[rows, :]).astype(BF)
        out.start(0, step)
        sums[0:8, :] += fold_rows(grad * unit)
        sums[8:16, :] += fold_rows(grad)
        other_core(mine_b, theirs_b, sems_b, step).wait_recv()
        grad = mine_b[rows, :].astype(F32) + theirs_b[rows, :].astype(F32)
        unit, scale = normalise(kv[rows, :].astype(F32))
        gkv_ref[rows, :] = norm_back(unit, scale, norms[2:3, :], grad).astype(BF)
        out.start(1, step)
        sums[16:24, :] += fold_rows(grad * unit)
        sums[24:32, :] += fold_rows(grad)
    middle = tokens // 2
    chunks(middle, close)
    more.relay()
    chunks(tokens, close, middle)
    parts = [sums[8 * i:8 * i + 8, :] for i in range(4)]
    parts += [sums_c[0:8, :], sums_c[8:16, :], sums_f[0:8, :], sums_f[8:16, :]]
    norm_mine[...] = jnp.concatenate([jnp.sum(part, 0, keepdims=True) for part in parts], 0)
    for copy in plane_copies:
        copy.wait_recv()
    for level in range(across):
        pieces[level] = four_sum((source.at[0], landing.at[1], landing.at[2], landing.at[3]), level)
    z_copies = z_sum_start(devices, places, pieces, landed, z_sems)
    n_copies = [send(norm_mine, norm_all.at[d], n_sems.at[0, d], n_sems.at[1, d], dp=other)
                for d, other in zip(range(1, devices), others)]
    more.diagonal()
    last_ref[0, 0] = z_sum_end(places, pieces, landed, z_copies)
    last = Spread(places, last_ref, *spread_sems[5:])
    last.start()
    last.relay()
    last.diagonal()
    total = norm_mine[...]
    for d, copy in zip(range(1, devices), n_copies):
        copy.wait_recv()
        total = total + norm_all[d]
    gnorm_ref[...] = total
    more.finish()
    last.finish()
    more.drain()
    last.drain()
    for copy in more_copies + plane_copies + z_copies + n_copies:
        copy.wait_send()
    out.drain(tokens)
    drain(tokens, mine_a, theirs_a, sems_a)
    drain(tokens, mine_b, theirs_b, sems_b)


def self_back(devices, ready_rows, dq, dk, dv, ws, nq, nkv, query, kv, gres, norms, sums_c, sums_f, parts):
    tokens, features = nq.shape
    cols = dq.shape[1]
    across, more_rows = devices // 4, parts[0].shape[1] - ready_rows
    flat_rows = whole_blocks(3 * cols, devices)
    rows = flat_rows // devices
    wide = (tokens, features)
    outs = [(wide, BF, "A"), (wide, BF, "A"), ((4, across, rows, features), BF, "V"), ((4, across, more_rows, features), BF, "V"),
            ((8, features), F32, "V")]
    low, high = pltpu.VMEM(wide, BF), pltpu.VMEM(wide, F32)
    small, tiny = pltpu.VMEM((across, more_rows, features), BF), pltpu.VMEM((across, rows, features), BF)
    four = pltpu.VMEM((4, across, rows, features), BF)
    D = pltpu.SemaphoreType.DMA
    scratch = [low, low, low, low, high, low, low, pltpu.VMEM((flat_rows, features), BF), four, four, tiny, tiny, small, small,
               pltpu.VMEM((8, features), F32), pltpu.VMEM((devices, 8, features), F32)]
    scratch += [low] * 4 + [pltpu.VMEM((32, features), F32)] + [pair_sems(tokens)] * 2
    scratch += [D((5,)), out_semaphores(2, tokens), D((2, across)), D((2, across)), D((2, 4)), D((2, devices))]
    scratch += [D((2, across))] * 10
    return call(partial(self_back_kernel, devices, ready_rows), "self_back",
                [dq, dk, dv, ws, nq, nkv, query, kv, gres, norms, sums_c, sums_f] + parts, "VVVVAAAAAVVVVVVV", outs, scratch, 5)


def update_kernel(devices, early_unit, late_unit, late_rows, owner_ref, me_ref, last, more, part0, part1, part2, part3,
                  master, first, second, gquery_in, gkv_in, grad_ref, first_ref, second_ref, new_ref, gquery_out, gkv_out,
                  held, taken, held_q, held_kv, sems):
    units = owner_ref.shape[0]
    slots = master.shape[0]
    across = devices // 4
    me = me_ref[0]
    here, level = lax.rem(me, 4), lax.div(me, 4)
    entering = Late([(gquery_in, held_q), (gkv_in, held_kv)], sems.at[0])

    def find(u, count):
        held[count] = u
        return count + (owner_ref[u] == me).astype(jnp.int32)
    count = lax.fori_loop(0, units, find, jnp.int32(0), unroll=4)
    entering.wait(0, 1)
    leaving = Late([(held_q, gquery_out), (held_kv, gkv_out)], sems.at[1])

    def lookup(row, size):
        block = lax.div(row, size)
        behind = lax.rem(level - lax.div(block, 4) + across, across)
        return lax.rem(block, 4) ^ here, behind, pl.ds(pl.multiple_of(lax.rem(row, size), UNIT), UNIT)

    def one(slot, carry):
        @pl.when(slot < count)
        def _():
            unit = held[slot]

            @pl.when(unit < early_unit)
            def _():
                taken[...] = last[lookup(unit * UNIT, last.shape[2])]

            @pl.when((unit >= early_unit) & (unit < late_unit))
            def _():
                taken[...] = more[lookup((unit - early_unit) * UNIT, more.shape[2])]

            @pl.when(unit >= late_unit)
            def _():
                offset, behind, rows = lookup((unit - late_unit) * UNIT, late_rows)
                for f, part in enumerate((part0, part1, part2, part3)):
                    @pl.when(offset == f)
                    def _():
                        taken[...] = part[behind, rows]
            gradient = taken[...].astype(F32)
            first_new, second_new, weight = adamw_step(gradient, first[slot], second[slot], master[slot], RATE_MATRIX, WEIGHT_DECAY)
            grad_ref[slot] = gradient
            first_ref[slot] = first_new
            second_ref[slot] = second_new
            new_ref[slot] = weight

        @pl.when(slot >= count)
        def _():
            for ref in (grad_ref, first_ref, second_ref, new_ref):
                ref[slot] = jnp.zeros(ref.shape[1:], F32)
        return carry
    lax.fori_loop(0, slots, one, 0)
    leaving.wait(0, 1)


def update(devices, early_unit, late_unit, late_rows, unit_owner, me, last, more, parts, master, first, second, gquery, gkv):
    outs = [(master.shape, F32, "V")] * 4 + [(gquery.shape, BF, "A")] * 2
    kernel = partial(update_kernel, devices, early_unit, late_unit, late_rows)
    return call(kernel, "update", [unit_owner, me, last, more] + parts + [master, first, second, gquery, gkv], "SSVVVVVVVVVAA", outs,
                [pltpu.SMEM((unit_owner.shape[0] + 8,), jnp.int32), pltpu.VMEM((UNIT, master.shape[2]), BF),
                 pltpu.VMEM(gquery.shape, BF), pltpu.VMEM(gkv.shape, BF), pltpu.SemaphoreType.DMA((2, 2))])


def adamw_step(gradient, first, second, weight, rate, decay):
    first_new = BETA_ONE * first + (1.0 - BETA_ONE) * gradient
    second_new = BETA_TWO * second + (1.0 - BETA_TWO) * gradient * gradient
    corr_one = 1.0 - BETA_ONE**STEP
    corr_two = 1.0 - BETA_TWO**STEP
    direction = first_new / corr_one / (jnp.sqrt(second_new / corr_two) + ADAM_EPS)
    return (first_new, second_new, weight - rate * (direction + decay * weight))


def local(
    query_stream, kv_stream, memory, out_grad, lengths, obs_rank, obs_count, unit_owner,
    master, first_moment, second_moment, norm_master, norm_first, norm_second,
):
    devices = lax.axis_size("dp")
    shards = lax.axis_size("head")
    me = lax.axis_index("dp")
    slots, unit_rows, features = master.shape[0], master.shape[2], master.shape[3]
    units = unit_owner.shape[0]
    norm_share = norm_master.shape[0]
    cols = features // shards
    hidden = (units * unit_rows - 8 * cols) // 2

    shape = (slots, unit_rows, features)
    norm_row = lax.dynamic_update_slice(
        jnp.zeros((1, features), F32), norm_master.reshape(1, norm_share), (0, lax.rem(me * norm_share, features)))
    rank_row, count_row = obs_rank.reshape(1, ROW), obs_count.reshape(1, ROW)
    place_of, steps = plan(unit_owner, lengths, devices, slots + 1)
    nq, nkv, qt, k, kt, v, vt, kc, kct, vc, vct, ws, wc, wo_self, wo_cross, w1, w2, norms, *tables = project(
        devices, place_of, lengths, master.reshape(shape), norm_row, rank_row,
        query_stream, kv_stream, memory, cols, hidden)
    mixed_self, mixed_self_t, total_self = attend_forward(steps, qt, k, vt, tables, count_row, True)
    residual, nc, qct = self_out(mixed_self, wo_self, query_stream, wc, norms)
    mixed_cross, mixed_cross_t, total_cross = attend_forward(steps, qct, kc, vct, tables, count_row, False)
    output, grad_cross_res, grad_mixed, *parts, sums_f = feed_forward(
        devices, mixed_cross, wo_cross, residual, w1, w2, out_grad, norms)
    tie = lax.optimization_barrier
    ready_rows = parts[0].shape[1]
    parts = [parts[0]] + [plane_swap(parts[f], devices, f) for f in (1, 2, 3)]
    dq, dk, dv, output = attend_backward(
        steps, qct, kc, kct, vc, grad_mixed, mixed_cross_t, total_cross, tables, count_row, output, False)
    parts, dq = tie((parts, dq))
    grad_memory, grad_residual, grad_mixed, *parts, sums_c = cross_back(
        devices, dq, dk, dv, wc, nc, memory, residual, grad_cross_res, mixed_self, wo_self, norms, parts)
    parts = [parts[0]] + [plane_swap(parts[f], devices, f) for f in (1, 2, 3)]
    dq, dk, dv, grad_memory = attend_backward(
        steps, qt, k, kt, v, grad_mixed, mixed_self_t, total_self, tables, count_row, grad_memory, True)
    parts, dq = tie((parts, dq))
    grad_query, grad_kv, last, more, norm_grads = self_back(
        devices, ready_rows, dq, dk, dv, ws, nq, nkv, query_stream, kv_stream, grad_residual, norms, sums_c, sums_f, parts)

    early, late = 3 * cols // unit_rows, 7 * cols // unit_rows
    weight_grad, weight_first, weight_second, weight_new, grad_query, grad_kv = update(
        devices, early, late, ready_rows, unit_owner, me.reshape(1), last, more, parts, master.reshape(shape),
        first_moment.reshape(shape), second_moment.reshape(shape), grad_query, grad_kv)
    weight_grad, weight_first, weight_second, weight_new = [
        part.reshape(master.shape) for part in (weight_grad, weight_first, weight_second, weight_new)]
    norm_grad = lax.dynamic_slice_in_dim(norm_grads.reshape(-1), me * norm_share, norm_share)
    norm_first_new, norm_second_new, norm_new = adamw_step(
        norm_grad, norm_first, norm_second, norm_master, RATE_NORM, 0.0)
    return (
        output, grad_query, grad_kv, grad_memory, weight_grad, weight_first, weight_second, weight_new,
        norm_grad, norm_first_new, norm_second_new, norm_new,
    )


def solution(mesh):
    in_specs = (
        P("dp", None),
        P("dp", None),
        P("dp", None),
        P("dp", None),
        P("dp", None),
        P("dp"),
        P("dp"),
        P(),
        P("dp", "head", None, None),
        P("dp", "head", None, None),
        P("dp", "head", None, None),
        P("dp"),
        P("dp"),
        P("dp"),
    )
    out_specs = (
        P("dp", None),
        P("dp", None),
        P("dp", None),
        P("dp", None),
        P("dp", "head", None, None),
        P("dp", "head", None, None),
        P("dp", "head", None, None),
        P("dp", "head", None, None),
        P("dp"),
        P("dp"),
        P("dp"),
        P("dp"),
    )
    return jax.shard_map(local, mesh=mesh, in_specs=in_specs, out_specs=out_specs, check_vma=False)
```

```python
from functools import partial

import jax
import jax.numpy as jnp
from jax import lax
from jax.experimental import pallas as pl
from jax.experimental.pallas import tpu as pltpu
from jax.sharding import PartitionSpec as P

HEAD_DIM = 64
ROW = 2048
DOCS = 32
STEP = 10
UNIT = 16

EPS_NORM = 1e-05
ADAM_EPS = 1e-08
BETA_ONE = 0.5
BETA_TWO = 0.5
RATE_MATRIX = 0.1
RATE_NORM = 0.3
WEIGHT_DECAY = 0.01

F32 = jnp.float32
BF = jnp.bfloat16
TQ = 256
TK = 512
FAR = 32768.0
LANES = (64, 72, 80)


def nt(a, b):
    return lax.dot_general(a, b, (((1,), (1,)), ((), ())), preferred_element_type=F32)


def nn(a, b):
    return lax.dot_general(a, b, (((1,), (0,)), ((), ())), preferred_element_type=F32)


def doc_bounds(len_ref):
    starts, ends = [], []
    at = jnp.int32(0)
    for d in range(DOCS):
        starts.append(at)
        at = at + len_ref[0, d]
        ends.append(at)
    return starts, ends


def key_range(starts, ends, q0):
    low = jnp.int32(0)
    high = jnp.int32(0)
    for d in range(DOCS):
        low = jnp.where(starts[d] <= q0, starts[d], low)
        high = jnp.where(starts[d] <= q0 + TQ - 1, ends[d], high)
    first = lax.div(low, 128) * 128
    steps = lax.div(high - first + TK - 1, TK)
    return first, steps


def mask_tables(len_ref, rank_ref, side_ref, hot_ref, rank_cols):
    starts, ends = doc_bounds(len_ref)
    lanes = lax.broadcasted_iota(jnp.int32, (1, 128), 1)
    start_lane = jnp.full((1, 128), -1, jnp.int32)
    end_lane = jnp.full((1, 128), -1, jnp.int32)
    for d in range(DOCS):
        start_lane = jnp.where(lanes == d, starts[d], start_lane)
        end_lane = jnp.where(lanes == d, ends[d], end_lane)
    one = (lanes == LANES[0]) | (lanes == LANES[1]) | (lanes == LANES[2])
    for t in range(ROW // 256):
        pos = lax.broadcasted_iota(jnp.int32, (256, 128), 0) + t * 256
        hot = (pos >= start_lane) & (pos < end_lane)
        side = jnp.where(hot | (lanes >= DOCS), jnp.where(one, -1.0, 0.0), -FAR)
        side_ref[t * 256:(t + 1) * 256, :] = side.astype(BF)
    pos = lax.broadcasted_iota(jnp.int32, (1, ROW), 1)
    first = jnp.zeros((1, ROW), jnp.bool_)
    rows = []
    for d in range(DOCS):
        first = first | (pos == starts[d])
        rows.append(jnp.where((pos >= starts[d]) & (pos < ends[d]), FAR, 0.0))
    hot_ref[...] = jnp.concatenate(rows + [jnp.zeros((128 - DOCS, ROW), F32)], 0).astype(BF)
    rank = jnp.where(first, -1.0, rank_ref[...].astype(F32))
    for t in range(ROW // 128):
        rank_cols[t * 128:(t + 1) * 128, :] = jnp.broadcast_to(rank[:, t * 128:(t + 1) * 128], (128, 128)).T


STEPS = (ROW // TQ) * -(-ROW // TK) + 8


def step_table(len_ref, table):
    starts, ends = doc_bounds(len_ref)
    idle = ROW // TQ

    def put(at, tile, first):
        table[0, at] = tile
        table[1, at] = first
    put(0, idle, ROW)
    put(1, idle, ROW)
    at = jnp.int32(2)
    for tile in range(idle):
        first, steps = key_range(starts, ends, tile * TQ)

        def fill(s, at):
            put(at, tile, first + s * TK)
            return at + 1
        at = lax.fori_loop(0, steps, fill, at)
    put(at, idle, ROW)
    put(at + 1, idle, ROW)
    table[0, STEPS - 1] = at


def step_of(table, i):
    return table[0, i], pl.multiple_of(table[1, i], 128)


def real_step(table, i):
    return jnp.minimum(table[0, i], ROW // TQ - 1), pl.multiple_of(table[1, i], 128)


def padded(ref):
    return ref.at[pl.ds(0, ROW)] if ref.shape[0] > ref.shape[1] else ref.at[:, pl.ds(0, ROW)]


def fill_padding(refs, side_ref):
    for ref in refs:
        if ref.shape[0] > ref.shape[1]:
            ref[ROW:, :] = jnp.zeros((TK, ref.shape[1]), ref.dtype)
        else:
            ref[:, ROW:] = jnp.zeros((ref.shape[0], TK), ref.dtype)
    lanes = lax.broadcasted_iota(jnp.int32, (TK, 128), 1)
    side_ref[ROW:, :] = jnp.where(lanes < DOCS, -FAR, 0.0).astype(BF)


def seen_bias(rank_cols, counts, tile, k0):
    rank = rank_cols[pl.ds(k0, TK), :]
    rank = jnp.concatenate([rank] * (TQ // 128), 1)
    kpos = lax.broadcasted_iota(jnp.int32, (TK, TQ), 0)
    qpos = lax.broadcasted_iota(jnp.int32, (TK, TQ), 1)
    off_diag = (kpos - qpos) != (tile * TQ - k0)
    allowed = (rank < counts[tile, 0:1, :]) & (off_diag | (rank < 0.0))
    return jnp.where(allowed, 0.0, -FAR * FAR)


def count_tiles(counts, count_ref):
    for tile in range(ROW // TQ):
        counts[tile] = jnp.broadcast_to(count_ref[:, tile * TQ:(tile + 1) * TQ].astype(F32), (8, TQ))


def query_columns(qt, qt_ref, side, tile, h, q0):
    rows = qt_ref[h * HEAD_DIM:(h + 1) * HEAD_DIM, pl.ds(q0, TQ)].astype(F32) * HEAD_DIM ** -0.5
    own, other = h % 2 * HEAD_DIM, (1 - h % 2) * HEAD_DIM
    qt[tile, h, own:own + HEAD_DIM, :] = rows.astype(BF)
    qt[tile, h, other:other + HEAD_DIM, :] = jnp.zeros((HEAD_DIM, TQ), BF)
    qt[tile, h, 128:256, :] = side


def pair_rows(ref, side_ref, h, k0):
    return jnp.concatenate([ref[pl.ds(k0, TK), h // 2 * 128:(h // 2 + 1) * 128], side_ref[pl.ds(k0, TK), :]], 1)


def attn_fwd_kernel(with_seen, heads, table, count_ref, qt_hbm, hot_hbm, k_hbm, vt_hbm, side_hbm, rank_hbm,
                    o_out, ot_out, lse_ref, qt, acc, top, sc, probs, fade, counts,
                    qt_ref, hot_ref, k_ref, vt_ref, side_ref, rank_cols, o_ref, ot_ref, late_sems, out_sems):
    pairs = [(qt_hbm, qt_ref), (hot_hbm, hot_ref), (k_hbm, padded(k_ref)), (vt_hbm, padded(vt_ref)),
             (side_hbm, padded(side_ref))]
    late = Late(pairs + ([(rank_hbm, padded(rank_cols))] if with_seen else []), late_sems)
    fill_padding((k_ref, vt_ref, rank_cols), side_ref)
    out = Out([(o_ref, o_out), (ot_ref, ot_out)], out_sems)
    tiles = ROW // TQ
    lse_ref[...] = jnp.zeros_like(lse_ref)
    acc[...] = jnp.zeros_like(acc)
    top[...] = jnp.full_like(top, -jnp.inf)
    if with_seen:
        count_tiles(counts, count_ref)
    late.wait(0, 1)

    def prepare(tile, c):
        q0 = pl.multiple_of(tile * TQ, TQ)
        for h in range(heads):
            query_columns(qt, qt_ref, hot_ref[:, pl.ds(q0, TQ)], tile, h, q0)
        return c
    lax.fori_loop(0, tiles, prepare, 0)
    late.wait(*range(2, 6 if with_seen else 5))
    ones = jnp.ones((16, TK), BF)

    def one_step(s, c):
        out_tile, _ = step_of(table, s)
        _, out_k = real_step(table, s)
        mid_tile, _ = step_of(table, s + 1)
        in_tile, in_k = real_step(table, s + 2)
        sums = []
        for h in range(heads):
            values = jnp.concatenate([vt_ref[h * HEAD_DIM:(h + 1) * HEAD_DIM, pl.ds(out_k, TK)], ones], 0)
            sums.append(acc[out_tile, h] * fade[h:h + 1, :] + nn(values, probs[h]))
        old = top[mid_tile]
        news = []
        for h in range(heads):
            score = sc[h]
            new = jnp.maximum(old[h:h + 1, :], jnp.max(score, 0, keepdims=True))
            probs[h] = jnp.exp(score - new).astype(BF)
            news.append(new)
        new = jnp.concatenate(news + [old[heads:, :]], 0)
        fade[...] = jnp.exp(old - new)
        bias = seen_bias(rank_cols, counts, in_tile, in_k) if with_seen else None
        for h in range(heads):
            score = nn(pair_rows(k_ref, side_ref, h, in_k), qt[in_tile, h])
            sc[h] = score + bias if with_seen else score
        top[mid_tile] = new
        for h in range(heads):
            acc[out_tile, h] = sums[h]
        return c
    lax.fori_loop(0, table[0, STEPS - 1], one_step, 0)

    def finish(tile, c):
        q0 = pl.multiple_of(tile * TQ, TQ)
        outs = []
        peak = top[tile]
        for h in range(heads):
            a = acc[tile, h]
            total = a[HEAD_DIM:HEAD_DIM + 1, :]
            outs.append(a[:HEAD_DIM, :] * (1.0 / total))
            lse_ref[h:h + 1, pl.ds(q0, TQ)] = peak[h:h + 1, :] + jnp.log(total)
        mixed = jnp.concatenate(outs, 0).astype(BF)
        ot_ref[:, pl.ds(q0, TQ)] = mixed
        out.start(1, tile)
        o_ref[pl.ds(q0, TQ), :] = mixed.T
        out.start(0, tile)
        return c
    lax.fori_loop(0, tiles, finish, 0)
    out.drain(ROW)


def attend_forward(steps, qt, k, vt, tables, count, with_seen):
    cols, rows = qt.shape
    heads = cols // HEAD_DIM
    side, hot, rank_cols = tables
    args = [steps, count, qt, hot, k, vt, side, rank_cols]
    across, down = (cols, rows), (rows, cols)
    held = [pltpu.VMEM(arg.shape, BF) for arg in (qt, hot)] + [
        pltpu.VMEM((rows + TK, cols), BF), pltpu.VMEM((cols, rows + TK), BF), pltpu.VMEM((rows + TK, 128), BF),
        pltpu.VMEM((rows + TK, 128), F32)]
    return call(partial(attn_fwd_kernel, with_seen, heads), "attend_self_forward" if with_seen else "attend_cross_forward",
                args, "SV" + "A" * 6, [(down, BF, "A"), (across, BF, "A"), ((8, rows), F32, "V")],
                [pltpu.VMEM((ROW // TQ, heads, 256, TQ), BF), pltpu.VMEM((ROW // TQ + 1, heads, HEAD_DIM + 16, TQ), F32),
                 pltpu.VMEM((ROW // TQ + 1, 8, TQ), F32), pltpu.VMEM((heads, TK, TQ), F32), pltpu.VMEM((heads, TK, TQ), BF),
                 pltpu.VMEM((8, TQ), F32), pltpu.VMEM((ROW // TQ, 8, TQ), F32)] + held
                + [pltpu.VMEM(down, BF), pltpu.VMEM(across, BF), pltpu.SemaphoreType.DMA((6,)), out_semaphores(2, rows)])


def three_rows(value):
    high = value.astype(BF).astype(F32)
    middle = (value - high).astype(BF).astype(F32)
    row = lax.broadcasted_iota(jnp.int32, (128, value.shape[1]), 0)
    return jnp.where(row == LANES[0], high, jnp.where(row == LANES[1], middle, jnp.where(row == LANES[2], value - high - middle, 0.0)))


def attn_bwd_kernel(with_seen, heads, table, count_ref, lse_ref, qt_hbm, hot_hbm, gt_hbm, ot_hbm, k_hbm, kt_hbm, v_hbm, side_hbm,
                    rank_hbm, *refs):
    passed = (len(refs) - 30) // 3
    pass_in, (dq_out, dk_out, dv_out), pass_out, refs = refs[:passed], refs[passed:passed + 3], refs[passed + 3:2 * passed + 3], refs[2 * passed + 3:]
    (dk_sum, dv_sum, dq_sum, qt, gt, q_own, g_own, sc, dps, all_ds, all_p, counts,
     qt_ref, hot_ref, gt_ref, ot_ref, k_ref, kt_ref, v_ref, side_ref, rank_cols, *held, dq_ref, dk_ref, dv_ref,
     late_sems, out_sems, pass_sem) = refs
    pairs = [(qt_hbm, qt_ref), (hot_hbm, hot_ref), (gt_hbm, gt_ref), (ot_hbm, ot_ref), (k_hbm, padded(k_ref)),
             (kt_hbm, padded(kt_ref)), (v_hbm, padded(v_ref)), (side_hbm, padded(side_ref))]
    late = Late(pairs + ([(rank_hbm, padded(rank_cols))] if with_seen else []), late_sems)
    fill_padding((k_ref, kt_ref, v_ref, rank_cols), side_ref)
    entering = Late(list(zip(pass_in, held)), pass_sem.at[0])
    out = Out([(dq_ref, dq_out), (dk_ref, dk_out), (dv_ref, dv_out)], out_sems)
    tiles = ROW // TQ
    dk_sum[...] = jnp.zeros_like(dk_sum)
    dv_sum[...] = jnp.zeros_like(dv_sum)
    dq_sum[...] = jnp.zeros_like(dq_sum)
    if with_seen:
        count_tiles(counts, count_ref)
    late.wait(0, 1, 2, 3)

    def prepare(tile, c):
        q0 = pl.multiple_of(tile * TQ, TQ)
        hot = hot_ref[:, pl.ds(q0, TQ)].astype(F32)
        for h in range(heads):
            rows = slice(h * HEAD_DIM, (h + 1) * HEAD_DIM)
            side = hot + three_rows(lse_ref[h:h + 1, pl.ds(q0, TQ)])
            query_columns(qt, qt_ref, side.astype(BF), tile, h, q0)
            grads = gt_ref[rows, pl.ds(q0, TQ)]
            delta = jnp.sum(grads.astype(F32) * ot_ref[rows, pl.ds(q0, TQ)].astype(F32), 0, keepdims=True)
            other = (1 - h % 2) * HEAD_DIM
            gt[tile, h, h % 2 * HEAD_DIM:(h % 2 + 1) * HEAD_DIM, :] = grads
            gt[tile, h, other:other + HEAD_DIM, :] = jnp.zeros((HEAD_DIM, TQ), BF)
            gt[tile, h, 128:256, :] = three_rows(delta).astype(BF)
        lane = lax.broadcasted_iota(jnp.int32, (TQ, heads * HEAD_DIM), 1)
        for held_rows, source in ((q_own, qt_ref), (g_own, gt_ref)):
            rows = source[:, pl.ds(q0, TQ)].T
            for h in range(heads):
                own = (lane >= h * HEAD_DIM) & (lane < (h + 1) * HEAD_DIM)
                held_rows[tile, h * TQ:(h + 1) * TQ, :] = jnp.where(own, rows, jnp.zeros_like(rows))
        return c
    lax.fori_loop(0, tiles, prepare, 0)
    late.wait(*range(4, 9 if with_seen else 8))
    entering.wait(*range(passed))
    leaving = Late(list(zip(held, pass_out)), pass_sem.at[1])

    def one_step(s, c):
        out_tile, out_k = step_of(table, s)
        read_tile, read_k = real_step(table, s)
        in_tile, in_k = real_step(table, s + 2)
        keys = pl.ds(out_k, TK)
        own = [slice(h * HEAD_DIM, (h + 1) * HEAD_DIM) for h in range(heads)]
        dk = dk_sum[keys, :] + nn(all_ds[...], q_own[read_tile])
        dv = dv_sum[keys, :] + nn(all_p[...], g_own[read_tile])
        dq = [dq_sum[out_tile, h] + nn(kt_ref[own[h], pl.ds(read_k, TK)], all_ds[:, h * TQ:(h + 1) * TQ]) for h in range(heads)]
        for h in range(heads):
            p = jnp.exp(sc[h])
            all_ds[:, h * TQ:(h + 1) * TQ] = (p * dps[h]).astype(BF)
            all_p[:, h * TQ:(h + 1) * TQ] = p.astype(BF)
        bias = seen_bias(rank_cols, counts, in_tile, in_k) if with_seen else None
        for h in range(heads):
            score = nn(pair_rows(k_ref, side_ref, h, in_k), qt[in_tile, h])
            sc[h] = score + bias if with_seen else score
            dps[h] = nn(pair_rows(v_ref, side_ref, h, in_k), gt[in_tile, h])
        dk_sum[keys, :] = dk
        dv_sum[keys, :] = dv
        for h in range(heads):
            dq_sum[out_tile, h] = dq[h]
        return c
    lax.fori_loop(0, table[0, STEPS - 1], one_step, 0)

    def finish(tile, c):
        q0 = pl.multiple_of(tile * TQ, TQ)
        rows = pl.ds(q0, TQ)
        dq = jnp.concatenate([dq_sum[tile, h] for h in range(heads)], 0) * HEAD_DIM ** -0.5
        dk = dk_sum[rows, :] * HEAD_DIM ** -0.5
        for i, (ref, value) in enumerate(((dq_ref, dq.astype(BF).T), (dk_ref, dk.astype(BF)), (dv_ref, dv_sum[rows, :].astype(BF)))):
            ref[rows, :] = value
            out.start(i, tile)
        return c
    lax.fori_loop(0, tiles, finish, 0)
    out.drain(ROW)
    leaving.wait(*range(passed))


def attend_backward(steps, qt, k, kt, v, gt, ot, lse, tables, count, passed, with_seen):
    rows, cols = v.shape
    heads = cols // HEAD_DIM
    side, hot, rank_cols = tables
    args = [steps, count, lse, qt, hot, gt, ot, k, kt, v, side, rank_cols] + passed
    tiles = ROW // TQ
    like = ((rows, cols), BF, "A")
    summed, own = pltpu.VMEM((rows + TK, cols), F32), pltpu.VMEM((tiles, heads * TQ, cols), BF)
    columns, square = pltpu.VMEM((tiles, heads, 256, TQ), BF), pltpu.VMEM((heads, TK, TQ), F32)
    small = pltpu.VMEM((TK, heads * TQ), BF)
    keys, keys_t = pltpu.VMEM((rows + TK, cols), BF), pltpu.VMEM((cols, rows + TK), BF)
    held = [pltpu.VMEM(arg.shape, BF) for arg in (qt, hot, gt, ot)] + [
        keys, keys_t, keys, pltpu.VMEM((rows + TK, 128), BF), pltpu.VMEM((rows + TK, 128), F32)] + [
        pltpu.VMEM(value.shape, value.dtype) for value in passed]
    return call(partial(attn_bwd_kernel, with_seen, heads), "attend_self_backward" if with_seen else "attend_cross_backward",
                args, "SVV" + "A" * (9 + len(passed)), [like, like, like] + [(value.shape, value.dtype, "A") for value in passed],
                [summed, summed, pltpu.VMEM((tiles + 1, heads, HEAD_DIM, TQ), F32), columns, columns, own, own, square, square,
                 small, small, pltpu.VMEM((ROW // TQ, 8, TQ), F32)] + held + [pltpu.VMEM((rows, cols), BF)] * 3
                + [pltpu.SemaphoreType.DMA((9,)), out_semaphores(3, rows), pltpu.SemaphoreType.DMA((2, 2))])


def send(src, dst, send_sem, recv_sem, **where):
    copy = pltpu.make_async_remote_copy(src_ref=src, dst_ref=dst, send_sem=send_sem, recv_sem=recv_sem,
                                        device_id=where, device_id_type=pl.DeviceIdType.MESH)
    copy.start()
    return copy

def greet(peers):
    barrier = pltpu.get_barrier_semaphore()
    for where in peers:
        pl.semaphore_signal(barrier, inc=1, device_id=where, device_id_type=pl.DeviceIdType.MESH)
    pl.semaphore_wait(barrier, len(peers))

def places_of(count):
    me = lax.axis_index("dp")
    across = count // 4
    x, y, z = lax.rem(me, 2), lax.rem(lax.div(me, 2), 2), lax.div(me, 4)
    xpeer, ypeer = me + 1 - 2 * x, me + 2 - 4 * y
    order = sorted(range(1, across), key=lambda d: min(d, across - d))
    ahead = lambda d: lax.rem(z + d, across) * 4 + y * 2 + x
    behind = lambda d: lax.rem(z + across - d, across) * 4 + y * 2 + x
    return me, x, y, z, xpeer, ypeer, order, ahead, behind

class LineGather:
    def __init__(self, count, piece, units, cut, places, zs, ds, xs, ys, gx, gy):
        self.across, self.piece, self.units, self.cut = count // 4, piece, units, cut
        self.places = places
        self.sems = dict(z=zs, d=ds, x=xs, y=ys, gx=gx, gy=gy)

    def copy(self, name, side, k, arriving=False):
        me, x, y, z, xpeer, ypeer = self.places[:6]
        place = x + 2 * y
        place = dict(z=place, x=place, y=place, d=3 - place, gy=place + 1 - 2 * x, gx=place + 2 - 4 * y)[name]
        if arriving:
            place = {"x": x + 2 * y + 1 - 2 * x, "y": x + 2 * y + 2 - 4 * y, "gx": 3 - x - 2 * y, "gy": 3 - x - 2 * y}.get(name, place)
        level = z + k * (2 * side - 1)
        whole = isinstance(k, int) and k == 0
        half = self.units // 2 if whole else (self.units - self.cut) // 2
        first = 0 if whole else self.cut
        start, size = dict(d=(0, self.cut), gy=(first, half), gx=(first + half, self.units - first - half)).get(name, (0, self.units))
        to = dict(x=xpeer, gx=xpeer, y=ypeer, gy=ypeer).get(name, me + 4 * (1 - 2 * side))
        hop = 1 if name in ("z", "d") and not arriving else 0
        if arriving:
            to = xpeer
        part, sems = self.piece(level * 4 + place, start, size), self.sems[name]
        return pltpu.make_async_remote_copy(
            src_ref=part, dst_ref=part, send_sem=sems.at[0, side, k], recv_sem=sems.at[1, side, k + hop],
            device_id={"dp": to}, device_id_type=pl.DeviceIdType.MESH)

    def here(self, side, k):
        z = self.places[3]
        return z >= k if side == 0 else z + k < self.across

    def onward(self, side):
        z = self.places[3]
        return z + 1 < self.across if side == 0 else z > 0

    def along(self, name, side, k, act):
        pl.when(self.here(side, k) & self.onward(side))(lambda: act(self.copy(name, side, k)))

    def run(self, at_start, at_first, at_second):
        start, wait_send = (lambda copy: copy.start()), (lambda copy: copy.wait_send())

        def diagonal(side, k):
            self.copy("x", side, k, True).wait_recv()
            self.copy("gy", side, k).start()
            self.copy("y", side, k, True).wait_recv()
            self.copy("gx", side, k).start()

        def later(side, k):
            diagonal(side, k)
            self.copy("d", side, k, True).wait_recv()
            pl.when(self.onward(side))(lambda: self.copy("d", side, k).start())
        for side in (0, 1):
            self.along("z", side, 0, start)
        self.copy("x", 0, 0).start()
        self.copy("y", 0, 0).start()
        at_start()
        diagonal(0, 0)

        def level(k, carry):
            for side in (0, 1):
                @pl.when(self.here(side, k))
                def _():
                    self.copy("z", side, k, True).wait_recv()
                    pl.when(self.onward(side))(lambda: self.copy("z", side, k).start())
                    self.copy("x", side, k).start()
                    self.copy("y", side, k).start()

            @pl.when(k == 1)
            def _():
                self.copy("gy", 0, 0, True).wait_recv()
                self.copy("gx", 0, 0, True).wait_recv()
                for side in (0, 1):
                    self.along("d", side, 0, start)
                at_first()

            @pl.when(k > 1)
            def _():
                for side in (0, 1):
                    pl.when(self.here(side, k - 1))(lambda: later(side, k - 1))
            pl.when(k == 2)(at_second)
            return carry
        lax.fori_loop(1, self.across, level, 0)
        for side in (0, 1):
            pl.when(self.here(side, self.across - 1))(lambda: later(side, self.across - 1))

        def settle(k, carry):
            for side in (0, 1):
                @pl.when(self.here(side, k))
                def _():
                    for name in ("gy", "gx"):
                        self.copy(name, side, k, True).wait_recv()
                    for name in ("x", "y", "gy", "gx"):
                        self.copy(name, side, k).wait_send()
                for name in ("z", "d"):
                    self.along(name, side, k, wait_send)
            return carry
        lax.fori_loop(1, self.across, settle, 0)
        for name in ("x", "y", "gy", "gx"):
            self.copy(name, 0, 0).wait_send()
        for side in (0, 1):
            for name in ("z", "d"):
                self.along(name, side, 0, wait_send)


class Spread:
    def __init__(self, places, out, zs, xs, ys, gx, gy):
        self.places, self.out, self.sems = places, out, dict(z=zs, x=xs, y=ys, gx=gx, gy=gy)
        self.rows = out.shape[2]
        self.half = self.rows // 2 // UNIT * UNIT
        self.copies = {}

    def go(self, name, d, f_from, d_from, f_to, d_to, to, start, size):
        part, sems = pl.ds(start, size), self.sems[name]
        self.copies[name, d] = send(self.out.at[f_from, d_from, part], self.out.at[f_to, d_to, part],
                                    sems.at[0, d], sems.at[1, d], dp=to)

    def over_plane(self, d):
        xpeer, ypeer = self.places[4], self.places[5]
        self.go("x", d, 0, d, 1, d, xpeer, 0, self.rows)
        self.go("y", d, 0, d, 2, d, ypeer, 0, self.rows)

    def start(self):
        order, ahead = self.places[6], self.places[7]
        for d in order:
            self.go("z", d, 0, 0, 0, d, ahead(d), 0, self.rows)
        self.over_plane(0)

    def relay(self):
        for d in self.places[6]:
            self.copies["z", d].wait_recv()
            self.over_plane(d)

    def diagonal(self):
        xpeer, ypeer, order = self.places[4:7]
        for d in [0] + order:
            self.copies["x", d].wait_recv()
            if self.half:
                self.go("gy", d, 1, d, 3, d, ypeer, 0, self.half)
            self.copies["y", d].wait_recv()
            self.go("gx", d, 2, d, 3, d, xpeer, self.half, self.rows - self.half)

    def finish(self):
        for (name, d), copy in self.copies.items():
            if name in ("gx", "gy"):
                copy.wait_recv()

    def drain(self):
        for copy in self.copies.values():
            copy.wait_send()


def plane_swap(value, count, f):
    return lax.ppermute(value, "dp", [(i, i // 4 * 4 + (i % 4 ^ f)) for i in range(count)])


def plane_offset(places, f):
    x, y = places[1], places[2]
    return lax.rem(x + f % 2, 2) + 2 * lax.rem(y + f // 2, 2)


def call(kernel, name, args, kinds, outs, scratch, number=None):
    space = {"V": pltpu.VMEM, "S": pltpu.SMEM, "A": pl.ANY}
    extra = {} if number is None else dict(collective_id=number, has_side_effects=True)
    return pl.pallas_call(
        kernel,
        out_shape=tuple(jax.ShapeDtypeStruct(shape, dtype) for shape, dtype, _ in outs),
        in_specs=[pl.BlockSpec(memory_space=space[kind]) for kind in kinds],
        out_specs=tuple(pl.BlockSpec(memory_space=space[kind]) for _, _, kind in outs),
        scratch_shapes=scratch,
        compiler_params=pltpu.CompilerParams(vmem_limit_bytes=60 * 2**20, **extra),
        cost_estimate=pl.CostEstimate(flops=4 * 10**10, bytes_accessed=16 * 2**20, transcendentals=0),
        name=name,
    )(*args)


CHUNK = 256


def tn(a, b):
    return lax.dot_general(a, b, (((0,), (0,)), ((), ())), preferred_element_type=F32)


def normalise(value):
    centred = value - jnp.mean(value, -1, keepdims=True)
    scale = lax.rsqrt(jnp.mean(centred * centred, -1, keepdims=True) + EPS_NORM)
    return centred * scale, scale


def norm_back(unit, scale, gain, grad):
    inner = grad * gain
    return scale * (inner - jnp.mean(inner, -1, keepdims=True) - unit * jnp.mean(inner * unit, -1, keepdims=True))


def fold_rows(value):
    return jnp.sum(value.reshape(value.shape[0] // 8, 8, value.shape[1]), 0)


def interleave(size):
    row = lax.broadcasted_iota(jnp.int32, (size, size), 0)
    col = lax.broadcasted_iota(jnp.int32, (size, size), 1)
    source = jnp.where((row & 1) == 0, row >> 1, (row >> 1) + size // 2)
    return jnp.where(col == source, 1.0, 0.0).astype(BF)


def part_rows(matrix, order):
    return lax.dot_general(order, matrix, (((0,), (0,)), ((), ())), preferred_element_type=F32).astype(BF)


def as_units(gradient, order):
    parted = part_rows(gradient.astype(BF), order)
    half = parted.shape[0] // 2
    return jnp.concatenate([parted[:half], parted[half:]], 1)


def other_core(mine, theirs, sems, step):
    rows = pl.ds(step * CHUNK, CHUNK)
    return pltpu.make_async_remote_copy(
        src_ref=mine.at[rows], dst_ref=theirs.at[rows], send_sem=sems.at[0, step], recv_sem=sems.at[1, step],
        device_id={"head": 1 - lax.axis_index("head")}, device_id_type=pl.DeviceIdType.MESH)


def greet_core():
    greet([{"head": 1 - lax.axis_index("head")}])


def chunks(total, body, begin=0):
    def one(step, carry):
        body(step, pl.ds(pl.multiple_of(step * CHUNK, CHUNK), CHUNK))
        return carry
    lax.fori_loop(begin // CHUNK, total // CHUNK, one, 0)


def drain(total, mine, theirs, sems):
    def body(step, rows):
        other_core(mine, theirs, sems, step).wait_send()
    chunks(total, body)


class Late:
    def __init__(self, pairs, sems):
        self.copies = [pltpu.make_async_copy(source, held, sems.at[i]) for i, (source, held) in enumerate(pairs)]
        for copy in self.copies:
            copy.start()

    def wait(self, *which):
        for i in which:
            self.copies[i].wait()


class Out:
    def __init__(self, pairs, sems):
        self.pairs, self.sems = pairs, sems

    def copy(self, i, step):
        held, out = self.pairs[i]
        part = pl.ds(pl.multiple_of(step * CHUNK, CHUNK), CHUNK)
        if held.shape[0] < held.shape[1]:
            held, out = held.at[:, part], out.at[:, part]
        else:
            held, out = held.at[part], out.at[part]
        return pltpu.make_async_copy(held, out, self.sems.at[i, step])

    def start(self, i, step):
        self.copy(i, step).start()

    def drain(self, tokens):
        def body(step, rows):
            for i in range(len(self.pairs)):
                self.copy(i, step).wait()
        chunks(tokens, body)


def plan_kernel(block, owner_ref, len_ref, rank_ref, count_ref, place_ref, rank_out, count_out, table, info):
    units = owner_ref.shape[1]
    owner = owner_ref[...].astype(F32)
    owner_cols = jnp.broadcast_to(owner, (128, units)).T
    owner_cols = jnp.concatenate([owner_cols] * (units // 128), 1)
    before = lax.broadcasted_iota(jnp.int32, (units, units), 0) < lax.broadcasted_iota(jnp.int32, (units, units), 1)
    slots = jnp.sum(jnp.where(before & (owner_cols == owner), 1.0, 0.0), 0, keepdims=True)
    place_ref[...] = (owner * block + slots).astype(jnp.int32)
    longest, first, at, start = jnp.int32(0), jnp.int32(0), jnp.int32(0), jnp.int32(0)
    for d in range(DOCS):
        length = len_ref[0, d]
        longer = length > longest
        first = jnp.where(longer, d, first)
        start = jnp.where(longer, at, start)
        longest = jnp.where(longer, length, longest)
        at = at + length
    for d in range(DOCS):
        info[0, d] = len_ref[0, lax.rem(first + d, DOCS)]
    info[0, DOCS] = start
    info[0, DOCS + 1] = lax.rem(ROW - start, ROW)
    turn = lax.rem(ROW - start, ROW)
    rank_out[...] = pltpu.roll(rank_ref[...], turn, 1)
    count_out[...] = pltpu.roll(count_ref[...], turn, 1)
    step_table(info, table)


def plan(unit_owner, lengths, rank_row, count_row, block):
    row = ((1, ROW), jnp.int32, "V")
    return call(partial(plan_kernel, block), "plan", [unit_owner.reshape(1, -1), lengths, rank_row, count_row], "VSVV",
                [((1, unit_owner.shape[0]), jnp.int32, "V"), row, row, ((2, STEPS), jnp.int32, "S"),
                 ((1, DOCS + 2), jnp.int32, "S")], [])


def turn_rows(source, target, shift):
    tiles = source.shape[0]
    whole, rest = lax.div(shift, UNIT), lax.rem(shift, UNIT)

    def one(i, carry):
        at = lax.rem(i + whole, tiles)
        both = jnp.concatenate([source[at].astype(F32), source[lax.rem(at + 1, tiles)].astype(F32)], 0)
        rows = pltpu.roll(both, lax.rem(2 * UNIT - rest, 2 * UNIT), 0)[:UNIT]
        target[pl.ds(pl.multiple_of(i * UNIT, UNIT), UNIT), :] = rows.astype(target.dtype)
        return carry
    lax.fori_loop(0, tiles, one, 0, unroll=4)


def in_tiles(value):
    return value.reshape(-1, UNIT, value.shape[1])


def project_kernel(devices, place_ref, info, master, norm_row, rank_ref, query_hbm, kv_hbm, memory_hbm, grad_hbm,
                   nq_out, nkv_out, qt_out, k_out, kt_out, v_out, vt_out, kc_out, kct_out, vc_out, vct_out,
                   query_out, kv_out, memory_out, grad_out,
                   ws_ref, wc_ref, wos_ref, woc_ref, w1_ref, w2_ref, norms, side_ref, hot_ref, rank_cols,
                   gathered, flat, stage_a, stage_b, query_ref, kv_ref, memory_ref, grad_ref, unit_q, unit_kv,
                   nq_ref, nkv_ref, qt_ref, k_ref, kt_ref, v_ref, vt_ref, kc_ref, kct_ref, vc_ref, vct_ref,
                   late_sems, turned_sems, out_sems, *line_sems):
    tokens, features = query_ref.shape
    units = place_ref.shape[1]
    late = Late([(query_hbm, stage_a), (kv_hbm, stage_b)], late_sems.at[0])
    held = (nq_ref, nkv_ref, qt_ref, k_ref, kt_ref, v_ref, vt_ref, kc_ref, kct_ref, vc_ref, vct_ref)
    out = Out(list(zip(held, (nq_out, nkv_out, qt_out, k_out, kt_out, v_out, vt_out, kc_out, kct_out, vc_out, vct_out))), out_sems)
    places = places_of(devices)
    me, x, y, z, xpeer, ypeer, order, ahead, behind = places
    slots = master.shape[0]
    block = slots + 1
    gathered[pl.ds(me * block, slots)] = master[...].astype(BF)
    gathered[me * block + slots] = jnp.broadcast_to(norm_row[...], (UNIT, features)).astype(BF)
    greet([{"dp": xpeer}, {"dp": ypeer}] + [{"dp": ahead(d)} for d in order])

    leaving = [(query_ref, query_out), (kv_ref, kv_out), (memory_ref, memory_out), (grad_ref, grad_out)]

    def leave(number):
        return pltpu.make_async_copy(*leaving[number], turned_sems.at[number])

    def turn(stage, number):
        turn_rows(stage, leaving[number][0], info[0, DOCS])
        leave(number).start()

    def first_turns():
        mask_tables(info, rank_ref, side_ref, hot_ref, rank_cols)
        late.wait(0, 1)
        turn(stage_a, 0)
        turn(stage_b, 1)

    def norms_of_streams():
        def units_of(step, rows):
            unit_q[rows, :] = normalise(query_ref[rows, :].astype(F32))[0]
            unit_kv[rows, :] = normalise(kv_ref[rows, :].astype(F32))[0]
        chunks(tokens, units_of)

    def last_turns():
        more = Late([(memory_hbm, stage_a), (grad_hbm, stage_b)], late_sems.at[1])
        more.wait(0, 1)
        turn(stage_a, 2)
        turn(stage_b, 3)
    LineGather(devices, lambda number, start, size: gathered.at[pl.ds(number * block + start, size)], block, block * 3 // 5,
               places, *line_sems).run(first_turns, norms_of_streams, last_turns)

    share = devices // 8
    vectors = []
    for number in range(8):
        pieces = [gathered[(number * share + i) * block + slots].astype(F32) for i in range(share)]
        total = pieces[0]
        for piece in pieces[1:]:
            total = total + piece
        vectors.append(total[0:1, :])
    norms[...] = jnp.concatenate(vectors, 0)

    def one_unit(u, carry):
        flat[pl.ds(pl.multiple_of(u * UNIT, UNIT), UNIT), :] = gathered[place_ref[0, u]]
        return carry
    lax.fori_loop(0, units, one_unit, 0, unroll=4)
    order = interleave(features)
    cols = v_ref.shape[1]
    for number in range(6):
        rows = flat[number * cols:(number + 1) * cols, :]
        stacked = jnp.concatenate([rows[:, :cols], rows[:, cols:]], 0)
        matrix = nn(order, stacked).astype(BF)
        if number < 3:
            ws_ref[number] = matrix
        else:
            wc_ref[number - 3] = matrix
    wos_ref[...] = flat[6 * cols:7 * cols, :]
    woc_ref[...] = flat[7 * cols:8 * cols, :]
    hidden = w2_ref.shape[0]
    for block in range(hidden // features):
        at = 8 * cols + block * features
        parted = part_rows(flat[at:at + features, :], order)
        half = features // 2
        w1_ref[block * half:(block + 1) * half, :] = jnp.concatenate([parted[:half], parted[half:]], 1)
    w2_ref[...] = flat[8 * cols + hidden:, :]

    def body(step, rows):
        nq = (unit_q[rows, :] * norms[0:1, :] + norms[1:2, :]).astype(BF)
        nkv = (unit_kv[rows, :] * norms[2:3, :] + norms[3:4, :]).astype(BF)
        source = memory_ref[rows, :]
        low = lambda left, right: nn(left, right).astype(BF)
        k, v, kc, vc = low(nkv, ws_ref[1]), low(nkv, ws_ref[2]), low(source, wc_ref[1]), low(source, wc_ref[2])
        results = [nq, nkv, low(nq, ws_ref[0]).T, k, k.T, v, v.T, kc, kc.T, vc, vc.T]
        for i, (ref, result) in enumerate(zip(held, results)):
            if ref.shape[0] < ref.shape[1]:
                ref[:, rows] = result
            else:
                ref[rows, :] = result
            out.start(i, step)
    chunks(tokens, body)
    out.drain(tokens)
    for number in range(4):
        leave(number).wait()


def pair_sems(tokens):
    return pltpu.SemaphoreType.DMA((2, tokens // CHUNK))


def out_semaphores(count, tokens):
    return pltpu.SemaphoreType.DMA((count, tokens // CHUNK))


def project(devices, place_of, info, master, norm_row, rank_row, query_stream, kv_stream, memory, out_grad, cols, hidden):
    tokens, features = query_stream.shape
    wide, narrow, across = (tokens, features), (tokens, cols), (cols, tokens)
    shapes = [wide, wide, across] + [narrow, across] * 4
    outs = [(shape, BF, "A") for shape in shapes] + [(wide, BF, "A")] * 4 + [
        ((3, features, cols), BF, "V"), ((3, features, cols), BF, "V"), ((cols, features), BF, "V"), ((cols, features), BF, "V"),
        ((features, hidden), BF, "V"), ((hidden, features), BF, "V"), ((8, features), F32, "V"),
        ((ROW, 128), BF, "V"), ((128, ROW), BF, "V"), ((ROW, 128), F32, "V")]
    D = pltpu.SemaphoreType.DMA
    streams = [in_tiles(stream) for stream in (query_stream, kv_stream, memory, out_grad)]
    scratch = [pltpu.VMEM((devices * (master.shape[0] + 1), UNIT, features), BF), pltpu.VMEM((8 * cols + 2 * hidden, features), BF)]
    scratch += [pltpu.VMEM(streams[0].shape, BF)] * 2 + [pltpu.VMEM(wide, BF)] * 4 + [pltpu.VMEM(wide, F32)] * 2
    scratch += [pltpu.VMEM(shape, BF) for shape in shapes]
    scratch += [D((2, 2)), D((4,)), out_semaphores(len(shapes), tokens)] + [D((2, 2, devices // 4 + 1))] * 6
    return call(partial(project_kernel, devices), "project",
                [place_of, info, master, norm_row, rank_row] + streams, "SSVVVAAAA", outs, scratch, 0)


def self_out_kernel(mixed, wo, query_hbm, wc, norms, res_out, nc_out, q_out,
                    query, res_ref, nc_ref, q_ref, mine, theirs, sems, late_sems, out_sems):
    tokens = query.shape[0]
    late = Late([(query_hbm, query)], late_sems)
    out = Out([(res_ref, res_out), (nc_ref, nc_out), (q_ref, q_out)], out_sems)
    greet_core()

    def give(step, rows):
        mine[rows, :] = nn(mixed[rows, :], wo[...]).astype(BF)
        other_core(mine, theirs, sems, step).start()
    chunks(tokens, give)
    late.wait(0)

    def take(step, rows):
        other_core(mine, theirs, sems, step).wait_recv()
        res = query[rows, :].astype(F32) + (mine[rows, :].astype(F32) + theirs[rows, :].astype(F32))
        res_ref[rows, :] = res
        out.start(0, step)
        nc = (normalise(res)[0] * norms[4:5, :] + norms[5:6, :]).astype(BF)
        nc_ref[rows, :] = nc
        out.start(1, step)
        q_ref[:, rows] = nn(nc, wc[0]).astype(BF).T
        out.start(2, step)
    chunks(tokens, take)
    drain(tokens, mine, theirs, sems)
    out.drain(tokens)


def self_out(mixed, wo, query, wc, norms):
    tokens, features = query.shape
    wide = (tokens, features)
    across = (mixed.shape[1], tokens)
    outs = [(wide, F32, "A"), (wide, BF, "A"), (across, BF, "A")]
    scratch = [pltpu.VMEM(wide, BF), pltpu.VMEM(wide, F32), pltpu.VMEM(wide, BF), pltpu.VMEM(across, BF),
               pltpu.VMEM(wide, BF), pltpu.VMEM(wide, BF), pair_sems(tokens), pltpu.SemaphoreType.DMA((1,)),
               out_semaphores(3, tokens)]
    return call(self_out_kernel, "self_out", [mixed, wo, query, wc, norms], "VVAVV", outs, scratch, 2)


def gelu_parts(value):
    bell = jnp.exp2(value * value * (-0.5 * 1.4426950408889634))
    base = 1.0 + (0.3275911 * 0.7071067811865476) * jnp.abs(value)
    t = pl.reciprocal(base, approx=True)
    t = t * (2.0 - base * t)
    poly = ((((0.5307027145 * t - 0.7265760135) * t + 0.7107068705) * t - 0.142248368) * t + 0.127414796) * t
    tail = poly * bell
    below = jnp.where(value < 0.0, tail, 1.0 - tail)
    return value * below, below + value * (bell * 0.3989422804014327)


def spread_flat(devices, places, flat, refs):
    rows = flat.shape[0] // devices
    for f, ref in enumerate(refs):
        place = plane_offset(places, f)
        for level in range(devices // 4):
            ref[level, ref.shape[1] - rows:, :] = flat[pl.ds(pl.multiple_of((level * 4 + place) * rows, UNIT), rows), :]


def feed_forward_kernel(devices, mixed, wo, res_hbm, w1, w2, out_grad_hbm, norms,
                        out_out, gres_out, gmix_out, part0, part1, part2, part3, sums_ref,
                        res, out_grad, out_ref, gres_ref, gmix_ref, flat,
                        mine, theirs, nf_all, hid_all, pre_all, low_all, mine_o, theirs_o, mine_g, theirs_g,
                        sems, sems_o, sems_g, late_sems, out_sems):
    tokens, features = out_grad.shape
    hidden = w2.shape[0]
    places = places_of(devices)
    late = Late([(res_hbm, res), (out_grad_hbm, out_grad)], late_sems)
    out = Out([(out_ref, out_out), (gres_ref, gres_out), (gmix_ref, gmix_out)], out_sems)
    greet_core()

    def give(step, rows):
        mine[rows, :] = nn(mixed[rows, :], wo[...]).astype(BF)
        other_core(mine, theirs, sems, step).start()
    chunks(tokens, give)
    late.wait(0, 1)

    def middle(step, rows):
        other_core(mine, theirs, sems, step).wait_recv()
        value = res[rows, :] + (mine[rows, :].astype(F32) + theirs[rows, :].astype(F32))
        gres_ref[rows, :] = value
        nf = (normalise(value)[0] * norms[6:7, :] + norms[7:8, :]).astype(BF)
        nf_all[rows, :] = nf
        grad = out_grad[rows, :]
        out_part = jnp.zeros((CHUNK, features), F32)
        grad_part = jnp.zeros((CHUNK, features), F32)
        for block in range(hidden // 256):
            at = slice(block * 256, (block + 1) * 256)
            act, slope = gelu_parts(nn(nf, w1[:, at]))
            act = act.astype(BF)
            hid_all[rows, at] = act
            pre = (slope * nt(grad, w2[at, :])).astype(BF)
            pre_all[rows, at] = pre
            out_part = out_part + nn(act, w2[at, :])
            grad_part = grad_part + nt(pre, w1[:, at])
        mine_o[rows, :] = out_part.astype(BF)
        other_core(mine_o, theirs_o, sems_o, step).start()
        mine_g[rows, :] = grad_part.astype(BF)
        other_core(mine_g, theirs_g, sems_g, step).start()
    chunks(tokens, middle)

    order = interleave(features)
    half, cols = features // 2, mixed.shape[1]
    for block in range(hidden // 256):
        at = slice(block * 256, (block + 1) * 256)
        flat[cols + hidden + block * 256:cols + hidden + (block + 1) * 256, :] = tn(hid_all[:, at], out_grad[...]).astype(BF)
    for block in range(hidden // features):
        gradient = tn(nf_all[:, block * half:(block + 1) * half], pre_all[...]).astype(BF)
        stacked = jnp.concatenate([gradient[:, :features], gradient[:, features:]], 0)
        flat[cols + block * features:cols + (block + 1) * features, :] = nn(order, stacked).astype(BF)
    sums_ref[...] = jnp.zeros_like(sums_ref)

    def close(step, rows):
        other_core(mine_o, theirs_o, sems_o, step).wait_recv()
        other_core(mine_g, theirs_g, sems_g, step).wait_recv()
        value = gres_ref[rows, :]
        out_ref[rows, :] = (value + (mine_o[rows, :].astype(F32) + theirs_o[rows, :].astype(F32))).astype(BF)
        out.start(0, step)
        grad = mine_g[rows, :].astype(F32) + theirs_g[rows, :].astype(F32)
        unit, scale = normalise(value)
        gres = norm_back(unit, scale, norms[6:7, :], grad) + out_grad[rows, :].astype(F32)
        gres_ref[rows, :] = gres
        out.start(1, step)
        sums_ref[0:8, :] += fold_rows(grad * unit)
        sums_ref[8:16, :] += fold_rows(grad)
        low = gres.astype(BF)
        low_all[rows, :] = low
        gmix_ref[:, rows] = nt(low, wo[...]).astype(BF).T
        out.start(2, step)
    chunks(tokens, close)
    flat[0:cols, :] = tn(mixed[...], low_all[...]).astype(BF)
    if flat.shape[0] > cols + 2 * hidden:
        flat[cols + 2 * hidden:, :] = jnp.zeros((flat.shape[0] - cols - 2 * hidden, features), BF)
    spread_flat(devices, places, flat, (part0, part1, part2, part3))
    out.drain(tokens)
    drain(tokens, mine, theirs, sems)
    drain(tokens, mine_o, theirs_o, sems_o)
    drain(tokens, mine_g, theirs_g, sems_g)


def whole_blocks(rows, devices):
    return -(-rows // (devices * UNIT)) * devices * UNIT


def feed_forward(devices, mixed, wo, res, w1, w2, out_grad, norms):
    tokens, features = out_grad.shape
    hidden = w2.shape[0]
    flat_rows = whole_blocks(wo.shape[0] + 2 * hidden, devices)
    part = ((devices // 4, flat_rows // devices, features), BF, "V")
    wide = (tokens, features)
    across = (mixed.shape[1], tokens)
    outs = [(wide, BF, "A"), (wide, F32, "A"), (across, BF, "A")] + [part] * 4 + [((16, features), F32, "V")]
    deep, narrow = pltpu.VMEM((tokens, hidden), BF), pltpu.VMEM(wide, BF)
    scratch = [pltpu.VMEM(wide, F32), narrow, narrow, pltpu.VMEM(wide, F32), pltpu.VMEM(across, BF),
               pltpu.VMEM((flat_rows, features), BF), narrow, narrow, narrow, deep, deep, narrow] + [narrow] * 4
    scratch += [pair_sems(tokens)] * 3 + [pltpu.SemaphoreType.DMA((2,)), out_semaphores(3, tokens)]
    return call(partial(feed_forward_kernel, devices), "feed_forward", [mixed, wo, res, w1, w2, out_grad, norms], "VVAVVAV",
                outs, scratch, 3)


def branch_give(dq, dk, dv, weights, mine_a, theirs_a, mine_b, theirs_b, sems_a, sems_b):
    def give(step, rows):
        mine_a[rows, :] = nt(dq[rows, :], weights[0]).astype(BF)
        other_core(mine_a, theirs_a, sems_a, step).start()
        mine_b[rows, :] = (nt(dk[rows, :], weights[1]) + nt(dv[rows, :], weights[2])).astype(BF)
        other_core(mine_b, theirs_b, sems_b, step).start()
    chunks(dq.shape[0], give)


def branch_weights(first_in, second_in, dq, dk, dv, flat):
    cols = dq.shape[1]
    order = interleave(first_in.shape[1])
    for number, (entering, grad) in enumerate(((first_in, dq), (second_in, dk), (second_in, dv))):
        flat[number * cols:(number + 1) * cols, :] = as_units(tn(entering[...], grad[...]), order)


def z_sum_start(devices, places, pieces, landed, sems):
    me, x, y, z, xpeer, ypeer, order, ahead, behind = places
    return [send(pieces.at[lax.rem(z + d, devices // 4)], landed.at[d], sems.at[0, d], sems.at[1, d], dp=ahead(d)) for d in order]


def z_sum_end(places, pieces, landed, copies):
    z, order = places[3], places[6]
    total = pieces[z].astype(F32)
    for copy, d in zip(copies, order):
        copy.wait_recv()
        total = total + landed[d].astype(F32)
    return total.astype(BF)


def four_sum(parts, at):
    return (parts[0][at].astype(F32) + parts[1][at].astype(F32) + parts[2][at].astype(F32) + parts[3][at].astype(F32)).astype(BF)


def cross_back_kernel(devices, info, dq, dk, dv, wc, nc_hbm, memory_hbm, res_hbm, gres_hbm, output_hbm, mixed, wo, norms,
                      part0, part1, part2, part3,
                      gmem_out, output_out, gnew_out, gmix_out, give0, give1, give2, give3, sums_ref,
                      nc, memory, res, gres, output_ref, gmem_ref, turned_a, turned_b, gnew_ref, gmix_ref, flat, pieces, landed, blocks,
                      mine_a, theirs_a, mine_b, theirs_b, low_all, sems_a, sems_b, late_sems, out_sems, turned_sems, z_sems, zz_sems):
    tokens, features = nc.shape
    cols = dq.shape[1]
    across = devices // 4
    places = places_of(devices)
    me, x, y, z, xpeer, ypeer, order, ahead, behind = places
    late = Late([(nc_hbm, nc), (memory_hbm, memory), (res_hbm, res), (gres_hbm, gres), (output_hbm, output_ref)], late_sems)
    out = Out([(gnew_ref, gnew_out), (gmix_ref, gmix_out)], out_sems)
    for level in range(across):
        pieces[level] = four_sum((part0, part1, part2, part3), level)
    greet([{"head": 1 - lax.axis_index("head")}] + [{"dp": ahead(d)} for d in order])
    z_copies = z_sum_start(devices, places, pieces, landed, z_sems)
    branch_give(dq, dk, dv, wc, mine_a, theirs_a, mine_b, theirs_b, sems_a, sems_b)
    late.wait(0, 1)
    branch_weights(nc, memory, dq, dk, dv, flat)
    blocks[0] = z_sum_end(places, pieces, landed, z_copies)
    zz_copies = [send(blocks.at[0], blocks.at[d], zz_sems.at[0, d], zz_sems.at[1, d], dp=ahead(d)) for d in order]
    sums_ref[...] = jnp.zeros_like(sums_ref)
    late.wait(2, 3)

    def close(step, rows):
        other_core(mine_a, theirs_a, sems_a, step).wait_recv()
        grad = mine_a[rows, :].astype(F32) + theirs_a[rows, :].astype(F32)
        unit, scale = normalise(res[rows, :])
        gnew = norm_back(unit, scale, norms[4:5, :], grad) + gres[rows, :]
        gnew_ref[rows, :] = gnew
        out.start(0, step)
        sums_ref[0:8, :] += fold_rows(grad * unit)
        sums_ref[8:16, :] += fold_rows(grad)
        low = gnew.astype(BF)
        low_all[rows, :] = low
        gmix_ref[:, rows] = nt(low, wo[...]).astype(BF).T
        out.start(1, step)
        other_core(mine_b, theirs_b, sems_b, step).wait_recv()
        total = (mine_b[rows, :].astype(F32) + theirs_b[rows, :].astype(F32)).astype(BF)
        gmem_ref[pl.ds(step * (CHUNK // UNIT), CHUNK // UNIT)] = in_tiles(total)
    chunks(tokens, close)
    flat[3 * cols:4 * cols, :] = tn(mixed[...], low_all[...]).astype(BF)
    if flat.shape[0] > 4 * cols:
        flat[4 * cols:, :] = jnp.zeros((flat.shape[0] - 4 * cols, features), BF)
    gives = (give0, give1, give2, give3)
    spread_flat(devices, places, flat, gives)
    late.wait(4)
    turn_rows(gmem_ref, turned_a, info[0, DOCS + 1])
    turn_rows(output_ref, turned_b, info[0, DOCS + 1])
    turned = Late([(turned_a, gmem_out), (turned_b, output_out)], turned_sems)
    for copy in zz_copies:
        copy.wait_recv()
    ready_rows = blocks.shape[1]
    for ref in gives:
        for d in range(across):
            ref[d, 0:ready_rows, :] = blocks[d]
    for copy in z_copies + zz_copies:
        copy.wait_send()
    turned.wait(0, 1)
    out.drain(tokens)
    drain(tokens, mine_a, theirs_a, sems_a)
    drain(tokens, mine_b, theirs_b, sems_b)


def cross_back(devices, info, dq, dk, dv, wc, nc, memory, res, gres, output, mixed, wo, norms, parts):
    tokens, features = nc.shape
    cols = dq.shape[1]
    across, ready_rows = devices // 4, parts[0].shape[1]
    flat_rows = whole_blocks(4 * cols, devices)
    give = ((across, ready_rows + flat_rows // devices, features), BF, "V")
    wide = (tokens, features)
    outs = [(wide, BF, "A"), (wide, BF, "A"), (wide, F32, "A"), ((cols, tokens), BF, "A")] + [give] * 4 + [((16, features), F32, "V")]
    low, high = pltpu.VMEM(wide, BF), pltpu.VMEM(wide, F32)
    small = pltpu.VMEM((across, ready_rows, features), BF)
    z_sems = pltpu.SemaphoreType.DMA((2, across))
    tiles = pltpu.VMEM((tokens // UNIT, UNIT, features), BF)
    scratch = [low, low, high, high, tiles, tiles, low, low, high, pltpu.VMEM((cols, tokens), BF), pltpu.VMEM((flat_rows, features), BF), small, small, small]
    scratch += [low] * 5 + [pair_sems(tokens)] * 2 + [pltpu.SemaphoreType.DMA((5,)), out_semaphores(2, tokens), pltpu.SemaphoreType.DMA((2,)), z_sems, z_sems]
    return call(partial(cross_back_kernel, devices), "cross_back",
                [info, dq, dk, dv, wc, nc, memory, res, gres, in_tiles(output), mixed, wo, norms] + parts, "SVVVVAAAAAVVVVVVV", outs, scratch, 4)


def self_back_kernel(devices, ready_rows, info, dq, dk, dv, ws, nq_hbm, nkv_hbm, query_hbm, kv_hbm, gres_hbm, norms, sums_c, sums_f,
                     part0, part1, part2, part3,
                     gquery_out, gkv_out, last_ref, more_ref, gnorm_ref,
                     nq, nkv, query, kv, gres, gquery_ref, gkv_ref, turned_a, turned_b, flat, source, landing, pieces, landed, more_pieces, more_landed,
                     norm_mine, norm_all, mine_a, theirs_a, mine_b, theirs_b, sums, sems_a, sems_b, late_sems, out_sems,
                     z_sems, more_z_sems, plane_sems, n_sems, *spread_sems):
    tokens, features = nq.shape
    across = devices // 4
    places = places_of(devices)
    me, x, y, z, xpeer, ypeer, order, ahead, behind = places
    late = Late([(nq_hbm, nq), (nkv_hbm, nkv), (query_hbm, query), (kv_hbm, kv), (gres_hbm, gres)], late_sems)
    more_rows = more_ref.shape[2]
    for level in range(across):
        more_pieces[level] = four_sum((part0, part1, part2, part3), (level, pl.ds(ready_rows, more_rows)))
    others = [lax.rem(me + d, devices) for d in range(1, devices)]
    greet([{"head": 1 - lax.axis_index("head")}] + [{"dp": other} for other in others])
    more_copies = z_sum_start(devices, places, more_pieces, more_landed, more_z_sems)
    branch_give(dq, dk, dv, ws, mine_a, theirs_a, mine_b, theirs_b, sems_a, sems_b)
    late.wait(0, 1)
    branch_weights(nq, nkv, dq, dk, dv, flat)
    if flat.shape[0] > 3 * dq.shape[1]:
        flat[3 * dq.shape[1]:, :] = jnp.zeros((flat.shape[0] - 3 * dq.shape[1], features), BF)
    spread_flat(devices, places, flat, [source.at[f] for f in range(4)])
    plane_copies = [send(source.at[f], landing.at[f], plane_sems.at[0, f], plane_sems.at[1, f], dp=peer)
                    for f, peer in ((3, me + 3 - 2 * x - 4 * y), (1, xpeer), (2, ypeer))]
    more_ref[0, 0] = z_sum_end(places, more_pieces, more_landed, more_copies)
    more = Spread(places, more_ref, *spread_sems[:5])
    more.start()
    sums[...] = jnp.zeros_like(sums)
    late.wait(2, 3, 4)

    def close(step, rows):
        other_core(mine_a, theirs_a, sems_a, step).wait_recv()
        grad = mine_a[rows, :].astype(F32) + theirs_a[rows, :].astype(F32)
        unit, scale = normalise(query[rows, :].astype(F32))
        tiles = pl.ds(step * (CHUNK // UNIT), CHUNK // UNIT)
        gquery_ref[tiles] = in_tiles((norm_back(unit, scale, norms[0:1, :], grad) + gres[rows, :]).astype(BF))
        sums[0:8, :] += fold_rows(grad * unit)
        sums[8:16, :] += fold_rows(grad)
        other_core(mine_b, theirs_b, sems_b, step).wait_recv()
        grad = mine_b[rows, :].astype(F32) + theirs_b[rows, :].astype(F32)
        unit, scale = normalise(kv[rows, :].astype(F32))
        gkv_ref[tiles] = in_tiles(norm_back(unit, scale, norms[2:3, :], grad).astype(BF))
        sums[16:24, :] += fold_rows(grad * unit)
        sums[24:32, :] += fold_rows(grad)
    middle = tokens // 2
    chunks(middle, close)
    more.relay()
    chunks(tokens, close, middle)
    parts = [sums[8 * i:8 * i + 8, :] for i in range(4)]
    parts += [sums_c[0:8, :], sums_c[8:16, :], sums_f[0:8, :], sums_f[8:16, :]]
    norm_mine[...] = jnp.concatenate([jnp.sum(part, 0, keepdims=True) for part in parts], 0)
    for copy in plane_copies:
        copy.wait_recv()
    for level in range(across):
        pieces[level] = four_sum((source.at[0], landing.at[1], landing.at[2], landing.at[3]), level)
    z_copies = z_sum_start(devices, places, pieces, landed, z_sems)
    n_copies = [send(norm_mine, norm_all.at[d], n_sems.at[0, d], n_sems.at[1, d], dp=other)
                for d, other in zip(range(1, devices), others)]
    turn_rows(gquery_ref, turned_a, info[0, DOCS + 1])
    more.diagonal()
    last_ref[0, 0] = z_sum_end(places, pieces, landed, z_copies)
    last = Spread(places, last_ref, *spread_sems[5:])
    last.start()
    turn_rows(gkv_ref, turned_b, info[0, DOCS + 1])
    turned = Late([(turned_a, gquery_out), (turned_b, gkv_out)], out_sems)
    last.relay()
    last.diagonal()
    total = norm_mine[...]
    for d, copy in zip(range(1, devices), n_copies):
        copy.wait_recv()
        total = total + norm_all[d]
    gnorm_ref[...] = total
    more.finish()
    last.finish()
    more.drain()
    last.drain()
    for copy in more_copies + plane_copies + z_copies + n_copies:
        copy.wait_send()
    turned.wait(0, 1)
    drain(tokens, mine_a, theirs_a, sems_a)
    drain(tokens, mine_b, theirs_b, sems_b)


def self_back(devices, ready_rows, info, dq, dk, dv, ws, nq, nkv, query, kv, gres, norms, sums_c, sums_f, parts):
    tokens, features = nq.shape
    cols = dq.shape[1]
    across, more_rows = devices // 4, parts[0].shape[1] - ready_rows
    flat_rows = whole_blocks(3 * cols, devices)
    rows = flat_rows // devices
    wide = (tokens, features)
    outs = [(wide, BF, "A"), (wide, BF, "A"), ((4, across, rows, features), BF, "V"), ((4, across, more_rows, features), BF, "V"),
            ((8, features), F32, "V")]
    low, high = pltpu.VMEM(wide, BF), pltpu.VMEM(wide, F32)
    small, tiny = pltpu.VMEM((across, more_rows, features), BF), pltpu.VMEM((across, rows, features), BF)
    four = pltpu.VMEM((4, across, rows, features), BF)
    D = pltpu.SemaphoreType.DMA
    tiles = pltpu.VMEM((tokens // UNIT, UNIT, features), BF)
    scratch = [low, low, low, low, high, tiles, tiles, low, low, pltpu.VMEM((flat_rows, features), BF), four, four, tiny, tiny, small, small,
               pltpu.VMEM((8, features), F32), pltpu.VMEM((devices, 8, features), F32)]
    scratch += [low] * 4 + [pltpu.VMEM((32, features), F32)] + [pair_sems(tokens)] * 2
    scratch += [D((5,)), D((2,)), D((2, across)), D((2, across)), D((2, 4)), D((2, devices))]
    scratch += [D((2, across))] * 10
    return call(partial(self_back_kernel, devices, ready_rows), "self_back",
                [info, dq, dk, dv, ws, nq, nkv, query, kv, gres, norms, sums_c, sums_f] + parts, "SVVVVAAAAAVVVVVVV", outs, scratch, 5)


def update_kernel(devices, early_unit, late_unit, late_rows, owner_ref, me_ref, last, more, part0, part1, part2, part3,
                  master_hbm, first_hbm, second_hbm, gquery_in, gkv_in,
                  grad_out, first_out, second_out, new_out, gquery_out, gkv_out,
                  held, taken, master, first, second, held_q, held_kv, grad_ref, first_ref, second_ref, new_ref, sems, out_sems):
    units = owner_ref.shape[0]
    slots = master.shape[0]
    across = devices // 4
    me = me_ref[0]
    here, level = lax.rem(me, 4), lax.div(me, 4)
    entering = Late([(master_hbm, master), (first_hbm, first), (second_hbm, second), (gquery_in, held_q), (gkv_in, held_kv)], sems)
    results = list(zip((grad_ref, first_ref, second_ref, new_ref), (grad_out, first_out, second_out, new_out)))

    def find(u, count):
        held[count] = u
        return count + (owner_ref[u] == me).astype(jnp.int32)
    count = lax.fori_loop(0, units, find, jnp.int32(0), unroll=4)
    entering.wait(3, 4)
    leaving = Late([(held_q, gquery_out), (held_kv, gkv_out)], out_sems.at[0])
    entering.wait(0, 1, 2)

    def lookup(row, size):
        block = lax.div(row, size)
        behind = lax.rem(level - lax.div(block, 4) + across, across)
        return lax.rem(block, 4) ^ here, behind, pl.ds(pl.multiple_of(lax.rem(row, size), UNIT), UNIT)

    def one(slot, carry):
        @pl.when(slot < count)
        def _():
            unit = held[slot]

            @pl.when(unit < early_unit)
            def _():
                taken[...] = last[lookup(unit * UNIT, last.shape[2])]

            @pl.when((unit >= early_unit) & (unit < late_unit))
            def _():
                taken[...] = more[lookup((unit - early_unit) * UNIT, more.shape[2])]

            @pl.when(unit >= late_unit)
            def _():
                offset, behind, rows = lookup((unit - late_unit) * UNIT, late_rows)
                for f, part in enumerate((part0, part1, part2, part3)):
                    @pl.when(offset == f)
                    def _():
                        taken[...] = part[behind, rows]
            gradient = taken[...].astype(F32)
            first_new, second_new, weight = adamw_step(gradient, first[slot], second[slot], master[slot], RATE_MATRIX, WEIGHT_DECAY)
            grad_ref[slot] = gradient
            first_ref[slot] = first_new
            second_ref[slot] = second_new
            new_ref[slot] = weight

        @pl.when(slot >= count)
        def _():
            for ref in (grad_ref, first_ref, second_ref, new_ref):
                ref[slot] = jnp.zeros(ref.shape[1:], F32)
        return carry
    half = slots // 2
    lax.fori_loop(0, half, one, 0)
    early = Late([(ref.at[pl.ds(0, half)], out.at[pl.ds(0, half)]) for ref, out in results], out_sems.at[1])
    lax.fori_loop(half, slots, one, 0)
    rest = Late([(ref.at[pl.ds(half, half)], out.at[pl.ds(half, half)]) for ref, out in results], out_sems.at[2])
    for copies in (early, rest):
        copies.wait(*range(4))
    leaving.wait(0, 1)


def update(devices, early_unit, late_unit, late_rows, unit_owner, me, last, more, parts, master, first, second, gquery, gkv):
    outs = [(master.shape, F32, "A")] * 4 + [(gquery.shape, BF, "A")] * 2
    kernel = partial(update_kernel, devices, early_unit, late_unit, late_rows)
    owned = pltpu.VMEM(master.shape, F32)
    return call(kernel, "update", [unit_owner, me, last, more] + parts + [master, first, second, gquery, gkv], "SSVVVVVVAAAAA", outs,
                [pltpu.SMEM((unit_owner.shape[0] + 8,), jnp.int32), pltpu.VMEM((UNIT, master.shape[2]), BF), owned, owned, owned,
                 pltpu.VMEM(gquery.shape, BF), pltpu.VMEM(gkv.shape, BF), owned, owned, owned, owned,
                 pltpu.SemaphoreType.DMA((5,)), pltpu.SemaphoreType.DMA((3, 4))])


def adamw_step(gradient, first, second, weight, rate, decay):
    first_new = BETA_ONE * first + (1.0 - BETA_ONE) * gradient
    second_new = BETA_TWO * second + (1.0 - BETA_TWO) * gradient * gradient
    corr_one = 1.0 - BETA_ONE**STEP
    corr_two = 1.0 - BETA_TWO**STEP
    direction = first_new / corr_one / (jnp.sqrt(second_new / corr_two) + ADAM_EPS)
    return (first_new, second_new, weight - rate * (direction + decay * weight))


def local(
    query_stream, kv_stream, memory, out_grad, lengths, obs_rank, obs_count, unit_owner,
    master, first_moment, second_moment, norm_master, norm_first, norm_second,
):
    devices = lax.axis_size("dp")
    shards = lax.axis_size("head")
    me = lax.axis_index("dp")
    slots, unit_rows, features = master.shape[0], master.shape[2], master.shape[3]
    units = unit_owner.shape[0]
    norm_share = norm_master.shape[0]
    cols = features // shards
    hidden = (units * unit_rows - 8 * cols) // 2

    shape = (slots, unit_rows, features)
    norm_row = lax.dynamic_update_slice(
        jnp.zeros((1, features), F32), norm_master.reshape(1, norm_share), (0, lax.rem(me * norm_share, features)))
    rank_row, count_row = obs_rank.reshape(1, ROW), obs_count.reshape(1, ROW)
    place_of, rank_row, count_row, steps, info = plan(unit_owner, lengths, rank_row, count_row, slots + 1)
    nq, nkv, qt, k, kt, v, vt, kc, kct, vc, vct, query, kv, source, cotangent, ws, wc, wo_self, wo_cross, w1, w2, norms, *tables = project(
        devices, place_of, info, master.reshape(shape), norm_row, rank_row, query_stream, kv_stream, memory, out_grad, cols, hidden)
    mixed_self, mixed_self_t, total_self = attend_forward(steps, qt, k, vt, tables, count_row, True)
    residual, nc, qct = self_out(mixed_self, wo_self, query, wc, norms)
    mixed_cross, mixed_cross_t, total_cross = attend_forward(steps, qct, kc, vct, tables, count_row, False)
    output, grad_cross_res, grad_mixed, *parts, sums_f = feed_forward(
        devices, mixed_cross, wo_cross, residual, w1, w2, cotangent, norms)
    tie = lax.optimization_barrier
    ready_rows = parts[0].shape[1]
    parts = [parts[0]] + [plane_swap(parts[f], devices, f) for f in (1, 2, 3)]
    dq, dk, dv = attend_backward(steps, qct, kc, kct, vc, grad_mixed, mixed_cross_t, total_cross, tables, count_row, [], False)
    parts, dq = tie((parts, dq))
    grad_memory, output, grad_residual, grad_mixed, *parts, sums_c = cross_back(
        devices, info, dq, dk, dv, wc, nc, source, residual, grad_cross_res, output, mixed_self, wo_self, norms, parts)
    parts = [parts[0]] + [plane_swap(parts[f], devices, f) for f in (1, 2, 3)]
    dq, dk, dv, grad_memory, output = attend_backward(
        steps, qt, k, kt, v, grad_mixed, mixed_self_t, total_self, tables, count_row, [grad_memory, output], True)
    parts, dq = tie((parts, dq))
    grad_query, grad_kv, last, more, norm_grads = self_back(
        devices, ready_rows, info, dq, dk, dv, ws, nq, nkv, query, kv, grad_residual, norms, sums_c, sums_f, parts)

    early, late = 3 * cols // unit_rows, 7 * cols // unit_rows
    weight_grad, weight_first, weight_second, weight_new, grad_query, grad_kv = update(
        devices, early, late, ready_rows, unit_owner, me.reshape(1), last, more, parts, master.reshape(shape),
        first_moment.reshape(shape), second_moment.reshape(shape), grad_query, grad_kv)
    weight_grad, weight_first, weight_second, weight_new = [
        part.reshape(master.shape) for part in (weight_grad, weight_first, weight_second, weight_new)]
    norm_grad = lax.dynamic_slice_in_dim(norm_grads.reshape(-1), me * norm_share, norm_share)
    norm_first_new, norm_second_new, norm_new = adamw_step(
        norm_grad, norm_first, norm_second, norm_master, RATE_NORM, 0.0)
    return (
        output, grad_query, grad_kv, grad_memory, weight_grad, weight_first, weight_second, weight_new,
        norm_grad, norm_first_new, norm_second_new, norm_new,
    )


def solution(mesh):
    in_specs = (
        P("dp", None),
        P("dp", None),
        P("dp", None),
        P("dp", None),
        P("dp", None),
        P("dp"),
        P("dp"),
        P(),
        P("dp", "head", None, None),
        P("dp", "head", None, None),
        P("dp", "head", None, None),
        P("dp"),
        P("dp"),
        P("dp"),
    )
    out_specs = (
        P("dp", None),
        P("dp", None),
        P("dp", None),
        P("dp", None),
        P("dp", "head", None, None),
        P("dp", "head", None, None),
        P("dp", "head", None, None),
        P("dp", "head", None, None),
        P("dp"),
        P("dp"),
        P("dp"),
        P("dp"),
    )
    return jax.shard_map(local, mesh=mesh, in_specs=in_specs, out_specs=out_specs, check_vma=False)
```

```python
from functools import partial

import jax
import jax.numpy as jnp
from jax import lax
from jax.experimental import pallas as pl
from jax.experimental.pallas import tpu as pltpu
from jax.sharding import PartitionSpec as P

HEAD_DIM = 64
ROW = 2048
DOCS = 32
STEP = 10
UNIT = 16

EPS_NORM = 1e-05
ADAM_EPS = 1e-08
BETA_ONE = 0.5
BETA_TWO = 0.5
RATE_MATRIX = 0.1
RATE_NORM = 0.3
WEIGHT_DECAY = 0.01

F32 = jnp.float32
BF = jnp.bfloat16
TQ = 256
TK = 512
FAR = 32768.0
LANES = (64, 72, 80)


def nt(a, b):
    return lax.dot_general(a, b, (((1,), (1,)), ((), ())), preferred_element_type=F32)


def nn(a, b):
    return lax.dot_general(a, b, (((1,), (0,)), ((), ())), preferred_element_type=F32)


def doc_bounds(len_ref):
    starts, ends = [], []
    at = jnp.int32(0)
    for d in range(DOCS):
        starts.append(at)
        at = at + len_ref[0, d]
        ends.append(at)
    return starts, ends


def key_range(starts, ends, q0):
    low = jnp.int32(0)
    high = jnp.int32(0)
    for d in range(DOCS):
        low = jnp.where(starts[d] <= q0, starts[d], low)
        high = jnp.where(starts[d] <= q0 + TQ - 1, ends[d], high)
    first = lax.div(low, 128) * 128
    steps = lax.div(high - first + TK - 1, TK)
    return first, steps


def mask_tables(len_ref, rank_ref, side_ref, hot_ref, rank_cols):
    starts, ends = doc_bounds(len_ref)
    lanes = lax.broadcasted_iota(jnp.int32, (1, 128), 1)
    start_lane = jnp.full((1, 128), -1, jnp.int32)
    end_lane = jnp.full((1, 128), -1, jnp.int32)
    for d in range(DOCS):
        start_lane = jnp.where(lanes == d, starts[d], start_lane)
        end_lane = jnp.where(lanes == d, ends[d], end_lane)
    one = (lanes == LANES[0]) | (lanes == LANES[1]) | (lanes == LANES[2])
    for t in range(ROW // 256):
        pos = lax.broadcasted_iota(jnp.int32, (256, 128), 0) + t * 256
        hot = (pos >= start_lane) & (pos < end_lane)
        side = jnp.where(hot | (lanes >= DOCS), jnp.where(one, -1.0, 0.0), -FAR)
        side_ref[t * 256:(t + 1) * 256, :] = side.astype(BF)
    pos = lax.broadcasted_iota(jnp.int32, (1, ROW), 1)
    first = jnp.zeros((1, ROW), jnp.bool_)
    rows = []
    for d in range(DOCS):
        first = first | (pos == starts[d])
        rows.append(jnp.where((pos >= starts[d]) & (pos < ends[d]), FAR, 0.0))
    hot_ref[...] = jnp.concatenate(rows + [jnp.zeros((128 - DOCS, ROW), F32)], 0).astype(BF)
    rank = jnp.where(first, -1.0, rank_ref[...].astype(F32))
    for t in range(ROW // 128):
        rank_cols[t * 128:(t + 1) * 128, :] = jnp.broadcast_to(rank[:, t * 128:(t + 1) * 128], (128, 128)).T


STEPS = (ROW // TQ) * -(-ROW // TK) + 8


def step_table(len_ref, table):
    starts, ends = doc_bounds(len_ref)
    idle = ROW // TQ

    def put(at, tile, first):
        table[0, at] = tile
        table[1, at] = first
    put(0, idle, ROW)
    put(1, idle, ROW)
    at = jnp.int32(2)
    for tile in range(idle):
        first, steps = key_range(starts, ends, tile * TQ)

        def fill(s, at):
            put(at, tile, first + s * TK)
            return at + 1
        at = lax.fori_loop(0, steps, fill, at)
    put(at, idle, ROW)
    put(at + 1, idle, ROW)
    table[0, STEPS - 1] = at


def step_of(table, i):
    return table[0, i], pl.multiple_of(table[1, i], 128)


def real_step(table, i):
    return jnp.minimum(table[0, i], ROW // TQ - 1), pl.multiple_of(table[1, i], 128)


def padded(ref):
    return ref.at[pl.ds(0, ROW)] if ref.shape[0] > ref.shape[1] else ref.at[:, pl.ds(0, ROW)]


def fill_padding(refs, side_ref):
    for ref in refs:
        if ref.shape[0] > ref.shape[1]:
            ref[ROW:, :] = jnp.zeros((TK, ref.shape[1]), ref.dtype)
        else:
            ref[:, ROW:] = jnp.zeros((ref.shape[0], TK), ref.dtype)
    lanes = lax.broadcasted_iota(jnp.int32, (TK, 128), 1)
    side_ref[ROW:, :] = jnp.where(lanes < DOCS, -FAR, 0.0).astype(BF)


def seen_bias(rank_cols, counts, tile, k0):
    rank = rank_cols[pl.ds(k0, TK), :]
    rank = jnp.concatenate([rank] * (TQ // 128), 1)
    kpos = lax.broadcasted_iota(jnp.int32, (TK, TQ), 0)
    qpos = lax.broadcasted_iota(jnp.int32, (TK, TQ), 1)
    off_diag = (kpos - qpos) != (tile * TQ - k0)
    allowed = (rank < counts[tile, 0:1, :]) & (off_diag | (rank < 0.0))
    return jnp.where(allowed, 0.0, -FAR * FAR)


def count_tiles(counts, count_ref):
    for tile in range(ROW // TQ):
        counts[tile] = jnp.broadcast_to(count_ref[:, tile * TQ:(tile + 1) * TQ].astype(F32), (8, TQ))


def query_columns(qt, qt_ref, side, tile, h, q0):
    rows = qt_ref[h * HEAD_DIM:(h + 1) * HEAD_DIM, pl.ds(q0, TQ)].astype(F32) * HEAD_DIM ** -0.5
    own, other = h % 2 * HEAD_DIM, (1 - h % 2) * HEAD_DIM
    qt[tile, h, own:own + HEAD_DIM, :] = rows.astype(BF)
    qt[tile, h, other:other + HEAD_DIM, :] = jnp.zeros((HEAD_DIM, TQ), BF)
    qt[tile, h, 128:256, :] = side


def pair_rows(ref, side_ref, h, k0):
    return jnp.concatenate([ref[pl.ds(k0, TK), h // 2 * 128:(h // 2 + 1) * 128], side_ref[pl.ds(k0, TK), :]], 1)


def attn_fwd_kernel(with_seen, heads, table, count_ref, qt_hbm, hot_hbm, k_hbm, vt_hbm, side_hbm, rank_hbm,
                    o_out, ot_out, lse_ref, qt, acc, top, sc, probs, fade, counts,
                    qt_ref, hot_ref, k_ref, vt_ref, side_ref, rank_cols, o_ref, ot_ref, late_sems, out_sems):
    pairs = [(qt_hbm, qt_ref), (hot_hbm, hot_ref), (k_hbm, padded(k_ref)), (vt_hbm, padded(vt_ref)),
             (side_hbm, padded(side_ref))]
    late = Late(pairs + ([(rank_hbm, padded(rank_cols))] if with_seen else []), late_sems)
    fill_padding((k_ref, vt_ref, rank_cols), side_ref)
    out = Out([(o_ref, o_out), (ot_ref, ot_out)], out_sems)
    tiles = ROW // TQ
    lse_ref[...] = jnp.zeros_like(lse_ref)
    acc[...] = jnp.zeros_like(acc)
    top[...] = jnp.full_like(top, -jnp.inf)
    if with_seen:
        count_tiles(counts, count_ref)
    late.wait(0, 1)

    def prepare(tile, c):
        q0 = pl.multiple_of(tile * TQ, TQ)
        for h in range(heads):
            query_columns(qt, qt_ref, hot_ref[:, pl.ds(q0, TQ)], tile, h, q0)
        return c
    lax.fori_loop(0, tiles, prepare, 0)
    late.wait(*range(2, 6 if with_seen else 5))
    ones = jnp.ones((16, TK), BF)

    def one_step(s, c):
        out_tile, _ = step_of(table, s)
        _, out_k = real_step(table, s)
        mid_tile, _ = step_of(table, s + 1)
        in_tile, in_k = real_step(table, s + 2)
        sums = []
        for h in range(heads):
            values = jnp.concatenate([vt_ref[h * HEAD_DIM:(h + 1) * HEAD_DIM, pl.ds(out_k, TK)], ones], 0)
            sums.append(acc[out_tile, h] * fade[h:h + 1, :] + nn(values, probs[h]))
        old = top[mid_tile]
        news = []
        for h in range(heads):
            score = sc[h]
            new = jnp.maximum(old[h:h + 1, :], jnp.max(score, 0, keepdims=True))
            probs[h] = jnp.exp(score - new).astype(BF)
            news.append(new)
        new = jnp.concatenate(news + [old[heads:, :]], 0)
        fade[...] = jnp.exp(old - new)
        bias = seen_bias(rank_cols, counts, in_tile, in_k) if with_seen else None
        for h in range(heads):
            score = nn(pair_rows(k_ref, side_ref, h, in_k), qt[in_tile, h])
            sc[h] = score + bias if with_seen else score
        top[mid_tile] = new
        for h in range(heads):
            acc[out_tile, h] = sums[h]
        return c
    lax.fori_loop(0, table[0, STEPS - 1], one_step, 0)

    def finish(tile, c):
        q0 = pl.multiple_of(tile * TQ, TQ)
        outs = []
        peak = top[tile]
        for h in range(heads):
            a = acc[tile, h]
            total = a[HEAD_DIM:HEAD_DIM + 1, :]
            outs.append(a[:HEAD_DIM, :] * (1.0 / total))
            lse_ref[h:h + 1, pl.ds(q0, TQ)] = peak[h:h + 1, :] + jnp.log(total)
        mixed = jnp.concatenate(outs, 0).astype(BF)
        ot_ref[:, pl.ds(q0, TQ)] = mixed
        out.start(1, tile)
        o_ref[pl.ds(q0, TQ), :] = mixed.T
        out.start(0, tile)
        return c
    lax.fori_loop(0, tiles, finish, 0)
    out.drain(ROW)


def attend_forward(steps, qt, k, vt, tables, count, with_seen):
    cols, rows = qt.shape
    heads = cols // HEAD_DIM
    side, hot, rank_cols = tables
    args = [steps, count, qt, hot, k, vt, side, rank_cols]
    across, down = (cols, rows), (rows, cols)
    held = [pltpu.VMEM(arg.shape, BF) for arg in (qt, hot)] + [
        pltpu.VMEM((rows + TK, cols), BF), pltpu.VMEM((cols, rows + TK), BF), pltpu.VMEM((rows + TK, 128), BF),
        pltpu.VMEM((rows + TK, 128), F32)]
    return call(partial(attn_fwd_kernel, with_seen, heads), "attend_self_forward" if with_seen else "attend_cross_forward",
                args, "SV" + "A" * 6, [(down, BF, "A"), (across, BF, "A"), ((8, rows), F32, "V")],
                [pltpu.VMEM((ROW // TQ, heads, 256, TQ), BF), pltpu.VMEM((ROW // TQ + 1, heads, HEAD_DIM + 16, TQ), F32),
                 pltpu.VMEM((ROW // TQ + 1, 8, TQ), F32), pltpu.VMEM((heads, TK, TQ), F32), pltpu.VMEM((heads, TK, TQ), BF),
                 pltpu.VMEM((8, TQ), F32), pltpu.VMEM((ROW // TQ, 8, TQ), F32)] + held
                + [pltpu.VMEM(down, BF), pltpu.VMEM(across, BF), pltpu.SemaphoreType.DMA((6,)), out_semaphores(2, rows)])


def three_rows(value):
    high = value.astype(BF).astype(F32)
    middle = (value - high).astype(BF).astype(F32)
    row = lax.broadcasted_iota(jnp.int32, (128, value.shape[1]), 0)
    return jnp.where(row == LANES[0], high, jnp.where(row == LANES[1], middle, jnp.where(row == LANES[2], value - high - middle, 0.0)))


def attn_bwd_kernel(with_seen, heads, table, count_ref, lse_ref, qt_hbm, hot_hbm, gt_hbm, ot_hbm, k_hbm, kt_hbm, v_hbm, side_hbm,
                    rank_hbm, *refs):
    passed = (len(refs) - 30) // 3
    pass_in, (dq_out, dk_out, dv_out), pass_out, refs = refs[:passed], refs[passed:passed + 3], refs[passed + 3:2 * passed + 3], refs[2 * passed + 3:]
    (dk_sum, dv_sum, dq_sum, qt, gt, q_own, g_own, sc, dps, all_ds, all_p, counts,
     qt_ref, hot_ref, gt_ref, ot_ref, k_ref, kt_ref, v_ref, side_ref, rank_cols, *held, dq_ref, dk_ref, dv_ref,
     late_sems, out_sems, pass_sem) = refs
    pairs = [(qt_hbm, qt_ref), (hot_hbm, hot_ref), (gt_hbm, gt_ref), (ot_hbm, ot_ref), (k_hbm, padded(k_ref)),
             (kt_hbm, padded(kt_ref)), (v_hbm, padded(v_ref)), (side_hbm, padded(side_ref))]
    late = Late(pairs + ([(rank_hbm, padded(rank_cols))] if with_seen else []), late_sems)
    fill_padding((k_ref, kt_ref, v_ref, rank_cols), side_ref)
    entering = Late(list(zip(pass_in, held)), pass_sem.at[0])
    out = Out([(dq_ref, dq_out), (dk_ref, dk_out), (dv_ref, dv_out)], out_sems)
    tiles = ROW // TQ
    dk_sum[...] = jnp.zeros_like(dk_sum)
    dv_sum[...] = jnp.zeros_like(dv_sum)
    dq_sum[...] = jnp.zeros_like(dq_sum)
    if with_seen:
        count_tiles(counts, count_ref)
    late.wait(0, 1, 2, 3)

    def prepare(tile, c):
        q0 = pl.multiple_of(tile * TQ, TQ)
        hot = hot_ref[:, pl.ds(q0, TQ)].astype(F32)
        for h in range(heads):
            rows = slice(h * HEAD_DIM, (h + 1) * HEAD_DIM)
            side = hot + three_rows(lse_ref[h:h + 1, pl.ds(q0, TQ)])
            query_columns(qt, qt_ref, side.astype(BF), tile, h, q0)
            grads = gt_ref[rows, pl.ds(q0, TQ)]
            delta = jnp.sum(grads.astype(F32) * ot_ref[rows, pl.ds(q0, TQ)].astype(F32), 0, keepdims=True)
            other = (1 - h % 2) * HEAD_DIM
            gt[tile, h, h % 2 * HEAD_DIM:(h % 2 + 1) * HEAD_DIM, :] = grads
            gt[tile, h, other:other + HEAD_DIM, :] = jnp.zeros((HEAD_DIM, TQ), BF)
            gt[tile, h, 128:256, :] = three_rows(delta).astype(BF)
        lane = lax.broadcasted_iota(jnp.int32, (TQ, heads * HEAD_DIM), 1)
        for held_rows, source in ((q_own, qt_ref), (g_own, gt_ref)):
            rows = source[:, pl.ds(q0, TQ)].T
            for h in range(heads):
                own = (lane >= h * HEAD_DIM) & (lane < (h + 1) * HEAD_DIM)
                held_rows[tile, h * TQ:(h + 1) * TQ, :] = jnp.where(own, rows, jnp.zeros_like(rows))
        return c
    lax.fori_loop(0, tiles, prepare, 0)
    late.wait(*range(4, 9 if with_seen else 8))
    entering.wait(*range(passed))
    leaving = Late(list(zip(held, pass_out)), pass_sem.at[1])

    def one_step(s, c):
        out_tile, out_k = step_of(table, s)
        read_tile, read_k = real_step(table, s)
        in_tile, in_k = real_step(table, s + 2)
        keys = pl.ds(out_k, TK)
        own = [slice(h * HEAD_DIM, (h + 1) * HEAD_DIM) for h in range(heads)]
        dk = dk_sum[keys, :] + nn(all_ds[...], q_own[read_tile])
        dv = dv_sum[keys, :] + nn(all_p[...], g_own[read_tile])
        dq = [dq_sum[out_tile, h] + nn(kt_ref[own[h], pl.ds(read_k, TK)], all_ds[:, h * TQ:(h + 1) * TQ]) for h in range(heads)]
        for h in range(heads):
            p = jnp.exp(sc[h])
            all_ds[:, h * TQ:(h + 1) * TQ] = (p * dps[h]).astype(BF)
            all_p[:, h * TQ:(h + 1) * TQ] = p.astype(BF)
        bias = seen_bias(rank_cols, counts, in_tile, in_k) if with_seen else None
        for h in range(heads):
            score = nn(pair_rows(k_ref, side_ref, h, in_k), qt[in_tile, h])
            sc[h] = score + bias if with_seen else score
            dps[h] = nn(pair_rows(v_ref, side_ref, h, in_k), gt[in_tile, h])
        dk_sum[keys, :] = dk
        dv_sum[keys, :] = dv
        for h in range(heads):
            dq_sum[out_tile, h] = dq[h]
        return c
    lax.fori_loop(0, table[0, STEPS - 1], one_step, 0)

    def finish(tile, c):
        q0 = pl.multiple_of(tile * TQ, TQ)
        rows = pl.ds(q0, TQ)
        dq = jnp.concatenate([dq_sum[tile, h] for h in range(heads)], 0) * HEAD_DIM ** -0.5
        dk = dk_sum[rows, :] * HEAD_DIM ** -0.5
        for i, (ref, value) in enumerate(((dq_ref, dq.astype(BF).T), (dk_ref, dk.astype(BF)), (dv_ref, dv_sum[rows, :].astype(BF)))):
            ref[rows, :] = value
            out.start(i, tile)
        return c
    lax.fori_loop(0, tiles, finish, 0)
    out.drain(ROW)
    leaving.wait(*range(passed))


def attend_backward(steps, qt, k, kt, v, gt, ot, lse, tables, count, passed, with_seen):
    rows, cols = v.shape
    heads = cols // HEAD_DIM
    side, hot, rank_cols = tables
    args = [steps, count, lse, qt, hot, gt, ot, k, kt, v, side, rank_cols] + passed
    tiles = ROW // TQ
    like = ((rows, cols), BF, "A")
    summed, own = pltpu.VMEM((rows + TK, cols), F32), pltpu.VMEM((tiles, heads * TQ, cols), BF)
    columns, square = pltpu.VMEM((tiles, heads, 256, TQ), BF), pltpu.VMEM((heads, TK, TQ), F32)
    small = pltpu.VMEM((TK, heads * TQ), BF)
    keys, keys_t = pltpu.VMEM((rows + TK, cols), BF), pltpu.VMEM((cols, rows + TK), BF)
    held = [pltpu.VMEM(arg.shape, BF) for arg in (qt, hot, gt, ot)] + [
        keys, keys_t, keys, pltpu.VMEM((rows + TK, 128), BF), pltpu.VMEM((rows + TK, 128), F32)] + [
        pltpu.VMEM(value.shape, value.dtype) for value in passed]
    return call(partial(attn_bwd_kernel, with_seen, heads), "attend_self_backward" if with_seen else "attend_cross_backward",
                args, "SVV" + "A" * (9 + len(passed)), [like, like, like] + [(value.shape, value.dtype, "A") for value in passed],
                [summed, summed, pltpu.VMEM((tiles + 1, heads, HEAD_DIM, TQ), F32), columns, columns, own, own, square, square,
                 small, small, pltpu.VMEM((ROW // TQ, 8, TQ), F32)] + held + [pltpu.VMEM((rows, cols), BF)] * 3
                + [pltpu.SemaphoreType.DMA((9,)), out_semaphores(3, rows), pltpu.SemaphoreType.DMA((2, 2))])


def send(src, dst, send_sem, recv_sem, **where):
    copy = pltpu.make_async_remote_copy(src_ref=src, dst_ref=dst, send_sem=send_sem, recv_sem=recv_sem,
                                        device_id=where, device_id_type=pl.DeviceIdType.MESH)
    copy.start()
    return copy

def greet(peers):
    barrier = pltpu.get_barrier_semaphore()
    for where in peers:
        pl.semaphore_signal(barrier, inc=1, device_id=where, device_id_type=pl.DeviceIdType.MESH)
    pl.semaphore_wait(barrier, len(peers))

def places_of(count):
    me = lax.axis_index("dp")
    across = count // 4
    x, y, z = lax.rem(me, 2), lax.rem(lax.div(me, 2), 2), lax.div(me, 4)
    xpeer, ypeer = me + 1 - 2 * x, me + 2 - 4 * y
    order = sorted(range(1, across), key=lambda d: min(d, across - d))
    ahead = lambda d: lax.rem(z + d, across) * 4 + y * 2 + x
    behind = lambda d: lax.rem(z + across - d, across) * 4 + y * 2 + x
    return me, x, y, z, xpeer, ypeer, order, ahead, behind

class LineGather:
    def __init__(self, count, piece, units, cut, places, zs, ds, xs, ys, gx, gy):
        self.across, self.piece, self.units, self.cut = count // 4, piece, units, cut
        self.places = places
        self.sems = dict(z=zs, d=ds, x=xs, y=ys, gx=gx, gy=gy)

    def copy(self, name, side, k, arriving=False):
        me, x, y, z, xpeer, ypeer = self.places[:6]
        place = x + 2 * y
        place = dict(z=place, x=place, y=place, d=3 - place, gy=place + 1 - 2 * x, gx=place + 2 - 4 * y)[name]
        if arriving:
            place = {"x": x + 2 * y + 1 - 2 * x, "y": x + 2 * y + 2 - 4 * y, "gx": 3 - x - 2 * y, "gy": 3 - x - 2 * y}.get(name, place)
        level = z + k * (2 * side - 1)
        whole = isinstance(k, int) and k == 0
        half = self.units // 2 if whole else (self.units - self.cut) // 2
        first = 0 if whole else self.cut
        start, size = dict(d=(0, self.cut), gy=(first, half), gx=(first + half, self.units - first - half)).get(name, (0, self.units))
        to = dict(x=xpeer, gx=xpeer, y=ypeer, gy=ypeer).get(name, me + 4 * (1 - 2 * side))
        hop = 1 if name in ("z", "d") and not arriving else 0
        if arriving:
            to = xpeer
        part, sems = self.piece(level * 4 + place, start, size), self.sems[name]
        return pltpu.make_async_remote_copy(
            src_ref=part, dst_ref=part, send_sem=sems.at[0, side, k], recv_sem=sems.at[1, side, k + hop],
            device_id={"dp": to}, device_id_type=pl.DeviceIdType.MESH)

    def here(self, side, k):
        z = self.places[3]
        return z >= k if side == 0 else z + k < self.across

    def onward(self, side):
        z = self.places[3]
        return z + 1 < self.across if side == 0 else z > 0

    def along(self, name, side, k, act):
        pl.when(self.here(side, k) & self.onward(side))(lambda: act(self.copy(name, side, k)))

    def run(self, at_start, at_first, at_second):
        start, wait_send = (lambda copy: copy.start()), (lambda copy: copy.wait_send())

        def diagonal(side, k):
            self.copy("x", side, k, True).wait_recv()
            self.copy("gy", side, k).start()
            self.copy("y", side, k, True).wait_recv()
            self.copy("gx", side, k).start()

        def later(side, k):
            diagonal(side, k)
            self.copy("d", side, k, True).wait_recv()
            pl.when(self.onward(side))(lambda: self.copy("d", side, k).start())
        for side in (0, 1):
            self.along("z", side, 0, start)
        self.copy("x", 0, 0).start()
        self.copy("y", 0, 0).start()
        at_start()
        diagonal(0, 0)

        def level(k, carry):
            for side in (0, 1):
                @pl.when(self.here(side, k))
                def _():
                    self.copy("z", side, k, True).wait_recv()
                    pl.when(self.onward(side))(lambda: self.copy("z", side, k).start())
                    self.copy("x", side, k).start()
                    self.copy("y", side, k).start()

            @pl.when(k == 1)
            def _():
                self.copy("gy", 0, 0, True).wait_recv()
                self.copy("gx", 0, 0, True).wait_recv()
                for side in (0, 1):
                    self.along("d", side, 0, start)
                at_first()

            @pl.when(k > 1)
            def _():
                for side in (0, 1):
                    pl.when(self.here(side, k - 1))(lambda: later(side, k - 1))
            pl.when(k == 2)(at_second)
            return carry
        lax.fori_loop(1, self.across, level, 0)
        for side in (0, 1):
            pl.when(self.here(side, self.across - 1))(lambda: later(side, self.across - 1))

        def settle(k, carry):
            for side in (0, 1):
                @pl.when(self.here(side, k))
                def _():
                    for name in ("gy", "gx"):
                        self.copy(name, side, k, True).wait_recv()
                    for name in ("x", "y", "gy", "gx"):
                        self.copy(name, side, k).wait_send()
                for name in ("z", "d"):
                    self.along(name, side, k, wait_send)
            return carry
        lax.fori_loop(1, self.across, settle, 0)
        for name in ("x", "y", "gy", "gx"):
            self.copy(name, 0, 0).wait_send()
        for side in (0, 1):
            for name in ("z", "d"):
                self.along(name, side, 0, wait_send)


class Spread:
    def __init__(self, places, out, zs, xs, ys, gx, gy):
        self.places, self.out, self.sems = places, out, dict(z=zs, x=xs, y=ys, gx=gx, gy=gy)
        self.rows = out.shape[2]
        self.half = self.rows // 2 // UNIT * UNIT
        self.copies = {}

    def go(self, name, d, f_from, d_from, f_to, d_to, to, start, size):
        part, sems = pl.ds(start, size), self.sems[name]
        self.copies[name, d] = send(self.out.at[f_from, d_from, part], self.out.at[f_to, d_to, part],
                                    sems.at[0, d], sems.at[1, d], dp=to)

    def over_plane(self, d):
        xpeer, ypeer = self.places[4], self.places[5]
        self.go("x", d, 0, d, 1, d, xpeer, 0, self.rows)
        self.go("y", d, 0, d, 2, d, ypeer, 0, self.rows)

    def start(self):
        order, ahead = self.places[6], self.places[7]
        for d in order:
            self.go("z", d, 0, 0, 0, d, ahead(d), 0, self.rows)
        self.over_plane(0)

    def relay(self):
        for d in self.places[6]:
            self.copies["z", d].wait_recv()
            self.over_plane(d)

    def diagonal(self):
        xpeer, ypeer, order = self.places[4:7]
        for d in [0] + order:
            self.copies["x", d].wait_recv()
            if self.half:
                self.go("gy", d, 1, d, 3, d, ypeer, 0, self.half)
            self.copies["y", d].wait_recv()
            self.go("gx", d, 2, d, 3, d, xpeer, self.half, self.rows - self.half)

    def finish(self):
        for (name, d), copy in self.copies.items():
            if name in ("gx", "gy"):
                copy.wait_recv()

    def drain(self):
        for copy in self.copies.values():
            copy.wait_send()


def plane_swap(value, count, f):
    return lax.ppermute(value, "dp", [(i, i // 4 * 4 + (i % 4 ^ f)) for i in range(count)])


def plane_offset(places, f):
    x, y = places[1], places[2]
    return lax.rem(x + f % 2, 2) + 2 * lax.rem(y + f // 2, 2)


def call(kernel, name, args, kinds, outs, scratch, number=None):
    space = {"V": pltpu.VMEM, "S": pltpu.SMEM, "A": pl.ANY}
    extra = {} if number is None else dict(collective_id=number, has_side_effects=True)
    return pl.pallas_call(
        kernel,
        out_shape=tuple(jax.ShapeDtypeStruct(shape, dtype) for shape, dtype, _ in outs),
        in_specs=[pl.BlockSpec(memory_space=space[kind]) for kind in kinds],
        out_specs=tuple(pl.BlockSpec(memory_space=space[kind]) for _, _, kind in outs),
        scratch_shapes=scratch,
        compiler_params=pltpu.CompilerParams(vmem_limit_bytes=60 * 2**20, **extra),
        cost_estimate=pl.CostEstimate(flops=4 * 10**10, bytes_accessed=16 * 2**20, transcendentals=0),
        name=name,
    )(*args)


CHUNK = 256


def tn(a, b):
    return lax.dot_general(a, b, (((0,), (0,)), ((), ())), preferred_element_type=F32)


def normalise(value):
    centred = value - jnp.mean(value, -1, keepdims=True)
    scale = lax.rsqrt(jnp.mean(centred * centred, -1, keepdims=True) + EPS_NORM)
    return centred * scale, scale


def norm_back(unit, scale, gain, grad):
    inner = grad * gain
    return scale * (inner - jnp.mean(inner, -1, keepdims=True) - unit * jnp.mean(inner * unit, -1, keepdims=True))


def fold_rows(value):
    return jnp.sum(value.reshape(value.shape[0] // 8, 8, value.shape[1]), 0)


def interleave(size):
    row = lax.broadcasted_iota(jnp.int32, (size, size), 0)
    col = lax.broadcasted_iota(jnp.int32, (size, size), 1)
    source = jnp.where((row & 1) == 0, row >> 1, (row >> 1) + size // 2)
    return jnp.where(col == source, 1.0, 0.0).astype(BF)


def part_rows(matrix, order):
    return lax.dot_general(order, matrix, (((0,), (0,)), ((), ())), preferred_element_type=F32).astype(BF)


def as_units(gradient, order):
    parted = part_rows(gradient.astype(BF), order)
    half = parted.shape[0] // 2
    return jnp.concatenate([parted[:half], parted[half:]], 1)


def other_core(mine, theirs, sems, step):
    rows = pl.ds(step * CHUNK, CHUNK)
    return pltpu.make_async_remote_copy(
        src_ref=mine.at[rows], dst_ref=theirs.at[rows], send_sem=sems.at[0, step], recv_sem=sems.at[1, step],
        device_id={"head": 1 - lax.axis_index("head")}, device_id_type=pl.DeviceIdType.MESH)


def greet_core():
    greet([{"head": 1 - lax.axis_index("head")}])


def chunks(total, body, begin=0):
    def one(step, carry):
        body(step, pl.ds(pl.multiple_of(step * CHUNK, CHUNK), CHUNK))
        return carry
    lax.fori_loop(begin // CHUNK, total // CHUNK, one, 0)


def drain(total, mine, theirs, sems):
    def body(step, rows):
        other_core(mine, theirs, sems, step).wait_send()
    chunks(total, body)


class Late:
    def __init__(self, pairs, sems):
        self.copies = [pltpu.make_async_copy(source, held, sems.at[i]) for i, (source, held) in enumerate(pairs)]
        for copy in self.copies:
            copy.start()

    def wait(self, *which):
        for i in which:
            self.copies[i].wait()


class Out:
    def __init__(self, pairs, sems):
        self.pairs, self.sems = pairs, sems

    def copy(self, i, step):
        held, out = self.pairs[i]
        part = pl.ds(pl.multiple_of(step * CHUNK, CHUNK), CHUNK)
        if held.shape[0] < held.shape[1]:
            held, out = held.at[:, part], out.at[:, part]
        else:
            held, out = held.at[part], out.at[part]
        return pltpu.make_async_copy(held, out, self.sems.at[i, step])

    def start(self, i, step):
        self.copy(i, step).start()

    def drain(self, tokens):
        def body(step, rows):
            for i in range(len(self.pairs)):
                self.copy(i, step).wait()
        chunks(tokens, body)


def plan_kernel(block, owner_ref, len_ref, me_ref, rank_ref, count_ref, place_ref, held_ref, rank_out, count_out, table, info):
    units = owner_ref.shape[1]
    owner = owner_ref[...].astype(F32)
    owner_cols = jnp.broadcast_to(owner, (128, units)).T
    owner_cols = jnp.concatenate([owner_cols] * (units // 128), 1)
    before = lax.broadcasted_iota(jnp.int32, (units, units), 0) < lax.broadcasted_iota(jnp.int32, (units, units), 1)
    slots = jnp.sum(jnp.where(before & (owner_cols == owner), 1.0, 0.0), 0, keepdims=True)
    place = owner * block + slots
    place_ref[...] = place.astype(jnp.int32)
    me = me_ref[0].astype(F32)
    place_cols = jnp.broadcast_to(place, (128, units)).T
    lane = lax.broadcasted_iota(jnp.int32, (units, 128), 1)
    unit = lax.broadcasted_iota(jnp.int32, (units, 128), 0).astype(F32)
    mine = jnp.where(place_cols == me * block + lane.astype(F32), unit, 0.0)
    mine = jnp.where(lane == 127, jnp.where(owner_cols[:, :128] == me, 1.0, 0.0), jnp.where(lane < block - 1, mine, 0.0))
    held_ref[...] = jnp.sum(mine, 0, keepdims=True).astype(jnp.int32)
    longest, first, at, start = jnp.int32(0), jnp.int32(0), jnp.int32(0), jnp.int32(0)
    for d in range(DOCS):
        length = len_ref[0, d]
        longer = length > longest
        first = jnp.where(longer, d, first)
        start = jnp.where(longer, at, start)
        longest = jnp.where(longer, length, longest)
        at = at + length
    for d in range(DOCS):
        info[0, d] = len_ref[0, lax.rem(first + d, DOCS)]
    info[0, DOCS] = start
    info[0, DOCS + 1] = lax.rem(ROW - start, ROW)
    turn = lax.rem(ROW - start, ROW)
    rank_out[...] = pltpu.roll(rank_ref[...], turn, 1)
    count_out[...] = pltpu.roll(count_ref[...], turn, 1)
    step_table(info, table)


def plan(unit_owner, lengths, me, rank_row, count_row, block):
    row = ((1, ROW), jnp.int32, "V")
    return call(partial(plan_kernel, block), "plan", [unit_owner.reshape(1, -1), lengths, me, rank_row, count_row], "VSSVV",
                [((1, unit_owner.shape[0]), jnp.int32, "V"), ((1, 128), jnp.int32, "V"), row, row, ((2, STEPS), jnp.int32, "S"),
                 ((1, DOCS + 2), jnp.int32, "S")], [])


def turn_rows(source, target, shift):
    tiles = source.shape[0]
    whole, rest = lax.div(shift, UNIT), lax.rem(shift, UNIT)

    def one(i, carry):
        at = lax.rem(i + whole, tiles)
        both = jnp.concatenate([source[at].astype(F32), source[lax.rem(at + 1, tiles)].astype(F32)], 0)
        rows = pltpu.roll(both, lax.rem(2 * UNIT - rest, 2 * UNIT), 0)[:UNIT]
        target[pl.ds(pl.multiple_of(i * UNIT, UNIT), UNIT), :] = rows.astype(target.dtype)
        return carry
    lax.fori_loop(0, tiles, one, 0, unroll=4)


def in_tiles(value):
    return value.reshape(-1, UNIT, value.shape[1])


def project_kernel(devices, place_ref, info, master, norm_row, rank_ref, query_hbm, kv_hbm, memory_hbm, grad_hbm,
                   nq_out, nkv_out, qt_out, k_out, kt_out, v_out, vt_out, kc_out, kct_out, vc_out, vct_out,
                   query_out, kv_out, memory_out, grad_out,
                   ws_ref, wc_ref, wos_ref, woc_ref, w1_ref, w2_ref, norms, side_ref, hot_ref, rank_cols,
                   gathered, flat, stage_a, stage_b, query_ref, kv_ref, memory_ref, grad_ref, unit_q, unit_kv,
                   nq_ref, nkv_ref, qt_ref, k_ref, kt_ref, v_ref, vt_ref, kc_ref, kct_ref, vc_ref, vct_ref,
                   late_sems, turned_sems, out_sems, *line_sems):
    tokens, features = query_ref.shape
    units = place_ref.shape[1]
    late = Late([(query_hbm, stage_a), (kv_hbm, stage_b)], late_sems.at[0])
    held = (nq_ref, nkv_ref, qt_ref, k_ref, kt_ref, v_ref, vt_ref, kc_ref, kct_ref, vc_ref, vct_ref)
    out = Out(list(zip(held, (nq_out, nkv_out, qt_out, k_out, kt_out, v_out, vt_out, kc_out, kct_out, vc_out, vct_out))), out_sems)
    places = places_of(devices)
    me, x, y, z, xpeer, ypeer, order, ahead, behind = places
    slots = master.shape[0]
    block = slots + 1
    gathered[pl.ds(me * block, slots)] = master[...].astype(BF)
    gathered[me * block + slots] = jnp.broadcast_to(norm_row[...], (UNIT, features)).astype(BF)
    greet([{"dp": xpeer}, {"dp": ypeer}] + [{"dp": ahead(d)} for d in order])

    leaving = [(query_ref, query_out), (kv_ref, kv_out), (memory_ref, memory_out), (grad_ref, grad_out)]

    def leave(number):
        return pltpu.make_async_copy(*leaving[number], turned_sems.at[number])

    def turn(stage, number):
        turn_rows(stage, leaving[number][0], info[0, DOCS])
        leave(number).start()

    def first_turns():
        mask_tables(info, rank_ref, side_ref, hot_ref, rank_cols)
        late.wait(0, 1)
        turn(stage_a, 0)
        turn(stage_b, 1)

    def norms_of_streams():
        def units_of(step, rows):
            unit_q[rows, :] = normalise(query_ref[rows, :].astype(F32))[0]
            unit_kv[rows, :] = normalise(kv_ref[rows, :].astype(F32))[0]
        chunks(tokens, units_of)

    def last_turns():
        more = Late([(memory_hbm, stage_a), (grad_hbm, stage_b)], late_sems.at[1])
        more.wait(0, 1)
        turn(stage_a, 2)
        turn(stage_b, 3)
    LineGather(devices, lambda number, start, size: gathered.at[pl.ds(number * block + start, size)], block, block * 3 // 5,
               places, *line_sems).run(first_turns, norms_of_streams, last_turns)

    share = devices // 8
    vectors = []
    for number in range(8):
        pieces = [gathered[(number * share + i) * block + slots].astype(F32) for i in range(share)]
        total = pieces[0]
        for piece in pieces[1:]:
            total = total + piece
        vectors.append(total[0:1, :])
    norms[...] = jnp.concatenate(vectors, 0)

    def one_unit(u, carry):
        flat[pl.ds(pl.multiple_of(u * UNIT, UNIT), UNIT), :] = gathered[place_ref[0, u]]
        return carry
    lax.fori_loop(0, units, one_unit, 0, unroll=4)
    order = interleave(features)
    cols = v_ref.shape[1]
    for number in range(6):
        rows = flat[number * cols:(number + 1) * cols, :]
        stacked = jnp.concatenate([rows[:, :cols], rows[:, cols:]], 0)
        matrix = nn(order, stacked).astype(BF)
        if number < 3:
            ws_ref[number] = matrix
        else:
            wc_ref[number - 3] = matrix
    wos_ref[...] = flat[6 * cols:7 * cols, :]
    woc_ref[...] = flat[7 * cols:8 * cols, :]
    hidden = w2_ref.shape[0]
    for block in range(hidden // features):
        at = 8 * cols + block * features
        parted = part_rows(flat[at:at + features, :], order)
        half = features // 2
        w1_ref[block * half:(block + 1) * half, :] = jnp.concatenate([parted[:half], parted[half:]], 1)
    w2_ref[...] = flat[8 * cols + hidden:, :]

    def body(step, rows):
        nq = (unit_q[rows, :] * norms[0:1, :] + norms[1:2, :]).astype(BF)
        nkv = (unit_kv[rows, :] * norms[2:3, :] + norms[3:4, :]).astype(BF)
        source = memory_ref[rows, :]
        low = lambda left, right: nn(left, right).astype(BF)
        k, v, kc, vc = low(nkv, ws_ref[1]), low(nkv, ws_ref[2]), low(source, wc_ref[1]), low(source, wc_ref[2])
        results = [nq, nkv, low(nq, ws_ref[0]).T, k, k.T, v, v.T, kc, kc.T, vc, vc.T]
        for i, (ref, result) in enumerate(zip(held, results)):
            if ref.shape[0] < ref.shape[1]:
                ref[:, rows] = result
            else:
                ref[rows, :] = result
            out.start(i, step)
    chunks(tokens, body)
    out.drain(tokens)
    for number in range(4):
        leave(number).wait()


def pair_sems(tokens):
    return pltpu.SemaphoreType.DMA((2, tokens // CHUNK))


def out_semaphores(count, tokens):
    return pltpu.SemaphoreType.DMA((count, tokens // CHUNK))


def project(devices, place_of, info, master, norm_row, rank_row, query_stream, kv_stream, memory, out_grad, cols, hidden):
    tokens, features = query_stream.shape
    wide, narrow, across = (tokens, features), (tokens, cols), (cols, tokens)
    shapes = [wide, wide, across] + [narrow, across] * 4
    outs = [(shape, BF, "A") for shape in shapes] + [(wide, BF, "A")] * 4 + [
        ((3, features, cols), BF, "V"), ((3, features, cols), BF, "V"), ((cols, features), BF, "V"), ((cols, features), BF, "V"),
        ((features, hidden), BF, "V"), ((hidden, features), BF, "V"), ((8, features), F32, "V"),
        ((ROW, 128), BF, "V"), ((128, ROW), BF, "V"), ((ROW, 128), F32, "V")]
    D = pltpu.SemaphoreType.DMA
    streams = [in_tiles(stream) for stream in (query_stream, kv_stream, memory, out_grad)]
    scratch = [pltpu.VMEM((devices * (master.shape[0] + 1), UNIT, features), BF), pltpu.VMEM((8 * cols + 2 * hidden, features), BF)]
    scratch += [pltpu.VMEM(streams[0].shape, BF)] * 2 + [pltpu.VMEM(wide, BF)] * 4 + [pltpu.VMEM(wide, F32)] * 2
    scratch += [pltpu.VMEM(shape, BF) for shape in shapes]
    scratch += [D((2, 2)), D((4,)), out_semaphores(len(shapes), tokens)] + [D((2, 2, devices // 4 + 1))] * 6
    return call(partial(project_kernel, devices), "project",
                [place_of, info, master, norm_row, rank_row] + streams, "SSVVVAAAA", outs, scratch, 0)


def self_out_kernel(mixed, wo, query_hbm, wc, norms, res_out, nc_out, q_out,
                    query, res_ref, nc_ref, q_ref, mine, theirs, sems, late_sems, out_sems):
    tokens = query.shape[0]
    late = Late([(query_hbm, query)], late_sems)
    out = Out([(res_ref, res_out), (nc_ref, nc_out), (q_ref, q_out)], out_sems)
    greet_core()

    def give(step, rows):
        mine[rows, :] = nn(mixed[rows, :], wo[...]).astype(BF)
        other_core(mine, theirs, sems, step).start()
    chunks(tokens, give)
    late.wait(0)

    def take(step, rows):
        other_core(mine, theirs, sems, step).wait_recv()
        res = query[rows, :].astype(F32) + (mine[rows, :].astype(F32) + theirs[rows, :].astype(F32))
        res_ref[rows, :] = res
        out.start(0, step)
        nc = (normalise(res)[0] * norms[4:5, :] + norms[5:6, :]).astype(BF)
        nc_ref[rows, :] = nc
        out.start(1, step)
        q_ref[:, rows] = nn(nc, wc[0]).astype(BF).T
        out.start(2, step)
    chunks(tokens, take)
    drain(tokens, mine, theirs, sems)
    out.drain(tokens)


def self_out(mixed, wo, query, wc, norms):
    tokens, features = query.shape
    wide = (tokens, features)
    across = (mixed.shape[1], tokens)
    outs = [(wide, F32, "A"), (wide, BF, "A"), (across, BF, "A")]
    scratch = [pltpu.VMEM(wide, BF), pltpu.VMEM(wide, F32), pltpu.VMEM(wide, BF), pltpu.VMEM(across, BF),
               pltpu.VMEM(wide, BF), pltpu.VMEM(wide, BF), pair_sems(tokens), pltpu.SemaphoreType.DMA((1,)),
               out_semaphores(3, tokens)]
    return call(self_out_kernel, "self_out", [mixed, wo, query, wc, norms], "VVAVV", outs, scratch, 2)


def gelu_parts(value):
    bell = jnp.exp2(value * value * (-0.5 * 1.4426950408889634))
    base = 1.0 + (0.3275911 * 0.7071067811865476) * jnp.abs(value)
    t = pl.reciprocal(base, approx=True)
    t = t * (2.0 - base * t)
    poly = ((((0.5307027145 * t - 0.7265760135) * t + 0.7107068705) * t - 0.142248368) * t + 0.127414796) * t
    tail = poly * bell
    below = jnp.where(value < 0.0, tail, 1.0 - tail)
    return value * below, below + value * (bell * 0.3989422804014327)


def spread_flat(devices, places, flat, refs):
    rows = flat.shape[0] // devices
    for f, ref in enumerate(refs):
        place = plane_offset(places, f)
        for level in range(devices // 4):
            ref[level, ref.shape[1] - rows:, :] = flat[pl.ds(pl.multiple_of((level * 4 + place) * rows, UNIT), rows), :]


def feed_forward_kernel(devices, mixed, wo, res_hbm, w1, w2, out_grad_hbm, norms,
                        out_out, gres_out, gmix_out, part0, part1, part2, part3, sums_ref,
                        res, out_grad, out_ref, gres_ref, gmix_ref, flat,
                        mine, theirs, nf_all, hid_all, pre_all, low_all, mine_o, theirs_o, mine_g, theirs_g,
                        sems, sems_o, sems_g, late_sems, out_sems):
    tokens, features = out_grad.shape
    hidden = w2.shape[0]
    places = places_of(devices)
    late = Late([(res_hbm, res), (out_grad_hbm, out_grad)], late_sems)
    out = Out([(out_ref, out_out), (gres_ref, gres_out), (gmix_ref, gmix_out)], out_sems)
    greet_core()

    def give(step, rows):
        mine[rows, :] = nn(mixed[rows, :], wo[...]).astype(BF)
        other_core(mine, theirs, sems, step).start()
    chunks(tokens, give)
    late.wait(0, 1)

    def middle(step, rows):
        other_core(mine, theirs, sems, step).wait_recv()
        value = res[rows, :] + (mine[rows, :].astype(F32) + theirs[rows, :].astype(F32))
        gres_ref[rows, :] = value
        nf = (normalise(value)[0] * norms[6:7, :] + norms[7:8, :]).astype(BF)
        nf_all[rows, :] = nf
        grad = out_grad[rows, :]
        out_part = jnp.zeros((CHUNK, features), F32)
        grad_part = jnp.zeros((CHUNK, features), F32)
        for block in range(hidden // 256):
            at = slice(block * 256, (block + 1) * 256)
            act, slope = gelu_parts(nn(nf, w1[:, at]))
            act = act.astype(BF)
            hid_all[rows, at] = act
            pre = (slope * nt(grad, w2[at, :])).astype(BF)
            pre_all[rows, at] = pre
            out_part = out_part + nn(act, w2[at, :])
            grad_part = grad_part + nt(pre, w1[:, at])
        mine_o[rows, :] = out_part.astype(BF)
        other_core(mine_o, theirs_o, sems_o, step).start()
        mine_g[rows, :] = grad_part.astype(BF)
        other_core(mine_g, theirs_g, sems_g, step).start()
    chunks(tokens, middle)

    order = interleave(features)
    half, cols = features // 2, mixed.shape[1]
    for block in range(hidden // 256):
        at = slice(block * 256, (block + 1) * 256)
        flat[cols + hidden + block * 256:cols + hidden + (block + 1) * 256, :] = tn(hid_all[:, at], out_grad[...]).astype(BF)
    for block in range(hidden // features):
        gradient = tn(nf_all[:, block * half:(block + 1) * half], pre_all[...]).astype(BF)
        stacked = jnp.concatenate([gradient[:, :features], gradient[:, features:]], 0)
        flat[cols + block * features:cols + (block + 1) * features, :] = nn(order, stacked).astype(BF)
    sums_ref[...] = jnp.zeros_like(sums_ref)

    def close(step, rows):
        other_core(mine_o, theirs_o, sems_o, step).wait_recv()
        other_core(mine_g, theirs_g, sems_g, step).wait_recv()
        value = gres_ref[rows, :]
        out_ref[rows, :] = (value + (mine_o[rows, :].astype(F32) + theirs_o[rows, :].astype(F32))).astype(BF)
        out.start(0, step)
        grad = mine_g[rows, :].astype(F32) + theirs_g[rows, :].astype(F32)
        unit, scale = normalise(value)
        gres = norm_back(unit, scale, norms[6:7, :], grad) + out_grad[rows, :].astype(F32)
        gres_ref[rows, :] = gres
        out.start(1, step)
        sums_ref[0:8, :] += fold_rows(grad * unit)
        sums_ref[8:16, :] += fold_rows(grad)
        low = gres.astype(BF)
        low_all[rows, :] = low
        gmix_ref[:, rows] = nt(low, wo[...]).astype(BF).T
        out.start(2, step)
    chunks(tokens, close)
    flat[0:cols, :] = tn(mixed[...], low_all[...]).astype(BF)
    if flat.shape[0] > cols + 2 * hidden:
        flat[cols + 2 * hidden:, :] = jnp.zeros((flat.shape[0] - cols - 2 * hidden, features), BF)
    spread_flat(devices, places, flat, (part0, part1, part2, part3))
    out.drain(tokens)
    drain(tokens, mine, theirs, sems)
    drain(tokens, mine_o, theirs_o, sems_o)
    drain(tokens, mine_g, theirs_g, sems_g)


def whole_blocks(rows, devices):
    return -(-rows // (devices * UNIT)) * devices * UNIT


def feed_forward(devices, mixed, wo, res, w1, w2, out_grad, norms):
    tokens, features = out_grad.shape
    hidden = w2.shape[0]
    flat_rows = whole_blocks(wo.shape[0] + 2 * hidden, devices)
    part = ((devices // 4, flat_rows // devices, features), BF, "V")
    wide = (tokens, features)
    across = (mixed.shape[1], tokens)
    outs = [(wide, BF, "A"), (wide, F32, "A"), (across, BF, "A")] + [part] * 4 + [((16, features), F32, "V")]
    deep, narrow = pltpu.VMEM((tokens, hidden), BF), pltpu.VMEM(wide, BF)
    scratch = [pltpu.VMEM(wide, F32), narrow, narrow, pltpu.VMEM(wide, F32), pltpu.VMEM(across, BF),
               pltpu.VMEM((flat_rows, features), BF), narrow, narrow, narrow, deep, deep, narrow] + [narrow] * 4
    scratch += [pair_sems(tokens)] * 3 + [pltpu.SemaphoreType.DMA((2,)), out_semaphores(3, tokens)]
    return call(partial(feed_forward_kernel, devices), "feed_forward", [mixed, wo, res, w1, w2, out_grad, norms], "VVAVVAV",
                outs, scratch, 3)


def branch_give(dq, dk, dv, weights, mine_a, theirs_a, mine_b, theirs_b, sems_a, sems_b):
    def give(step, rows):
        mine_a[rows, :] = nt(dq[rows, :], weights[0]).astype(BF)
        other_core(mine_a, theirs_a, sems_a, step).start()
        mine_b[rows, :] = (nt(dk[rows, :], weights[1]) + nt(dv[rows, :], weights[2])).astype(BF)
        other_core(mine_b, theirs_b, sems_b, step).start()
    chunks(dq.shape[0], give)


def branch_weights(first_in, second_in, dq, dk, dv, flat):
    cols = dq.shape[1]
    order = interleave(first_in.shape[1])
    for number, (entering, grad) in enumerate(((first_in, dq), (second_in, dk), (second_in, dv))):
        flat[number * cols:(number + 1) * cols, :] = as_units(tn(entering[...], grad[...]), order)


def z_sum_start(devices, places, pieces, landed, sems):
    me, x, y, z, xpeer, ypeer, order, ahead, behind = places
    return [send(pieces.at[lax.rem(z + d, devices // 4)], landed.at[d], sems.at[0, d], sems.at[1, d], dp=ahead(d)) for d in order]


def z_sum_end(places, pieces, landed, copies):
    z, order = places[3], places[6]
    total = pieces[z].astype(F32)
    for copy, d in zip(copies, order):
        copy.wait_recv()
        total = total + landed[d].astype(F32)
    return total.astype(BF)


def plane_sum_start(devices, places, flat, used, source, landing, sems):
    me, x, y, z, xpeer, ypeer = places[:6]
    if flat.shape[0] > used:
        flat[used:, :] = jnp.zeros((flat.shape[0] - used, flat.shape[1]), BF)
    spread_flat(devices, places, flat, [source.at[f] for f in range(4)])
    return [send(source.at[f], landing.at[f], sems.at[0, f], sems.at[1, f], dp=peer)
            for f, peer in ((3, me + 3 - 2 * x - 4 * y), (1, xpeer), (2, ypeer))]


def four_sum(parts, at):
    return (parts[0][at].astype(F32) + parts[1][at].astype(F32) + parts[2][at].astype(F32) + parts[3][at].astype(F32)).astype(BF)


def cross_back_kernel(devices, info, dq, dk, dv, wc, nc_hbm, memory_hbm, res_hbm, gres_hbm, output_hbm, mixed, wo, norms,
                      part0, part1, part2, part3,
                      gmem_out, output_out, gnew_out, gmix_out, give0, give1, give2, give3, more_ref, sums_ref,
                      nc, memory, res, gres, output_ref, gmem_ref, turned_a, turned_b, gmix_ref, flat, flat_o, source, landing, pieces, landed, blocks,
                      mine_a, theirs_a, mine_b, theirs_b, low_all, sems_a, sems_b, late_sems, out_sems, turned_sems, z_sems, zz_sems, plane_sems):
    tokens, features = nc.shape
    cols = dq.shape[1]
    across = devices // 4
    places = places_of(devices)
    me, x, y, z, xpeer, ypeer, order, ahead, behind = places
    late = Late([(nc_hbm, nc), (memory_hbm, memory), (res_hbm, res), (gres_hbm, gres), (output_hbm, output_ref)], late_sems)
    out = Out([(gres, gnew_out), (gmix_ref, gmix_out)], out_sems)
    for level in range(across):
        pieces[level] = four_sum((part0, part1, part2, part3), level)
    greet([{"head": 1 - lax.axis_index("head")}] + [{"dp": ahead(d)} for d in order]
          + [{"dp": peer} for peer in (xpeer, ypeer, me + 3 - 2 * x - 4 * y)])
    z_copies = z_sum_start(devices, places, pieces, landed, z_sems)
    branch_give(dq, dk, dv, wc, mine_a, theirs_a, mine_b, theirs_b, sems_a, sems_b)
    late.wait(0, 1)
    branch_weights(nc, memory, dq, dk, dv, flat)
    plane_copies = plane_sum_start(devices, places, flat, 3 * cols, source, landing, plane_sems)
    blocks[0] = z_sum_end(places, pieces, landed, z_copies)
    zz_copies = [send(blocks.at[0], blocks.at[d], zz_sems.at[0, d], zz_sems.at[1, d], dp=ahead(d)) for d in order]
    sums_ref[...] = jnp.zeros_like(sums_ref)
    late.wait(2, 3)

    def close(step, rows):
        other_core(mine_a, theirs_a, sems_a, step).wait_recv()
        grad = mine_a[rows, :].astype(F32) + theirs_a[rows, :].astype(F32)
        unit, scale = normalise(res[rows, :])
        gnew = norm_back(unit, scale, norms[4:5, :], grad) + gres[rows, :]
        gres[rows, :] = gnew
        out.start(0, step)
        sums_ref[0:8, :] += fold_rows(grad * unit)
        sums_ref[8:16, :] += fold_rows(grad)
        low = gnew.astype(BF)
        low_all[rows, :] = low
        gmix_ref[:, rows] = nt(low, wo[...]).astype(BF).T
        out.start(1, step)
        other_core(mine_b, theirs_b, sems_b, step).wait_recv()
        total = (mine_b[rows, :].astype(F32) + theirs_b[rows, :].astype(F32)).astype(BF)
        gmem_ref[pl.ds(step * (CHUNK // UNIT), CHUNK // UNIT)] = in_tiles(total)
    chunks(tokens, close)
    flat_o[0:cols, :] = tn(mixed[...], low_all[...]).astype(BF)
    if flat_o.shape[0] > cols:
        flat_o[cols:, :] = jnp.zeros((flat_o.shape[0] - cols, features), BF)
    gives = (give0, give1, give2, give3)
    spread_flat(devices, places, flat_o, gives)
    for copy in plane_copies:
        copy.wait_recv()
    for d in range(across):
        more_ref[d] = four_sum((source.at[0], landing.at[1], landing.at[2], landing.at[3]), d)
    late.wait(4)
    turn_rows(gmem_ref, turned_a, info[0, DOCS + 1])
    turn_rows(output_ref, turned_b, info[0, DOCS + 1])
    turned = Late([(turned_a, gmem_out), (turned_b, output_out)], turned_sems)
    for copy in zz_copies:
        copy.wait_recv()
    ready_rows = blocks.shape[1]
    for ref in gives:
        for d in range(across):
            ref[d, 0:ready_rows, :] = blocks[d]
    for copy in z_copies + zz_copies + plane_copies:
        copy.wait_send()
    turned.wait(0, 1)
    out.drain(tokens)
    drain(tokens, mine_a, theirs_a, sems_a)
    drain(tokens, mine_b, theirs_b, sems_b)


def cross_back(devices, info, dq, dk, dv, wc, nc, memory, res, gres, output, mixed, wo, norms, parts):
    tokens, features = nc.shape
    cols = dq.shape[1]
    across, ready_rows = devices // 4, parts[0].shape[1]
    flat_rows, o_rows = whole_blocks(3 * cols, devices), whole_blocks(cols, devices)
    give = ((across, ready_rows + o_rows // devices, features), BF, "V")
    part = (across, flat_rows // devices, features)
    wide = (tokens, features)
    outs = [(wide, BF, "A"), (wide, BF, "A"), (wide, F32, "A"), ((cols, tokens), BF, "A")] + [give] * 4 + [
        (part, BF, "V"), ((16, features), F32, "V")]
    low, high = pltpu.VMEM(wide, BF), pltpu.VMEM(wide, F32)
    small = pltpu.VMEM((across, ready_rows, features), BF)
    z_sems = pltpu.SemaphoreType.DMA((2, across))
    tiles = pltpu.VMEM((tokens // UNIT, UNIT, features), BF)
    scratch = [low, low, high, high, tiles, tiles, low, low, pltpu.VMEM((cols, tokens), BF), pltpu.VMEM((flat_rows, features), BF),
               pltpu.VMEM((o_rows, features), BF), pltpu.VMEM((4,) + part, BF), pltpu.VMEM((4,) + part, BF), small, small, small]
    scratch += [low] * 5 + [pair_sems(tokens)] * 2 + [pltpu.SemaphoreType.DMA((5,)), out_semaphores(2, tokens), pltpu.SemaphoreType.DMA((2,)), z_sems, z_sems,
                                                 pltpu.SemaphoreType.DMA((2, 4))]
    return call(partial(cross_back_kernel, devices), "cross_back",
                [info, dq, dk, dv, wc, nc, memory, res, gres, in_tiles(output), mixed, wo, norms] + parts, "SVVVVAAAAAVVVVVVV", outs, scratch, 4)


def self_back_kernel(devices, ready_rows, info, dq, dk, dv, ws, nq_hbm, nkv_hbm, query_hbm, kv_hbm, gres_hbm, norms, sums_c, sums_f, more_in,
                     part0, part1, part2, part3,
                     gquery_out, gkv_out, last_ref, more_ref, gnorm_ref,
                     nq, nkv, query, kv, gres, gquery_ref, gkv_ref, turned_a, turned_b, flat, source, landing, pieces, landed, more_pieces, more_landed,
                     norm_mine, norm_all, mine_a, theirs_a, mine_b, theirs_b, sums, sems_a, sems_b, late_sems, out_sems,
                     z_sems, more_z_sems, plane_sems, n_sems, part_rows, part_sems, *spread_sems):
    tokens, features = nq.shape
    across = devices // 4
    places = places_of(devices)
    me, x, y, z, xpeer, ypeer, order, ahead, behind = places
    late = Late([(nq_hbm, nq), (nkv_hbm, nkv), (query_hbm, query), (kv_hbm, kv), (gres_hbm, gres)], late_sems)
    in_rows, more_rows = more_in.shape[1], more_ref.shape[2]
    late_parts = Late([(part.at[:, pl.ds(ready_rows, more_rows - in_rows)], part_rows.at[f])
                       for f, part in enumerate((part0, part1, part2, part3))], part_sems)
    others = [lax.rem(me + d, devices) for d in range(1, devices)]
    greet([{"head": 1 - lax.axis_index("head")}] + [{"dp": other} for other in others])
    late.wait(0, 1)
    branch_weights(nq, nkv, dq, dk, dv, flat)
    plane_copies = plane_sum_start(devices, places, flat, 3 * dq.shape[1], source, landing, plane_sems)
    late_parts.wait(0, 1, 2, 3)
    for level in range(across):
        more_pieces[level, 0:in_rows, :] = more_in[level]
        more_pieces[level, in_rows:, :] = four_sum([part_rows.at[f] for f in range(4)], level)
    more_copies = z_sum_start(devices, places, more_pieces, more_landed, more_z_sems)
    branch_give(dq, dk, dv, ws, mine_a, theirs_a, mine_b, theirs_b, sems_a, sems_b)
    more_ref[0, 0] = z_sum_end(places, more_pieces, more_landed, more_copies)
    more = Spread(places, more_ref, *spread_sems[:5])
    more.start()
    sums[...] = jnp.zeros_like(sums)
    late.wait(2, 3, 4)

    def close(step, rows):
        other_core(mine_a, theirs_a, sems_a, step).wait_recv()
        grad = mine_a[rows, :].astype(F32) + theirs_a[rows, :].astype(F32)
        unit, scale = normalise(query[rows, :].astype(F32))
        tiles = pl.ds(step * (CHUNK // UNIT), CHUNK // UNIT)
        gquery_ref[tiles] = in_tiles((norm_back(unit, scale, norms[0:1, :], grad) + gres[rows, :]).astype(BF))
        sums[0:8, :] += fold_rows(grad * unit)
        sums[8:16, :] += fold_rows(grad)
        other_core(mine_b, theirs_b, sems_b, step).wait_recv()
        grad = mine_b[rows, :].astype(F32) + theirs_b[rows, :].astype(F32)
        unit, scale = normalise(kv[rows, :].astype(F32))
        gkv_ref[tiles] = in_tiles(norm_back(unit, scale, norms[2:3, :], grad).astype(BF))
        sums[16:24, :] += fold_rows(grad * unit)
        sums[24:32, :] += fold_rows(grad)
    middle = tokens // 2
    chunks(middle, close)
    more.relay()
    chunks(tokens, close, middle)
    parts = [sums[8 * i:8 * i + 8, :] for i in range(4)]
    parts += [sums_c[0:8, :], sums_c[8:16, :], sums_f[0:8, :], sums_f[8:16, :]]
    norm_mine[...] = jnp.concatenate([jnp.sum(part, 0, keepdims=True) for part in parts], 0)
    for copy in plane_copies:
        copy.wait_recv()
    for level in range(across):
        pieces[level] = four_sum((source.at[0], landing.at[1], landing.at[2], landing.at[3]), level)
    z_copies = z_sum_start(devices, places, pieces, landed, z_sems)
    n_copies = [send(norm_mine, norm_all.at[d], n_sems.at[0, d], n_sems.at[1, d], dp=other)
                for d, other in zip(range(1, devices), others)]
    turn_rows(gquery_ref, turned_a, info[0, DOCS + 1])
    more.diagonal()
    last_ref[0, 0] = z_sum_end(places, pieces, landed, z_copies)
    last = Spread(places, last_ref, *spread_sems[5:])
    last.start()
    turn_rows(gkv_ref, turned_b, info[0, DOCS + 1])
    turned = Late([(turned_a, gquery_out), (turned_b, gkv_out)], out_sems)
    last.relay()
    last.diagonal()
    total = norm_mine[...]
    for d, copy in zip(range(1, devices), n_copies):
        copy.wait_recv()
        total = total + norm_all[d]
    gnorm_ref[...] = total
    more.finish()
    last.finish()
    more.drain()
    last.drain()
    for copy in more_copies + plane_copies + z_copies + n_copies:
        copy.wait_send()
    turned.wait(0, 1)
    drain(tokens, mine_a, theirs_a, sems_a)
    drain(tokens, mine_b, theirs_b, sems_b)


def self_back(devices, ready_rows, info, dq, dk, dv, ws, nq, nkv, query, kv, gres, norms, sums_c, sums_f, more_in, parts):
    tokens, features = nq.shape
    cols = dq.shape[1]
    across, more_rows = devices // 4, more_in.shape[1] + parts[0].shape[1] - ready_rows
    flat_rows = whole_blocks(3 * cols, devices)
    rows = flat_rows // devices
    wide = (tokens, features)
    outs = [(wide, BF, "A"), (wide, BF, "A"), ((4, across, rows, features), BF, "V"), ((4, across, more_rows, features), BF, "V"),
            ((8, features), F32, "V")]
    low, high = pltpu.VMEM(wide, BF), pltpu.VMEM(wide, F32)
    small, tiny = pltpu.VMEM((across, more_rows, features), BF), pltpu.VMEM((across, rows, features), BF)
    four = pltpu.VMEM((4, across, rows, features), BF)
    D = pltpu.SemaphoreType.DMA
    tiles = pltpu.VMEM((tokens // UNIT, UNIT, features), BF)
    scratch = [low, low, low, low, high, tiles, tiles, low, low, pltpu.VMEM((flat_rows, features), BF), four, four, tiny, tiny, small, small,
               pltpu.VMEM((8, features), F32), pltpu.VMEM((devices, 8, features), F32)]
    scratch += [low] * 4 + [pltpu.VMEM((32, features), F32)] + [pair_sems(tokens)] * 2
    scratch += [D((5,)), D((2,)), D((2, across)), D((2, across)), D((2, 4)), D((2, devices)),
                pltpu.VMEM((4, across, more_rows - more_in.shape[1], features), BF), D((4,))]
    scratch += [D((2, across))] * 10
    return call(partial(self_back_kernel, devices, ready_rows), "self_back",
                [info, dq, dk, dv, ws, nq, nkv, query, kv, gres, norms, sums_c, sums_f, more_in] + parts, "SVVVVAAAAAVVVVAAAA", outs, scratch, 5)


def update_kernel(devices, firsts, late_rows, more_first, held, me_ref, *refs):
    hbm, (grad_out, first_out, second_out, new_out, gquery_out, gkv_out) = refs[:11], refs[11:17]
    last, more, part0, part1, part2, part3, master, first, second, held_q, held_kv = refs[17:28]
    taken, grad_ref, first_ref, second_ref, new_ref, sems, out_sems = refs[28:]
    entering = Late(list(zip(hbm, refs[17:28])), sems)
    slots = master.shape[0]
    across = devices // 4
    me = me_ref[0]
    here, level = lax.rem(me, 4), lax.div(me, 4)
    count = held[0, 127]
    results = list(zip((grad_ref, first_ref, second_ref, new_ref), (grad_out, first_out, second_out, new_out)))
    entering.wait(9, 10)
    leaving = Late([(held_q, gquery_out), (held_kv, gkv_out)], out_sems.at[0])
    entering.wait(*range(9))

    def lookup(row, size, start=0):
        block = lax.div(row, size)
        behind = lax.rem(level - lax.div(block, 4) + across, across)
        return lax.rem(block, 4) ^ here, behind, pl.ds(pl.multiple_of(lax.rem(row, size) + start, UNIT), UNIT)

    def one(slot, carry):
        @pl.when(slot < count)
        def _():
            unit = held[0, slot]

            @pl.when(unit < firsts[0])
            def _():
                taken[...] = last[lookup(unit * UNIT, last.shape[2])]

            @pl.when((unit >= firsts[0]) & (unit < firsts[1]))
            def _():
                taken[...] = more[lookup((unit - firsts[0]) * UNIT, more_first)]

            @pl.when((unit >= firsts[1]) & (unit < firsts[2]))
            def _():
                taken[...] = more[lookup((unit - firsts[1]) * UNIT, more.shape[2] - more_first, more_first)]

            @pl.when(unit >= firsts[2])
            def _():
                offset, behind, rows = lookup((unit - firsts[2]) * UNIT, late_rows)
                for f, part in enumerate((part0, part1, part2, part3)):
                    @pl.when(offset == f)
                    def _():
                        taken[...] = part[behind, rows]
            gradient = taken[...].astype(F32)
            first_new, second_new, weight = adamw_step(gradient, first[slot], second[slot], master[slot], RATE_MATRIX, WEIGHT_DECAY)
            grad_ref[slot] = gradient
            first_ref[slot] = first_new
            second_ref[slot] = second_new
            new_ref[slot] = weight

        @pl.when(slot >= count)
        def _():
            for ref in (grad_ref, first_ref, second_ref, new_ref):
                ref[slot] = jnp.zeros(ref.shape[1:], F32)
        return carry
    half = slots // 2
    lax.fori_loop(0, half, one, 0)
    early = Late([(ref.at[pl.ds(0, half)], out.at[pl.ds(0, half)]) for ref, out in results], out_sems.at[1])
    lax.fori_loop(half, slots, one, 0)
    rest = Late([(ref.at[pl.ds(half, half)], out.at[pl.ds(half, half)]) for ref, out in results], out_sems.at[2])
    for copies in (early, rest):
        copies.wait(*range(4))
    leaving.wait(0, 1)


def update(devices, firsts, late_rows, more_first, held, me, last, more, parts, master, first, second, gquery, gkv):
    outs = [(master.shape, F32, "A")] * 4 + [(gquery.shape, BF, "A")] * 2
    args = [last, more] + parts + [master, first, second, gquery, gkv]
    scratch = [pltpu.VMEM(arg.shape, arg.dtype) for arg in args] + [pltpu.VMEM((UNIT, master.shape[2]), BF)]
    scratch += [pltpu.VMEM(master.shape, F32)] * 4 + [pltpu.SemaphoreType.DMA((11,)), pltpu.SemaphoreType.DMA((3, 4))]
    return call(partial(update_kernel, devices, firsts, late_rows, more_first), "update", [held, me] + args, "SS" + "A" * 11,
                outs, scratch)


def adamw_step(gradient, first, second, weight, rate, decay):
    first_new = BETA_ONE * first + (1.0 - BETA_ONE) * gradient
    second_new = BETA_TWO * second + (1.0 - BETA_TWO) * gradient * gradient
    corr_one = 1.0 - BETA_ONE**STEP
    corr_two = 1.0 - BETA_TWO**STEP
    direction = first_new / corr_one / (jnp.sqrt(second_new / corr_two) + ADAM_EPS)
    return (first_new, second_new, weight - rate * (direction + decay * weight))


def local(
    query_stream, kv_stream, memory, out_grad, lengths, obs_rank, obs_count, unit_owner,
    master, first_moment, second_moment, norm_master, norm_first, norm_second,
):
    devices = lax.axis_size("dp")
    shards = lax.axis_size("head")
    me = lax.axis_index("dp")
    slots, unit_rows, features = master.shape[0], master.shape[2], master.shape[3]
    units = unit_owner.shape[0]
    norm_share = norm_master.shape[0]
    cols = features // shards
    hidden = (units * unit_rows - 8 * cols) // 2

    shape = (slots, unit_rows, features)
    norm_row = lax.dynamic_update_slice(
        jnp.zeros((1, features), F32), norm_master.reshape(1, norm_share), (0, lax.rem(me * norm_share, features)))
    rank_row, count_row = obs_rank.reshape(1, ROW), obs_count.reshape(1, ROW)
    place_of, held, rank_row, count_row, steps, info = plan(unit_owner, lengths, me.reshape(1), rank_row, count_row, slots + 1)
    nq, nkv, qt, k, kt, v, vt, kc, kct, vc, vct, query, kv, source, cotangent, ws, wc, wo_self, wo_cross, w1, w2, norms, *tables = project(
        devices, place_of, info, master.reshape(shape), norm_row, rank_row, query_stream, kv_stream, memory, out_grad, cols, hidden)
    mixed_self, mixed_self_t, total_self = attend_forward(steps, qt, k, vt, tables, count_row, True)
    residual, nc, qct = self_out(mixed_self, wo_self, query, wc, norms)
    mixed_cross, mixed_cross_t, total_cross = attend_forward(steps, qct, kc, vct, tables, count_row, False)
    output, grad_cross_res, grad_mixed, *parts, sums_f = feed_forward(
        devices, mixed_cross, wo_cross, residual, w1, w2, cotangent, norms)
    tie = lax.optimization_barrier
    ready_rows = parts[0].shape[1]
    parts = [parts[0]] + [plane_swap(parts[f], devices, f) for f in (1, 2, 3)]
    dq, dk, dv = attend_backward(steps, qct, kc, kct, vc, grad_mixed, mixed_cross_t, total_cross, tables, count_row, [], False)
    parts, dq = tie((parts, dq))
    grad_memory, output, grad_residual, grad_mixed, *parts, more, sums_c = cross_back(
        devices, info, dq, dk, dv, wc, nc, source, residual, grad_cross_res, output, mixed_self, wo_self, norms, parts)
    parts = [parts[0]] + [plane_swap(parts[f], devices, f) for f in (1, 2, 3)]
    dq, dk, dv, grad_memory, output = attend_backward(
        steps, qt, k, kt, v, grad_mixed, mixed_self_t, total_self, tables, count_row, [grad_memory, output], True)
    parts, dq = tie((parts, dq))
    more_first = more.shape[1]
    grad_query, grad_kv, last, more, norm_grads = self_back(
        devices, ready_rows, info, dq, dk, dv, ws, nq, nkv, query, kv, grad_residual, norms, sums_c, sums_f, more, parts)

    firsts = [count * cols // unit_rows for count in (3, 6, 7)]
    weight_grad, weight_first, weight_second, weight_new, grad_query, grad_kv = update(
        devices, firsts, ready_rows, more_first, held, me.reshape(1), last, more, parts, master.reshape(shape),
        first_moment.reshape(shape), second_moment.reshape(shape), grad_query, grad_kv)
    weight_grad, weight_first, weight_second, weight_new = [
        part.reshape(master.shape) for part in (weight_grad, weight_first, weight_second, weight_new)]
    norm_grad = lax.dynamic_slice_in_dim(norm_grads.reshape(-1), me * norm_share, norm_share)
    norm_first_new, norm_second_new, norm_new = adamw_step(
        norm_grad, norm_first, norm_second, norm_master, RATE_NORM, 0.0)
    return (
        output, grad_query, grad_kv, grad_memory, weight_grad, weight_first, weight_second, weight_new,
        norm_grad, norm_first_new, norm_second_new, norm_new,
    )


def solution(mesh):
    in_specs = (
        P("dp", None),
        P("dp", None),
        P("dp", None),
        P("dp", None),
        P("dp", None),
        P("dp"),
        P("dp"),
        P(),
        P("dp", "head", None, None),
        P("dp", "head", None, None),
        P("dp", "head", None, None),
        P("dp"),
        P("dp"),
        P("dp"),
    )
    out_specs = (
        P("dp", None),
        P("dp", None),
        P("dp", None),
        P("dp", None),
        P("dp", "head", None, None),
        P("dp", "head", None, None),
        P("dp", "head", None, None),
        P("dp", "head", None, None),
        P("dp"),
        P("dp"),
        P("dp"),
        P("dp"),
    )
    return jax.shard_map(local, mesh=mesh, in_specs=in_specs, out_specs=out_specs, check_vma=False)
```

```python
from functools import partial

import jax
import jax.numpy as jnp
from jax import lax
from jax.experimental import pallas as pl
from jax.experimental.pallas import tpu as pltpu
from jax.sharding import PartitionSpec as P

HEAD_DIM = 64
ROW = 2048
DOCS = 32
STEP = 10
UNIT = 16

EPS_NORM = 1e-05
ADAM_EPS = 1e-08
BETA_ONE = 0.5
BETA_TWO = 0.5
RATE_MATRIX = 0.1
RATE_NORM = 0.3
WEIGHT_DECAY = 0.01

F32 = jnp.float32
BF = jnp.bfloat16
TQ = 256
TK = 512
FAR = 32768.0
LANES = (64, 72, 80)


def nt(a, b):
    return lax.dot_general(a, b, (((1,), (1,)), ((), ())), preferred_element_type=F32)


def nn(a, b):
    return lax.dot_general(a, b, (((1,), (0,)), ((), ())), preferred_element_type=F32)


def doc_bounds(len_ref):
    starts, ends = [], []
    at = jnp.int32(0)
    for d in range(DOCS):
        starts.append(at)
        at = at + len_ref[0, d]
        ends.append(at)
    return starts, ends


def key_range(starts, ends, q0):
    low = jnp.int32(0)
    high = jnp.int32(0)
    for d in range(DOCS):
        low = jnp.where(starts[d] <= q0, starts[d], low)
        high = jnp.where(starts[d] <= q0 + TQ - 1, ends[d], high)
    first = lax.div(low, 128) * 128
    steps = lax.div(high - first + TK - 1, TK)
    return first, steps


def mask_tables(len_ref, rank_ref, side_ref, hot_ref, rank_cols):
    starts, ends = doc_bounds(len_ref)
    lanes = lax.broadcasted_iota(jnp.int32, (1, 128), 1)
    start_lane = jnp.full((1, 128), -1, jnp.int32)
    end_lane = jnp.full((1, 128), -1, jnp.int32)
    for d in range(DOCS):
        start_lane = jnp.where(lanes == d, starts[d], start_lane)
        end_lane = jnp.where(lanes == d, ends[d], end_lane)
    one = (lanes == LANES[0]) | (lanes == LANES[1]) | (lanes == LANES[2])
    for t in range(ROW // 256):
        pos = lax.broadcasted_iota(jnp.int32, (256, 128), 0) + t * 256
        hot = (pos >= start_lane) & (pos < end_lane)
        side = jnp.where(hot | (lanes >= DOCS), jnp.where(one, -1.0, 0.0), -FAR)
        side_ref[t * 256:(t + 1) * 256, :] = side.astype(BF)
    pos = lax.broadcasted_iota(jnp.int32, (1, ROW), 1)
    first = jnp.zeros((1, ROW), jnp.bool_)
    rows = []
    for d in range(DOCS):
        first = first | (pos == starts[d])
        rows.append(jnp.where((pos >= starts[d]) & (pos < ends[d]), FAR, 0.0))
    hot_ref[...] = jnp.concatenate(rows + [jnp.zeros((128 - DOCS, ROW), F32)], 0).astype(BF)
    rank = jnp.where(first, -1.0, rank_ref[...].astype(F32))
    for t in range(ROW // 128):
        rank_cols[t * 128:(t + 1) * 128, :] = jnp.broadcast_to(rank[:, t * 128:(t + 1) * 128], (128, 128)).T


STEPS = (ROW // TQ) * -(-ROW // TK) + 8


def step_table(len_ref, table):
    starts, ends = doc_bounds(len_ref)
    idle = ROW // TQ

    def put(at, tile, first):
        table[0, at] = tile
        table[1, at] = first
    put(0, idle, ROW)
    put(1, idle, ROW)
    at = jnp.int32(2)
    for tile in range(idle):
        first, steps = key_range(starts, ends, tile * TQ)

        def fill(s, at):
            put(at, tile, first + s * TK)
            return at + 1
        at = lax.fori_loop(0, steps, fill, at)
    put(at, idle, ROW)
    put(at + 1, idle, ROW)
    table[0, STEPS - 1] = at


def step_of(table, i):
    return table[0, i], pl.multiple_of(table[1, i], 128)


def real_step(table, i):
    return jnp.minimum(table[0, i], ROW // TQ - 1), pl.multiple_of(table[1, i], 128)


def padded(ref):
    return ref.at[pl.ds(0, ROW)] if ref.shape[0] > ref.shape[1] else ref.at[:, pl.ds(0, ROW)]


def fill_padding(refs, side_ref):
    for ref in refs:
        if ref.shape[0] > ref.shape[1]:
            ref[ROW:, :] = jnp.zeros((TK, ref.shape[1]), ref.dtype)
        else:
            ref[:, ROW:] = jnp.zeros((ref.shape[0], TK), ref.dtype)
    lanes = lax.broadcasted_iota(jnp.int32, (TK, 128), 1)
    side_ref[ROW:, :] = jnp.where(lanes < DOCS, -FAR, 0.0).astype(BF)


def seen_bias(rank_cols, counts, tile, k0):
    rank = rank_cols[pl.ds(k0, TK), :]
    rank = jnp.concatenate([rank] * (TQ // 128), 1)
    kpos = lax.broadcasted_iota(jnp.int32, (TK, TQ), 0)
    qpos = lax.broadcasted_iota(jnp.int32, (TK, TQ), 1)
    off_diag = (kpos - qpos) != (tile * TQ - k0)
    allowed = (rank < counts[tile, 0:1, :]) & (off_diag | (rank < 0.0))
    return jnp.where(allowed, 0.0, -FAR * FAR)


def count_tiles(counts, count_ref):
    for tile in range(ROW // TQ):
        counts[tile] = jnp.broadcast_to(count_ref[:, tile * TQ:(tile + 1) * TQ].astype(F32), (8, TQ))


def query_columns(qt, qt_ref, side, tile, h, q0):
    rows = qt_ref[h * HEAD_DIM:(h + 1) * HEAD_DIM, pl.ds(q0, TQ)].astype(F32) * HEAD_DIM ** -0.5
    own, other = h % 2 * HEAD_DIM, (1 - h % 2) * HEAD_DIM
    qt[tile, h, own:own + HEAD_DIM, :] = rows.astype(BF)
    qt[tile, h, other:other + HEAD_DIM, :] = jnp.zeros((HEAD_DIM, TQ), BF)
    qt[tile, h, 128:256, :] = side


def pair_rows(ref, side_ref, h, k0):
    return jnp.concatenate([ref[pl.ds(k0, TK), h // 2 * 128:(h // 2 + 1) * 128], side_ref[pl.ds(k0, TK), :]], 1)


def attn_fwd_kernel(with_seen, heads, table, count_ref, qt_hbm, hot_hbm, k_hbm, vt_hbm, side_hbm, rank_hbm,
                    o_out, ot_out, lse_ref, qt, acc, top, sc, probs, fade, counts,
                    qt_ref, hot_ref, k_ref, vt_ref, side_ref, rank_cols, o_ref, ot_ref, late_sems, out_sems):
    pairs = [(qt_hbm, qt_ref), (hot_hbm, hot_ref), (k_hbm, padded(k_ref)), (vt_hbm, padded(vt_ref)),
             (side_hbm, padded(side_ref))]
    late = Late(pairs + ([(rank_hbm, padded(rank_cols))] if with_seen else []), late_sems)
    fill_padding((k_ref, vt_ref, rank_cols), side_ref)
    out = Out([(o_ref, o_out), (ot_ref, ot_out)], out_sems)
    tiles = ROW // TQ
    lse_ref[...] = jnp.zeros_like(lse_ref)
    acc[...] = jnp.zeros_like(acc)
    top[...] = jnp.full_like(top, -jnp.inf)
    if with_seen:
        count_tiles(counts, count_ref)
    late.wait(0, 1)

    def prepare(tile, c):
        q0 = pl.multiple_of(tile * TQ, TQ)
        for h in range(heads):
            query_columns(qt, qt_ref, hot_ref[:, pl.ds(q0, TQ)], tile, h, q0)
        return c
    lax.fori_loop(0, tiles, prepare, 0)
    late.wait(*range(2, 6 if with_seen else 5))
    ones = jnp.ones((16, TK), BF)

    def one_step(s, c):
        out_tile, _ = step_of(table, s)
        _, out_k = real_step(table, s)
        mid_tile, _ = step_of(table, s + 1)
        in_tile, in_k = real_step(table, s + 2)
        sums = []
        for h in range(heads):
            values = jnp.concatenate([vt_ref[h * HEAD_DIM:(h + 1) * HEAD_DIM, pl.ds(out_k, TK)], ones], 0)
            sums.append(acc[out_tile, h] * fade[h:h + 1, :] + nn(values, probs[h]))
        old = top[mid_tile]
        news = []
        for h in range(heads):
            score = sc[h]
            new = jnp.maximum(old[h:h + 1, :], jnp.max(score, 0, keepdims=True))
            probs[h] = jnp.exp(score - new).astype(BF)
            news.append(new)
        new = jnp.concatenate(news + [old[heads:, :]], 0)
        fade[...] = jnp.exp(old - new)
        bias = seen_bias(rank_cols, counts, in_tile, in_k) if with_seen else None
        for h in range(heads):
            score = nn(pair_rows(k_ref, side_ref, h, in_k), qt[in_tile, h])
            sc[h] = score + bias if with_seen else score
        top[mid_tile] = new
        for h in range(heads):
            acc[out_tile, h] = sums[h]
        return c
    lax.fori_loop(0, table[0, STEPS - 1], one_step, 0)

    def finish(tile, c):
        q0 = pl.multiple_of(tile * TQ, TQ)
        outs = []
        peak = top[tile]
        for h in range(heads):
            a = acc[tile, h]
            total = a[HEAD_DIM:HEAD_DIM + 1, :]
            outs.append(a[:HEAD_DIM, :] * (1.0 / total))
            lse_ref[h:h + 1, pl.ds(q0, TQ)] = peak[h:h + 1, :] + jnp.log(total)
        mixed = jnp.concatenate(outs, 0).astype(BF)
        ot_ref[:, pl.ds(q0, TQ)] = mixed
        out.start(1, tile)
        o_ref[pl.ds(q0, TQ), :] = mixed.T
        out.start(0, tile)
        return c
    lax.fori_loop(0, tiles, finish, 0)
    out.drain(ROW)


def attend_forward(steps, qt, k, vt, tables, count, with_seen):
    cols, rows = qt.shape
    heads = cols // HEAD_DIM
    side, hot, rank_cols = tables
    args = [steps, count, qt, hot, k, vt, side, rank_cols]
    across, down = (cols, rows), (rows, cols)
    held = [pltpu.VMEM(arg.shape, BF) for arg in (qt, hot)] + [
        pltpu.VMEM((rows + TK, cols), BF), pltpu.VMEM((cols, rows + TK), BF), pltpu.VMEM((rows + TK, 128), BF),
        pltpu.VMEM((rows + TK, 128), F32)]
    return call(partial(attn_fwd_kernel, with_seen, heads), "attend_self_forward" if with_seen else "attend_cross_forward",
                args, "SV" + "A" * 6, [(down, BF, "A"), (across, BF, "A"), ((8, rows), F32, "V")],
                [pltpu.VMEM((ROW // TQ, heads, 256, TQ), BF), pltpu.VMEM((ROW // TQ + 1, heads, HEAD_DIM + 16, TQ), F32),
                 pltpu.VMEM((ROW // TQ + 1, 8, TQ), F32), pltpu.VMEM((heads, TK, TQ), F32), pltpu.VMEM((heads, TK, TQ), BF),
                 pltpu.VMEM((8, TQ), F32), pltpu.VMEM((ROW // TQ, 8, TQ), F32)] + held
                + [pltpu.VMEM(down, BF), pltpu.VMEM(across, BF), pltpu.SemaphoreType.DMA((6,)), out_semaphores(2, rows)])


def three_rows(value):
    high = value.astype(BF).astype(F32)
    middle = (value - high).astype(BF).astype(F32)
    row = lax.broadcasted_iota(jnp.int32, (128, value.shape[1]), 0)
    return jnp.where(row == LANES[0], high, jnp.where(row == LANES[1], middle, jnp.where(row == LANES[2], value - high - middle, 0.0)))


def attn_bwd_kernel(with_seen, heads, table, count_ref, lse_ref, qt_hbm, hot_hbm, gt_hbm, ot_hbm, k_hbm, kt_hbm, v_hbm, side_hbm,
                    rank_hbm, *refs):
    passed = (len(refs) - 30) // 3
    pass_in, (dq_out, dk_out, dv_out), pass_out, refs = refs[:passed], refs[passed:passed + 3], refs[passed + 3:2 * passed + 3], refs[2 * passed + 3:]
    (dk_sum, dv_sum, dq_sum, qt, gt, q_own, g_own, sc, dps, all_ds, all_p, counts,
     qt_ref, hot_ref, gt_ref, ot_ref, k_ref, kt_ref, v_ref, side_ref, rank_cols, *held, dq_ref, dk_ref, dv_ref,
     late_sems, out_sems, pass_sem) = refs
    pairs = [(qt_hbm, qt_ref), (hot_hbm, hot_ref), (gt_hbm, gt_ref), (ot_hbm, ot_ref), (k_hbm, padded(k_ref)),
             (kt_hbm, padded(kt_ref)), (v_hbm, padded(v_ref)), (side_hbm, padded(side_ref))]
    late = Late(pairs + ([(rank_hbm, padded(rank_cols))] if with_seen else []), late_sems)
    fill_padding((k_ref, kt_ref, v_ref, rank_cols), side_ref)
    entering = Late(list(zip(pass_in, held)), pass_sem.at[0])
    out = Out([(dq_ref, dq_out), (dk_ref, dk_out), (dv_ref, dv_out)], out_sems)
    tiles = ROW // TQ
    dk_sum[...] = jnp.zeros_like(dk_sum)
    dv_sum[...] = jnp.zeros_like(dv_sum)
    dq_sum[...] = jnp.zeros_like(dq_sum)
    if with_seen:
        count_tiles(counts, count_ref)
    late.wait(0, 1, 2, 3)

    def prepare(tile, c):
        q0 = pl.multiple_of(tile * TQ, TQ)
        hot = hot_ref[:, pl.ds(q0, TQ)].astype(F32)
        for h in range(heads):
            rows = slice(h * HEAD_DIM, (h + 1) * HEAD_DIM)
            side = hot + three_rows(lse_ref[h:h + 1, pl.ds(q0, TQ)])
            query_columns(qt, qt_ref, side.astype(BF), tile, h, q0)
            grads = gt_ref[rows, pl.ds(q0, TQ)]
            delta = jnp.sum(grads.astype(F32) * ot_ref[rows, pl.ds(q0, TQ)].astype(F32), 0, keepdims=True)
            other = (1 - h % 2) * HEAD_DIM
            gt[tile, h, h % 2 * HEAD_DIM:(h % 2 + 1) * HEAD_DIM, :] = grads
            gt[tile, h, other:other + HEAD_DIM, :] = jnp.zeros((HEAD_DIM, TQ), BF)
            gt[tile, h, 128:256, :] = three_rows(delta).astype(BF)
        lane = lax.broadcasted_iota(jnp.int32, (TQ, heads * HEAD_DIM), 1)
        for held_rows, source in ((q_own, qt_ref), (g_own, gt_ref)):
            rows = source[:, pl.ds(q0, TQ)].T
            for h in range(heads):
                own = (lane >= h * HEAD_DIM) & (lane < (h + 1) * HEAD_DIM)
                held_rows[tile, h * TQ:(h + 1) * TQ, :] = jnp.where(own, rows, jnp.zeros_like(rows))
        return c
    lax.fori_loop(0, tiles, prepare, 0)
    late.wait(*range(4, 9 if with_seen else 8))
    entering.wait(*range(passed))
    leaving = Late(list(zip(held, pass_out)), pass_sem.at[1])

    def one_step(s, c):
        out_tile, out_k = step_of(table, s)
        read_tile, read_k = real_step(table, s)
        in_tile, in_k = real_step(table, s + 2)
        keys = pl.ds(out_k, TK)
        own = [slice(h * HEAD_DIM, (h + 1) * HEAD_DIM) for h in range(heads)]
        dk = dk_sum[keys, :] + nn(all_ds[...], q_own[read_tile])
        dv = dv_sum[keys, :] + nn(all_p[...], g_own[read_tile])
        dq = [dq_sum[out_tile, h] + nn(kt_ref[own[h], pl.ds(read_k, TK)], all_ds[:, h * TQ:(h + 1) * TQ]) for h in range(heads)]
        for h in range(heads):
            p = jnp.exp(sc[h])
            all_ds[:, h * TQ:(h + 1) * TQ] = (p * dps[h]).astype(BF)
            all_p[:, h * TQ:(h + 1) * TQ] = p.astype(BF)
        bias = seen_bias(rank_cols, counts, in_tile, in_k) if with_seen else None
        for h in range(heads):
            score = nn(pair_rows(k_ref, side_ref, h, in_k), qt[in_tile, h])
            sc[h] = score + bias if with_seen else score
            dps[h] = nn(pair_rows(v_ref, side_ref, h, in_k), gt[in_tile, h])
        dk_sum[keys, :] = dk
        dv_sum[keys, :] = dv
        for h in range(heads):
            dq_sum[out_tile, h] = dq[h]
        return c
    lax.fori_loop(0, table[0, STEPS - 1], one_step, 0)

    def finish(tile, c):
        q0 = pl.multiple_of(tile * TQ, TQ)
        rows = pl.ds(q0, TQ)
        dq = jnp.concatenate([dq_sum[tile, h] for h in range(heads)], 0) * HEAD_DIM ** -0.5
        dk = dk_sum[rows, :] * HEAD_DIM ** -0.5
        for i, (ref, value) in enumerate(((dq_ref, dq.astype(BF).T), (dk_ref, dk.astype(BF)), (dv_ref, dv_sum[rows, :].astype(BF)))):
            ref[rows, :] = value
            out.start(i, tile)
        return c
    lax.fori_loop(0, tiles, finish, 0)
    out.drain(ROW)
    leaving.wait(*range(passed))


def attend_backward(steps, qt, k, kt, v, gt, ot, lse, tables, count, passed, with_seen):
    rows, cols = v.shape
    heads = cols // HEAD_DIM
    side, hot, rank_cols = tables
    args = [steps, count, lse, qt, hot, gt, ot, k, kt, v, side, rank_cols] + passed
    tiles = ROW // TQ
    like = ((rows, cols), BF, "A")
    summed, own = pltpu.VMEM((rows + TK, cols), F32), pltpu.VMEM((tiles, heads * TQ, cols), BF)
    columns, square = pltpu.VMEM((tiles, heads, 256, TQ), BF), pltpu.VMEM((heads, TK, TQ), F32)
    small = pltpu.VMEM((TK, heads * TQ), BF)
    keys, keys_t = pltpu.VMEM((rows + TK, cols), BF), pltpu.VMEM((cols, rows + TK), BF)
    held = [pltpu.VMEM(arg.shape, BF) for arg in (qt, hot, gt, ot)] + [
        keys, keys_t, keys, pltpu.VMEM((rows + TK, 128), BF), pltpu.VMEM((rows + TK, 128), F32)] + [
        pltpu.VMEM(value.shape, value.dtype) for value in passed]
    return call(partial(attn_bwd_kernel, with_seen, heads), "attend_self_backward" if with_seen else "attend_cross_backward",
                args, "SVV" + "A" * (9 + len(passed)), [like, like, like] + [(value.shape, value.dtype, "A") for value in passed],
                [summed, summed, pltpu.VMEM((tiles + 1, heads, HEAD_DIM, TQ), F32), columns, columns, own, own, square, square,
                 small, small, pltpu.VMEM((ROW // TQ, 8, TQ), F32)] + held + [pltpu.VMEM((rows, cols), BF)] * 3
                + [pltpu.SemaphoreType.DMA((9,)), out_semaphores(3, rows), pltpu.SemaphoreType.DMA((2, 2))])


def send(src, dst, send_sem, recv_sem, **where):
    copy = pltpu.make_async_remote_copy(src_ref=src, dst_ref=dst, send_sem=send_sem, recv_sem=recv_sem,
                                        device_id=where, device_id_type=pl.DeviceIdType.MESH)
    copy.start()
    return copy

def greet(peers):
    barrier = pltpu.get_barrier_semaphore()
    for where in peers:
        pl.semaphore_signal(barrier, inc=1, device_id=where, device_id_type=pl.DeviceIdType.MESH)
    pl.semaphore_wait(barrier, len(peers))

def places_of(count):
    me = lax.axis_index("dp")
    across = count // 4
    x, y, z = lax.rem(me, 2), lax.rem(lax.div(me, 2), 2), lax.div(me, 4)
    xpeer, ypeer = me + 1 - 2 * x, me + 2 - 4 * y
    order = sorted(range(1, across), key=lambda d: min(d, across - d))
    ahead = lambda d: lax.rem(z + d, across) * 4 + y * 2 + x
    behind = lambda d: lax.rem(z + across - d, across) * 4 + y * 2 + x
    return me, x, y, z, xpeer, ypeer, order, ahead, behind

class LineGather:
    def __init__(self, count, piece, units, cut, places, zs, ds, xs, ys, gx, gy):
        self.across, self.piece, self.units, self.cut = count // 4, piece, units, cut
        self.places = places
        self.sems = dict(z=zs, d=ds, x=xs, y=ys, gx=gx, gy=gy)

    def copy(self, name, side, k, arriving=False):
        me, x, y, z, xpeer, ypeer = self.places[:6]
        place = x + 2 * y
        place = dict(z=place, x=place, y=place, d=3 - place, gy=place + 1 - 2 * x, gx=place + 2 - 4 * y)[name]
        if arriving:
            place = {"x": x + 2 * y + 1 - 2 * x, "y": x + 2 * y + 2 - 4 * y, "gx": 3 - x - 2 * y, "gy": 3 - x - 2 * y}.get(name, place)
        level = z + k * (2 * side - 1)
        whole = isinstance(k, int) and k == 0
        half = self.units // 2 if whole else (self.units - self.cut) // 2
        first = 0 if whole else self.cut
        start, size = dict(d=(0, self.cut), gy=(first, half), gx=(first + half, self.units - first - half)).get(name, (0, self.units))
        to = dict(x=xpeer, gx=xpeer, y=ypeer, gy=ypeer).get(name, me + 4 * (1 - 2 * side))
        hop = 1 if name in ("z", "d") and not arriving else 0
        if arriving:
            to = xpeer
        part, sems = self.piece(level * 4 + place, start, size), self.sems[name]
        return pltpu.make_async_remote_copy(
            src_ref=part, dst_ref=part, send_sem=sems.at[0, side, k], recv_sem=sems.at[1, side, k + hop],
            device_id={"dp": to}, device_id_type=pl.DeviceIdType.MESH)

    def here(self, side, k):
        z = self.places[3]
        return z >= k if side == 0 else z + k < self.across

    def onward(self, side):
        z = self.places[3]
        return z + 1 < self.across if side == 0 else z > 0

    def along(self, name, side, k, act):
        pl.when(self.here(side, k) & self.onward(side))(lambda: act(self.copy(name, side, k)))

    def run(self, at_start, at_first, at_second):
        start, wait_send = (lambda copy: copy.start()), (lambda copy: copy.wait_send())

        def diagonal(side, k):
            self.copy("x", side, k, True).wait_recv()
            self.copy("gy", side, k).start()
            self.copy("y", side, k, True).wait_recv()
            self.copy("gx", side, k).start()

        def later(side, k):
            diagonal(side, k)
            self.copy("d", side, k, True).wait_recv()
            pl.when(self.onward(side))(lambda: self.copy("d", side, k).start())
        for side in (0, 1):
            self.along("z", side, 0, start)
        self.copy("x", 0, 0).start()
        self.copy("y", 0, 0).start()
        at_start()
        diagonal(0, 0)

        def level(k, carry):
            for side in (0, 1):
                @pl.when(self.here(side, k))
                def _():
                    self.copy("z", side, k, True).wait_recv()
                    pl.when(self.onward(side))(lambda: self.copy("z", side, k).start())
                    self.copy("x", side, k).start()
                    self.copy("y", side, k).start()

            @pl.when(k == 1)
            def _():
                self.copy("gy", 0, 0, True).wait_recv()
                self.copy("gx", 0, 0, True).wait_recv()
                for side in (0, 1):
                    self.along("d", side, 0, start)
                at_first()

            @pl.when(k > 1)
            def _():
                for side in (0, 1):
                    pl.when(self.here(side, k - 1))(lambda: later(side, k - 1))
            pl.when(k == 2)(at_second)
            return carry
        lax.fori_loop(1, self.across, level, 0)
        for side in (0, 1):
            pl.when(self.here(side, self.across - 1))(lambda: later(side, self.across - 1))

        def settle(k, carry):
            for side in (0, 1):
                @pl.when(self.here(side, k))
                def _():
                    for name in ("gy", "gx"):
                        self.copy(name, side, k, True).wait_recv()
                    for name in ("x", "y", "gy", "gx"):
                        self.copy(name, side, k).wait_send()
                for name in ("z", "d"):
                    self.along(name, side, k, wait_send)
            return carry
        lax.fori_loop(1, self.across, settle, 0)
        for name in ("x", "y", "gy", "gx"):
            self.copy(name, 0, 0).wait_send()
        for side in (0, 1):
            for name in ("z", "d"):
                self.along(name, side, 0, wait_send)


class Spread:
    def __init__(self, places, out, zs, xs, ys, gx, gy, direct=False):
        self.places, self.out, self.sems, self.direct = places, out, dict(z=zs, x=xs, y=ys, gx=gx, gy=gy), direct
        self.rows = out.shape[2]
        self.half = self.rows // 2 // UNIT * UNIT
        self.copies = {}

    def go(self, name, d, f_from, d_from, f_to, d_to, to, start, size):
        part, sems = pl.ds(start, size), self.sems[name]
        self.copies[name, d] = send(self.out.at[f_from, d_from, part], self.out.at[f_to, d_to, part],
                                    sems.at[0, d], sems.at[1, d], dp=to)

    def over_plane(self, d):
        xpeer, ypeer = self.places[4], self.places[5]
        self.go("x", d, 0, d, 1, d, xpeer, 0, self.rows)
        self.go("y", d, 0, d, 2, d, ypeer, 0, self.rows)
        if self.direct:
            me, x, y = self.places[:3]
            self.go("gx", d, 0, d, 3, d, me + 3 - 2 * x - 4 * y, 0, self.rows)

    def start(self):
        order, ahead = self.places[6], self.places[7]
        for d in order:
            self.go("z", d, 0, 0, 0, d, ahead(d), 0, self.rows)
        self.over_plane(0)

    def relay(self):
        for d in self.places[6]:
            self.copies["z", d].wait_recv()
            self.over_plane(d)

    def diagonal(self):
        xpeer, ypeer, order = self.places[4:7]
        for d in [0] + order:
            self.copies["x", d].wait_recv()
            if self.half and not self.direct:
                self.go("gy", d, 1, d, 3, d, ypeer, 0, self.half)
            self.copies["y", d].wait_recv()
            if not self.direct:
                self.go("gx", d, 2, d, 3, d, xpeer, self.half, self.rows - self.half)

    def finish(self):
        for (name, d), copy in self.copies.items():
            if name in ("gx", "gy"):
                copy.wait_recv()

    def drain(self):
        for copy in self.copies.values():
            copy.wait_send()


def plane_swap(value, count, f):
    return lax.ppermute(value, "dp", [(i, i // 4 * 4 + (i % 4 ^ f)) for i in range(count)])


def plane_offset(places, f):
    x, y = places[1], places[2]
    return lax.rem(x + f % 2, 2) + 2 * lax.rem(y + f // 2, 2)


def call(kernel, name, args, kinds, outs, scratch, number=None):
    space = {"V": pltpu.VMEM, "S": pltpu.SMEM, "A": pl.ANY}
    extra = {} if number is None else dict(collective_id=number, has_side_effects=True)
    return pl.pallas_call(
        kernel,
        out_shape=tuple(jax.ShapeDtypeStruct(shape, dtype) for shape, dtype, _ in outs),
        in_specs=[pl.BlockSpec(memory_space=space[kind]) for kind in kinds],
        out_specs=tuple(pl.BlockSpec(memory_space=space[kind]) for _, _, kind in outs),
        scratch_shapes=scratch,
        compiler_params=pltpu.CompilerParams(vmem_limit_bytes=60 * 2**20, **extra),
        cost_estimate=pl.CostEstimate(flops=4 * 10**10, bytes_accessed=16 * 2**20, transcendentals=0),
        name=name,
    )(*args)


CHUNK = 256


def tn(a, b):
    return lax.dot_general(a, b, (((0,), (0,)), ((), ())), preferred_element_type=F32)


def normalise(value):
    centred = value - jnp.mean(value, -1, keepdims=True)
    scale = lax.rsqrt(jnp.mean(centred * centred, -1, keepdims=True) + EPS_NORM)
    return centred * scale, scale


def norm_back(unit, scale, gain, grad):
    inner = grad * gain
    return scale * (inner - jnp.mean(inner, -1, keepdims=True) - unit * jnp.mean(inner * unit, -1, keepdims=True))


def fold_rows(value):
    return jnp.sum(value.reshape(value.shape[0] // 8, 8, value.shape[1]), 0)


def interleave(size):
    row = lax.broadcasted_iota(jnp.int32, (size, size), 0)
    col = lax.broadcasted_iota(jnp.int32, (size, size), 1)
    source = jnp.where((row & 1) == 0, row >> 1, (row >> 1) + size // 2)
    return jnp.where(col == source, 1.0, 0.0).astype(BF)


def part_rows(matrix, order):
    return lax.dot_general(order, matrix, (((0,), (0,)), ((), ())), preferred_element_type=F32).astype(BF)


def as_units(gradient, order):
    parted = part_rows(gradient.astype(BF), order)
    half = parted.shape[0] // 2
    return jnp.concatenate([parted[:half], parted[half:]], 1)


def other_core(mine, theirs, sems, step):
    rows = pl.ds(step * CHUNK, CHUNK)
    return pltpu.make_async_remote_copy(
        src_ref=mine.at[rows], dst_ref=theirs.at[rows], send_sem=sems.at[0, step], recv_sem=sems.at[1, step],
        device_id={"head": 1 - lax.axis_index("head")}, device_id_type=pl.DeviceIdType.MESH)


def greet_core():
    greet([{"head": 1 - lax.axis_index("head")}])


def chunks(total, body, begin=0):
    def one(step, carry):
        body(step, pl.ds(pl.multiple_of(step * CHUNK, CHUNK), CHUNK))
        return carry
    lax.fori_loop(begin // CHUNK, total // CHUNK, one, 0)


def drain(total, mine, theirs, sems):
    def body(step, rows):
        other_core(mine, theirs, sems, step).wait_send()
    chunks(total, body)


class Late:
    def __init__(self, pairs, sems):
        self.copies = [pltpu.make_async_copy(source, held, sems.at[i]) for i, (source, held) in enumerate(pairs)]
        for copy in self.copies:
            copy.start()

    def wait(self, *which):
        for i in which:
            self.copies[i].wait()


class Out:
    def __init__(self, pairs, sems):
        self.pairs, self.sems = pairs, sems

    def copy(self, i, step):
        held, out = self.pairs[i]
        part = pl.ds(pl.multiple_of(step * CHUNK, CHUNK), CHUNK)
        if held.shape[0] < held.shape[1]:
            held, out = held.at[:, part], out.at[:, part]
        else:
            held, out = held.at[part], out.at[part]
        return pltpu.make_async_copy(held, out, self.sems.at[i, step])

    def start(self, i, step):
        self.copy(i, step).start()

    def drain(self, tokens):
        def body(step, rows):
            for i in range(len(self.pairs)):
                self.copy(i, step).wait()
        chunks(tokens, body)


def plan_kernel(block, owner_ref, len_ref, me_ref, rank_ref, count_ref, place_ref, held_ref, rank_out, count_out, table, info):
    units = owner_ref.shape[1]
    owner = owner_ref[...].astype(F32)
    owner_cols = jnp.broadcast_to(owner, (128, units)).T
    owner_cols = jnp.concatenate([owner_cols] * (units // 128), 1)
    before = lax.broadcasted_iota(jnp.int32, (units, units), 0) < lax.broadcasted_iota(jnp.int32, (units, units), 1)
    slots = jnp.sum(jnp.where(before & (owner_cols == owner), 1.0, 0.0), 0, keepdims=True)
    place = owner * block + slots
    place_ref[...] = place.astype(jnp.int32)
    me = me_ref[0].astype(F32)
    place_cols = jnp.broadcast_to(place, (128, units)).T
    lane = lax.broadcasted_iota(jnp.int32, (units, 128), 1)
    unit = lax.broadcasted_iota(jnp.int32, (units, 128), 0).astype(F32)
    mine = jnp.where(place_cols == me * block + lane.astype(F32), unit, 0.0)
    mine = jnp.where(lane == 127, jnp.where(owner_cols[:, :128] == me, 1.0, 0.0), jnp.where(lane < block - 1, mine, 0.0))
    held_ref[...] = jnp.sum(mine, 0, keepdims=True).astype(jnp.int32)
    longest, first, at, start = jnp.int32(0), jnp.int32(0), jnp.int32(0), jnp.int32(0)
    for d in range(DOCS):
        length = len_ref[0, d]
        longer = length > longest
        first = jnp.where(longer, d, first)
        start = jnp.where(longer, at, start)
        longest = jnp.where(longer, length, longest)
        at = at + length
    for d in range(DOCS):
        info[0, d] = len_ref[0, lax.rem(first + d, DOCS)]
    info[0, DOCS] = start
    info[0, DOCS + 1] = lax.rem(ROW - start, ROW)
    turn = lax.rem(ROW - start, ROW)
    rank_out[...] = pltpu.roll(rank_ref[...], turn, 1)
    count_out[...] = pltpu.roll(count_ref[...], turn, 1)
    step_table(info, table)


def plan(unit_owner, lengths, me, rank_row, count_row, block):
    row = ((1, ROW), jnp.int32, "V")
    return call(partial(plan_kernel, block), "plan", [unit_owner.reshape(1, -1), lengths, me, rank_row, count_row], "VSSVV",
                [((1, unit_owner.shape[0]), jnp.int32, "V"), ((1, 128), jnp.int32, "V"), row, row, ((2, STEPS), jnp.int32, "S"),
                 ((1, DOCS + 2), jnp.int32, "S")], [])


def turn_rows(source, target, shift):
    tiles = source.shape[0]
    whole, rest = lax.div(shift, UNIT), lax.rem(shift, UNIT)

    def one(i, carry):
        at = lax.rem(i + whole, tiles)
        both = jnp.concatenate([source[at].astype(F32), source[lax.rem(at + 1, tiles)].astype(F32)], 0)
        rows = pltpu.roll(both, lax.rem(2 * UNIT - rest, 2 * UNIT), 0)[:UNIT]
        target[pl.ds(pl.multiple_of(i * UNIT, UNIT), UNIT), :] = rows.astype(target.dtype)
        return carry
    lax.fori_loop(0, tiles, one, 0, unroll=4)


def in_tiles(value):
    return value.reshape(-1, UNIT, value.shape[1])


def project_kernel(devices, place_ref, info, master, norm_row, rank_ref, query_hbm, kv_hbm, memory_hbm, grad_hbm,
                   nq_out, nkv_out, qt_out, k_out, kt_out, v_out, vt_out, kc_out, kct_out, vc_out, vct_out,
                   query_out, kv_out, memory_out, grad_out,
                   ws_ref, wc_ref, wos_ref, woc_ref, w1_ref, w2_ref, norms, side_ref, hot_ref, rank_cols,
                   gathered, flat, stage_a, stage_b, query_ref, kv_ref, memory_ref, grad_ref, unit_q, unit_kv,
                   nq_ref, nkv_ref, qt_ref, k_ref, kt_ref, v_ref, vt_ref, kc_ref, kct_ref, vc_ref, vct_ref,
                   late_sems, turned_sems, out_sems, *line_sems):
    tokens, features = query_ref.shape
    units = place_ref.shape[1]
    late = Late([(query_hbm, stage_a), (kv_hbm, stage_b)], late_sems.at[0])
    held = (nq_ref, nkv_ref, qt_ref, k_ref, kt_ref, v_ref, vt_ref, kc_ref, kct_ref, vc_ref, vct_ref)
    out = Out(list(zip(held, (nq_out, nkv_out, qt_out, k_out, kt_out, v_out, vt_out, kc_out, kct_out, vc_out, vct_out))), out_sems)
    places = places_of(devices)
    me, x, y, z, xpeer, ypeer, order, ahead, behind = places
    slots = master.shape[0]
    block = slots + 1
    gathered[pl.ds(me * block, slots)] = master[...].astype(BF)
    gathered[me * block + slots] = jnp.broadcast_to(norm_row[...], (UNIT, features)).astype(BF)
    greet([{"dp": xpeer}, {"dp": ypeer}] + [{"dp": ahead(d)} for d in order])

    leaving = [(query_ref, query_out), (kv_ref, kv_out), (memory_ref, memory_out), (grad_ref, grad_out)]

    def leave(number):
        return pltpu.make_async_copy(*leaving[number], turned_sems.at[number])

    def turn(stage, number):
        turn_rows(stage, leaving[number][0], info[0, DOCS])
        leave(number).start()

    def first_turns():
        mask_tables(info, rank_ref, side_ref, hot_ref, rank_cols)
        late.wait(0, 1)
        turn(stage_a, 0)
        turn(stage_b, 1)

    def norms_of_streams():
        def units_of(step, rows):
            unit_q[rows, :] = normalise(query_ref[rows, :].astype(F32))[0]
            unit_kv[rows, :] = normalise(kv_ref[rows, :].astype(F32))[0]
        chunks(tokens, units_of)

    def last_turns():
        more = Late([(memory_hbm, stage_a), (grad_hbm, stage_b)], late_sems.at[1])
        more.wait(0, 1)
        turn(stage_a, 2)
        turn(stage_b, 3)
    LineGather(devices, lambda number, start, size: gathered.at[pl.ds(number * block + start, size)], block, block * 3 // 5,
               places, *line_sems).run(first_turns, norms_of_streams, last_turns)

    share = devices // 8
    vectors = []
    for number in range(8):
        pieces = [gathered[(number * share + i) * block + slots].astype(F32) for i in range(share)]
        total = pieces[0]
        for piece in pieces[1:]:
            total = total + piece
        vectors.append(total[0:1, :])
    norms[...] = jnp.concatenate(vectors, 0)

    def one_unit(u, carry):
        flat[pl.ds(pl.multiple_of(u * UNIT, UNIT), UNIT), :] = gathered[place_ref[0, u]]
        return carry
    lax.fori_loop(0, units, one_unit, 0, unroll=4)
    order = interleave(features)
    cols = v_ref.shape[1]
    for number in range(6):
        rows = flat[number * cols:(number + 1) * cols, :]
        stacked = jnp.concatenate([rows[:, :cols], rows[:, cols:]], 0)
        matrix = nn(order, stacked).astype(BF)
        if number < 3:
            ws_ref[number] = matrix
        else:
            wc_ref[number - 3] = matrix
    wos_ref[...] = flat[6 * cols:7 * cols, :]
    woc_ref[...] = flat[7 * cols:8 * cols, :]
    hidden = w2_ref.shape[0]
    for block in range(hidden // features):
        at = 8 * cols + block * features
        parted = part_rows(flat[at:at + features, :], order)
        half = features // 2
        w1_ref[block * half:(block + 1) * half, :] = jnp.concatenate([parted[:half], parted[half:]], 1)
    w2_ref[...] = flat[8 * cols + hidden:, :]

    def body(step, rows):
        nq = (unit_q[rows, :] * norms[0:1, :] + norms[1:2, :]).astype(BF)
        nkv = (unit_kv[rows, :] * norms[2:3, :] + norms[3:4, :]).astype(BF)
        source = memory_ref[rows, :]
        low = lambda left, right: nn(left, right).astype(BF)
        k, v, kc, vc = low(nkv, ws_ref[1]), low(nkv, ws_ref[2]), low(source, wc_ref[1]), low(source, wc_ref[2])
        results = [nq, nkv, low(nq, ws_ref[0]).T, k, k.T, v, v.T, kc, kc.T, vc, vc.T]
        for i, (ref, result) in enumerate(zip(held, results)):
            if ref.shape[0] < ref.shape[1]:
                ref[:, rows] = result
            else:
                ref[rows, :] = result
            out.start(i, step)
    chunks(tokens, body)
    out.drain(tokens)
    for number in range(4):
        leave(number).wait()


def pair_sems(tokens):
    return pltpu.SemaphoreType.DMA((2, tokens // CHUNK))


def out_semaphores(count, tokens):
    return pltpu.SemaphoreType.DMA((count, tokens // CHUNK))


def project(devices, place_of, info, master, norm_row, rank_row, query_stream, kv_stream, memory, out_grad, cols, hidden):
    tokens, features = query_stream.shape
    wide, narrow, across = (tokens, features), (tokens, cols), (cols, tokens)
    shapes = [wide, wide, across] + [narrow, across] * 4
    outs = [(shape, BF, "A") for shape in shapes] + [(wide, BF, "A")] * 4 + [
        ((3, features, cols), BF, "V"), ((3, features, cols), BF, "V"), ((cols, features), BF, "V"), ((cols, features), BF, "V"),
        ((features, hidden), BF, "V"), ((hidden, features), BF, "V"), ((8, features), F32, "V"),
        ((ROW, 128), BF, "V"), ((128, ROW), BF, "V"), ((ROW, 128), F32, "V")]
    D = pltpu.SemaphoreType.DMA
    streams = [in_tiles(stream) for stream in (query_stream, kv_stream, memory, out_grad)]
    scratch = [pltpu.VMEM((devices * (master.shape[0] + 1), UNIT, features), BF), pltpu.VMEM((8 * cols + 2 * hidden, features), BF)]
    scratch += [pltpu.VMEM(streams[0].shape, BF)] * 2 + [pltpu.VMEM(wide, BF)] * 4 + [pltpu.VMEM(wide, F32)] * 2
    scratch += [pltpu.VMEM(shape, BF) for shape in shapes]
    scratch += [D((2, 2)), D((4,)), out_semaphores(len(shapes), tokens)] + [D((2, 2, devices // 4 + 1))] * 6
    return call(partial(project_kernel, devices), "project",
                [place_of, info, master, norm_row, rank_row] + streams, "SSVVVAAAA", outs, scratch, 0)


def self_out_kernel(mixed, wo, query_hbm, wc, norms, res_out, nc_out, q_out,
                    query, res_ref, nc_ref, q_ref, mine, theirs, sems, late_sems, out_sems):
    tokens = query.shape[0]
    late = Late([(query_hbm, query)], late_sems)
    out = Out([(res_ref, res_out), (nc_ref, nc_out), (q_ref, q_out)], out_sems)
    greet_core()

    def give(step, rows):
        mine[rows, :] = nn(mixed[rows, :], wo[...]).astype(BF)
        other_core(mine, theirs, sems, step).start()
    chunks(tokens, give)
    late.wait(0)

    def take(step, rows):
        other_core(mine, theirs, sems, step).wait_recv()
        res = query[rows, :].astype(F32) + (mine[rows, :].astype(F32) + theirs[rows, :].astype(F32))
        res_ref[rows, :] = res
        out.start(0, step)
        nc = (normalise(res)[0] * norms[4:5, :] + norms[5:6, :]).astype(BF)
        nc_ref[rows, :] = nc
        out.start(1, step)
        q_ref[:, rows] = nn(nc, wc[0]).astype(BF).T
        out.start(2, step)
    chunks(tokens, take)
    drain(tokens, mine, theirs, sems)
    out.drain(tokens)


def self_out(mixed, wo, query, wc, norms):
    tokens, features = query.shape
    wide = (tokens, features)
    across = (mixed.shape[1], tokens)
    outs = [(wide, F32, "A"), (wide, BF, "A"), (across, BF, "A")]
    scratch = [pltpu.VMEM(wide, BF), pltpu.VMEM(wide, F32), pltpu.VMEM(wide, BF), pltpu.VMEM(across, BF),
               pltpu.VMEM(wide, BF), pltpu.VMEM(wide, BF), pair_sems(tokens), pltpu.SemaphoreType.DMA((1,)),
               out_semaphores(3, tokens)]
    return call(self_out_kernel, "self_out", [mixed, wo, query, wc, norms], "VVAVV", outs, scratch, 2)


def gelu_parts(value):
    bell = jnp.exp2(value * value * (-0.5 * 1.4426950408889634))
    base = 1.0 + (0.3275911 * 0.7071067811865476) * jnp.abs(value)
    t = pl.reciprocal(base, approx=True)
    t = t * (2.0 - base * t)
    poly = ((((0.5307027145 * t - 0.7265760135) * t + 0.7107068705) * t - 0.142248368) * t + 0.127414796) * t
    tail = poly * bell
    below = jnp.where(value < 0.0, tail, 1.0 - tail)
    return value * below, below + value * (bell * 0.3989422804014327)


def spread_flat(devices, places, flat, refs):
    rows = flat.shape[0] // devices
    for f, ref in enumerate(refs):
        place = plane_offset(places, f)
        for level in range(devices // 4):
            ref[level, ref.shape[1] - rows:, :] = flat[pl.ds(pl.multiple_of((level * 4 + place) * rows, UNIT), rows), :]


def feed_forward_kernel(devices, mixed, wo, res_hbm, w1_hbm, w2_hbm, out_grad_hbm, norms,
                        out_out, gres_out, gmix_out, part0, part1, part2, part3, sums_ref,
                        w1, w2, res, out_grad, out_ref, gres_ref, gmix_ref, flat,
                        mine, theirs, nf_all, hid_all, pre_all, low_all, mine_o, theirs_o, mine_g, theirs_g,
                        sems, sems_o, sems_g, late_sems, out_sems):
    tokens, features = out_grad.shape
    hidden = w2.shape[0]
    places = places_of(devices)
    late = Late([(res_hbm, res), (out_grad_hbm, out_grad), (w1_hbm, w1), (w2_hbm, w2)], late_sems)
    out = Out([(out_ref, out_out), (gres_ref, gres_out), (gmix_ref, gmix_out)], out_sems)
    greet_core()

    def give(step, rows):
        mine[rows, :] = nn(mixed[rows, :], wo[...]).astype(BF)
        other_core(mine, theirs, sems, step).start()
    chunks(tokens, give)
    late.wait(0, 1, 2, 3)

    def middle(step, rows):
        other_core(mine, theirs, sems, step).wait_recv()
        value = res[rows, :] + (mine[rows, :].astype(F32) + theirs[rows, :].astype(F32))
        gres_ref[rows, :] = value
        nf = (normalise(value)[0] * norms[6:7, :] + norms[7:8, :]).astype(BF)
        nf_all[rows, :] = nf
        grad = out_grad[rows, :]
        out_part = jnp.zeros((CHUNK, features), F32)
        grad_part = jnp.zeros((CHUNK, features), F32)
        for block in range(hidden // 256):
            at = slice(block * 256, (block + 1) * 256)
            act, slope = gelu_parts(nn(nf, w1[:, at]))
            act = act.astype(BF)
            hid_all[rows, at] = act
            pre = (slope * nt(grad, w2[at, :])).astype(BF)
            pre_all[rows, at] = pre
            out_part = out_part + nn(act, w2[at, :])
            grad_part = grad_part + nt(pre, w1[:, at])
        mine_o[rows, :] = out_part.astype(BF)
        other_core(mine_o, theirs_o, sems_o, step).start()
        mine_g[rows, :] = grad_part.astype(BF)
        other_core(mine_g, theirs_g, sems_g, step).start()
    chunks(tokens, middle)

    order = interleave(features)
    half, cols = features // 2, mixed.shape[1]
    for block in range(hidden // 256):
        at = slice(block * 256, (block + 1) * 256)
        flat[cols + hidden + block * 256:cols + hidden + (block + 1) * 256, :] = tn(hid_all[:, at], out_grad[...]).astype(BF)
    for block in range(hidden // features):
        gradient = tn(nf_all[:, block * half:(block + 1) * half], pre_all[...]).astype(BF)
        stacked = jnp.concatenate([gradient[:, :features], gradient[:, features:]], 0)
        flat[cols + block * features:cols + (block + 1) * features, :] = nn(order, stacked).astype(BF)
    sums_ref[...] = jnp.zeros_like(sums_ref)

    def close(step, rows):
        other_core(mine_o, theirs_o, sems_o, step).wait_recv()
        other_core(mine_g, theirs_g, sems_g, step).wait_recv()
        value = gres_ref[rows, :]
        out_ref[rows, :] = (value + (mine_o[rows, :].astype(F32) + theirs_o[rows, :].astype(F32))).astype(BF)
        out.start(0, step)
        grad = mine_g[rows, :].astype(F32) + theirs_g[rows, :].astype(F32)
        unit, scale = normalise(value)
        gres = norm_back(unit, scale, norms[6:7, :], grad) + out_grad[rows, :].astype(F32)
        gres_ref[rows, :] = gres
        out.start(1, step)
        sums_ref[0:8, :] += fold_rows(grad * unit)
        sums_ref[8:16, :] += fold_rows(grad)
        low = gres.astype(BF)
        low_all[rows, :] = low
        gmix_ref[:, rows] = nt(low, wo[...]).astype(BF).T
        out.start(2, step)
    chunks(tokens, close)
    flat[0:cols, :] = tn(mixed[...], low_all[...]).astype(BF)
    if flat.shape[0] > cols + 2 * hidden:
        flat[cols + 2 * hidden:, :] = jnp.zeros((flat.shape[0] - cols - 2 * hidden, features), BF)
    spread_flat(devices, places, flat, (part0, part1, part2, part3))
    out.drain(tokens)
    drain(tokens, mine, theirs, sems)
    drain(tokens, mine_o, theirs_o, sems_o)
    drain(tokens, mine_g, theirs_g, sems_g)


def whole_blocks(rows, devices):
    return -(-rows // (devices * UNIT)) * devices * UNIT


def feed_forward(devices, mixed, wo, res, w1, w2, out_grad, norms):
    tokens, features = out_grad.shape
    hidden = w2.shape[0]
    flat_rows = whole_blocks(wo.shape[0] + 2 * hidden, devices)
    part = ((devices // 4, flat_rows // devices, features), BF, "V")
    wide = (tokens, features)
    across = (mixed.shape[1], tokens)
    outs = [(wide, BF, "A"), (wide, F32, "A"), (across, BF, "A")] + [part] * 4 + [((16, features), F32, "V")]
    deep, narrow = pltpu.VMEM((tokens, hidden), BF), pltpu.VMEM(wide, BF)
    scratch = [pltpu.VMEM(w1.shape, BF), pltpu.VMEM(w2.shape, BF), pltpu.VMEM(wide, F32), narrow, narrow, pltpu.VMEM(wide, F32), pltpu.VMEM(across, BF),
               pltpu.VMEM((flat_rows, features), BF), narrow, narrow, narrow, deep, deep, narrow] + [narrow] * 4
    scratch += [pair_sems(tokens)] * 3 + [pltpu.SemaphoreType.DMA((4,)), out_semaphores(3, tokens)]
    return call(partial(feed_forward_kernel, devices), "feed_forward", [mixed, wo, res, w1, w2, out_grad, norms], "VVAAAAV",
                outs, scratch, 3)


def branch_give(dq, dk, dv, weights, mine_a, theirs_a, mine_b, theirs_b, sems_a, sems_b):
    def give(step, rows):
        mine_a[rows, :] = nt(dq[rows, :], weights[0]).astype(BF)
        other_core(mine_a, theirs_a, sems_a, step).start()
        mine_b[rows, :] = (nt(dk[rows, :], weights[1]) + nt(dv[rows, :], weights[2])).astype(BF)
        other_core(mine_b, theirs_b, sems_b, step).start()
    chunks(dq.shape[0], give)


def branch_weights(first_in, second_in, dq, dk, dv, flat):
    cols = dq.shape[1]
    order = interleave(first_in.shape[1])
    for number, (entering, grad) in enumerate(((first_in, dq), (second_in, dk), (second_in, dv))):
        flat[number * cols:(number + 1) * cols, :] = as_units(tn(entering[...], grad[...]), order)


def z_sum_start(devices, places, pieces, landed, sems):
    me, x, y, z, xpeer, ypeer, order, ahead, behind = places
    return [send(pieces.at[lax.rem(z + d, devices // 4)], landed.at[d], sems.at[0, d], sems.at[1, d], dp=ahead(d)) for d in order]


def z_sum_end(places, pieces, landed, copies):
    z, order = places[3], places[6]
    total = pieces[z].astype(F32)
    for copy, d in zip(copies, order):
        copy.wait_recv()
        total = total + landed[d].astype(F32)
    return total.astype(BF)


def plane_sum_start(devices, places, flat, used, source, landing, sems):
    me, x, y, z, xpeer, ypeer = places[:6]
    if flat.shape[0] > used:
        flat[used:, :] = jnp.zeros((flat.shape[0] - used, flat.shape[1]), BF)
    spread_flat(devices, places, flat, [source.at[f] for f in range(4)])
    return [send(source.at[f], landing.at[f], sems.at[0, f], sems.at[1, f], dp=peer)
            for f, peer in ((3, me + 3 - 2 * x - 4 * y), (1, xpeer), (2, ypeer))]


def four_sum(parts, at):
    return (parts[0][at].astype(F32) + parts[1][at].astype(F32) + parts[2][at].astype(F32) + parts[3][at].astype(F32)).astype(BF)


def cross_back_kernel(devices, info, dq_hbm, dk_hbm, dv_hbm, wc_hbm, nc_hbm, memory_hbm, res_hbm, gres_hbm, output_hbm, mixed_hbm, wo, norms,
                      part0, part1, part2, part3,
                      gmem_out, output_out, gnew_out, gmix_out, give0, give1, give2, give3, more_ref, sums_ref,
                      dq, dk, dv, wc, mixed, nc, memory, res, gres, output_ref, gmem_ref, turned_a, turned_b, gmix_ref, flat, flat_o, source, landing, pieces, landed, blocks,
                      mine_a, theirs_a, mine_b, theirs_b, low_all, sems_a, sems_b, late_sems, out_sems, turned_sems, z_sems, zz_sems, plane_sems):
    tokens, features = nc.shape
    cols = dq.shape[1]
    across = devices // 4
    places = places_of(devices)
    me, x, y, z, xpeer, ypeer, order, ahead, behind = places
    late = Late([(nc_hbm, nc), (memory_hbm, memory), (res_hbm, res), (gres_hbm, gres), (output_hbm, output_ref), (dq_hbm, dq),
                 (wc_hbm, wc), (dk_hbm, dk), (dv_hbm, dv), (mixed_hbm, mixed)], late_sems)
    out = Out([(gres, gnew_out), (gmix_ref, gmix_out)], out_sems)
    for level in range(across):
        pieces[level] = four_sum((part0, part1, part2, part3), level)
    greet([{"head": 1 - lax.axis_index("head")}] + [{"dp": ahead(d)} for d in order]
          + [{"dp": peer} for peer in (xpeer, ypeer, me + 3 - 2 * x - 4 * y)])
    z_copies = z_sum_start(devices, places, pieces, landed, z_sems)
    late.wait(5, 6, 7, 8)
    branch_give(dq, dk, dv, wc, mine_a, theirs_a, mine_b, theirs_b, sems_a, sems_b)
    late.wait(0, 1)
    branch_weights(nc, memory, dq, dk, dv, flat)
    plane_copies = plane_sum_start(devices, places, flat, 3 * cols, source, landing, plane_sems)
    blocks[0] = z_sum_end(places, pieces, landed, z_copies)
    zz_copies = [send(blocks.at[0], blocks.at[d], zz_sems.at[0, d], zz_sems.at[1, d], dp=ahead(d)) for d in order]
    sums_ref[...] = jnp.zeros_like(sums_ref)
    late.wait(2, 3)

    def close(step, rows):
        other_core(mine_a, theirs_a, sems_a, step).wait_recv()
        grad = mine_a[rows, :].astype(F32) + theirs_a[rows, :].astype(F32)
        unit, scale = normalise(res[rows, :])
        gnew = norm_back(unit, scale, norms[4:5, :], grad) + gres[rows, :]
        gres[rows, :] = gnew
        out.start(0, step)
        sums_ref[0:8, :] += fold_rows(grad * unit)
        sums_ref[8:16, :] += fold_rows(grad)
        low = gnew.astype(BF)
        low_all[rows, :] = low
        gmix_ref[:, rows] = nt(low, wo[...]).astype(BF).T
        out.start(1, step)
        other_core(mine_b, theirs_b, sems_b, step).wait_recv()
        total = (mine_b[rows, :].astype(F32) + theirs_b[rows, :].astype(F32)).astype(BF)
        gmem_ref[pl.ds(step * (CHUNK // UNIT), CHUNK // UNIT)] = in_tiles(total)
    chunks(tokens, close)
    late.wait(9)
    flat_o[0:cols, :] = tn(mixed[...], low_all[...]).astype(BF)
    if flat_o.shape[0] > cols:
        flat_o[cols:, :] = jnp.zeros((flat_o.shape[0] - cols, features), BF)
    gives = (give0, give1, give2, give3)
    spread_flat(devices, places, flat_o, gives)
    for copy in plane_copies:
        copy.wait_recv()
    for d in range(across):
        more_ref[d] = four_sum((source.at[0], landing.at[1], landing.at[2], landing.at[3]), d)
    late.wait(4)
    turn_rows(gmem_ref, turned_a, info[0, DOCS + 1])
    turn_rows(output_ref, turned_b, info[0, DOCS + 1])
    turned = Late([(turned_a, gmem_out), (turned_b, output_out)], turned_sems)
    for copy in zz_copies:
        copy.wait_recv()
    ready_rows = blocks.shape[1]
    for ref in gives:
        for d in range(across):
            ref[d, 0:ready_rows, :] = blocks[d]
    for copy in z_copies + zz_copies + plane_copies:
        copy.wait_send()
    turned.wait(0, 1)
    out.drain(tokens)
    drain(tokens, mine_a, theirs_a, sems_a)
    drain(tokens, mine_b, theirs_b, sems_b)


def cross_back(devices, info, dq, dk, dv, wc, nc, memory, res, gres, output, mixed, wo, norms, parts):
    tokens, features = nc.shape
    cols = dq.shape[1]
    across, ready_rows = devices // 4, parts[0].shape[1]
    flat_rows, o_rows = whole_blocks(3 * cols, devices), whole_blocks(cols, devices)
    give = ((across, ready_rows + o_rows // devices, features), BF, "V")
    part = (across, flat_rows // devices, features)
    wide = (tokens, features)
    outs = [(wide, BF, "A"), (wide, BF, "A"), (wide, F32, "A"), ((cols, tokens), BF, "A")] + [give] * 4 + [
        (part, BF, "V"), ((16, features), F32, "V")]
    low, high = pltpu.VMEM(wide, BF), pltpu.VMEM(wide, F32)
    small = pltpu.VMEM((across, ready_rows, features), BF)
    z_sems = pltpu.SemaphoreType.DMA((2, across))
    tiles = pltpu.VMEM((tokens // UNIT, UNIT, features), BF)
    scratch = [pltpu.VMEM(arg.shape, BF) for arg in (dq, dk, dv, wc, mixed)]
    scratch += [low, low, high, high, tiles, tiles, low, low, pltpu.VMEM((cols, tokens), BF), pltpu.VMEM((flat_rows, features), BF),
               pltpu.VMEM((o_rows, features), BF), pltpu.VMEM((4,) + part, BF), pltpu.VMEM((4,) + part, BF), small, small, small]
    scratch += [low] * 5 + [pair_sems(tokens)] * 2 + [pltpu.SemaphoreType.DMA((10,)), out_semaphores(2, tokens), pltpu.SemaphoreType.DMA((2,)), z_sems, z_sems,
                                                 pltpu.SemaphoreType.DMA((2, 4))]
    return call(partial(cross_back_kernel, devices), "cross_back",
                [info, dq, dk, dv, wc, nc, memory, res, gres, in_tiles(output), mixed, wo, norms] + parts, "SAAAAAAAAAAVVVVVV", outs, scratch, 4)


def self_back_kernel(devices, ready_rows, info, dq, dk, dv, ws, nq_hbm, nkv_hbm, query_hbm, kv_hbm, gres_hbm, norms, sums_c, sums_f, more_in,
                     part0, part1, part2, part3,
                     gquery_out, gkv_out, last_ref, more_ref, gnorm_ref,
                     nq, nkv, query, kv, gres, gquery_ref, gkv_ref, turned_a, turned_b, flat, source, landing, pieces, landed, more_pieces, more_landed,
                     norm_mine, norm_all, mine_a, theirs_a, mine_b, theirs_b, sums, sems_a, sems_b, late_sems, out_sems,
                     z_sems, more_z_sems, plane_sems, n_sems, part_rows, part_sems, *spread_sems):
    tokens, features = nq.shape
    across = devices // 4
    places = places_of(devices)
    me, x, y, z, xpeer, ypeer, order, ahead, behind = places
    late = Late([(nq_hbm, nq), (nkv_hbm, nkv), (query_hbm, query), (kv_hbm, kv), (gres_hbm, gres)], late_sems)
    in_rows, more_rows = more_in.shape[1], more_ref.shape[2]
    late_parts = Late([(part.at[:, pl.ds(ready_rows, more_rows - in_rows)], part_rows.at[f])
                       for f, part in enumerate((part0, part1, part2, part3))], part_sems)
    others = [lax.rem(me + d, devices) for d in range(1, devices)]
    greet([{"head": 1 - lax.axis_index("head")}] + [{"dp": other} for other in others])
    late.wait(0, 1)
    branch_weights(nq, nkv, dq, dk, dv, flat)
    plane_copies = plane_sum_start(devices, places, flat, 3 * dq.shape[1], source, landing, plane_sems)
    late_parts.wait(0, 1, 2, 3)
    for level in range(across):
        more_pieces[level, 0:in_rows, :] = more_in[level]
        more_pieces[level, in_rows:, :] = four_sum([part_rows.at[f] for f in range(4)], level)
    more_copies = z_sum_start(devices, places, more_pieces, more_landed, more_z_sems)
    branch_give(dq, dk, dv, ws, mine_a, theirs_a, mine_b, theirs_b, sems_a, sems_b)
    more_ref[0, 0] = z_sum_end(places, more_pieces, more_landed, more_copies)
    more = Spread(places, more_ref, *spread_sems[:5])
    more.start()
    sums[...] = jnp.zeros_like(sums)
    late.wait(2, 3, 4)

    def close(step, rows):
        other_core(mine_a, theirs_a, sems_a, step).wait_recv()
        grad = mine_a[rows, :].astype(F32) + theirs_a[rows, :].astype(F32)
        unit, scale = normalise(query[rows, :].astype(F32))
        tiles = pl.ds(step * (CHUNK // UNIT), CHUNK // UNIT)
        gquery_ref[tiles] = in_tiles((norm_back(unit, scale, norms[0:1, :], grad) + gres[rows, :]).astype(BF))
        sums[0:8, :] += fold_rows(grad * unit)
        sums[8:16, :] += fold_rows(grad)
        other_core(mine_b, theirs_b, sems_b, step).wait_recv()
        grad = mine_b[rows, :].astype(F32) + theirs_b[rows, :].astype(F32)
        unit, scale = normalise(kv[rows, :].astype(F32))
        gkv_ref[tiles] = in_tiles(norm_back(unit, scale, norms[2:3, :], grad).astype(BF))
        sums[16:24, :] += fold_rows(grad * unit)
        sums[24:32, :] += fold_rows(grad)
    middle = tokens // 2
    chunks(middle, close)
    more.relay()
    chunks(tokens, close, middle)
    parts = [sums[8 * i:8 * i + 8, :] for i in range(4)]
    parts += [sums_c[0:8, :], sums_c[8:16, :], sums_f[0:8, :], sums_f[8:16, :]]
    norm_mine[...] = jnp.concatenate([jnp.sum(part, 0, keepdims=True) for part in parts], 0)
    for copy in plane_copies:
        copy.wait_recv()
    for level in range(across):
        pieces[level] = four_sum((source.at[0], landing.at[1], landing.at[2], landing.at[3]), level)
    z_copies = z_sum_start(devices, places, pieces, landed, z_sems)
    n_copies = [send(norm_mine, norm_all.at[d], n_sems.at[0, d], n_sems.at[1, d], dp=other)
                for d, other in zip(range(1, devices), others)]
    turn_rows(gquery_ref, turned_a, info[0, DOCS + 1])
    more.diagonal()
    last_ref[0, 0] = z_sum_end(places, pieces, landed, z_copies)
    last = Spread(places, last_ref, *spread_sems[5:], direct=True)
    last.start()
    turn_rows(gkv_ref, turned_b, info[0, DOCS + 1])
    turned = Late([(turned_a, gquery_out), (turned_b, gkv_out)], out_sems)
    last.relay()
    last.diagonal()
    total = norm_mine[...]
    for d, copy in zip(range(1, devices), n_copies):
        copy.wait_recv()
        total = total + norm_all[d]
    gnorm_ref[...] = total
    more.finish()
    last.finish()
    more.drain()
    last.drain()
    for copy in more_copies + plane_copies + z_copies + n_copies:
        copy.wait_send()
    turned.wait(0, 1)
    drain(tokens, mine_a, theirs_a, sems_a)
    drain(tokens, mine_b, theirs_b, sems_b)


def self_back(devices, ready_rows, info, dq, dk, dv, ws, nq, nkv, query, kv, gres, norms, sums_c, sums_f, more_in, parts):
    tokens, features = nq.shape
    cols = dq.shape[1]
    across, more_rows = devices // 4, more_in.shape[1] + parts[0].shape[1] - ready_rows
    flat_rows = whole_blocks(3 * cols, devices)
    rows = flat_rows // devices
    wide = (tokens, features)
    outs = [(wide, BF, "A"), (wide, BF, "A"), ((4, across, rows, features), BF, "V"), ((4, across, more_rows, features), BF, "V"),
            ((8, features), F32, "V")]
    low, high = pltpu.VMEM(wide, BF), pltpu.VMEM(wide, F32)
    small, tiny = pltpu.VMEM((across, more_rows, features), BF), pltpu.VMEM((across, rows, features), BF)
    four = pltpu.VMEM((4, across, rows, features), BF)
    D = pltpu.SemaphoreType.DMA
    tiles = pltpu.VMEM((tokens // UNIT, UNIT, features), BF)
    scratch = [low, low, low, low, high, tiles, tiles, low, low, pltpu.VMEM((flat_rows, features), BF), four, four, tiny, tiny, small, small,
               pltpu.VMEM((8, features), F32), pltpu.VMEM((devices, 8, features), F32)]
    scratch += [low] * 4 + [pltpu.VMEM((32, features), F32)] + [pair_sems(tokens)] * 2
    scratch += [D((5,)), D((2,)), D((2, across)), D((2, across)), D((2, 4)), D((2, devices)),
                pltpu.VMEM((4, across, more_rows - more_in.shape[1], features), BF), D((4,))]
    scratch += [D((2, across))] * 10
    return call(partial(self_back_kernel, devices, ready_rows), "self_back",
                [info, dq, dk, dv, ws, nq, nkv, query, kv, gres, norms, sums_c, sums_f, more_in] + parts, "SVVVVAAAAAVVVVAAAA", outs, scratch, 5)


def update_kernel(devices, firsts, late_rows, more_first, held, me_ref, *refs):
    norm_grads, *norm_in = refs[:4]
    hbm, (grad_out, first_out, second_out, new_out, gquery_out, gkv_out) = refs[4:15], refs[15:21]
    norm_out, vmem = refs[21:25], refs[25:36]
    last, more, part0, part1, part2, part3, master, first, second, held_q, held_kv = vmem
    taken, grad_ref, first_ref, second_ref, new_ref, sems, out_sems = refs[36:]
    entering = Late(list(zip(hbm, vmem)), sems)
    share = norm_in[0].shape[1]
    if share % 128 == 0:
        at = me_ref[0] * share
        features = norm_grads.shape[1]
        norm_grad = norm_grads[pl.ds(lax.div(at, features), 1), pl.ds(pl.multiple_of(lax.rem(at, features), 128), share)]
        norm_values = (norm_grad,) + adamw_step(norm_grad, *(ref[...] for ref in norm_in), RATE_NORM, 0.0)
        for ref, value in zip(norm_out, norm_values):
            ref[...] = value
    else:
        for ref in norm_out:
            ref[...] = jnp.zeros_like(ref)
    slots = master.shape[0]
    across = devices // 4
    me = me_ref[0]
    here, level = lax.rem(me, 4), lax.div(me, 4)
    count = held[0, 127]
    results = list(zip((grad_ref, first_ref, second_ref, new_ref), (grad_out, first_out, second_out, new_out)))
    entering.wait(9, 10)
    leaving = Late([(held_q, gquery_out), (held_kv, gkv_out)], out_sems.at[0])
    entering.wait(*range(9))

    def lookup(row, size, start=0):
        block = lax.div(row, size)
        behind = lax.rem(level - lax.div(block, 4) + across, across)
        return lax.rem(block, 4) ^ here, behind, pl.ds(pl.multiple_of(lax.rem(row, size) + start, UNIT), UNIT)

    def one(slot, carry):
        @pl.when(slot < count)
        def _():
            unit = held[0, slot]

            @pl.when(unit < firsts[0])
            def _():
                taken[...] = last[lookup(unit * UNIT, last.shape[2])]

            @pl.when((unit >= firsts[0]) & (unit < firsts[1]))
            def _():
                taken[...] = more[lookup((unit - firsts[0]) * UNIT, more_first)]

            @pl.when((unit >= firsts[1]) & (unit < firsts[2]))
            def _():
                taken[...] = more[lookup((unit - firsts[1]) * UNIT, more.shape[2] - more_first, more_first)]

            @pl.when(unit >= firsts[2])
            def _():
                offset, behind, rows = lookup((unit - firsts[2]) * UNIT, late_rows)
                for f, part in enumerate((part0, part1, part2, part3)):
                    @pl.when(offset == f)
                    def _():
                        taken[...] = part[behind, rows]
            gradient = taken[...].astype(F32)
            first_new, second_new, weight = adamw_step(gradient, first[slot], second[slot], master[slot], RATE_MATRIX, WEIGHT_DECAY)
            grad_ref[slot] = gradient
            first_ref[slot] = first_new
            second_ref[slot] = second_new
            new_ref[slot] = weight

        @pl.when(slot >= count)
        def _():
            for ref in (grad_ref, first_ref, second_ref, new_ref):
                ref[slot] = jnp.zeros(ref.shape[1:], F32)
        return carry
    half = slots // 2
    lax.fori_loop(0, half, one, 0)
    early = Late([(ref.at[pl.ds(0, half)], out.at[pl.ds(0, half)]) for ref, out in results], out_sems.at[1])
    lax.fori_loop(half, slots, one, 0)
    rest = Late([(ref.at[pl.ds(half, half)], out.at[pl.ds(half, half)]) for ref, out in results], out_sems.at[2])
    for copies in (early, rest):
        copies.wait(*range(4))
    leaving.wait(0, 1)


def update(devices, firsts, late_rows, more_first, held, me, norm_args, last, more, parts, master, first, second, gquery, gkv):
    outs = [(master.shape, F32, "A")] * 4 + [(gquery.shape, BF, "A")] * 2 + [(norm_args[1].shape, F32, "V")] * 4
    args = [last, more] + parts + [master, first, second, gquery, gkv]
    scratch = [pltpu.VMEM(arg.shape, arg.dtype) for arg in args] + [pltpu.VMEM((UNIT, master.shape[2]), BF)]
    scratch += [pltpu.VMEM(master.shape, F32)] * 4 + [pltpu.SemaphoreType.DMA((11,)), pltpu.SemaphoreType.DMA((3, 4))]
    return call(partial(update_kernel, devices, firsts, late_rows, more_first), "update", [held, me] + norm_args + args, "SSVVVV" + "A" * 11,
                outs, scratch)


def adamw_step(gradient, first, second, weight, rate, decay):
    first_new = BETA_ONE * first + (1.0 - BETA_ONE) * gradient
    second_new = BETA_TWO * second + (1.0 - BETA_TWO) * gradient * gradient
    corr_one = 1.0 - BETA_ONE**STEP
    corr_two = 1.0 - BETA_TWO**STEP
    direction = first_new / corr_one / (jnp.sqrt(second_new / corr_two) + ADAM_EPS)
    return (first_new, second_new, weight - rate * (direction + decay * weight))


def local(
    query_stream, kv_stream, memory, out_grad, lengths, obs_rank, obs_count, unit_owner,
    master, first_moment, second_moment, norm_master, norm_first, norm_second,
):
    devices = lax.axis_size("dp")
    shards = lax.axis_size("head")
    me = lax.axis_index("dp")
    slots, unit_rows, features = master.shape[0], master.shape[2], master.shape[3]
    units = unit_owner.shape[0]
    norm_share = norm_master.shape[0]
    cols = features // shards
    hidden = (units * unit_rows - 8 * cols) // 2

    shape = (slots, unit_rows, features)
    norm_row = lax.dynamic_update_slice(
        jnp.zeros((1, features), F32), norm_master.reshape(1, norm_share), (0, lax.rem(me * norm_share, features)))
    rank_row, count_row = obs_rank.reshape(1, ROW), obs_count.reshape(1, ROW)
    place_of, held, rank_row, count_row, steps, info = plan(unit_owner, lengths, me.reshape(1), rank_row, count_row, slots + 1)
    nq, nkv, qt, k, kt, v, vt, kc, kct, vc, vct, query, kv, source, cotangent, ws, wc, wo_self, wo_cross, w1, w2, norms, *tables = project(
        devices, place_of, info, master.reshape(shape), norm_row, rank_row, query_stream, kv_stream, memory, out_grad, cols, hidden)
    mixed_self, mixed_self_t, total_self = attend_forward(steps, qt, k, vt, tables, count_row, True)
    residual, nc, qct = self_out(mixed_self, wo_self, query, wc, norms)
    mixed_cross, mixed_cross_t, total_cross = attend_forward(steps, qct, kc, vct, tables, count_row, False)
    output, grad_cross_res, grad_mixed, *parts, sums_f = feed_forward(
        devices, mixed_cross, wo_cross, residual, w1, w2, cotangent, norms)
    tie = lax.optimization_barrier
    ready_rows = parts[0].shape[1]
    parts = [parts[0]] + [plane_swap(parts[f], devices, f) for f in (1, 2, 3)]
    dq, dk, dv = attend_backward(steps, qct, kc, kct, vc, grad_mixed, mixed_cross_t, total_cross, tables, count_row, [], False)
    parts, dq = tie((parts, dq))
    grad_memory, output, grad_residual, grad_mixed, *parts, more, sums_c = cross_back(
        devices, info, dq, dk, dv, wc, nc, source, residual, grad_cross_res, output, mixed_self, wo_self, norms, parts)
    parts = [parts[0]] + [plane_swap(parts[f], devices, f) for f in (1, 2, 3)]
    dq, dk, dv, grad_memory, output = attend_backward(
        steps, qt, k, kt, v, grad_mixed, mixed_self_t, total_self, tables, count_row, [grad_memory, output], True)
    parts, dq = tie((parts, dq))
    more_first = more.shape[1]
    grad_query, grad_kv, last, more, norm_grads = self_back(
        devices, ready_rows, info, dq, dk, dv, ws, nq, nkv, query, kv, grad_residual, norms, sums_c, sums_f, more, parts)

    firsts = [count * cols // unit_rows for count in (3, 6, 7)]
    norm_args = [norm_grads] + [value.reshape(1, norm_share) for value in (norm_first, norm_second, norm_master)]
    weight_grad, weight_first, weight_second, weight_new, grad_query, grad_kv, *norm_results = update(
        devices, firsts, ready_rows, more_first, held, me.reshape(1), norm_args, last, more, parts, master.reshape(shape),
        first_moment.reshape(shape), second_moment.reshape(shape), grad_query, grad_kv)
    weight_grad, weight_first, weight_second, weight_new = [
        part.reshape(master.shape) for part in (weight_grad, weight_first, weight_second, weight_new)]
    if norm_share % 128 == 0:
        norm_grad, norm_first_new, norm_second_new, norm_new = [value.reshape(norm_share) for value in norm_results]
    else:
        norm_grad = lax.dynamic_slice_in_dim(norm_grads.reshape(-1), me * norm_share, norm_share)
        norm_first_new, norm_second_new, norm_new = adamw_step(
            norm_grad, norm_first, norm_second, norm_master, RATE_NORM, 0.0)
    return (
        output, grad_query, grad_kv, grad_memory, weight_grad, weight_first, weight_second, weight_new,
        norm_grad, norm_first_new, norm_second_new, norm_new,
    )


def solution(mesh):
    in_specs = (
        P("dp", None),
        P("dp", None),
        P("dp", None),
        P("dp", None),
        P("dp", None),
        P("dp"),
        P("dp"),
        P(),
        P("dp", "head", None, None),
        P("dp", "head", None, None),
        P("dp", "head", None, None),
        P("dp"),
        P("dp"),
        P("dp"),
    )
    out_specs = (
        P("dp", None),
        P("dp", None),
        P("dp", None),
        P("dp", None),
        P("dp", "head", None, None),
        P("dp", "head", None, None),
        P("dp", "head", None, None),
        P("dp", "head", None, None),
        P("dp"),
        P("dp"),
        P("dp"),
        P("dp"),
    )
    return jax.shard_map(local, mesh=mesh, in_specs=in_specs, out_specs=out_specs, check_vma=False)
```

```python
from functools import partial

import jax
import jax.numpy as jnp
from jax import lax
from jax.experimental import pallas as pl
from jax.experimental.pallas import tpu as pltpu
from jax.sharding import PartitionSpec as P

HEAD_DIM = 64
ROW = 2048
DOCS = 32
STEP = 10
UNIT = 16

EPS_NORM = 1e-05
ADAM_EPS = 1e-08
BETA_ONE = 0.5
BETA_TWO = 0.5
RATE_MATRIX = 0.1
RATE_NORM = 0.3
WEIGHT_DECAY = 0.01

F32 = jnp.float32
BF = jnp.bfloat16
TQ = 256
TK = 512
FAR = 32768.0
LANES = (64, 72, 80)


def nt(a, b):
    return lax.dot_general(a, b, (((1,), (1,)), ((), ())), preferred_element_type=F32)


def nn(a, b):
    return lax.dot_general(a, b, (((1,), (0,)), ((), ())), preferred_element_type=F32)


def doc_bounds(len_ref):
    starts, ends = [], []
    at = jnp.int32(0)
    for d in range(DOCS):
        starts.append(at)
        at = at + len_ref[0, d]
        ends.append(at)
    return starts, ends


def key_range(starts, ends, q0):
    low = jnp.int32(0)
    high = jnp.int32(0)
    for d in range(DOCS):
        low = jnp.where(starts[d] <= q0, starts[d], low)
        high = jnp.where(starts[d] <= q0 + TQ - 1, ends[d], high)
    first = lax.div(low, 128) * 128
    steps = lax.div(high - first + TK - 1, TK)
    return first, steps


def mask_tables(len_ref, rank_ref, side_ref, hot_ref, rank_cols):
    starts, ends = doc_bounds(len_ref)
    lanes = lax.broadcasted_iota(jnp.int32, (1, 128), 1)
    start_lane = jnp.full((1, 128), -1, jnp.int32)
    end_lane = jnp.full((1, 128), -1, jnp.int32)
    for d in range(DOCS):
        start_lane = jnp.where(lanes == d, starts[d], start_lane)
        end_lane = jnp.where(lanes == d, ends[d], end_lane)
    one = (lanes == LANES[0]) | (lanes == LANES[1]) | (lanes == LANES[2])
    for t in range(ROW // 256):
        pos = lax.broadcasted_iota(jnp.int32, (256, 128), 0) + t * 256
        hot = (pos >= start_lane) & (pos < end_lane)
        side = jnp.where(hot | (lanes >= DOCS), jnp.where(one, -1.0, 0.0), -FAR)
        side_ref[t * 256:(t + 1) * 256, :] = side.astype(BF)
    pos = lax.broadcasted_iota(jnp.int32, (1, ROW), 1)
    first = jnp.zeros((1, ROW), jnp.bool_)
    rows = []
    for d in range(DOCS):
        first = first | (pos == starts[d])
        rows.append(jnp.where((pos >= starts[d]) & (pos < ends[d]), FAR, 0.0))
    hot_ref[...] = jnp.concatenate(rows + [jnp.zeros((128 - DOCS, ROW), F32)], 0).astype(BF)
    rank = jnp.where(first, -1.0, rank_ref[...].astype(F32))
    for t in range(ROW // 128):
        rank_cols[t * 128:(t + 1) * 128, :] = jnp.broadcast_to(rank[:, t * 128:(t + 1) * 128], (128, 128)).T


STEPS = (ROW // TQ) * -(-ROW // TK) + 8


def step_table(len_ref, table):
    starts, ends = doc_bounds(len_ref)
    idle = ROW // TQ

    def put(at, tile, first):
        table[0, at] = tile
        table[1, at] = first
    put(0, idle, ROW)
    put(1, idle, ROW)
    at = jnp.int32(2)
    for tile in range(idle):
        first, steps = key_range(starts, ends, tile * TQ)

        def fill(s, at):
            put(at, tile, first + s * TK)
            return at + 1
        at = lax.fori_loop(0, steps, fill, at)
    put(at, idle, ROW)
    put(at + 1, idle, ROW)
    table[0, STEPS - 1] = at


def step_of(table, i):
    return table[0, i], pl.multiple_of(table[1, i], 128)


def real_step(table, i):
    return jnp.minimum(table[0, i], ROW // TQ - 1), pl.multiple_of(table[1, i], 128)


def padded(ref):
    return ref.at[pl.ds(0, ROW)] if ref.shape[0] > ref.shape[1] else ref.at[:, pl.ds(0, ROW)]


def fill_padding(refs, side_ref):
    for ref in refs:
        if ref.shape[0] > ref.shape[1]:
            ref[ROW:, :] = jnp.zeros((TK, ref.shape[1]), ref.dtype)
        else:
            ref[:, ROW:] = jnp.zeros((ref.shape[0], TK), ref.dtype)
    lanes = lax.broadcasted_iota(jnp.int32, (TK, 128), 1)
    side_ref[ROW:, :] = jnp.where(lanes < DOCS, -FAR, 0.0).astype(BF)


def seen_bias(rank_cols, counts, tile, k0):
    rank = rank_cols[pl.ds(k0, TK), :]
    rank = jnp.concatenate([rank] * (TQ // 128), 1)
    kpos = lax.broadcasted_iota(jnp.int32, (TK, TQ), 0)
    qpos = lax.broadcasted_iota(jnp.int32, (TK, TQ), 1)
    off_diag = (kpos - qpos) != (tile * TQ - k0)
    allowed = (rank < counts[tile, 0:1, :]) & (off_diag | (rank < 0.0))
    return jnp.where(allowed, 0.0, -FAR * FAR)


def count_tiles(counts, count_ref):
    for tile in range(ROW // TQ):
        counts[tile] = jnp.broadcast_to(count_ref[:, tile * TQ:(tile + 1) * TQ].astype(F32), (8, TQ))


def query_columns(qt, qt_ref, side, tile, h, q0):
    rows = qt_ref[h * HEAD_DIM:(h + 1) * HEAD_DIM, pl.ds(q0, TQ)].astype(F32) * HEAD_DIM ** -0.5
    own, other = h % 2 * HEAD_DIM, (1 - h % 2) * HEAD_DIM
    qt[tile, h, own:own + HEAD_DIM, :] = rows.astype(BF)
    qt[tile, h, other:other + HEAD_DIM, :] = jnp.zeros((HEAD_DIM, TQ), BF)
    qt[tile, h, 128:256, :] = side


def pair_rows(ref, side_ref, h, k0):
    return jnp.concatenate([ref[pl.ds(k0, TK), h // 2 * 128:(h // 2 + 1) * 128], side_ref[pl.ds(k0, TK), :]], 1)


def attn_fwd_kernel(with_seen, heads, table, count_ref, qt_hbm, hot_hbm, k_hbm, vt_hbm, side_hbm, rank_hbm,
                    o_out, ot_out, lse_ref, qt, acc, top, sc, probs, fade, counts,
                    qt_ref, hot_ref, k_ref, vt_ref, side_ref, rank_cols, o_ref, ot_ref, late_sems, out_sems):
    pairs = [(qt_hbm, qt_ref), (hot_hbm, hot_ref), (k_hbm, padded(k_ref)), (vt_hbm, padded(vt_ref)),
             (side_hbm, padded(side_ref))]
    late = Late(pairs + ([(rank_hbm, padded(rank_cols))] if with_seen else []), late_sems)
    fill_padding((k_ref, vt_ref, rank_cols), side_ref)
    out = Out([(o_ref, o_out), (ot_ref, ot_out)], out_sems)
    tiles = ROW // TQ
    lse_ref[...] = jnp.zeros_like(lse_ref)
    acc[...] = jnp.zeros_like(acc)
    top[...] = jnp.full_like(top, -jnp.inf)
    if with_seen:
        count_tiles(counts, count_ref)
    late.wait(0, 1)

    def prepare(tile, c):
        q0 = pl.multiple_of(tile * TQ, TQ)
        for h in range(heads):
            query_columns(qt, qt_ref, hot_ref[:, pl.ds(q0, TQ)], tile, h, q0)
        return c
    lax.fori_loop(0, tiles, prepare, 0)
    late.wait(*range(2, 6 if with_seen else 5))
    ones = jnp.ones((16, TK), BF)

    def one_step(s, c):
        out_tile, _ = step_of(table, s)
        _, out_k = real_step(table, s)
        mid_tile, _ = step_of(table, s + 1)
        in_tile, in_k = real_step(table, s + 2)
        sums = []
        for h in range(heads):
            values = jnp.concatenate([vt_ref[h * HEAD_DIM:(h + 1) * HEAD_DIM, pl.ds(out_k, TK)], ones], 0)
            sums.append(acc[out_tile, h] * fade[h:h + 1, :] + nn(values, probs[h]))
        old = top[mid_tile]
        news = []
        for h in range(heads):
            score = sc[h]
            new = jnp.maximum(old[h:h + 1, :], jnp.max(score, 0, keepdims=True))
            probs[h] = jnp.exp(score - new).astype(BF)
            news.append(new)
        new = jnp.concatenate(news + [old[heads:, :]], 0)
        fade[...] = jnp.exp(old - new)
        bias = seen_bias(rank_cols, counts, in_tile, in_k) if with_seen else None
        for h in range(heads):
            score = nn(pair_rows(k_ref, side_ref, h, in_k), qt[in_tile, h])
            sc[h] = score + bias if with_seen else score
        top[mid_tile] = new
        for h in range(heads):
            acc[out_tile, h] = sums[h]
        return c
    lax.fori_loop(0, table[0, STEPS - 1], one_step, 0)

    def finish(tile, c):
        q0 = pl.multiple_of(tile * TQ, TQ)
        outs = []
        peak = top[tile]
        for h in range(heads):
            a = acc[tile, h]
            total = a[HEAD_DIM:HEAD_DIM + 1, :]
            outs.append(a[:HEAD_DIM, :] * (1.0 / total))
            lse_ref[h:h + 1, pl.ds(q0, TQ)] = peak[h:h + 1, :] + jnp.log(total)
        mixed = jnp.concatenate(outs, 0).astype(BF)
        ot_ref[:, pl.ds(q0, TQ)] = mixed
        out.start(1, tile)
        o_ref[pl.ds(q0, TQ), :] = mixed.T
        out.start(0, tile)
        return c
    lax.fori_loop(0, tiles, finish, 0)
    out.drain(ROW)


def attend_forward(steps, qt, k, vt, tables, count, with_seen):
    cols, rows = qt.shape
    heads = cols // HEAD_DIM
    side, hot, rank_cols = tables
    args = [steps, count, qt, hot, k, vt, side, rank_cols]
    across, down = (cols, rows), (rows, cols)
    held = [pltpu.VMEM(arg.shape, BF) for arg in (qt, hot)] + [
        pltpu.VMEM((rows + TK, cols), BF), pltpu.VMEM((cols, rows + TK), BF), pltpu.VMEM((rows + TK, 128), BF),
        pltpu.VMEM((rows + TK, 128), F32)]
    return call(partial(attn_fwd_kernel, with_seen, heads), "attend_self_forward" if with_seen else "attend_cross_forward",
                args, "SV" + "A" * 6, [(down, BF, "A"), (across, BF, "A"), ((8, rows), F32, "V")],
                [pltpu.VMEM((ROW // TQ, heads, 256, TQ), BF), pltpu.VMEM((ROW // TQ + 1, heads, HEAD_DIM + 16, TQ), F32),
                 pltpu.VMEM((ROW // TQ + 1, 8, TQ), F32), pltpu.VMEM((heads, TK, TQ), F32), pltpu.VMEM((heads, TK, TQ), BF),
                 pltpu.VMEM((8, TQ), F32), pltpu.VMEM((ROW // TQ, 8, TQ), F32)] + held
                + [pltpu.VMEM(down, BF), pltpu.VMEM(across, BF), pltpu.SemaphoreType.DMA((6,)), out_semaphores(2, rows)])


def three_rows(value):
    high = value.astype(BF).astype(F32)
    middle = (value - high).astype(BF).astype(F32)
    row = lax.broadcasted_iota(jnp.int32, (128, value.shape[1]), 0)
    return jnp.where(row == LANES[0], high, jnp.where(row == LANES[1], middle, jnp.where(row == LANES[2], value - high - middle, 0.0)))


def attn_bwd_kernel(with_seen, heads, table, count_ref, lse_ref, qt_hbm, hot_hbm, gt_hbm, ot_hbm, k_hbm, kt_hbm, v_hbm, side_hbm,
                    rank_hbm, *refs):
    passed = (len(refs) - 30) // 3
    pass_in, (dq_out, dk_out, dv_out), pass_out, refs = refs[:passed], refs[passed:passed + 3], refs[passed + 3:2 * passed + 3], refs[2 * passed + 3:]
    (dk_sum, dv_sum, dq_sum, qt, gt, q_own, g_own, sc, dps, all_ds, all_p, counts,
     qt_ref, hot_ref, gt_ref, ot_ref, k_ref, kt_ref, v_ref, side_ref, rank_cols, *held, dq_ref, dk_ref, dv_ref,
     late_sems, out_sems, pass_sem) = refs
    pairs = [(qt_hbm, qt_ref), (hot_hbm, hot_ref), (gt_hbm, gt_ref), (ot_hbm, ot_ref), (k_hbm, padded(k_ref)),
             (kt_hbm, padded(kt_ref)), (v_hbm, padded(v_ref)), (side_hbm, padded(side_ref))]
    late = Late(pairs + ([(rank_hbm, padded(rank_cols))] if with_seen else []), late_sems)
    fill_padding((k_ref, kt_ref, v_ref, rank_cols), side_ref)
    entering = Late(list(zip(pass_in, held)), pass_sem.at[0])
    out = Out([(dq_ref, dq_out), (dk_ref, dk_out), (dv_ref, dv_out)], out_sems)
    tiles = ROW // TQ
    dk_sum[...] = jnp.zeros_like(dk_sum)
    dv_sum[...] = jnp.zeros_like(dv_sum)
    dq_sum[...] = jnp.zeros_like(dq_sum)
    if with_seen:
        count_tiles(counts, count_ref)
    late.wait(0, 1, 2, 3)

    def prepare(tile, c):
        q0 = pl.multiple_of(tile * TQ, TQ)
        hot = hot_ref[:, pl.ds(q0, TQ)].astype(F32)
        for h in range(heads):
            rows = slice(h * HEAD_DIM, (h + 1) * HEAD_DIM)
            side = hot + three_rows(lse_ref[h:h + 1, pl.ds(q0, TQ)])
            query_columns(qt, qt_ref, side.astype(BF), tile, h, q0)
            grads = gt_ref[rows, pl.ds(q0, TQ)]
            delta = jnp.sum(grads.astype(F32) * ot_ref[rows, pl.ds(q0, TQ)].astype(F32), 0, keepdims=True)
            other = (1 - h % 2) * HEAD_DIM
            gt[tile, h, h % 2 * HEAD_DIM:(h % 2 + 1) * HEAD_DIM, :] = grads
            gt[tile, h, other:other + HEAD_DIM, :] = jnp.zeros((HEAD_DIM, TQ), BF)
            gt[tile, h, 128:256, :] = three_rows(delta).astype(BF)
        lane = lax.broadcasted_iota(jnp.int32, (TQ, heads * HEAD_DIM), 1)
        for held_rows, source in ((q_own, qt_ref), (g_own, gt_ref)):
            rows = source[:, pl.ds(q0, TQ)].T
            for h in range(heads):
                own = (lane >= h * HEAD_DIM) & (lane < (h + 1) * HEAD_DIM)
                held_rows[tile, h * TQ:(h + 1) * TQ, :] = jnp.where(own, rows, jnp.zeros_like(rows))
        return c
    lax.fori_loop(0, tiles, prepare, 0)
    late.wait(*range(4, 9 if with_seen else 8))
    entering.wait(*range(passed))
    leaving = Late(list(zip(held, pass_out)), pass_sem.at[1])

    def one_step(s, c):
        out_tile, out_k = step_of(table, s)
        read_tile, read_k = real_step(table, s)
        in_tile, in_k = real_step(table, s + 2)
        keys = pl.ds(out_k, TK)
        own = [slice(h * HEAD_DIM, (h + 1) * HEAD_DIM) for h in range(heads)]
        dk = dk_sum[keys, :] + nn(all_ds[...], q_own[read_tile])
        dv = dv_sum[keys, :] + nn(all_p[...], g_own[read_tile])
        dq = [dq_sum[out_tile, h] + nn(kt_ref[own[h], pl.ds(read_k, TK)], all_ds[:, h * TQ:(h + 1) * TQ]) for h in range(heads)]
        for h in range(heads):
            p = jnp.exp(sc[h])
            all_ds[:, h * TQ:(h + 1) * TQ] = (p * dps[h]).astype(BF)
            all_p[:, h * TQ:(h + 1) * TQ] = p.astype(BF)
        bias = seen_bias(rank_cols, counts, in_tile, in_k) if with_seen else None
        for h in range(heads):
            score = nn(pair_rows(k_ref, side_ref, h, in_k), qt[in_tile, h])
            sc[h] = score + bias if with_seen else score
            dps[h] = nn(pair_rows(v_ref, side_ref, h, in_k), gt[in_tile, h])
        dk_sum[keys, :] = dk
        dv_sum[keys, :] = dv
        for h in range(heads):
            dq_sum[out_tile, h] = dq[h]
        return c
    lax.fori_loop(0, table[0, STEPS - 1], one_step, 0)

    def finish(tile, c):
        q0 = pl.multiple_of(tile * TQ, TQ)
        rows = pl.ds(q0, TQ)
        dq = jnp.concatenate([dq_sum[tile, h] for h in range(heads)], 0) * HEAD_DIM ** -0.5
        dk = dk_sum[rows, :] * HEAD_DIM ** -0.5
        for i, (ref, value) in enumerate(((dq_ref, dq.astype(BF).T), (dk_ref, dk.astype(BF)), (dv_ref, dv_sum[rows, :].astype(BF)))):
            ref[rows, :] = value
            out.start(i, tile)
        return c
    lax.fori_loop(0, tiles, finish, 0)
    out.drain(ROW)
    leaving.wait(*range(passed))


def attend_backward(steps, qt, k, kt, v, gt, ot, lse, tables, count, passed, with_seen):
    rows, cols = v.shape
    heads = cols // HEAD_DIM
    side, hot, rank_cols = tables
    args = [steps, count, lse, qt, hot, gt, ot, k, kt, v, side, rank_cols] + passed
    tiles = ROW // TQ
    like = ((rows, cols), BF, "A")
    summed, own = pltpu.VMEM((rows + TK, cols), F32), pltpu.VMEM((tiles, heads * TQ, cols), BF)
    columns, square = pltpu.VMEM((tiles, heads, 256, TQ), BF), pltpu.VMEM((heads, TK, TQ), F32)
    small = pltpu.VMEM((TK, heads * TQ), BF)
    keys, keys_t = pltpu.VMEM((rows + TK, cols), BF), pltpu.VMEM((cols, rows + TK), BF)
    held = [pltpu.VMEM(arg.shape, BF) for arg in (qt, hot, gt, ot)] + [
        keys, keys_t, keys, pltpu.VMEM((rows + TK, 128), BF), pltpu.VMEM((rows + TK, 128), F32)] + [
        pltpu.VMEM(value.shape, value.dtype) for value in passed]
    return call(partial(attn_bwd_kernel, with_seen, heads), "attend_self_backward" if with_seen else "attend_cross_backward",
                args, "SVV" + "A" * (9 + len(passed)), [like, like, like] + [(value.shape, value.dtype, "A") for value in passed],
                [summed, summed, pltpu.VMEM((tiles + 1, heads, HEAD_DIM, TQ), F32), columns, columns, own, own, square, square,
                 small, small, pltpu.VMEM((ROW // TQ, 8, TQ), F32)] + held + [pltpu.VMEM((rows, cols), BF)] * 3
                + [pltpu.SemaphoreType.DMA((9,)), out_semaphores(3, rows), pltpu.SemaphoreType.DMA((2, 2))])


def send(src, dst, send_sem, recv_sem, **where):
    copy = pltpu.make_async_remote_copy(src_ref=src, dst_ref=dst, send_sem=send_sem, recv_sem=recv_sem,
                                        device_id=where, device_id_type=pl.DeviceIdType.MESH)
    copy.start()
    return copy

def greet(peers):
    barrier = pltpu.get_barrier_semaphore()
    for where in peers:
        pl.semaphore_signal(barrier, inc=1, device_id=where, device_id_type=pl.DeviceIdType.MESH)
    pl.semaphore_wait(barrier, len(peers))

def places_of(count):
    me = lax.axis_index("dp")
    across = count // 4
    x, y, z = lax.rem(me, 2), lax.rem(lax.div(me, 2), 2), lax.div(me, 4)
    xpeer, ypeer = me + 1 - 2 * x, me + 2 - 4 * y
    order = sorted(range(1, across), key=lambda d: min(d, across - d))
    ahead = lambda d: lax.rem(z + d, across) * 4 + y * 2 + x
    behind = lambda d: lax.rem(z + across - d, across) * 4 + y * 2 + x
    return me, x, y, z, xpeer, ypeer, order, ahead, behind

class LineGather:
    def __init__(self, count, piece, units, cut, places, zs, ds, xs, ys, gx, gy):
        self.across, self.piece, self.units, self.cut = count // 4, piece, units, cut
        self.places = places
        self.sems = dict(z=zs, d=ds, x=xs, y=ys, gx=gx, gy=gy)

    def copy(self, name, side, k, arriving=False):
        me, x, y, z, xpeer, ypeer = self.places[:6]
        place = x + 2 * y
        place = dict(z=place, x=place, y=place, d=3 - place, gy=place + 1 - 2 * x, gx=place + 2 - 4 * y)[name]
        if arriving:
            place = {"x": x + 2 * y + 1 - 2 * x, "y": x + 2 * y + 2 - 4 * y, "gx": 3 - x - 2 * y, "gy": 3 - x - 2 * y}.get(name, place)
        level = z + k * (2 * side - 1)
        whole = isinstance(k, int) and k == 0
        half = self.units // 2 if whole else (self.units - self.cut) // 2
        first = 0 if whole else self.cut
        start, size = dict(d=(0, self.cut), gy=(first, half), gx=(first + half, self.units - first - half)).get(name, (0, self.units))
        to = dict(x=xpeer, gx=xpeer, y=ypeer, gy=ypeer).get(name, me + 4 * (1 - 2 * side))
        hop = 1 if name in ("z", "d") and not arriving else 0
        if arriving:
            to = xpeer
        part, sems = self.piece(level * 4 + place, start, size), self.sems[name]
        return pltpu.make_async_remote_copy(
            src_ref=part, dst_ref=part, send_sem=sems.at[0, side, k], recv_sem=sems.at[1, side, k + hop],
            device_id={"dp": to}, device_id_type=pl.DeviceIdType.MESH)

    def here(self, side, k):
        z = self.places[3]
        return z >= k if side == 0 else z + k < self.across

    def onward(self, side):
        z = self.places[3]
        return z + 1 < self.across if side == 0 else z > 0

    def along(self, name, side, k, act):
        pl.when(self.here(side, k) & self.onward(side))(lambda: act(self.copy(name, side, k)))

    def run(self, at_start, at_first, at_second):
        start, wait_send = (lambda copy: copy.start()), (lambda copy: copy.wait_send())

        def diagonal(side, k):
            self.copy("x", side, k, True).wait_recv()
            self.copy("gy", side, k).start()
            self.copy("y", side, k, True).wait_recv()
            self.copy("gx", side, k).start()

        def later(side, k):
            diagonal(side, k)
            self.copy("d", side, k, True).wait_recv()
            pl.when(self.onward(side))(lambda: self.copy("d", side, k).start())
        for side in (0, 1):
            self.along("z", side, 0, start)
        self.copy("x", 0, 0).start()
        self.copy("y", 0, 0).start()
        at_start()
        diagonal(0, 0)

        def level(k, carry):
            for side in (0, 1):
                @pl.when(self.here(side, k))
                def _():
                    self.copy("z", side, k, True).wait_recv()
                    pl.when(self.onward(side))(lambda: self.copy("z", side, k).start())
                    self.copy("x", side, k).start()
                    self.copy("y", side, k).start()

            @pl.when(k == 1)
            def _():
                self.copy("gy", 0, 0, True).wait_recv()
                self.copy("gx", 0, 0, True).wait_recv()
                for side in (0, 1):
                    self.along("d", side, 0, start)
                at_first()

            @pl.when(k > 1)
            def _():
                for side in (1, 0):
                    pl.when(self.here(side, k - 1))(lambda: later(side, k - 1))
            pl.when(k == 2)(at_second)
            return carry
        lax.fori_loop(1, self.across, level, 0)
        for side in (1, 0):
            pl.when(self.here(side, self.across - 1))(lambda: later(side, self.across - 1))

        def settle(k, carry):
            for side in (0, 1):
                @pl.when(self.here(side, k))
                def _():
                    for name in ("gy", "gx"):
                        self.copy(name, side, k, True).wait_recv()
                    for name in ("x", "y", "gy", "gx"):
                        self.copy(name, side, k).wait_send()
                for name in ("z", "d"):
                    self.along(name, side, k, wait_send)
            return carry
        lax.fori_loop(1, self.across, settle, 0)
        for name in ("x", "y", "gy", "gx"):
            self.copy(name, 0, 0).wait_send()
        for side in (0, 1):
            for name in ("z", "d"):
                self.along(name, side, 0, wait_send)


class Spread:
    def __init__(self, places, out, zs, xs, ys, gx, gy, direct=False):
        self.places, self.out, self.sems, self.direct = places, out, dict(z=zs, x=xs, y=ys, gx=gx, gy=gy), direct
        self.rows = out.shape[2]
        self.half = self.rows // 2 // UNIT * UNIT
        self.copies = {}

    def go(self, name, d, f_from, d_from, f_to, d_to, to, start, size):
        part, sems = pl.ds(start, size), self.sems[name]
        self.copies[name, d] = send(self.out.at[f_from, d_from, part], self.out.at[f_to, d_to, part],
                                    sems.at[0, d], sems.at[1, d], dp=to)

    def over_plane(self, d):
        xpeer, ypeer = self.places[4], self.places[5]
        self.go("x", d, 0, d, 1, d, xpeer, 0, self.rows)
        self.go("y", d, 0, d, 2, d, ypeer, 0, self.rows)
        if self.direct:
            me, x, y = self.places[:3]
            self.go("gx", d, 0, d, 3, d, me + 3 - 2 * x - 4 * y, 0, self.rows)

    def start(self):
        order, ahead = self.places[6], self.places[7]
        for d in order:
            self.go("z", d, 0, 0, 0, d, ahead(d), 0, self.rows)
        self.over_plane(0)

    def relay(self):
        for d in self.places[6]:
            self.copies["z", d].wait_recv()
            self.over_plane(d)

    def diagonal(self):
        xpeer, ypeer, order = self.places[4:7]
        for d in [0] + order:
            self.copies["x", d].wait_recv()
            if self.half and not self.direct:
                self.go("gy", d, 1, d, 3, d, ypeer, 0, self.half)
            self.copies["y", d].wait_recv()
            if not self.direct:
                self.go("gx", d, 2, d, 3, d, xpeer, self.half, self.rows - self.half)

    def finish(self):
        for (name, d), copy in self.copies.items():
            if name in ("gx", "gy"):
                copy.wait_recv()

    def drain(self):
        for copy in self.copies.values():
            copy.wait_send()


def plane_swap(value, count, f):
    return lax.ppermute(value, "dp", [(i, i // 4 * 4 + (i % 4 ^ f)) for i in range(count)])


def plane_offset(places, f):
    x, y = places[1], places[2]
    return lax.rem(x + f % 2, 2) + 2 * lax.rem(y + f // 2, 2)


def call(kernel, name, args, kinds, outs, scratch, number=None):
    space = {"V": pltpu.VMEM, "S": pltpu.SMEM, "A": pl.ANY}
    extra = {} if number is None else dict(collective_id=number, has_side_effects=True)
    return pl.pallas_call(
        kernel,
        out_shape=tuple(jax.ShapeDtypeStruct(shape, dtype) for shape, dtype, _ in outs),
        in_specs=[pl.BlockSpec(memory_space=space[kind]) for kind in kinds],
        out_specs=tuple(pl.BlockSpec(memory_space=space[kind]) for _, _, kind in outs),
        scratch_shapes=scratch,
        compiler_params=pltpu.CompilerParams(vmem_limit_bytes=60 * 2**20, **extra),
        cost_estimate=pl.CostEstimate(flops=4 * 10**10, bytes_accessed=16 * 2**20, transcendentals=0),
        name=name,
    )(*args)


CHUNK = 256


def tn(a, b):
    return lax.dot_general(a, b, (((0,), (0,)), ((), ())), preferred_element_type=F32)


def normalise(value):
    centred = value - jnp.mean(value, -1, keepdims=True)
    scale = lax.rsqrt(jnp.mean(centred * centred, -1, keepdims=True) + EPS_NORM)
    return centred * scale, scale


def norm_back(unit, scale, gain, grad):
    inner = grad * gain
    return scale * (inner - jnp.mean(inner, -1, keepdims=True) - unit * jnp.mean(inner * unit, -1, keepdims=True))


def fold_rows(value):
    return jnp.sum(value.reshape(value.shape[0] // 8, 8, value.shape[1]), 0)


def interleave(size):
    row = lax.broadcasted_iota(jnp.int32, (size, size), 0)
    col = lax.broadcasted_iota(jnp.int32, (size, size), 1)
    source = jnp.where((row & 1) == 0, row >> 1, (row >> 1) + size // 2)
    return jnp.where(col == source, 1.0, 0.0).astype(BF)


def part_rows(matrix, order):
    return lax.dot_general(order, matrix, (((0,), (0,)), ((), ())), preferred_element_type=F32).astype(BF)


def as_units(gradient, order):
    parted = part_rows(gradient.astype(BF), order)
    half = parted.shape[0] // 2
    return jnp.concatenate([parted[:half], parted[half:]], 1)


def other_core(mine, theirs, sems, step):
    rows = pl.ds(step * CHUNK, CHUNK)
    return pltpu.make_async_remote_copy(
        src_ref=mine.at[rows], dst_ref=theirs.at[rows], send_sem=sems.at[0, step], recv_sem=sems.at[1, step],
        device_id={"head": 1 - lax.axis_index("head")}, device_id_type=pl.DeviceIdType.MESH)


def greet_core():
    greet([{"head": 1 - lax.axis_index("head")}])


def chunks(total, body, begin=0):
    def one(step, carry):
        body(step, pl.ds(pl.multiple_of(step * CHUNK, CHUNK), CHUNK))
        return carry
    lax.fori_loop(begin // CHUNK, total // CHUNK, one, 0)


def drain(total, mine, theirs, sems):
    def body(step, rows):
        other_core(mine, theirs, sems, step).wait_send()
    chunks(total, body)


class Late:
    def __init__(self, pairs, sems):
        self.copies = [pltpu.make_async_copy(source, held, sems.at[i]) for i, (source, held) in enumerate(pairs)]
        for copy in self.copies:
            copy.start()

    def wait(self, *which):
        for i in which:
            self.copies[i].wait()


class Out:
    def __init__(self, pairs, sems):
        self.pairs, self.sems = pairs, sems

    def copy(self, i, step):
        held, out = self.pairs[i]
        part = pl.ds(pl.multiple_of(step * CHUNK, CHUNK), CHUNK)
        if held.shape[0] < held.shape[1]:
            held, out = held.at[:, part], out.at[:, part]
        else:
            held, out = held.at[part], out.at[part]
        return pltpu.make_async_copy(held, out, self.sems.at[i, step])

    def start(self, i, step):
        self.copy(i, step).start()

    def drain(self, tokens):
        def body(step, rows):
            for i in range(len(self.pairs)):
                self.copy(i, step).wait()
        chunks(tokens, body)


def plan_kernel(block, owner_ref, len_ref, me_ref, rank_ref, count_ref, place_ref, held_ref, rank_out, count_out, table, info):
    units = owner_ref.shape[1]
    owner = owner_ref[...].astype(F32)
    owner_cols = jnp.broadcast_to(owner, (128, units)).T
    owner_cols = jnp.concatenate([owner_cols] * (units // 128), 1)
    before = lax.broadcasted_iota(jnp.int32, (units, units), 0) < lax.broadcasted_iota(jnp.int32, (units, units), 1)
    slots = jnp.sum(jnp.where(before & (owner_cols == owner), 1.0, 0.0), 0, keepdims=True)
    place = owner * block + slots
    place_ref[...] = place.astype(jnp.int32)
    me = me_ref[0].astype(F32)
    place_cols = jnp.broadcast_to(place, (128, units)).T
    lane = lax.broadcasted_iota(jnp.int32, (units, 128), 1)
    unit = lax.broadcasted_iota(jnp.int32, (units, 128), 0).astype(F32)
    mine = jnp.where(place_cols == me * block + lane.astype(F32), unit, 0.0)
    mine = jnp.where(lane == 127, jnp.where(owner_cols[:, :128] == me, 1.0, 0.0), jnp.where(lane < block, mine, 0.0))
    held_ref[...] = jnp.sum(mine, 0, keepdims=True).astype(jnp.int32)
    longest, first, at, start = jnp.int32(0), jnp.int32(0), jnp.int32(0), jnp.int32(0)
    for d in range(DOCS):
        length = len_ref[0, d]
        longer = length > longest
        first = jnp.where(longer, d, first)
        start = jnp.where(longer, at, start)
        longest = jnp.where(longer, length, longest)
        at = at + length
    for d in range(DOCS):
        info[0, d] = len_ref[0, lax.rem(first + d, DOCS)]
    info[0, DOCS] = start
    info[0, DOCS + 1] = lax.rem(ROW - start, ROW)
    turn = lax.rem(ROW - start, ROW)
    rank_out[...] = pltpu.roll(rank_ref[...], turn, 1)
    count_out[...] = pltpu.roll(count_ref[...], turn, 1)
    step_table(info, table)


def plan(unit_owner, lengths, me, rank_row, count_row, block):
    row = ((1, ROW), jnp.int32, "V")
    return call(partial(plan_kernel, block), "plan", [unit_owner.reshape(1, -1), lengths, me, rank_row, count_row], "VSSVV",
                [((1, unit_owner.shape[0]), jnp.int32, "V"), ((1, 128), jnp.int32, "V"), row, row, ((2, STEPS), jnp.int32, "S"),
                 ((1, DOCS + 2), jnp.int32, "S")], [])


def turn_rows(source, target, shift):
    tiles = source.shape[0]
    whole, rest = lax.div(shift, UNIT), lax.rem(shift, UNIT)

    def one(i, carry):
        at = lax.rem(i + whole, tiles)
        both = jnp.concatenate([source[at].astype(F32), source[lax.rem(at + 1, tiles)].astype(F32)], 0)
        rows = pltpu.roll(both, lax.rem(2 * UNIT - rest, 2 * UNIT), 0)[:UNIT]
        target[pl.ds(pl.multiple_of(i * UNIT, UNIT), UNIT), :] = rows.astype(target.dtype)
        return carry
    lax.fori_loop(0, tiles, one, 0, unroll=4)


def in_tiles(value):
    return value.reshape(-1, UNIT, value.shape[1])


def project_kernel(devices, place_ref, info, master, norm_row, rank_ref, query_hbm, kv_hbm, memory_hbm, grad_hbm,
                   nq_out, nkv_out, qt_out, k_out, kt_out, v_out, vt_out, kc_out, kct_out, vc_out, vct_out,
                   query_out, kv_out, memory_out, grad_out,
                   ws_ref, wc_ref, wos_ref, woc_ref, w1_ref, w2_ref, norms, side_ref, hot_ref, rank_cols,
                   gathered, norm_all, flat, stage_a, stage_b, query_ref, kv_ref, memory_ref, grad_ref, unit_q, unit_kv,
                   nq_ref, nkv_ref, qt_ref, k_ref, kt_ref, v_ref, vt_ref, kc_ref, kct_ref, vc_ref, vct_ref,
                   late_sems, turned_sems, out_sems, norm_sems, *line_sems):
    tokens, features = query_ref.shape
    units = place_ref.shape[1]
    late = Late([(query_hbm, stage_a), (kv_hbm, stage_b)], late_sems.at[0])
    held = (nq_ref, nkv_ref, qt_ref, k_ref, kt_ref, v_ref, vt_ref, kc_ref, kct_ref, vc_ref, vct_ref)
    out = Out(list(zip(held, (nq_out, nkv_out, qt_out, k_out, kt_out, v_out, vt_out, kc_out, kct_out, vc_out, vct_out))), out_sems)
    places = places_of(devices)
    me, x, y, z, xpeer, ypeer, order, ahead, behind = places
    block = master.shape[0]
    gathered[pl.ds(me * block, block)] = master[...].astype(BF)
    others = [lax.rem(me + d, devices) for d in range(1, devices)]
    norm_all[me] = norm_row[...]
    greet([{"dp": other} for other in others])
    norm_copies = [send(norm_row, norm_all.at[me], norm_sems.at[0, d], norm_sems.at[1, d], dp=other)
                   for d, other in zip(range(1, devices), others)]

    leaving = [(query_ref, query_out), (kv_ref, kv_out), (memory_ref, memory_out), (grad_ref, grad_out)]

    def leave(number):
        return pltpu.make_async_copy(*leaving[number], turned_sems.at[number])

    def turn(stage, number):
        turn_rows(stage, leaving[number][0], info[0, DOCS])
        leave(number).start()

    def first_turns():
        mask_tables(info, rank_ref, side_ref, hot_ref, rank_cols)
        late.wait(0, 1)
        turn(stage_a, 0)
        turn(stage_b, 1)

    def norms_of_streams():
        def units_of(step, rows):
            unit_q[rows, :] = normalise(query_ref[rows, :].astype(F32))[0]
            unit_kv[rows, :] = normalise(kv_ref[rows, :].astype(F32))[0]
        chunks(tokens, units_of)

    def last_turns():
        more = Late([(memory_hbm, stage_a), (grad_hbm, stage_b)], late_sems.at[1])
        more.wait(0, 1)
        turn(stage_a, 2)
        turn(stage_b, 3)
    LineGather(devices, lambda number, start, size: gathered.at[pl.ds(number * block + start, size)], block, block * 3 // 5,
               places, *line_sems).run(first_turns, norms_of_streams, last_turns)

    for copy in norm_copies:
        copy.wait()
    share, whole_lanes = devices // 8, norm_row.shape[1] < features
    vectors = []
    for number in range(8):
        pieces = [norm_all[number * share + i] for i in range(share)]
        if whole_lanes:
            vectors.append(jnp.concatenate(pieces, 1))
        else:
            total = pieces[0]
            for piece in pieces[1:]:
                total = total + piece
            vectors.append(total)
    norms[...] = jnp.concatenate(vectors, 0).astype(BF).astype(F32)

    def one_unit(u, carry):
        flat[pl.ds(pl.multiple_of(u * UNIT, UNIT), UNIT), :] = gathered[place_ref[0, u]]
        return carry
    lax.fori_loop(0, units, one_unit, 0, unroll=4)
    order = interleave(features)
    cols = v_ref.shape[1]
    for number in range(6):
        rows = flat[number * cols:(number + 1) * cols, :]
        stacked = jnp.concatenate([rows[:, :cols], rows[:, cols:]], 0)
        matrix = nn(order, stacked).astype(BF)
        if number < 3:
            ws_ref[number] = matrix
        else:
            wc_ref[number - 3] = matrix
    wos_ref[...] = flat[6 * cols:7 * cols, :]
    woc_ref[...] = flat[7 * cols:8 * cols, :]
    hidden = w2_ref.shape[0]
    for block in range(hidden // features):
        at = 8 * cols + block * features
        parted = part_rows(flat[at:at + features, :], order)
        half = features // 2
        w1_ref[block * half:(block + 1) * half, :] = jnp.concatenate([parted[:half], parted[half:]], 1)
    w2_ref[...] = flat[8 * cols + hidden:, :]

    def body(step, carry):
        rows = pl.ds(pl.multiple_of(step * 2 * CHUNK, 2 * CHUNK), 2 * CHUNK)
        nq = (unit_q[rows, :] * norms[0:1, :] + norms[1:2, :]).astype(BF)
        nkv = (unit_kv[rows, :] * norms[2:3, :] + norms[3:4, :]).astype(BF)
        source = memory_ref[rows, :]
        low = lambda left, right: nn(left, right).astype(BF)
        k, v, kc, vc = low(nkv, ws_ref[1]), low(nkv, ws_ref[2]), low(source, wc_ref[1]), low(source, wc_ref[2])
        results = [nq, nkv, low(nq, ws_ref[0]).T, k, k.T, v, v.T, kc, kc.T, vc, vc.T]
        for i, (ref, result) in enumerate(zip(held, results)):
            if ref.shape[0] < ref.shape[1]:
                ref[:, rows] = result
            else:
                ref[rows, :] = result
            out.start(i, 2 * step)
            out.start(i, 2 * step + 1)
        return carry
    lax.fori_loop(0, tokens // (2 * CHUNK), body, 0)
    out.drain(tokens)
    for number in range(4):
        leave(number).wait()


def pair_sems(tokens):
    return pltpu.SemaphoreType.DMA((2, tokens // CHUNK))


def out_semaphores(count, tokens):
    return pltpu.SemaphoreType.DMA((count, tokens // CHUNK))


def project(devices, place_of, info, master, norm_row, rank_row, query_stream, kv_stream, memory, out_grad, cols, hidden):
    tokens, features = query_stream.shape
    wide, narrow, across = (tokens, features), (tokens, cols), (cols, tokens)
    shapes = [wide, wide, across] + [narrow, across] * 4
    outs = [(shape, BF, "A") for shape in shapes] + [(wide, BF, "A")] * 4 + [
        ((3, features, cols), BF, "V"), ((3, features, cols), BF, "V"), ((cols, features), BF, "V"), ((cols, features), BF, "V"),
        ((features, hidden), BF, "V"), ((hidden, features), BF, "V"), ((8, features), F32, "V"),
        ((ROW, 128), BF, "V"), ((128, ROW), BF, "V"), ((ROW, 128), F32, "V")]
    D = pltpu.SemaphoreType.DMA
    streams = [in_tiles(stream) for stream in (query_stream, kv_stream, memory, out_grad)]
    scratch = [pltpu.VMEM((devices * master.shape[0], UNIT, features), BF), pltpu.VMEM((devices,) + norm_row.shape, F32),
               pltpu.VMEM((8 * cols + 2 * hidden, features), BF)]
    scratch += [pltpu.VMEM(streams[0].shape, BF)] * 2 + [pltpu.VMEM(wide, BF)] * 4 + [pltpu.VMEM(wide, F32)] * 2
    scratch += [pltpu.VMEM(shape, BF) for shape in shapes]
    scratch += [D((2, 2)), D((4,)), out_semaphores(len(shapes), tokens), D((2, devices))] + [D((2, 2, devices // 4 + 1))] * 6
    return call(partial(project_kernel, devices), "project",
                [place_of, info, master, norm_row, rank_row] + streams, "SSVVVAAAA", outs, scratch, 0)


def self_out_kernel(mixed, wo, query_hbm, wc, norms, res_out, nc_out, q_out,
                    query, res_ref, nc_ref, q_ref, mine, theirs, sems, late_sems, out_sems):
    tokens = query.shape[0]
    late = Late([(query_hbm, query)], late_sems)
    out = Out([(res_ref, res_out), (nc_ref, nc_out), (q_ref, q_out)], out_sems)
    greet_core()

    def give(step, rows):
        mine[rows, :] = nn(mixed[rows, :], wo[...]).astype(BF)
        other_core(mine, theirs, sems, step).start()
    chunks(tokens, give)
    late.wait(0)

    def take(step, rows):
        other_core(mine, theirs, sems, step).wait_recv()
        res = query[rows, :].astype(F32) + (mine[rows, :].astype(F32) + theirs[rows, :].astype(F32))
        res_ref[rows, :] = res
        out.start(0, step)
        nc = (normalise(res)[0] * norms[4:5, :] + norms[5:6, :]).astype(BF)
        nc_ref[rows, :] = nc
        out.start(1, step)
        q_ref[:, rows] = nn(nc, wc[0]).astype(BF).T
        out.start(2, step)
    chunks(tokens, take)
    drain(tokens, mine, theirs, sems)
    out.drain(tokens)


def self_out(mixed, wo, query, wc, norms):
    tokens, features = query.shape
    wide = (tokens, features)
    across = (mixed.shape[1], tokens)
    outs = [(wide, F32, "A"), (wide, BF, "A"), (across, BF, "A")]
    scratch = [pltpu.VMEM(wide, BF), pltpu.VMEM(wide, F32), pltpu.VMEM(wide, BF), pltpu.VMEM(across, BF),
               pltpu.VMEM(wide, BF), pltpu.VMEM(wide, BF), pair_sems(tokens), pltpu.SemaphoreType.DMA((1,)),
               out_semaphores(3, tokens)]
    return call(self_out_kernel, "self_out", [mixed, wo, query, wc, norms], "VVAVV", outs, scratch, 2)


def gelu_parts(value):
    bell = jnp.exp2(value * value * (-0.5 * 1.4426950408889634))
    base = 1.0 + (0.3275911 * 0.7071067811865476) * jnp.abs(value)
    t = pl.reciprocal(base, approx=True)
    t = t * (2.0 - base * t)
    poly = ((((0.5307027145 * t - 0.7265760135) * t + 0.7107068705) * t - 0.142248368) * t + 0.127414796) * t
    tail = poly * bell
    below = jnp.where(value < 0.0, tail, 1.0 - tail)
    return value * below, below + value * (bell * 0.3989422804014327)


def spread_flat(devices, places, flat, refs):
    rows = flat.shape[0] // devices
    for f, ref in enumerate(refs):
        place = plane_offset(places, f)
        for level in range(devices // 4):
            ref[level, ref.shape[1] - rows:, :] = flat[pl.ds(pl.multiple_of((level * 4 + place) * rows, UNIT), rows), :]


def feed_forward_kernel(devices, mixed, wo, res_hbm, w1_hbm, w2_hbm, out_grad_hbm, norms,
                        out_out, gres_out, gmix_out, part0, part1, part2, part3, sums_ref,
                        w1, w2, res, out_grad, out_ref, gres_ref, gmix_ref, flat,
                        mine, theirs, nf_all, hid_all, pre_all, low_all, mine_o, theirs_o, mine_g, theirs_g,
                        sems, sems_o, sems_g, late_sems, out_sems):
    tokens, features = out_grad.shape
    hidden = w2.shape[0]
    places = places_of(devices)
    late = Late([(res_hbm, res), (out_grad_hbm, out_grad), (w1_hbm, w1), (w2_hbm, w2)], late_sems)
    out = Out([(out_ref, out_out), (gres_ref, gres_out), (gmix_ref, gmix_out)], out_sems)
    greet_core()

    def give(step, rows):
        mine[rows, :] = nn(mixed[rows, :], wo[...]).astype(BF)
        other_core(mine, theirs, sems, step).start()
    chunks(tokens, give)
    late.wait(0, 1, 2, 3)

    def middle(step, rows):
        other_core(mine, theirs, sems, step).wait_recv()
        value = res[rows, :] + (mine[rows, :].astype(F32) + theirs[rows, :].astype(F32))
        gres_ref[rows, :] = value
        nf = (normalise(value)[0] * norms[6:7, :] + norms[7:8, :]).astype(BF)
        nf_all[rows, :] = nf
        grad = out_grad[rows, :]
        out_part = jnp.zeros((CHUNK, features), F32)
        grad_part = jnp.zeros((CHUNK, features), F32)
        for block in range(hidden // 256):
            at = slice(block * 256, (block + 1) * 256)
            act, slope = gelu_parts(nn(nf, w1[:, at]))
            act = act.astype(BF)
            hid_all[rows, at] = act
            pre = (slope * nt(grad, w2[at, :])).astype(BF)
            pre_all[rows, at] = pre
            out_part = out_part + nn(act, w2[at, :])
            grad_part = grad_part + nt(pre, w1[:, at])
        mine_o[rows, :] = out_part.astype(BF)
        other_core(mine_o, theirs_o, sems_o, step).start()
        mine_g[rows, :] = grad_part.astype(BF)
        other_core(mine_g, theirs_g, sems_g, step).start()
    chunks(tokens, middle)

    order = interleave(features)
    half, cols = features // 2, mixed.shape[1]
    for block in range(hidden // 256):
        at = slice(block * 256, (block + 1) * 256)
        flat[cols + hidden + block * 256:cols + hidden + (block + 1) * 256, :] = tn(hid_all[:, at], out_grad[...]).astype(BF)
    for block in range(hidden // features):
        gradient = tn(nf_all[:, block * half:(block + 1) * half], pre_all[...]).astype(BF)
        stacked = jnp.concatenate([gradient[:, :features], gradient[:, features:]], 0)
        flat[cols + block * features:cols + (block + 1) * features, :] = nn(order, stacked).astype(BF)
    sums_ref[...] = jnp.zeros_like(sums_ref)

    def close(step, rows):
        other_core(mine_o, theirs_o, sems_o, step).wait_recv()
        other_core(mine_g, theirs_g, sems_g, step).wait_recv()
        value = gres_ref[rows, :]
        out_ref[rows, :] = (value + (mine_o[rows, :].astype(F32) + theirs_o[rows, :].astype(F32))).astype(BF)
        out.start(0, step)
        grad = mine_g[rows, :].astype(F32) + theirs_g[rows, :].astype(F32)
        unit, scale = normalise(value)
        gres = norm_back(unit, scale, norms[6:7, :], grad) + out_grad[rows, :].astype(F32)
        gres_ref[rows, :] = gres
        out.start(1, step)
        sums_ref[0:8, :] += fold_rows(grad * unit)
        sums_ref[8:16, :] += fold_rows(grad)
        low = gres.astype(BF)
        low_all[rows, :] = low
        gmix_ref[:, rows] = nt(low, wo[...]).astype(BF).T
        out.start(2, step)
    chunks(tokens, close)
    flat[0:cols, :] = tn(mixed[...], low_all[...]).astype(BF)
    if flat.shape[0] > cols + 2 * hidden:
        flat[cols + 2 * hidden:, :] = jnp.zeros((flat.shape[0] - cols - 2 * hidden, features), BF)
    spread_flat(devices, places, flat, (part0, part1, part2, part3))
    out.drain(tokens)
    drain(tokens, mine, theirs, sems)
    drain(tokens, mine_o, theirs_o, sems_o)
    drain(tokens, mine_g, theirs_g, sems_g)


def whole_blocks(rows, devices):
    return -(-rows // (devices * UNIT)) * devices * UNIT


def feed_forward(devices, mixed, wo, res, w1, w2, out_grad, norms):
    tokens, features = out_grad.shape
    hidden = w2.shape[0]
    flat_rows = whole_blocks(wo.shape[0] + 2 * hidden, devices)
    part = ((devices // 4, flat_rows // devices, features), BF, "V")
    wide = (tokens, features)
    across = (mixed.shape[1], tokens)
    outs = [(wide, BF, "A"), (wide, F32, "A"), (across, BF, "A")] + [part] * 4 + [((16, features), F32, "V")]
    deep, narrow = pltpu.VMEM((tokens, hidden), BF), pltpu.VMEM(wide, BF)
    scratch = [pltpu.VMEM(w1.shape, BF), pltpu.VMEM(w2.shape, BF), pltpu.VMEM(wide, F32), narrow, narrow, pltpu.VMEM(wide, F32), pltpu.VMEM(across, BF),
               pltpu.VMEM((flat_rows, features), BF), narrow, narrow, narrow, deep, deep, narrow] + [narrow] * 4
    scratch += [pair_sems(tokens)] * 3 + [pltpu.SemaphoreType.DMA((4,)), out_semaphores(3, tokens)]
    return call(partial(feed_forward_kernel, devices), "feed_forward", [mixed, wo, res, w1, w2, out_grad, norms], "VVAAAAV",
                outs, scratch, 3)


def branch_give(dq, dk, dv, weights, mine_a, theirs_a, mine_b, theirs_b, sems_a, sems_b):
    def give(step, rows):
        mine_a[rows, :] = nt(dq[rows, :], weights[0]).astype(BF)
        other_core(mine_a, theirs_a, sems_a, step).start()
        mine_b[rows, :] = (nt(dk[rows, :], weights[1]) + nt(dv[rows, :], weights[2])).astype(BF)
        other_core(mine_b, theirs_b, sems_b, step).start()
    chunks(dq.shape[0], give)


def branch_weights(first_in, second_in, dq, dk, dv, flat, between=lambda: None):
    cols = dq.shape[1]
    order = interleave(first_in.shape[1])
    for number, (entering, grad) in enumerate(((first_in, dq), (second_in, dk), (second_in, dv))):
        if number == 1:
            between()
        flat[number * cols:(number + 1) * cols, :] = as_units(tn(entering[...], grad[...]), order)


def z_sum_start(devices, places, pieces, landed, sems):
    me, x, y, z, xpeer, ypeer, order, ahead, behind = places
    return [send(pieces.at[lax.rem(z + d, devices // 4)], landed.at[d], sems.at[0, d], sems.at[1, d], dp=ahead(d)) for d in order]


def z_sum_end(places, pieces, landed, copies):
    z, order = places[3], places[6]
    total = pieces[z].astype(F32)
    for copy, d in zip(copies, order):
        copy.wait_recv()
        total = total + landed[d].astype(F32)
    return total.astype(BF)


def plane_sum_start(devices, places, flat, used, source, landing, sems):
    me, x, y, z, xpeer, ypeer = places[:6]
    if flat.shape[0] > used:
        flat[used:, :] = jnp.zeros((flat.shape[0] - used, flat.shape[1]), BF)
    spread_flat(devices, places, flat, [source.at[f] for f in range(4)])
    return [send(source.at[f], landing.at[f], sems.at[0, f], sems.at[1, f], dp=peer)
            for f, peer in ((3, me + 3 - 2 * x - 4 * y), (1, xpeer), (2, ypeer))]


def four_sum(parts, at):
    return (parts[0][at].astype(F32) + parts[1][at].astype(F32) + parts[2][at].astype(F32) + parts[3][at].astype(F32)).astype(BF)


def cross_back_kernel(devices, info, dq_hbm, dk_hbm, dv_hbm, wc_hbm, nc_hbm, memory_hbm, res_hbm, gres_hbm, output_hbm, mixed_hbm, wo, norms,
                      part0, part1, part2, part3,
                      gmem_out, output_out, gnew_out, gmix_out, give0, give1, give2, give3, more_ref, sums_ref,
                      dq, dk, dv, wc, mixed, nc, memory, res, gres, output_ref, gmem_ref, turned_a, turned_b, gmix_ref, flat, flat_o, source, landing, pieces, landed, blocks,
                      mine_a, theirs_a, mine_b, theirs_b, low_all, sems_a, sems_b, late_sems, out_sems, turned_sems, z_sems, zz_sems, plane_sems):
    tokens, features = nc.shape
    cols = dq.shape[1]
    across = devices // 4
    places = places_of(devices)
    me, x, y, z, xpeer, ypeer, order, ahead, behind = places
    late = Late([(nc_hbm, nc), (memory_hbm, memory), (res_hbm, res), (gres_hbm, gres), (output_hbm, output_ref), (dq_hbm, dq),
                 (wc_hbm, wc), (dk_hbm, dk), (dv_hbm, dv), (mixed_hbm, mixed)], late_sems)
    out = Out([(gres, gnew_out), (gmix_ref, gmix_out)], out_sems)
    for level in range(across):
        pieces[level] = four_sum((part0, part1, part2, part3), level)
    greet([{"head": 1 - lax.axis_index("head")}] + [{"dp": ahead(d)} for d in order]
          + [{"dp": peer} for peer in (xpeer, ypeer, me + 3 - 2 * x - 4 * y)])
    z_copies = z_sum_start(devices, places, pieces, landed, z_sems)
    late.wait(5, 6, 7, 8)
    branch_give(dq, dk, dv, wc, mine_a, theirs_a, mine_b, theirs_b, sems_a, sems_b)
    late.wait(0, 1)
    branch_weights(nc, memory, dq, dk, dv, flat)
    plane_copies = plane_sum_start(devices, places, flat, 3 * cols, source, landing, plane_sems)
    blocks[0] = z_sum_end(places, pieces, landed, z_copies)
    zz_copies = [send(blocks.at[0], blocks.at[d], zz_sems.at[0, d], zz_sems.at[1, d], dp=ahead(d)) for d in order]
    sums_ref[...] = jnp.zeros_like(sums_ref)
    late.wait(2, 3)

    def close(step, rows):
        other_core(mine_a, theirs_a, sems_a, step).wait_recv()
        grad = mine_a[rows, :].astype(F32) + theirs_a[rows, :].astype(F32)
        unit, scale = normalise(res[rows, :])
        gnew = norm_back(unit, scale, norms[4:5, :], grad) + gres[rows, :]
        gres[rows, :] = gnew
        out.start(0, step)
        sums_ref[0:8, :] += fold_rows(grad * unit)
        sums_ref[8:16, :] += fold_rows(grad)
        low = gnew.astype(BF)
        low_all[rows, :] = low
        gmix_ref[:, rows] = nt(low, wo[...]).astype(BF).T
        out.start(1, step)
        other_core(mine_b, theirs_b, sems_b, step).wait_recv()
        total = (mine_b[rows, :].astype(F32) + theirs_b[rows, :].astype(F32)).astype(BF)
        gmem_ref[pl.ds(step * (CHUNK // UNIT), CHUNK // UNIT)] = in_tiles(total)
    chunks(tokens, close)
    late.wait(9)
    flat_o[0:cols, :] = tn(mixed[...], low_all[...]).astype(BF)
    if flat_o.shape[0] > cols:
        flat_o[cols:, :] = jnp.zeros((flat_o.shape[0] - cols, features), BF)
    gives = (give0, give1, give2, give3)
    spread_flat(devices, places, flat_o, gives)
    for copy in plane_copies:
        copy.wait_recv()
    for d in range(across):
        more_ref[d] = four_sum((source.at[0], landing.at[1], landing.at[2], landing.at[3]), d)
    late.wait(4)
    turn_rows(gmem_ref, turned_a, info[0, DOCS + 1])
    turn_rows(output_ref, turned_b, info[0, DOCS + 1])
    turned = Late([(turned_a, gmem_out), (turned_b, output_out)], turned_sems)
    for copy in zz_copies:
        copy.wait_recv()
    ready_rows = blocks.shape[1]
    for ref in gives:
        for d in range(across):
            ref[d, 0:ready_rows, :] = blocks[d]
    for copy in z_copies + zz_copies + plane_copies:
        copy.wait_send()
    turned.wait(0, 1)
    out.drain(tokens)
    drain(tokens, mine_a, theirs_a, sems_a)
    drain(tokens, mine_b, theirs_b, sems_b)


def cross_back(devices, info, dq, dk, dv, wc, nc, memory, res, gres, output, mixed, wo, norms, parts):
    tokens, features = nc.shape
    cols = dq.shape[1]
    across, ready_rows = devices // 4, parts[0].shape[1]
    flat_rows, o_rows = whole_blocks(3 * cols, devices), whole_blocks(cols, devices)
    give = ((across, ready_rows + o_rows // devices, features), BF, "V")
    part = (across, flat_rows // devices, features)
    wide = (tokens, features)
    outs = [(wide, BF, "A"), (wide, BF, "A"), (wide, F32, "A"), ((cols, tokens), BF, "A")] + [give] * 4 + [
        (part, BF, "V"), ((16, features), F32, "V")]
    low, high = pltpu.VMEM(wide, BF), pltpu.VMEM(wide, F32)
    small = pltpu.VMEM((across, ready_rows, features), BF)
    z_sems = pltpu.SemaphoreType.DMA((2, across))
    tiles = pltpu.VMEM((tokens // UNIT, UNIT, features), BF)
    scratch = [pltpu.VMEM(arg.shape, BF) for arg in (dq, dk, dv, wc, mixed)]
    scratch += [low, low, high, high, tiles, tiles, low, low, pltpu.VMEM((cols, tokens), BF), pltpu.VMEM((flat_rows, features), BF),
               pltpu.VMEM((o_rows, features), BF), pltpu.VMEM((4,) + part, BF), pltpu.VMEM((4,) + part, BF), small, small, small]
    scratch += [low] * 5 + [pair_sems(tokens)] * 2 + [pltpu.SemaphoreType.DMA((10,)), out_semaphores(2, tokens), pltpu.SemaphoreType.DMA((2,)), z_sems, z_sems,
                                                 pltpu.SemaphoreType.DMA((2, 4))]
    return call(partial(cross_back_kernel, devices), "cross_back",
                [info, dq, dk, dv, wc, nc, memory, res, gres, in_tiles(output), mixed, wo, norms] + parts, "SAAAAAAAAAAVVVVVV", outs, scratch, 4)


def self_back_kernel(devices, ready_rows, info, dq, dk, dv, ws, nq_hbm, nkv_hbm, query_hbm, kv_hbm, gres_hbm, norms, sums_c, sums_f, more_in,
                     part0, part1, part2, part3,
                     gquery_out, gkv_out, last_ref, more_ref, gnorm_ref,
                     nq, nkv, query, kv, gres, gquery_ref, gkv_ref, turned_a, turned_b, flat, source, landing, pieces, landed, more_pieces, more_landed,
                     norm_mine, norm_all, mine_a, theirs_a, mine_b, theirs_b, sums, sems_a, sems_b, late_sems, out_sems,
                     z_sems, more_z_sems, plane_sems, n_sems, part_rows, part_sems, *spread_sems):
    tokens, features = nq.shape
    across = devices // 4
    places = places_of(devices)
    me, x, y, z, xpeer, ypeer, order, ahead, behind = places
    late = Late([(nq_hbm, nq), (nkv_hbm, nkv), (query_hbm, query), (kv_hbm, kv), (gres_hbm, gres)], late_sems)
    in_rows, more_rows = more_in.shape[1], more_ref.shape[2]
    late_parts = Late([(part.at[:, pl.ds(ready_rows, more_rows - in_rows)], part_rows.at[f])
                       for f, part in enumerate((part0, part1, part2, part3))], part_sems)
    others = [lax.rem(me + d, devices) for d in range(1, devices)]
    greet([{"head": 1 - lax.axis_index("head")}] + [{"dp": other} for other in others])
    late.wait(0)
    branch_weights(nq, nkv, dq, dk, dv, flat, lambda: late.wait(1))
    plane_copies = plane_sum_start(devices, places, flat, 3 * dq.shape[1], source, landing, plane_sems)
    late_parts.wait(0, 1, 2, 3)
    for level in range(across):
        more_pieces[level, 0:in_rows, :] = more_in[level]
        more_pieces[level, in_rows:, :] = four_sum([part_rows.at[f] for f in range(4)], level)
    more_copies = z_sum_start(devices, places, more_pieces, more_landed, more_z_sems)
    branch_give(dq, dk, dv, ws, mine_a, theirs_a, mine_b, theirs_b, sems_a, sems_b)
    more_ref[0, 0] = z_sum_end(places, more_pieces, more_landed, more_copies)
    more = Spread(places, more_ref, *spread_sems[:5])
    more.start()
    sums[...] = jnp.zeros_like(sums)
    late.wait(2, 3, 4)

    def close(step, rows):
        other_core(mine_a, theirs_a, sems_a, step).wait_recv()
        grad = mine_a[rows, :].astype(F32) + theirs_a[rows, :].astype(F32)
        unit, scale = normalise(query[rows, :].astype(F32))
        tiles = pl.ds(step * (CHUNK // UNIT), CHUNK // UNIT)
        gquery_ref[tiles] = in_tiles((norm_back(unit, scale, norms[0:1, :], grad) + gres[rows, :]).astype(BF))
        sums[0:8, :] += fold_rows(grad * unit)
        sums[8:16, :] += fold_rows(grad)
        other_core(mine_b, theirs_b, sems_b, step).wait_recv()
        grad = mine_b[rows, :].astype(F32) + theirs_b[rows, :].astype(F32)
        unit, scale = normalise(kv[rows, :].astype(F32))
        gkv_ref[tiles] = in_tiles(norm_back(unit, scale, norms[2:3, :], grad).astype(BF))
        sums[16:24, :] += fold_rows(grad * unit)
        sums[24:32, :] += fold_rows(grad)
    middle = tokens // 4 * 3
    chunks(middle, close)
    more.relay()
    chunks(tokens, close, middle)
    parts = [sums[8 * i:8 * i + 8, :] for i in range(4)]
    parts += [sums_c[0:8, :], sums_c[8:16, :], sums_f[0:8, :], sums_f[8:16, :]]
    norm_mine[...] = jnp.concatenate([jnp.sum(part, 0, keepdims=True) for part in parts], 0)
    for copy in plane_copies:
        copy.wait_recv()
    for level in range(across):
        pieces[level] = four_sum((source.at[0], landing.at[1], landing.at[2], landing.at[3]), level)
    z_copies = z_sum_start(devices, places, pieces, landed, z_sems)
    n_copies = [send(norm_mine, norm_all.at[d], n_sems.at[0, d], n_sems.at[1, d], dp=other)
                for d, other in zip(range(1, devices), others)]
    turn_rows(gquery_ref, turned_a, info[0, DOCS + 1])
    more.diagonal()
    last_ref[0, 0] = z_sum_end(places, pieces, landed, z_copies)
    last = Spread(places, last_ref, *spread_sems[5:], direct=True)
    last.start()
    turn_rows(gkv_ref, turned_b, info[0, DOCS + 1])
    turned = Late([(turned_a, gquery_out), (turned_b, gkv_out)], out_sems)
    last.relay()
    last.diagonal()
    total = norm_mine[...]
    for d, copy in zip(range(1, devices), n_copies):
        copy.wait_recv()
        total = total + norm_all[d]
    gnorm_ref[...] = total
    more.finish()
    last.finish()
    more.drain()
    last.drain()
    for copy in more_copies + plane_copies + z_copies + n_copies:
        copy.wait_send()
    turned.wait(0, 1)
    drain(tokens, mine_a, theirs_a, sems_a)
    drain(tokens, mine_b, theirs_b, sems_b)


def self_back(devices, ready_rows, info, dq, dk, dv, ws, nq, nkv, query, kv, gres, norms, sums_c, sums_f, more_in, parts):
    tokens, features = nq.shape
    cols = dq.shape[1]
    across, more_rows = devices // 4, more_in.shape[1] + parts[0].shape[1] - ready_rows
    flat_rows = whole_blocks(3 * cols, devices)
    rows = flat_rows // devices
    wide = (tokens, features)
    outs = [(wide, BF, "A"), (wide, BF, "A"), ((4, across, rows, features), BF, "V"), ((4, across, more_rows, features), BF, "V"),
            ((8, features), F32, "V")]
    low, high = pltpu.VMEM(wide, BF), pltpu.VMEM(wide, F32)
    small, tiny = pltpu.VMEM((across, more_rows, features), BF), pltpu.VMEM((across, rows, features), BF)
    four = pltpu.VMEM((4, across, rows, features), BF)
    D = pltpu.SemaphoreType.DMA
    tiles = pltpu.VMEM((tokens // UNIT, UNIT, features), BF)
    scratch = [low, low, low, low, high, tiles, tiles, low, low, pltpu.VMEM((flat_rows, features), BF), four, four, tiny, tiny, small, small,
               pltpu.VMEM((8, features), F32), pltpu.VMEM((devices, 8, features), F32)]
    scratch += [low] * 4 + [pltpu.VMEM((32, features), F32)] + [pair_sems(tokens)] * 2
    scratch += [D((5,)), D((2,)), D((2, across)), D((2, across)), D((2, 4)), D((2, devices)),
                pltpu.VMEM((4, across, more_rows - more_in.shape[1], features), BF), D((4,))]
    scratch += [D((2, across))] * 10
    return call(partial(self_back_kernel, devices, ready_rows), "self_back",
                [info, dq, dk, dv, ws, nq, nkv, query, kv, gres, norms, sums_c, sums_f, more_in] + parts, "SVVVVAAAAAVVVVAAAA", outs, scratch, 5)


def update_kernel(devices, firsts, late_rows, more_first, held, me_ref, *refs):
    norm_grads, *norm_in = refs[:4]
    hbm, (grad_out, first_out, second_out, new_out, gquery_out, gkv_out) = refs[4:15], refs[15:21]
    norm_out, vmem = refs[21:25], refs[25:36]
    last, more, part0, part1, part2, part3, master, first, second, held_q, held_kv = vmem
    taken, grad_ref, first_ref, second_ref, new_ref, sems, out_sems = refs[36:]
    entering = Late(list(zip(hbm, vmem)), sems)
    share = norm_in[0].shape[1]
    if share % 128 == 0:
        at = me_ref[0] * share
        features = norm_grads.shape[1]
        norm_grad = norm_grads[pl.ds(lax.div(at, features), 1), pl.ds(pl.multiple_of(lax.rem(at, features), 128), share)]
        norm_values = (norm_grad,) + adamw_step(norm_grad, *(ref[...] for ref in norm_in), RATE_NORM, 0.0)
        for ref, value in zip(norm_out, norm_values):
            ref[...] = value
    else:
        for ref in norm_out:
            ref[...] = jnp.zeros_like(ref)
    slots = master.shape[0]
    across = devices // 4
    me = me_ref[0]
    here, level = lax.rem(me, 4), lax.div(me, 4)
    count = held[0, 127]
    results = list(zip((grad_ref, first_ref, second_ref, new_ref), (grad_out, first_out, second_out, new_out)))
    entering.wait(9, 10)
    leaving = Late([(held_q, gquery_out), (held_kv, gkv_out)], out_sems.at[0])
    entering.wait(*range(9))

    def lookup(row, size, start=0):
        block = lax.div(row, size)
        behind = lax.rem(level - lax.div(block, 4) + across, across)
        return lax.rem(block, 4) ^ here, behind, pl.ds(pl.multiple_of(lax.rem(row, size) + start, UNIT), UNIT)

    def one(slot, carry):
        @pl.when(slot < count)
        def _():
            unit = held[0, slot]

            @pl.when(unit < firsts[0])
            def _():
                taken[...] = last[lookup(unit * UNIT, last.shape[2])]

            @pl.when((unit >= firsts[0]) & (unit < firsts[1]))
            def _():
                taken[...] = more[lookup((unit - firsts[0]) * UNIT, more_first)]

            @pl.when((unit >= firsts[1]) & (unit < firsts[2]))
            def _():
                taken[...] = more[lookup((unit - firsts[1]) * UNIT, more.shape[2] - more_first, more_first)]

            @pl.when(unit >= firsts[2])
            def _():
                offset, behind, rows = lookup((unit - firsts[2]) * UNIT, late_rows)
                for f, part in enumerate((part0, part1, part2, part3)):
                    @pl.when(offset == f)
                    def _():
                        taken[...] = part[behind, rows]
            gradient = taken[...].astype(F32)
            first_new, second_new, weight = adamw_step(gradient, first[slot], second[slot], master[slot], RATE_MATRIX, WEIGHT_DECAY)
            grad_ref[slot] = gradient
            first_ref[slot] = first_new
            second_ref[slot] = second_new
            new_ref[slot] = weight

        @pl.when(slot >= count)
        def _():
            for ref in (grad_ref, first_ref, second_ref, new_ref):
                ref[slot] = jnp.zeros(ref.shape[1:], F32)
        return carry
    half = slots // 2
    lax.fori_loop(0, half, one, 0)
    early = Late([(ref.at[pl.ds(0, half)], out.at[pl.ds(0, half)]) for ref, out in results], out_sems.at[1])
    lax.fori_loop(half, slots, one, 0)
    rest = Late([(ref.at[pl.ds(half, half)], out.at[pl.ds(half, half)]) for ref, out in results], out_sems.at[2])
    for copies in (early, rest):
        copies.wait(*range(4))
    leaving.wait(0, 1)


def update(devices, firsts, late_rows, more_first, held, me, norm_args, last, more, parts, master, first, second, gquery, gkv):
    outs = [(master.shape, F32, "A")] * 4 + [(gquery.shape, BF, "A")] * 2 + [(norm_args[1].shape, F32, "V")] * 4
    args = [last, more] + parts + [master, first, second, gquery, gkv]
    scratch = [pltpu.VMEM(arg.shape, arg.dtype) for arg in args] + [pltpu.VMEM((UNIT, master.shape[2]), BF)]
    scratch += [pltpu.VMEM(master.shape, F32)] * 4 + [pltpu.SemaphoreType.DMA((11,)), pltpu.SemaphoreType.DMA((3, 4))]
    return call(partial(update_kernel, devices, firsts, late_rows, more_first), "update", [held, me] + norm_args + args, "SSVVVV" + "A" * 11,
                outs, scratch)


def adamw_step(gradient, first, second, weight, rate, decay):
    first_new = BETA_ONE * first + (1.0 - BETA_ONE) * gradient
    second_new = BETA_TWO * second + (1.0 - BETA_TWO) * gradient * gradient
    corr_one = 1.0 - BETA_ONE**STEP
    corr_two = 1.0 - BETA_TWO**STEP
    direction = first_new / corr_one / (jnp.sqrt(second_new / corr_two) + ADAM_EPS)
    return (first_new, second_new, weight - rate * (direction + decay * weight))


def local(
    query_stream, kv_stream, memory, out_grad, lengths, obs_rank, obs_count, unit_owner,
    master, first_moment, second_moment, norm_master, norm_first, norm_second,
):
    devices = lax.axis_size("dp")
    shards = lax.axis_size("head")
    me = lax.axis_index("dp")
    slots, unit_rows, features = master.shape[0], master.shape[2], master.shape[3]
    units = unit_owner.shape[0]
    norm_share = norm_master.shape[0]
    cols = features // shards
    hidden = (units * unit_rows - 8 * cols) // 2

    shape = (slots, unit_rows, features)
    norm_row = norm_master.reshape(1, norm_share)
    if norm_share % 128:
        norm_row = lax.dynamic_update_slice(jnp.zeros((1, features), F32), norm_row, (0, lax.rem(me * norm_share, features)))
    rank_row, count_row = obs_rank.reshape(1, ROW), obs_count.reshape(1, ROW)
    place_of, held, rank_row, count_row, steps, info = plan(unit_owner, lengths, me.reshape(1), rank_row, count_row, slots)
    nq, nkv, qt, k, kt, v, vt, kc, kct, vc, vct, query, kv, source, cotangent, ws, wc, wo_self, wo_cross, w1, w2, norms, *tables = project(
        devices, place_of, info, master.reshape(shape), norm_row, rank_row, query_stream, kv_stream, memory, out_grad, cols, hidden)
    mixed_self, mixed_self_t, total_self = attend_forward(steps, qt, k, vt, tables, count_row, True)
    residual, nc, qct = self_out(mixed_self, wo_self, query, wc, norms)
    mixed_cross, mixed_cross_t, total_cross = attend_forward(steps, qct, kc, vct, tables, count_row, False)
    output, grad_cross_res, grad_mixed, *parts, sums_f = feed_forward(
        devices, mixed_cross, wo_cross, residual, w1, w2, cotangent, norms)
    tie = lax.optimization_barrier
    ready_rows = parts[0].shape[1]
    parts = [parts[0]] + [plane_swap(parts[f], devices, f) for f in (1, 2, 3)]
    dq, dk, dv = attend_backward(steps, qct, kc, kct, vc, grad_mixed, mixed_cross_t, total_cross, tables, count_row, [], False)
    parts, dq = tie((parts, dq))
    grad_memory, output, grad_residual, grad_mixed, *parts, more, sums_c = cross_back(
        devices, info, dq, dk, dv, wc, nc, source, residual, grad_cross_res, output, mixed_self, wo_self, norms, parts)
    parts = [parts[0]] + [plane_swap(parts[f], devices, f) for f in (1, 2, 3)]
    dq, dk, dv, grad_memory, output = attend_backward(
        steps, qt, k, kt, v, grad_mixed, mixed_self_t, total_self, tables, count_row, [grad_memory, output], True)
    parts, dq = tie((parts, dq))
    more_first = more.shape[1]
    grad_query, grad_kv, last, more, norm_grads = self_back(
        devices, ready_rows, info, dq, dk, dv, ws, nq, nkv, query, kv, grad_residual, norms, sums_c, sums_f, more, parts)

    firsts = [count * cols // unit_rows for count in (3, 6, 7)]
    norm_args = [norm_grads] + [value.reshape(1, norm_share) for value in (norm_first, norm_second, norm_master)]
    weight_grad, weight_first, weight_second, weight_new, grad_query, grad_kv, *norm_results = update(
        devices, firsts, ready_rows, more_first, held, me.reshape(1), norm_args, last, more, parts, master.reshape(shape),
        first_moment.reshape(shape), second_moment.reshape(shape), grad_query, grad_kv)
    weight_grad, weight_first, weight_second, weight_new = [
        part.reshape(master.shape) for part in (weight_grad, weight_first, weight_second, weight_new)]
    if norm_share % 128 == 0:
        norm_grad, norm_first_new, norm_second_new, norm_new = [value.reshape(norm_share) for value in norm_results]
    else:
        norm_grad = lax.dynamic_slice_in_dim(norm_grads.reshape(-1), me * norm_share, norm_share)
        norm_first_new, norm_second_new, norm_new = adamw_step(
            norm_grad, norm_first, norm_second, norm_master, RATE_NORM, 0.0)
    return (
        output, grad_query, grad_kv, grad_memory, weight_grad, weight_first, weight_second, weight_new,
        norm_grad, norm_first_new, norm_second_new, norm_new,
    )


def solution(mesh):
    in_specs = (
        P("dp", None),
        P("dp", None),
        P("dp", None),
        P("dp", None),
        P("dp", None),
        P("dp"),
        P("dp"),
        P(),
        P("dp", "head", None, None),
        P("dp", "head", None, None),
        P("dp", "head", None, None),
        P("dp"),
        P("dp"),
        P("dp"),
    )
    out_specs = (
        P("dp", None),
        P("dp", None),
        P("dp", None),
        P("dp", None),
        P("dp", "head", None, None),
        P("dp", "head", None, None),
        P("dp", "head", None, None),
        P("dp", "head", None, None),
        P("dp"),
        P("dp"),
        P("dp"),
        P("dp"),
    )
    return jax.shard_map(local, mesh=mesh, in_specs=in_specs, out_specs=out_specs, check_vma=False)
```
